32 devices in a mesh: seq: 4 (over z), wide: 8 (over y, x, core).
Axes of the slice: x: 2, y: 2, z: 4, core: 2. Of those that a mesh axis runs over, the one named last changes fastest.
Arguments:
- layer_input: bfloat16 [8192, 8192], P(('wide', 'seq')), may hold values from -6 to 6
- head_inputs: bfloat16 [8192, 8192], P(('wide', 'seq')), may hold values from -6 to 6
- output_grad: bfloat16 [8192, 8192], P(('wide', 'seq')), may hold values from -6 to 6
- step_raw: bfloat16 [8192, 128], P(('wide', 'seq'))
- state_write: bfloat16 [8192, 64], P(('wide', 'seq')), may hold values from -5 to 5
- state_read: bfloat16 [8192, 64], P(('wide', 'seq')), may hold values from -5 to 5
- decay_log: float32 [128], replicated
- step_bias: float32 [128], replicated, may hold values from -1 to 0.5
- skip_gain: float32 [128], replicated, may hold values from 0.5 to 1.5
Outputs:
- grad_x: bfloat16 [8192, 8192], P(('wide', 'seq'))
- weight_grad: float32 [8192, 256], P(('seq', 'wide'))
The draws below stay inside these ranges and needn't reach their ends.
All inputs are finite; a program needn't handle non-finite values.
Results may differ from the reference program's by a relative error of at most 0.0029.
Values may be sent and summed in bfloat16 or wider, within the bound.
No kernel may reach another device: no remote copies, remote signals or barrier semaphores. Data moves between devices by JAX's collectives and lax.ppermute only.
A program may use at most 384 MiB of HBM per device.

```python
import math
import jax
import jax.numpy as jnp
from jax import lax

MODEL = 8192
HEADS = 128
HEAD_DIM = 64
STATE = 64
SPAN = 256
TOK_DEV = 256
TOKENS = 8192


def draw_step_raw(key, part):
    key = jax.random.fold_in(key, 23)
    jitter_key, offset_key = jax.random.split(key)
    blocks = TOKENS // TOK_DEV
    offset = jax.random.uniform(offset_key, (blocks, 1, 1), minval=-1.2, maxval=1.2)
    jitter = jax.random.normal(jitter_key, (blocks, TOK_DEV, HEADS))
    return (jitter + offset).reshape(TOKENS, HEADS).astype(jnp.float32).astype(jnp.bfloat16)


def draw_decay_log(key, part):
    key = jax.random.fold_in(key, 37)
    mark_key, slow_key, fast_key = jax.random.split(key, 3)
    slow_share = 0.5
    slow_heads = jax.random.uniform(mark_key, (HEADS,)) < slow_share
    slow_value = jnp.log(0.3 / TOKENS) + jax.random.uniform(slow_key, (HEADS,)) * jnp.log(1.0 / 0.3)
    fast_value = jnp.log(1.0 / 40.0) + jax.random.uniform(fast_key, (HEADS,)) * jnp.log(40.0 / 15.0)
    return jnp.where(slow_heads, slow_value, fast_value).astype(jnp.float32)


def spiked(drawn, own_key, source, target, blocks, factor):
    owner, partner = [(jnp.arange(drawn.shape[position]) // (drawn.shape[position] // blocks)).reshape([-1 if axis == position else 1 for axis in range(drawn.ndim)]) for position in (source, target)]
    chosen = jax.random.permutation(own_key, blocks)[partner]
    strong = (owner == chosen) | (owner == (partner + blocks // 2) % blocks)
    return jnp.where(strong, factor * drawn, drawn)


def steps_of(own_key, shape, cuts, low, top_value):
    factor_of, own = 1.0, jax.random.fold_in(own_key, 6)
    for dim, shards_of in cuts:
        heights = jnp.exp(jax.random.uniform(jax.random.fold_in(own, dim), (shards_of,), jnp.float32, low / len(cuts), top_value / len(cuts)))
        factor_of = factor_of * jnp.repeat(heights, shape[dim] // shards_of).reshape([-1 if axis == dim else 1 for axis in range(len(shape))])
    return factor_of


def centred(stream_key, dims, scale, most, cuts=(), dtype=jnp.bfloat16):
    entries = scale * jax.random.normal(stream_key, dims, jnp.float32)
    if cuts:
        entries = entries * steps_of(stream_key, dims, cuts, -0.22, 0.18)
    return jnp.clip(entries, -most, most).astype(dtype)


def bell_draw_with(rng, dims, scale, most, cuts, heavy, held_as=jnp.bfloat16):
    entries = scale * jax.random.normal(rng, dims, jnp.float32)
    if cuts:
        entries = entries * steps_of(rng, dims, cuts, -0.22, 0.18)
    return jnp.clip(spiked(entries, jax.random.fold_in(rng, 3), *heavy), -most, most).astype(held_as)


def setup_inputs(seed: int = 0) -> dict:
    seeds = jax.random.split(jax.random.key(seed), 10)
    return {
        "layer_input": bell_draw_with(seeds[0], (TOKENS, MODEL), 1.0, 6.0, ((0, 32),), (0, 1, 32, 2.75)),
        "head_inputs": centred(seeds[1], (TOKENS, HEADS * HEAD_DIM), 1.0, 6.0, ((0, 32),)),
        "output_grad": centred(seeds[2], (TOKENS, HEADS * HEAD_DIM), 1.0, 6.0, ((0, 32),)),
        "step_raw": draw_step_raw(jax.random.fold_in(seeds[9], 71), 0),
        "state_write": centred(seeds[4], (TOKENS, STATE), 1.0, 5.0, ((0, 32),)),
        "state_read": centred(seeds[5], (TOKENS, STATE), 1.0, 5.0, ((0, 32),)),
        "decay_log": draw_decay_log(jax.random.fold_in(seeds[9], 71), 0),
        "step_bias": jnp.clip(jax.random.uniform(seeds[7], (HEADS,), jnp.float32, -1.0, 0.5), -1.0, 0.5),
        "skip_gain": jnp.clip(jax.random.uniform(seeds[8], (HEADS,), jnp.float32, 0.5, 1.5), 0.5, 1.5),
    }


PRECISE = lax.Precision.HIGHEST

def summarize(inputs, cotangent, step_size, cumulative, write_rows, read_rows):
    finish = cumulative[-1]
    to_end = jnp.exp(finish[None, :] - cumulative)
    forward_state = jnp.einsum('qhp,qn->hpn', (to_end * step_size)[:, :, None] * inputs, write_rows, precision=PRECISE)
    backward_state = jnp.einsum('qhp,qn->hpn', jnp.exp(cumulative)[:, :, None] * cotangent, read_rows, precision=PRECISE)
    return (finish, forward_state, backward_state)

def span_grads(inputs, cotangent, step_size, cumulative, write_rows, read_rows, start_state, end_grad, decay_rate, skip_weight):
    finish = cumulative[-1]
    to_end = jnp.exp(finish[None, :] - cumulative)
    from_start = jnp.exp(cumulative)
    length = cumulative.shape[0]
    row_pos = lax.broadcasted_iota(jnp.int32, (length, length), 0)
    col_pos = lax.broadcasted_iota(jnp.int32, (length, length), 1)
    causal = (row_pos >= col_pos)[None]
    strict = (row_pos > col_pos)[None]
    spread = cumulative.T[:, :, None] - cumulative.T[:, None, :]
    decay_mask = jnp.exp(jnp.where(causal, spread, -1e+30))
    read_write = jnp.dot(read_rows, write_rows.T, precision=PRECISE)
    grad_input = jnp.einsum('jhp,khp->hjk', cotangent, inputs, precision=PRECISE)
    weighted = decay_mask * grad_input * step_size.T[:, None, :]
    carried_write = jnp.einsum('hpn,kn->khp', end_grad, write_rows, precision=PRECISE)
    state_write = jnp.einsum('hjk,jhp->khp', decay_mask * read_write[None], cotangent, precision=PRECISE) + to_end[:, :, None] * carried_write
    grad_inputs = step_size[:, :, None] * state_write + skip_weight[None, :, None] * cotangent
    write_grad = jnp.einsum('hjk,jn->kn', weighted, read_rows, precision=PRECISE) + jnp.einsum('khp,hpn->kn', (step_size * to_end)[:, :, None] * inputs, end_grad, precision=PRECISE)
    read_grad = jnp.einsum('hjk,kn->jn', weighted, write_rows, precision=PRECISE) + jnp.einsum('jhp,hpn->jn', from_start[:, :, None] * cotangent, start_state, precision=PRECISE)
    pair_terms = jnp.where(strict, weighted * read_write[None], 0.0)
    net_flow = (lax.optimization_barrier(jnp.sum(pair_terms, axis=1)) - lax.optimization_barrier(jnp.sum(pair_terms, axis=2))).T
    within = jnp.cumsum(net_flow, axis=0) - net_flow
    start_read = jnp.einsum('hpn,jn->jhp', start_state, read_rows, precision=PRECISE)
    from_past = from_start * lax.optimization_barrier(jnp.sum(cotangent * start_read, axis=2))
    to_future = step_size * to_end * lax.optimization_barrier(jnp.sum(inputs * carried_write, axis=2))
    through = jnp.exp(finish) * lax.optimization_barrier(jnp.sum(end_grad * start_state, axis=(1, 2)))
    past_total = jnp.flip(jnp.cumsum(jnp.flip(from_past, 0), axis=0), 0)
    future_total = jnp.cumsum(to_future, axis=0) - to_future
    decay_grad = within + past_total + future_total + through[None, :]
    step_grad = lax.optimization_barrier(jnp.sum(inputs * state_write, axis=2)) + decay_rate[None, :] * decay_grad
    return (grad_inputs, write_grad, read_grad, step_grad)

def reference(layer_input, head_inputs, output_grad, step_raw, state_write, state_read, decay_log, step_bias, skip_gain):
    span_count = TOKENS // SPAN
    state_scale = float(TOKENS * STATE) ** (-0.25)
    decay_rate = -jnp.exp(decay_log)
    shifted = step_raw.astype(jnp.float32) + step_bias[None, :]
    step_size = jax.nn.softplus(shifted)
    input_blocks = head_inputs.reshape(span_count, SPAN, HEADS, HEAD_DIM)
    grad_blocks = output_grad.reshape(span_count, SPAN, HEADS, HEAD_DIM)
    step_blocks = step_size.reshape(span_count, SPAN, HEADS)
    write_blocks = (state_write.astype(jnp.float32) * state_scale).reshape(span_count, SPAN, STATE)
    read_blocks = (state_read.astype(jnp.float32) * state_scale).reshape(span_count, SPAN, STATE)

    def forward(carry_state, pieces):
        inputs, cotangent, step_part, write_part, read_part = pieces
        cumulative = jnp.cumsum(step_part * decay_rate[None, :], axis=0)
        finish, forward_state, backward_state = summarize(inputs.astype(jnp.float32), cotangent.astype(jnp.float32), step_part, cumulative, write_part, read_part)
        return (jnp.exp(finish)[:, None, None] * carry_state + forward_state, carry_state)
    zero_state = jnp.zeros((HEADS, HEAD_DIM, STATE), jnp.float32)
    final_state, starts = lax.scan(forward, zero_state, (input_blocks, grad_blocks, step_blocks, write_blocks, read_blocks))

    def backward(end_grad, pieces):
        inputs, cotangent, step_part, write_part, read_part, start_state = pieces
        cumulative = jnp.cumsum(step_part * decay_rate[None, :], axis=0)
        input_float = inputs.astype(jnp.float32)
        grad_float = cotangent.astype(jnp.float32)
        finish, forward_state, backward_state = summarize(input_float, grad_float, step_part, cumulative, write_part, read_part)
        results = span_grads(input_float, grad_float, step_part, cumulative, write_part, read_part, start_state, end_grad, decay_rate, skip_gain)
        return (jnp.exp(finish)[:, None, None] * end_grad + backward_state, results)
    first_grad, results = lax.scan(backward, zero_state, (input_blocks, grad_blocks, step_blocks, write_blocks, read_blocks, starts), reverse=True)
    grad_inputs, write_grad, read_grad, step_grad = results
    grad_x = grad_inputs.reshape(TOKENS, HEADS * HEAD_DIM).astype(jnp.bfloat16)
    raw_grad = (step_grad.reshape(TOKENS, HEADS) * jax.nn.sigmoid(shifted)).astype(jnp.bfloat16)
    grad_table = jnp.concatenate([raw_grad, (write_grad.reshape(TOKENS, STATE) * state_scale).astype(jnp.bfloat16), (read_grad.reshape(TOKENS, STATE) * state_scale).astype(jnp.bfloat16)], axis=1)
    weight_grad = jnp.dot(layer_input.T, grad_table, preferred_element_type=jnp.float32) / math.sqrt(TOKENS)
    return (grad_x, weight_grad)
```

```python
import functools
import math

import jax
import jax.numpy as jnp
from jax import lax
from jax.experimental import pallas as pl
from jax.experimental.pallas import tpu as pltpu
from jax.sharding import PartitionSpec as P

F32 = jnp.float32
BF16 = jnp.bfloat16
EXACT = lax.Precision.HIGHEST
VMEM_LIMIT = 56 * 1024 * 1024
TOP_POWER = 30.0
PRODUCT_BOUND = 30.0
CARRY_HEADS = 16
PAIR_HEADS = 8


def mul(a, b):
    return lax.dot_general(a, b, (((1,), (0,)), ((), ())), preferred_element_type=F32)


def mul_nt(a, b):
    return lax.dot_general(a, b, (((1,), (1,)), ((), ())), preferred_element_type=F32)


def mul_exact(a, b, dims=((1,), (0,))):
    return lax.dot_general(a, b, (dims, ((), ())), preferred_element_type=F32, precision=EXACT)


def halves(value):
    top = value.astype(BF16)
    return top, (value - top.astype(F32)).astype(BF16)


def power_scale(bound):
    power = jnp.floor(TOP_POWER - jnp.log2(jnp.maximum(bound, 1e-37)))
    return jnp.exp2(jnp.clip(power, -100.0, 100.0))


def encode(value):
    square = value * value
    fourth = square * square
    return jnp.where(value < 0, -fourth, fourth).astype(BF16)


def decode(coded):
    coded = coded.astype(F32)
    size = jnp.maximum(jnp.abs(coded), 1e-37)
    inverse = lax.rsqrt(size)
    return coded * inverse * lax.rsqrt(size * inverse)


def head_selector(first_head, heads, lanes, head_width):
    row = lax.broadcasted_iota(jnp.int32, (heads, lanes), 0)
    lane = lax.broadcasted_iota(jnp.int32, (heads, lanes), 1)
    return jnp.where(row == first_head + lane // head_width, 1.0, 0.0).astype(BF16)


def triangle(length, keep):
    row = lax.broadcasted_iota(jnp.int32, (length, length), 0)
    col = lax.broadcasted_iota(jnp.int32, (length, length), 1)
    return jnp.where(keep(row, col), 1.0, 0.0).astype(F32)


def summary_kernel(
    head_width,
    raw_ref,
    bias_ref,
    decay_ref,
    write_ref,
    read_ref,
    x_ref,
    dy_ref,
    message_ref,
    step_ref,
    cum_ref,
    fact_ref,
    write_t,
    read_t,
    weight_f,
    weight_b,
):
    turn = pl.program_id(0)
    heads = raw_ref.shape[1]
    rows, lanes = x_ref.shape
    state = write_ref.shape[1]

    @pl.when(turn == 0)
    def _():
        step = jax.nn.softplus(raw_ref[...].astype(F32) + bias_ref[...])
        rate = -jnp.exp(decay_ref[...])
        cum = mul_exact(triangle(rows, lambda r, c: r >= c), step * rate)
        finish = cum[rows - 1 : rows, :]
        forward = step * jnp.exp(finish - cum)
        backward = jnp.exp(cum)
        scale_f = power_scale(PRODUCT_BOUND * jnp.sum(forward, axis=0, keepdims=True))
        scale_b = power_scale(PRODUCT_BOUND * jnp.sum(backward, axis=0, keepdims=True))
        step_ref[...] = step
        cum_ref[...] = cum
        fact_ref[...] = jnp.concatenate(
            [finish, scale_f, scale_b, jnp.zeros((5, heads), F32)], axis=0
        )
        top, low = halves(forward * scale_f)
        weight_f[...] = jnp.concatenate([top, low], axis=1)
        top, low = halves(backward * scale_b)
        weight_b[...] = jnp.concatenate([top, low], axis=1)
        write_t[...] = write_ref[...].astype(F32).T.astype(BF16)
        read_t[...] = read_ref[...].astype(F32).T.astype(BF16)

    pick = head_selector(turn * (lanes // head_width), heads, lanes, head_width)
    pick = jnp.concatenate([pick, pick], axis=0)

    def summed(tokens_ref, weight, rows_t, start):
        top, low = halves(tokens_ref[...].astype(F32) * mul(weight[...], pick))
        coded = encode(mul(rows_t[...], top) + mul(rows_t[...], low))
        width = message_ref.shape[2]
        for owner in range(message_ref.shape[0]):
            message_ref[owner, start : start + state, :] = coded[
                :, owner * width : (owner + 1) * width
            ]

    summed(x_ref, weight_f, write_t, 0)
    summed(dy_ref, weight_b, read_t, state)


def table_kernel(blocks, fact_ref, table_ref):
    heads = fact_ref.shape[2]
    finish = fact_ref[0]
    decay = jnp.exp(finish)
    table_ref[0] = decay
    table_ref[1] = 1.0 / fact_ref[1]
    table_ref[2] = 1.0 / fact_ref[2]
    top = 2.0**TOP_POWER

    def forward(block, bound):
        here = pl.ds(block, 1)
        table_ref[3, here, :] = power_scale(bound)
        return table_ref[0, here, :] * bound + top * table_ref[1, here, :]

    def backward(turn, bound):
        here = pl.ds(blocks - 1 - turn, 1)
        table_ref[4, here, :] = power_scale(bound)
        return table_ref[0, here, :] * bound + top * table_ref[2, here, :]

    lax.fori_loop(0, blocks, forward, jnp.zeros((1, heads), F32))
    lax.fori_loop(0, blocks, backward, jnp.zeros((1, heads), F32))


def scan_kernel(table_ref, message_ref, answer_ref):
    blocks, double, lanes = message_ref.shape
    state = double // 2

    def forward(block, running):
        here = pl.ds(block, 1)
        answer_ref[block, 0:state, :] = encode(running * table_ref[3, here, :])
        own = decode(message_ref[block, 0:state, :]) * table_ref[1, here, :]
        return running * table_ref[0, here, :] + own

    def backward(turn, running):
        block = blocks - 1 - turn
        here = pl.ds(block, 1)
        answer_ref[block, state:double, :] = encode(running * table_ref[4, here, :])
        own = decode(message_ref[block, state:double, :]) * table_ref[2, here, :]
        return running * table_ref[0, here, :] + own

    lax.fori_loop(0, blocks, forward, jnp.zeros((state, lanes), F32))
    lax.fori_loop(0, blocks, backward, jnp.zeros((state, lanes), F32))


def block_kernel(
    head_width,
    scale,
    step_ref,
    cum_ref,
    write_ref,
    read_ref,
    x_ref,
    dy_ref,
    inner_ref,
    own_ref,
    within_ref,
    maps_ref,
    read_write,
    source,
    cum_rows,
    pair_sum,
    out_flow,
):
    turn = pl.program_id(0)
    rows, lanes = x_ref.shape
    half = rows // 2
    heads = step_ref.shape[1]
    group = lanes // head_width

    @pl.when(turn == 0)
    def _():
        flow = scale * mul_nt(write_ref[...], read_ref[...])
        read_write[...] = flow
        source[...] = jnp.log(step_ref[...]) - cum_ref[...]
        cum_rows[...] = cum_ref[...].T
        pair_sum[...] = jnp.zeros_like(pair_sum)
        own_ref[...] = jnp.zeros_like(own_ref)

    shift = lax.rem(heads - turn * group, heads)
    near = pltpu.roll(source[...], shift, axis=1)
    near_cum = cum_rows[pl.ds(turn * group, group), :]
    row = lax.broadcasted_iota(jnp.int32, (half, half), 0)
    col = lax.broadcasted_iota(jnp.int32, (half, half), 1)
    ahead = col >= row
    lane = lax.broadcasted_iota(jnp.int32, (half, 2 * head_width), 1)
    first_half = lane < head_width
    head_lane = lax.broadcasted_iota(jnp.int32, (half, heads), 1)
    flow_aa = read_write[0:half, 0:half]
    flow_ab = read_write[0:half, half:rows]
    flow_bb = read_write[half:rows, half:rows]
    sum_aa = jnp.zeros((half, half), F32)
    sum_ab = jnp.zeros((half, half), F32)
    sum_bb = jnp.zeros((half, half), F32)
    own_a = jnp.zeros((half, heads), F32)
    own_b = jnp.zeros((half, heads), F32)
    zero = jnp.zeros((half, 2 * head_width), BF16)
    flows = []
    for pair in range(group // 2):
        span = slice(pair * 2 * head_width, (pair + 1) * 2 * head_width)
        x_a, x_b = x_ref[0:half, span], x_ref[half:rows, span]
        dy_a, dy_b = dy_ref[0:half, span], dy_ref[half:rows, span]
        early_a, late_a = jnp.where(first_half, dy_a, zero), jnp.where(first_half, zero, dy_a)
        early_b, late_b = jnp.where(first_half, dy_b, zero), jnp.where(first_half, zero, dy_b)
        stack = jnp.concatenate([early_a, early_b, late_a, late_b], axis=0)
        stack_b = jnp.concatenate([early_b, late_b], axis=0)
        grad_a = mul_nt(x_a, stack)
        grad_b = mul_nt(x_b, stack_b)
        masks_a, masks_b = [], []
        for side in range(2):
            place = pair * 2 + side
            head = turn * group + place
            from_a = near[0:half, place : place + 1]
            from_b = near[half:rows, place : place + 1]
            to_a = near_cum[place : place + 1, 0:half]
            to_b = near_cum[place : place + 1, half:rows]
            fade_aa = jnp.exp(jnp.where(ahead, to_a + from_a, -1e30))
            fade_ab = jnp.exp(to_b + from_a)
            fade_bb = jnp.exp(jnp.where(ahead, to_b + from_b, -1e30))
            weigh_aa = fade_aa * grad_a[:, side * rows : side * rows + half]
            weigh_ab = fade_ab * grad_a[:, side * rows + half : (side + 1) * rows]
            weigh_bb = fade_bb * grad_b[:, side * half : (side + 1) * half]
            sum_aa += weigh_aa
            sum_ab += weigh_ab
            sum_bb += weigh_bb
            masks_a += [(fade_aa * flow_aa).astype(BF16), (fade_ab * flow_ab).astype(BF16)]
            masks_b += [(fade_bb * flow_bb).astype(BF16)]
            pair_aa = weigh_aa * flow_aa
            pair_ab = weigh_ab * flow_ab
            pair_bb = weigh_bb * flow_bb
            flow_out = jnp.sum(pair_aa + pair_ab, axis=1, keepdims=True)
            own_a = jnp.where(head_lane == head, flow_out, own_a)
            flow_out = jnp.sum(pair_bb, axis=1, keepdims=True)
            own_b = jnp.where(head_lane == head, flow_out, own_b)
            flow_in = [
                jnp.sum(pair_aa, axis=0, keepdims=True),
                jnp.sum(pair_ab, axis=0, keepdims=True) + jnp.sum(pair_bb, axis=0, keepdims=True),
            ]
            flows.append(jnp.concatenate(flow_in, axis=1))
        inner_ref[0:half, span] = mul(jnp.concatenate(masks_a, axis=1), stack).astype(BF16)
        inner_ref[half:rows, span] = mul(jnp.concatenate(masks_b, axis=1), stack_b).astype(BF16)
    out_flow[pl.ds(turn * group, group), :] = jnp.concatenate(flows, axis=0)
    pair_sum[0:half, 0:half] += sum_aa
    pair_sum[0:half, half:rows] += sum_ab
    pair_sum[half:rows, half:rows] += sum_bb
    own_ref[0:half, :] += own_a
    own_ref[half:rows, :] += own_b

    @pl.when(turn == pl.num_programs(0) - 1)
    def _():
        net = own_ref[...] - out_flow[...].T
        within_ref[...] = mul_exact(triangle(rows, lambda r, c: r > c), net)
        weighted = scale * pair_sum[...]
        maps_ref[...] = jnp.concatenate(
            [
                mul_exact(weighted, read_ref[...].astype(F32)),
                mul_exact(weighted, write_ref[...].astype(F32), ((0,), (0,))),
            ],
            axis=1,
        )


def carry_kernel(
    head_width,
    scale,
    raw_ref,
    bias_ref,
    decay_ref,
    step_ref,
    cum_ref,
    scale_ref,
    write_ref,
    read_ref,
    skip_ref,
    within_ref,
    maps_ref,
    own_ref,
    x_ref,
    dy_ref,
    inner_ref,
    answer_ref,
    grad_ref,
    table_ref,
    weight_e,
    weight_s,
    future,
    past,
    through,
    write_sum,
    read_sum,
):
    turn = pl.program_id(0)
    rows, lanes = x_ref.shape
    heads = step_ref.shape[1]
    state = write_ref.shape[1]

    @pl.when(turn == 0)
    def _():
        cum = cum_ref[...]
        finish = cum[rows - 1 : rows, :]
        top, low = halves(step_ref[...] * jnp.exp(finish - cum) * (scale / scale_ref[1:2, :]))
        weight_e[...] = jnp.concatenate([top, low], axis=1)
        top, low = halves(jnp.exp(cum) * (scale / scale_ref[0:1, :]))
        weight_s[...] = jnp.concatenate([top, low], axis=1)
        future[...] = jnp.zeros_like(future)
        past[...] = jnp.zeros_like(past)
        through[...] = jnp.zeros_like(through)
        write_sum[...] = jnp.zeros_like(write_sum)
        read_sum[...] = jnp.zeros_like(read_sum)

    pick = head_selector(turn * (lanes // head_width), heads, lanes, head_width)
    pick_twice = jnp.concatenate([pick, pick], axis=0)
    pieces = range(answer_ref.shape[0])
    start = jnp.concatenate([decode(answer_ref[p, 0:state, :]) for p in pieces], axis=1)
    end = jnp.concatenate([decode(answer_ref[p, state : 2 * state, :]) for p in pieces], axis=1)
    start_parts = jnp.concatenate(halves(start), axis=0)
    end_parts = jnp.concatenate(halves(end), axis=0)
    x = x_ref[...].astype(F32)
    dy = dy_ref[...].astype(F32)

    spread_e = mul(weight_e[...], pick_twice)
    write_twice = jnp.concatenate([write_ref[...], write_ref[...]], axis=1)
    carried = mul(write_twice, end_parts) * spread_e
    grad_ref[...] = (inner_ref[...].astype(F32) + skip_ref[...] * dy + carried).astype(BF16)
    top, low = halves(x * carried)
    future[...] += mul_nt(top, pick) + mul_nt(low, pick)
    top, low = halves(x * spread_e)
    write_sum[...] += mul_nt(top, end_parts) + mul_nt(low, end_parts)

    spread_s = mul(weight_s[...], pick_twice)
    read_twice = jnp.concatenate([read_ref[...], read_ref[...]], axis=1)
    weighted = dy * spread_s
    top, low = halves(weighted * mul(read_twice, start_parts))
    past[...] += mul_nt(top, pick) + mul_nt(low, pick)
    top, low = halves(weighted)
    read_sum[...] += mul_nt(top, start_parts) + mul_nt(low, start_parts)

    both = jnp.sum(start * end, axis=0, keepdims=True)
    both = jnp.broadcast_to(both, (8, lanes))
    top, low = halves(both)
    through[...] += mul_nt(top, pick) + mul_nt(low, pick)

    @pl.when(turn == pl.num_programs(0) - 1)
    def _():
        shifted = raw_ref[...].astype(F32) + bias_ref[...]
        rate = -jnp.exp(decay_ref[...])
        step = step_ref[...]
        gate = jax.nn.sigmoid(shifted)
        finish = cum_ref[rows - 1 : rows, :]
        crossing = jnp.exp(finish) * scale * (through[0:1, :] / scale_ref[0:1, :])
        decay_grad = (
            within_ref[...]
            + mul_exact(triangle(rows, lambda r, c: r <= c), past[...])
            + mul_exact(triangle(rows, lambda r, c: r > c), future[...])
            + crossing / scale_ref[1:2, :]
        )
        ratio = jnp.where(step > 1e-30, gate / jnp.maximum(step, 1e-30), 1.0)
        raw_grad = (own_ref[...] + future[...]) * ratio + rate * decay_grad * gate
        maps = maps_ref[...]
        write_all = write_sum[:, 0:state] + write_sum[:, state : 2 * state] + maps[:, 0:state]
        read_all = read_sum[:, 0:state] + read_sum[:, state : 2 * state] + maps[:, state:]
        table_ref[...] = jnp.concatenate([raw_grad, write_all, read_all], axis=1).astype(BF16)


def whole(shape):
    return pl.BlockSpec(shape, lambda i: (0,) * len(shape))


def call(kernel, grid, in_specs, out_specs, out_shape, scratch, cost):
    return pl.pallas_call(
        kernel,
        grid=grid,
        in_specs=in_specs,
        out_specs=out_specs,
        out_shape=out_shape,
        scratch_shapes=scratch,
        compiler_params=pltpu.CompilerParams(vmem_limit_bytes=VMEM_LIMIT),
        cost_estimate=cost,
    )


def body(
    layer_input,
    head_inputs,
    output_grad,
    step_raw,
    state_write,
    state_read,
    decay_log,
    step_bias,
    skip_gain,
):
    rows, channels = head_inputs.shape
    heads = step_raw.shape[1]
    head_width = channels // heads
    state = state_write.shape[1]
    axes = ("wide", "seq")
    blocks = lax.axis_size("wide") * lax.axis_size("seq")
    place = lax.axis_index("wide") * lax.axis_size("seq") + lax.axis_index("seq")
    scale = float(rows * blocks * state) ** -0.5
    owner_lanes = channels // blocks
    piece_lanes = max(owner_lanes, 128)
    pieces = channels // piece_lanes
    bias = step_bias[None, :]
    decay = decay_log[None, :]
    skip = jnp.repeat(skip_gain, head_width)[None, :]

    def shape(dims, dtype=F32):
        return jax.ShapeDtypeStruct(dims, dtype)

    lanes = CARRY_HEADS * head_width
    here = lanes // piece_lanes
    token_spec = pl.BlockSpec((rows, lanes), lambda i: (0, i))
    message_spec = pl.BlockSpec((here, 2 * state, piece_lanes), lambda i: (i, 0, 0))
    head_spec = whole((rows, heads))
    line_spec = whole((1, heads))
    map_spec = whole((rows, state))
    with jax.named_scope("summaries"):
        message, step, cum, fact = call(
            functools.partial(summary_kernel, head_width),
            (channels // lanes,),
            [head_spec, line_spec, line_spec, map_spec, map_spec, token_spec, token_spec],
            [message_spec, head_spec, head_spec, whole((8, heads))],
            [
                shape((pieces, 2 * state, piece_lanes), BF16),
                shape((rows, heads)),
                shape((rows, heads)),
                shape((8, heads)),
            ],
            [
                pltpu.VMEM((state, rows), BF16),
                pltpu.VMEM((state, rows), BF16),
                pltpu.VMEM((rows, 2 * heads), BF16),
                pltpu.VMEM((rows, 2 * heads), BF16),
            ],
            pl.CostEstimate(
                flops=8 * rows * channels * state, bytes_accessed=10 * 2**20, transcendentals=0
            ),
        )(step_raw, bias, decay, state_write, state_read, head_inputs, output_grad)

    def to_owner(array):
        if owner_lanes < piece_lanes:
            split = array.reshape(pieces, 2 * state, piece_lanes // owner_lanes, owner_lanes)
            array = jnp.moveaxis(split, 2, 1).reshape(blocks, 2 * state, owner_lanes)
        return array

    def from_owner(array):
        if owner_lanes < piece_lanes:
            split = array.reshape(pieces, piece_lanes // owner_lanes, 2 * state, owner_lanes)
            array = jnp.moveaxis(split, 1, 2).reshape(pieces, 2 * state, piece_lanes)
        return array

    with jax.named_scope("scan"):
        facts = lax.all_gather(fact, axes)
        arrived = lax.all_to_all(to_owner(message), axes, split_axis=0, concat_axis=0, tiled=True)
        table = pl.pallas_call(
            functools.partial(table_kernel, blocks), out_shape=shape((5, blocks, heads))
        )(jnp.moveaxis(facts[:, 0:3, :], 1, 0))
        owned = heads // blocks
        own_table = lax.dynamic_slice_in_dim(table, place * owned, owned, 2)
        own_table = jnp.repeat(own_table, head_width, axis=2)
        own_scale = lax.dynamic_slice_in_dim(table[3:5], place, 1, 1)[:, 0, :]
        answer = call(
            scan_kernel,
            (1,),
            [whole((5, blocks, owner_lanes)), whole((blocks, 2 * state, owner_lanes))],
            whole((blocks, 2 * state, owner_lanes)),
            shape((blocks, 2 * state, owner_lanes), BF16),
            [],
            pl.CostEstimate(flops=2**22, bytes_accessed=4 * 2**20, transcendentals=0),
        )(own_table, arrived)
        returned = lax.all_to_all(answer, axes, split_axis=0, concat_axis=0, tiled=True)
        returned = from_owner(returned)

    pair_lanes = PAIR_HEADS * head_width
    pair_spec = pl.BlockSpec((rows, pair_lanes), lambda i: (0, i))
    with jax.named_scope("own_block"):
        inner, own, within, maps = call(
            functools.partial(block_kernel, head_width, scale),
            (channels // pair_lanes,),
            [head_spec, head_spec, map_spec, map_spec, pair_spec, pair_spec],
            [pair_spec, head_spec, head_spec, whole((rows, 2 * state))],
            [
                shape((rows, channels), BF16),
                shape((rows, heads)),
                shape((rows, heads)),
                shape((rows, 2 * state)),
            ],
            [
                pltpu.VMEM((rows, rows), F32),
                pltpu.VMEM((rows, heads), F32),
                pltpu.VMEM((heads, rows), F32),
                pltpu.VMEM((rows, rows), F32),
                pltpu.VMEM((heads, rows), F32),
            ],
            pl.CostEstimate(
                flops=16 * rows * rows * channels,
                bytes_accessed=12 * 2**20,
                transcendentals=rows * rows * heads,
            ),
        )(step, cum, state_write, state_read, head_inputs, output_grad)

    with jax.named_scope("carried"):
        grad_x, grad_table = call(
            functools.partial(carry_kernel, head_width, scale),
            (channels // lanes,),
            [
                head_spec,
                line_spec,
                line_spec,
                head_spec,
                head_spec,
                whole((2, heads)),
                map_spec,
                map_spec,
                pl.BlockSpec((1, lanes), lambda i: (0, i)),
                head_spec,
                whole((rows, 2 * state)),
                head_spec,
                token_spec,
                token_spec,
                token_spec,
                message_spec,
            ],
            [token_spec, whole((rows, heads + 2 * state))],
            [shape((rows, channels), BF16), shape((rows, heads + 2 * state), BF16)],
            [
                pltpu.VMEM((rows, 2 * heads), BF16),
                pltpu.VMEM((rows, 2 * heads), BF16),
                pltpu.VMEM((rows, heads), F32),
                pltpu.VMEM((rows, heads), F32),
                pltpu.VMEM((8, heads), F32),
                pltpu.VMEM((rows, 2 * state), F32),
                pltpu.VMEM((rows, 2 * state), F32),
            ],
            pl.CostEstimate(
                flops=32 * rows * channels * state, bytes_accessed=18 * 2**20, transcendentals=0
            ),
        )(
            step_raw,
            bias,
            decay,
            step,
            cum,
            own_scale,
            state_write,
            state_read,
            skip,
            within,
            maps,
            own,
            head_inputs,
            output_grad,
            inner,
            returned,
        )
    with jax.named_scope("projection"):
        weight_grad = lax.psum_scatter(
            lax.dot_general(
                layer_input,
                grad_table,
                (((0,), (0,)), ((), ())),
                preferred_element_type=F32,
            ),
            ("seq", "wide"),
            scatter_dimension=0,
            tiled=True,
        )
    return (grad_x, weight_grad / math.sqrt(rows * blocks))


def solution(mesh):
    in_specs = (
        P(("wide", "seq"), None),
        P(("wide", "seq"), None),
        P(("wide", "seq"), None),
        P(("wide", "seq"), None),
        P(("wide", "seq"), None),
        P(("wide", "seq"), None),
        P(),
        P(),
        P(),
    )
    out_specs = (P(("wide", "seq"), None), P(("seq", "wide"), None))
    return jax.shard_map(body, mesh=mesh, in_specs=in_specs, out_specs=out_specs, check_vma=False)
```

```python
import functools
import math

import jax
import jax.numpy as jnp
from jax import lax
from jax.experimental import pallas as pl
from jax.experimental.pallas import tpu as pltpu
from jax.sharding import PartitionSpec as P

F32 = jnp.float32
BF16 = jnp.bfloat16
EXACT = lax.Precision.HIGHEST
VMEM_LIMIT = 56 * 1024 * 1024
TOP_POWER = 30.0
PRODUCT_BOUND = 30.0
CARRY_HEADS = 16
PAIR_HEADS = 8
META = 16
HALVES = 2


def mul(a, b):
    return lax.dot_general(a, b, (((1,), (0,)), ((), ())), preferred_element_type=F32)


def mul_nt(a, b):
    return lax.dot_general(a, b, (((1,), (1,)), ((), ())), preferred_element_type=F32)


def mul_exact(a, b, dims=((1,), (0,))):
    return lax.dot_general(a, b, (dims, ((), ())), preferred_element_type=F32, precision=EXACT)


def halves(value):
    top = value.astype(BF16)
    return top, (value - top.astype(F32)).astype(BF16)


def power_for(bound):
    power = jnp.floor(TOP_POWER - jnp.log2(jnp.maximum(bound, 1e-37)))
    return jnp.clip(power, -100.0, 100.0)


def thirds(value):
    top, rest = value.astype(BF16), value
    rest = rest - top.astype(F32)
    middle = rest.astype(BF16)
    return top, middle, (rest - middle.astype(F32)).astype(BF16)


def encode(value):
    square = value * value
    fourth = square * square
    return jnp.where(value < 0, -fourth, fourth).astype(BF16)


def decode(coded):
    coded = coded.astype(F32)
    size = jnp.maximum(jnp.abs(coded), 1e-37)
    inverse = lax.rsqrt(size)
    return coded * inverse * lax.rsqrt(size * inverse)


def head_selector(first_head, heads, lanes, head_width):
    row = lax.broadcasted_iota(jnp.int32, (heads, lanes), 0)
    lane = lax.broadcasted_iota(jnp.int32, (heads, lanes), 1)
    return jnp.where(row == first_head + lane // head_width, 1.0, 0.0).astype(BF16)


def triangle(length, keep):
    row = lax.broadcasted_iota(jnp.int32, (length, length), 0)
    col = lax.broadcasted_iota(jnp.int32, (length, length), 1)
    return jnp.where(keep(row, col), 1.0, 0.0).astype(F32)


def summary_kernel(
    head_width,
    first_head,
    raw_ref,
    bias_ref,
    decay_ref,
    write_ref,
    read_ref,
    x_ref,
    dy_ref,
    message_ref,
    step_ref,
    cum_ref,
    weight_f,
    weight_b,
    facts,
):
    turn = pl.program_id(0)
    heads = raw_ref.shape[1]
    rows, lanes = x_ref.shape
    state = write_ref.shape[0]

    @pl.when(turn == 0)
    def _():
        step = jax.nn.softplus(raw_ref[...].astype(F32) + bias_ref[...])
        rate = -jnp.exp(decay_ref[...])
        cum = mul_exact(triangle(rows, lambda r, c: r >= c), step * rate)
        finish = cum[rows - 1 : rows, :]
        forward = step * jnp.exp(finish - cum)
        backward = jnp.exp(cum)
        power_f = power_for(PRODUCT_BOUND * jnp.sum(forward, axis=0, keepdims=True))
        power_b = power_for(PRODUCT_BOUND * jnp.sum(backward, axis=0, keepdims=True))
        step_ref[...] = step
        cum_ref[...] = cum
        parts = thirds(jnp.maximum(finish, -1e30))
        facts[...] = jnp.concatenate(
            [part.astype(F32) for part in parts]
            + [power_f, power_b, jnp.zeros((META - 5, heads), F32)],
            axis=0,
        ).astype(BF16)
        top, low = halves(forward * jnp.exp2(power_f))
        weight_f[...] = jnp.concatenate([top, low], axis=1)
        top, low = halves(backward * jnp.exp2(power_b))
        weight_b[...] = jnp.concatenate([top, low], axis=1)

    pick = head_selector(first_head + turn * (lanes // head_width), heads, lanes, head_width)
    pick_twice = jnp.concatenate([pick, pick], axis=0)
    width = message_ref.shape[2]

    def put(start, value):
        for owner in range(message_ref.shape[0]):
            message_ref[owner, start : start + value.shape[0], :] = value[
                :, owner * width : (owner + 1) * width
            ]

    def summed(tokens_ref, weight, rows_t):
        top, low = halves(tokens_ref[...].astype(F32) * mul(weight[...], pick_twice))
        return encode(mul(rows_t[...], top) + mul(rows_t[...], low))

    put(0, summed(x_ref, weight_f, write_ref))
    put(state, summed(dy_ref, weight_b, read_ref))
    put(2 * state, mul(facts[...], pick).astype(BF16))


def scan_kernel(message_ref, answer_ref, powers):
    blocks, double, lanes = message_ref.shape
    state = (double - META) // 2
    top = 2.0**TOP_POWER

    def one(block, start, power_row, side, running, bound):
        facts = message_ref[block, 2 * state : double, :].astype(F32)
        decay = jnp.exp(facts[0:1] + facts[1:2] + facts[2:3])
        back = jnp.exp2(-facts[power_row : power_row + 1])
        power = power_for(bound)
        powers[side, pl.ds(block, 1), :] = power
        answer_ref[block, start : start + state, :] = encode(running * jnp.exp2(power))
        own = decode(message_ref[block, start : start + state, :]) * back
        return running * decay + own, bound * decay + top * back

    def both(block, carry):
        ahead, ahead_bound, behind, behind_bound = carry
        return one(block, 0, 3, 0, ahead, ahead_bound) + one(
            blocks - 1 - block, state, 4, 1, behind, behind_bound
        )

    zero, none = jnp.zeros((state, lanes), F32), jnp.zeros((1, lanes), F32)
    lax.fori_loop(0, blocks, both, (zero, none, zero, none), unroll=4)
    row = lax.broadcasted_iota(jnp.int32, (blocks, META, lanes), 1)
    ahead, behind = powers[0][:, None, :], powers[1][:, None, :]
    meta = jnp.where(row == 0, ahead, jnp.where(row == 1, behind, 0.0))
    answer_ref[:, 2 * state : double, :] = meta.astype(BF16)


def block_kernel(
    head_width,
    scale,
    first_head,
    step_ref,
    cum_ref,
    write_ref,
    read_ref,
    x_ref,
    dy_ref,
    inner_ref,
    own_ref,
    within_ref,
    maps_ref,
    read_write,
    source,
    cum_rows,
    pair_sum,
    out_flow,
):
    turn = pl.program_id(0)
    rows, lanes = x_ref.shape
    half = rows // 2
    heads = step_ref.shape[1]
    group = lanes // head_width

    @pl.when(turn == 0)
    def _():
        read_write[...] = scale * lax.dot_general(
            write_ref[...], read_ref[...], (((0,), (0,)), ((), ())), preferred_element_type=F32
        )
        source[...] = jnp.log(step_ref[...]) - cum_ref[...]
        cum_rows[...] = cum_ref[...].T
        pair_sum[...] = jnp.zeros_like(pair_sum)
        out_flow[...] = jnp.zeros_like(out_flow)
        own_ref[...] = jnp.zeros_like(own_ref)

    first = first_head + turn * group
    near = pltpu.roll(source[...], lax.rem(heads - first, heads), axis=1)
    near_cum = cum_rows[pl.ds(first, group), :]
    row = lax.broadcasted_iota(jnp.int32, (half, half), 0)
    col = lax.broadcasted_iota(jnp.int32, (half, half), 1)
    ahead = col >= row
    lane = lax.broadcasted_iota(jnp.int32, (half, 2 * head_width), 1)
    first_half = lane < head_width
    head_lane = lax.broadcasted_iota(jnp.int32, (half, heads), 1)
    flow_aa = read_write[0:half, 0:half]
    flow_ab = read_write[0:half, half:rows]
    flow_bb = read_write[half:rows, half:rows]
    sum_aa = jnp.zeros((half, half), F32)
    sum_ab = jnp.zeros((half, half), F32)
    sum_bb = jnp.zeros((half, half), F32)
    own_a = jnp.zeros((half, heads), F32)
    own_b = jnp.zeros((half, heads), F32)
    zero = jnp.zeros((half, 2 * head_width), BF16)
    flows = []
    for pair in range(group // 2):
        span = slice(pair * 2 * head_width, (pair + 1) * 2 * head_width)
        x_a, x_b = x_ref[0:half, span], x_ref[half:rows, span]
        dy_a, dy_b = dy_ref[0:half, span], dy_ref[half:rows, span]
        early_a, late_a = jnp.where(first_half, dy_a, zero), jnp.where(first_half, zero, dy_a)
        early_b, late_b = jnp.where(first_half, dy_b, zero), jnp.where(first_half, zero, dy_b)
        stack = jnp.concatenate([early_a, early_b, late_a, late_b], axis=0)
        stack_b = jnp.concatenate([early_b, late_b], axis=0)
        grad_a = mul_nt(x_a, stack)
        grad_b = mul_nt(x_b, stack_b)
        masks_a, masks_b = [], []
        for side in range(2):
            place = pair * 2 + side
            head = first + place
            from_a = near[0:half, place : place + 1]
            from_b = near[half:rows, place : place + 1]
            to_a = near_cum[place : place + 1, 0:half]
            to_b = near_cum[place : place + 1, half:rows]
            fade_aa = jnp.exp(jnp.where(ahead, to_a + from_a, -1e30))
            fade_ab = jnp.exp(to_b + from_a)
            fade_bb = jnp.exp(jnp.where(ahead, to_b + from_b, -1e30))
            weigh_aa = fade_aa * grad_a[:, side * rows : side * rows + half]
            weigh_ab = fade_ab * grad_a[:, side * rows + half : (side + 1) * rows]
            weigh_bb = fade_bb * grad_b[:, side * half : (side + 1) * half]
            sum_aa += weigh_aa
            sum_ab += weigh_ab
            sum_bb += weigh_bb
            masks_a += [(fade_aa * flow_aa).astype(BF16), (fade_ab * flow_ab).astype(BF16)]
            masks_b += [(fade_bb * flow_bb).astype(BF16)]
            pair_aa = weigh_aa * flow_aa
            pair_ab = weigh_ab * flow_ab
            pair_bb = weigh_bb * flow_bb
            flow_out = jnp.sum(pair_aa + pair_ab, axis=1, keepdims=True)
            own_a = jnp.where(head_lane == head, flow_out, own_a)
            flow_out = jnp.sum(pair_bb, axis=1, keepdims=True)
            own_b = jnp.where(head_lane == head, flow_out, own_b)
            flow_in = [
                jnp.sum(pair_aa, axis=0, keepdims=True),
                jnp.sum(pair_ab, axis=0, keepdims=True) + jnp.sum(pair_bb, axis=0, keepdims=True),
            ]
            flows.append(jnp.concatenate(flow_in, axis=1))
        inner_ref[0:half, span] = mul(jnp.concatenate(masks_a, axis=1), stack).astype(BF16)
        inner_ref[half:rows, span] = mul(jnp.concatenate(masks_b, axis=1), stack_b).astype(BF16)
    out_flow[pl.ds(first, group), :] = jnp.concatenate(flows, axis=0)
    pair_sum[0:half, 0:half] += sum_aa
    pair_sum[0:half, half:rows] += sum_ab
    pair_sum[half:rows, half:rows] += sum_bb
    own_ref[0:half, :] += own_a
    own_ref[half:rows, :] += own_b

    @pl.when(turn == pl.num_programs(0) - 1)
    def _():
        net = own_ref[...] - out_flow[...].T
        within_ref[...] = mul_exact(triangle(rows, lambda r, c: r > c), net)
        weighted = scale * pair_sum[...]
        maps_ref[...] = jnp.concatenate(
            [
                mul_exact(weighted, read_ref[...].astype(F32), ((1,), (1,))),
                mul_exact(weighted, write_ref[...].astype(F32), ((0,), (1,))),
            ],
            axis=1,
        )


def carry_kernel(head_width, scale, first_head, parts, first, last, *refs):
    refs = list(refs)
    take = lambda count: [refs.pop(0) for _ in range(count)]
    raw_ref, bias_ref, decay_ref, step_ref, cum_ref, write_ref, read_ref, skip_ref = take(8)
    x_ref, dy_ref, inner_ref, answer_ref = take(4)
    if not first:
        early_sums, early_through, _ = take(3)
    if last:
        own_refs, within_refs, map_refs = take(parts), take(parts), take(parts)
        grad_ref, table_ref, sums, through, weight_e, weight_s, maps = take(7)
    else:
        grad_ref, sums, through, weight_e, weight_s, maps = take(6)
    turn = pl.program_id(0)
    rows, lanes = x_ref.shape
    heads = step_ref.shape[1]
    state = write_ref.shape[0]
    future, past = slice(0, heads), slice(heads, 2 * heads)
    write_sum = slice(2 * heads, 2 * heads + 2 * state)
    read_sum = slice(2 * heads + 2 * state, 2 * heads + 4 * state)

    @pl.when(turn == 0)
    def _():
        cum = cum_ref[...]
        finish = cum[rows - 1 : rows, :]
        top, low = halves(step_ref[...] * jnp.exp(finish - cum) * scale)
        weight_e[...] = jnp.concatenate([top, low], axis=1)
        top, low = halves(jnp.exp(cum) * scale)
        weight_s[...] = jnp.concatenate([top, low], axis=1)
        write = write_ref[...].astype(F32).T.astype(BF16)
        read = read_ref[...].astype(F32).T.astype(BF16)
        maps[...] = jnp.concatenate([write, write, read, read], axis=1)
        if first:
            sums[...] = jnp.zeros_like(sums)
            through[...] = jnp.zeros_like(through)
        else:
            sums[...] = early_sums[...]
            through[...] = early_through[...]

    pick = head_selector(first_head + turn * (lanes // head_width), heads, lanes, head_width)
    pick_twice = jnp.concatenate([pick, pick], axis=0)
    starts, ends = [], []
    for piece in range(answer_ref.shape[0]):
        back = jnp.exp2(-answer_ref[piece, 2 * state : 2 * state + META, :].astype(F32))
        starts.append(decode(answer_ref[piece, 0:state, :]) * back[0:1])
        ends.append(decode(answer_ref[piece, state : 2 * state, :]) * back[1:2])
    start = jnp.concatenate(starts, axis=1)
    end = jnp.concatenate(ends, axis=1)
    start_parts = jnp.concatenate(halves(start), axis=0)
    end_parts = jnp.concatenate(halves(end), axis=0)
    x = x_ref[...].astype(F32)
    dy = dy_ref[...].astype(F32)
    skip = jnp.concatenate(
        [part.astype(F32) for part in thirds(skip_ref[...])] + [jnp.zeros((13, heads), F32)], axis=0
    )
    skip = jnp.sum(mul(skip.astype(BF16), pick), axis=0, keepdims=True)

    spread_e = mul(weight_e[...], pick_twice)
    carried = mul(maps[:, 0 : 2 * state], end_parts) * spread_e
    grad_ref[...] = (inner_ref[...].astype(F32) + skip * dy + carried).astype(BF16)
    top, low = halves(x * carried)
    sums[:, future] += mul_nt(top, pick) + mul_nt(low, pick)
    top, low = halves(x * spread_e)
    sums[:, write_sum] += mul_nt(top, end_parts) + mul_nt(low, end_parts)

    weighted = dy * mul(weight_s[...], pick_twice)
    top, low = halves(weighted * mul(maps[:, 2 * state : 4 * state], start_parts))
    sums[:, past] += mul_nt(top, pick) + mul_nt(low, pick)
    top, low = halves(weighted)
    sums[:, read_sum] += mul_nt(top, start_parts) + mul_nt(low, start_parts)

    both = jnp.broadcast_to(jnp.sum(start * end, axis=0, keepdims=True), (8, lanes))
    top, low = halves(both)
    through[...] += mul_nt(top, pick) + mul_nt(low, pick)

    if not last:
        return

    @pl.when(turn == pl.num_programs(0) - 1)
    def _():
        rate = -jnp.exp(decay_ref[...])
        step = step_ref[...]
        gate = jax.nn.sigmoid(raw_ref[...].astype(F32) + bias_ref[...])
        finish = cum_ref[rows - 1 : rows, :]
        to_come = sums[:, future]
        decay_grad = (
            sum(ref[...] for ref in within_refs)
            + mul_exact(triangle(rows, lambda r, c: r <= c), sums[:, past])
            + mul_exact(triangle(rows, lambda r, c: r > c), to_come)
            + jnp.exp(finish) * scale * through[0:1, :]
        )
        ratio = jnp.where(step > 1e-30, gate / jnp.maximum(step, 1e-30), 1.0)
        inner = sum(ref[...] for ref in own_refs) + to_come
        raw_grad = inner * ratio + rate * decay_grad * gate
        map_sum = sums[:, 2 * heads :] + 0.0
        write_all = map_sum[:, 0:state] + map_sum[:, state : 2 * state]
        read_all = map_sum[:, 2 * state : 3 * state] + map_sum[:, 3 * state :]
        map_grad = jnp.concatenate([write_all, read_all], axis=1)
        map_grad += sum(ref[...] for ref in map_refs)
        table_ref[...] = jnp.concatenate([raw_grad.T, map_grad.T], axis=0).astype(BF16)


def projection_kernel(table_ref, layer_ref, out_ref):
    product = mul(table_ref[...], layer_ref[...])
    width = out_ref.shape[2]
    for piece in range(out_ref.shape[0]):
        out_ref[piece, :, :] = product[:, piece * width : (piece + 1) * width]


def whole(shape):
    return pl.BlockSpec(shape, lambda i: (0,) * len(shape))


def call(kernel, steps, in_specs, out, scratch, flops, bytes_accessed, aliases=None):
    return pl.pallas_call(
        kernel,
        grid=(steps,),
        in_specs=in_specs,
        out_specs=[spec for spec, _, _ in out],
        out_shape=[jax.ShapeDtypeStruct(dims, dtype) for _, dims, dtype in out],
        scratch_shapes=[pltpu.VMEM(dims, dtype) for dims, dtype in scratch],
        compiler_params=pltpu.CompilerParams(vmem_limit_bytes=VMEM_LIMIT),
        cost_estimate=pl.CostEstimate(
            flops=flops, bytes_accessed=bytes_accessed, transcendentals=0
        ),
        input_output_aliases=aliases or {},
    )


def body(
    layer_input,
    head_inputs,
    output_grad,
    step_raw,
    state_write,
    state_read,
    decay_log,
    step_bias,
    skip_gain,
):
    rows, channels = head_inputs.shape
    heads = step_raw.shape[1]
    head_width = channels // heads
    state = state_write.shape[1]
    model = layer_input.shape[1]
    columns = heads + 2 * state
    axes = ("wide", "seq")
    blocks = lax.axis_size("wide") * lax.axis_size("seq")
    scale = float(rows * blocks * state) ** -0.5
    parts = HALVES if heads % (HALVES * blocks) == 0 else 1
    part_heads = heads // parts
    part_lanes = channels // parts
    owner_lanes = part_lanes // blocks
    piece_lanes = max(owner_lanes, 128)
    pieces = part_lanes // piece_lanes
    depth = 2 * state + META
    bias = step_bias[None, :]
    decay = decay_log[None, :]
    skip = skip_gain[None, :]
    write_t, read_t = state_write.T, state_read.T

    lanes = CARRY_HEADS * head_width
    steps = part_lanes // lanes
    here = lanes // piece_lanes

    def tokens(part, width):
        first = part * (part_lanes // width)
        return pl.BlockSpec((rows, width), lambda i: (0, first + i))

    message_spec = pl.BlockSpec((here, depth, piece_lanes), lambda i: (i, 0, 0))
    head_spec = whole((rows, heads))
    line_spec = whole((1, heads))
    map_spec = whole((state, rows))
    head_out = (head_spec, (rows, heads), F32)

    def summaries(part):
        return call(
            functools.partial(summary_kernel, head_width, part * part_heads),
            steps,
            [head_spec, line_spec, line_spec, map_spec, map_spec]
            + [tokens(part, lanes), tokens(part, lanes)],
            [(message_spec, (pieces, depth, piece_lanes), BF16), head_out, head_out],
            [((rows, 2 * heads), BF16), ((rows, 2 * heads), BF16), ((META, heads), BF16)],
            8 * rows * part_lanes * state,
            10 * 2**20 // parts,
        )(step_raw, bias, decay, write_t, read_t, head_inputs, output_grad)

    def exchange(array):
        return lax.all_to_all(array, axes, split_axis=0, concat_axis=0, tiled=True)

    def to_owner(array):
        if owner_lanes < piece_lanes:
            split = array.reshape(pieces, depth, piece_lanes // owner_lanes, owner_lanes)
            array = jnp.moveaxis(split, 2, 1).reshape(blocks, depth, owner_lanes)
        return exchange(array)

    def from_owner(array):
        array = exchange(array)
        if owner_lanes < piece_lanes:
            split = array.reshape(pieces, piece_lanes // owner_lanes, depth, owner_lanes)
            array = jnp.moveaxis(split, 1, 2).reshape(pieces, depth, piece_lanes)
        return array

    def scan(message):
        spec = whole((blocks, depth, owner_lanes))
        (answer,) = call(
            scan_kernel,
            1,
            [spec],
            [(spec, (blocks, depth, owner_lanes), BF16)],
            [((2, blocks, owner_lanes), F32)],
            2**22,
            4 * 2**20 // parts,
        )(message)
        return answer

    def own_block(part, step, cum):
        width = PAIR_HEADS * head_width
        part_spec = pl.BlockSpec((rows, width), lambda i: (0, i))
        return call(
            functools.partial(block_kernel, head_width, scale, part * part_heads),
            part_lanes // width,
            [head_spec, head_spec, map_spec, map_spec, tokens(part, width), tokens(part, width)],
            [
                (part_spec, (rows, part_lanes), BF16),
                head_out,
                head_out,
                (whole((rows, 2 * state)), (rows, 2 * state), F32),
            ],
            [
                ((rows, rows), F32),
                ((rows, heads), F32),
                ((heads, rows), F32),
                ((rows, rows), F32),
                ((heads, rows), F32),
            ],
            16 * rows * rows * part_lanes,
            12 * 2**20 // parts,
        )(step, cum, write_t, read_t, head_inputs, output_grad)

    with jax.named_scope("summaries"):
        summed = [summaries(part) for part in range(parts)]
    step, cum = summed[0][1:]
    with jax.named_scope("own_block"):
        own_parts = [own_block(part, step, cum) for part in range(parts)]
    with jax.named_scope("scan"):
        returned = [from_owner(scan(to_owner(one[0]))) for one in summed]

    sums_out = (whole((rows, 2 * heads + 4 * state)), (rows, 2 * heads + 4 * state), F32)
    through_out = (whole((8, heads)), (8, heads), F32)
    early = ()
    with jax.named_scope("carried"):
        for part in range(parts):
            first, last = part == 0, part == parts - 1
            in_specs = [head_spec, line_spec, line_spec, head_spec, head_spec, map_spec, map_spec]
            in_specs += [line_spec, tokens(part, lanes), tokens(part, lanes)]
            in_specs += [pl.BlockSpec((rows, lanes), lambda i: (0, i)), message_spec]
            operands = [step_raw, bias, decay, step, cum, write_t, read_t, skip]
            operands += [head_inputs, output_grad, own_parts[part][0], returned[part]]
            aliases = {}
            if not first:
                in_specs += [sums_out[0], through_out[0], pl.BlockSpec(memory_space=pl.ANY)]
                operands += [early[1], early[2], early[0]]
                aliases = {len(operands) - 1: 0}
            scratch = [((rows, 2 * heads), BF16)] * 2 + [((rows, 4 * state), BF16)]
            out = [(tokens(part, lanes), (rows, channels), BF16)]
            if last:
                for which in (1, 2, 3):
                    operands += [one[which] for one in own_parts]
                    in_specs += [whole(one[which].shape) for one in own_parts]
                out += [(whole((columns, rows)), (columns, rows), BF16)]
                scratch = [sums_out[1:], through_out[1:]] + scratch
            else:
                out += [sums_out, through_out]
            early = call(
                functools.partial(
                    carry_kernel, head_width, scale, part * part_heads, parts, first, last
                ),
                steps,
                in_specs,
                out,
                scratch,
                32 * rows * part_lanes * state,
                18 * 2**20 // parts,
                aliases,
            )(*operands)
    grad_x, table = early

    with jax.named_scope("projection"):
        own_model = model // blocks
        model_lanes = max(own_model, min(model, 1024))
        (product,) = call(
            projection_kernel,
            model // model_lanes,
            [whole((columns, rows)), pl.BlockSpec((rows, model_lanes), lambda i: (0, i))],
            [
                (
                    pl.BlockSpec((model_lanes // own_model, columns, own_model), lambda i: (i, 0, 0)),
                    (blocks, columns, own_model),
                    F32,
                )
            ],
            [],
            2 * rows * model * columns,
            12 * 2**20,
        )(table, layer_input)
        weight_grad = lax.psum_scatter(
            product, ("seq", "wide"), scatter_dimension=0, tiled=True
        )
    return (grad_x, weight_grad[0].T / math.sqrt(rows * blocks))


def solution(mesh):
    in_specs = (
        P(("wide", "seq"), None),
        P(("wide", "seq"), None),
        P(("wide", "seq"), None),
        P(("wide", "seq"), None),
        P(("wide", "seq"), None),
        P(("wide", "seq"), None),
        P(),
        P(),
        P(),
    )
    out_specs = (P(("wide", "seq"), None), P(("seq", "wide"), None))
    return jax.shard_map(body, mesh=mesh, in_specs=in_specs, out_specs=out_specs, check_vma=False)
```

```python
import functools
import math

import jax
import jax.numpy as jnp
from jax import lax
from jax.experimental import pallas as pl
from jax.experimental.pallas import tpu as pltpu
from jax.sharding import PartitionSpec as P

F32 = jnp.float32
BF16 = jnp.bfloat16
EXACT = lax.Precision.HIGHEST
VMEM_LIMIT = 56 * 1024 * 1024
TOP_POWER = 30.0
PRODUCT_BOUND = 30.0
CARRY_HEADS = 16
PAIR_HEADS = 8
META = 16
HALVES = 2


def mul(a, b):
    return lax.dot_general(a, b, (((1,), (0,)), ((), ())), preferred_element_type=F32)


def mul_nt(a, b):
    return lax.dot_general(a, b, (((1,), (1,)), ((), ())), preferred_element_type=F32)


def mul_exact(a, b, dims=((1,), (0,))):
    return lax.dot_general(a, b, (dims, ((), ())), preferred_element_type=F32, precision=EXACT)


def halves(value):
    top = value.astype(BF16)
    return top, (value - top.astype(F32)).astype(BF16)


def power_for(bound):
    power = jnp.floor(TOP_POWER - jnp.log2(jnp.maximum(bound, 1e-37)))
    return jnp.clip(power, -100.0, 100.0)


def thirds(value):
    top, rest = value.astype(BF16), value
    rest = rest - top.astype(F32)
    middle = rest.astype(BF16)
    return top, middle, (rest - middle.astype(F32)).astype(BF16)


def encode(value):
    square = value * value
    fourth = square * square
    return jnp.where(value < 0, -fourth, fourth).astype(BF16)


def decode(coded):
    coded = coded.astype(F32)
    size = jnp.maximum(jnp.abs(coded), 1e-37)
    inverse = lax.rsqrt(size)
    return coded * inverse * lax.rsqrt(size * inverse)


def head_selector(first_head, heads, lanes, head_width):
    row = lax.broadcasted_iota(jnp.int32, (heads, lanes), 0)
    lane = lax.broadcasted_iota(jnp.int32, (heads, lanes), 1)
    return jnp.where(row == first_head + lane // head_width, 1.0, 0.0).astype(BF16)


def triangle(length, keep):
    row = lax.broadcasted_iota(jnp.int32, (length, length), 0)
    col = lax.broadcasted_iota(jnp.int32, (length, length), 1)
    return jnp.where(keep(row, col), 1.0, 0.0).astype(F32)


def summary_kernel(
    head_width,
    first_head,
    raw_ref,
    bias_ref,
    decay_ref,
    write_ref,
    read_ref,
    x_ref,
    dy_ref,
    message_ref,
    step_ref,
    cum_ref,
    weight_f,
    weight_b,
    facts,
):
    turn = pl.program_id(0)
    heads = raw_ref.shape[1]
    rows, lanes = x_ref.shape
    state = write_ref.shape[0]

    @pl.when(turn == 0)
    def _():
        step = jax.nn.softplus(raw_ref[...].astype(F32) + bias_ref[...])
        rate = -jnp.exp(decay_ref[...])
        cum = mul_exact(triangle(rows, lambda r, c: r >= c), step * rate)
        finish = cum[rows - 1 : rows, :]
        forward = step * jnp.exp(finish - cum)
        backward = jnp.exp(cum)
        power_f = power_for(PRODUCT_BOUND * jnp.sum(forward, axis=0, keepdims=True))
        power_b = power_for(PRODUCT_BOUND * jnp.sum(backward, axis=0, keepdims=True))
        step_ref[...] = step
        cum_ref[...] = cum
        parts = thirds(jnp.maximum(finish, -1e30))
        facts[...] = jnp.concatenate(
            [part.astype(F32) for part in parts]
            + [power_f, power_b, jnp.zeros((META - 5, heads), F32)],
            axis=0,
        ).astype(BF16)
        top, low = halves(forward * jnp.exp2(power_f))
        weight_f[...] = jnp.concatenate([top, low], axis=1)
        top, low = halves(backward * jnp.exp2(power_b))
        weight_b[...] = jnp.concatenate([top, low], axis=1)

    pick = head_selector(first_head + turn * (lanes // head_width), heads, lanes, head_width)
    pick_twice = jnp.concatenate([pick, pick], axis=0)
    width = message_ref.shape[2]

    def put(start, value):
        for owner in range(message_ref.shape[0]):
            message_ref[owner, start : start + value.shape[0], :] = value[
                :, owner * width : (owner + 1) * width
            ]

    def summed(tokens_ref, weight, rows_t):
        top, low = halves(tokens_ref[...].astype(F32) * mul(weight[...], pick_twice))
        return encode(mul(rows_t[...], top) + mul(rows_t[...], low))

    put(0, summed(x_ref, weight_f, write_ref))
    put(state, summed(dy_ref, weight_b, read_ref))
    put(2 * state, mul(facts[...], pick).astype(BF16))


def scan_kernel(message_ref, after_ref, answer_ref, powers):
    blocks, double, lanes = message_ref.shape
    state = (double - META) // 2
    top = 2.0**TOP_POWER

    def one(block, start, power_row, side, running, bound):
        facts = message_ref[block, 2 * state : double, :].astype(F32)
        decay = jnp.exp(facts[0:1] + facts[1:2] + facts[2:3])
        back = jnp.exp2(-facts[power_row : power_row + 1])
        power = power_for(bound)
        powers[side, pl.ds(block, 1), :] = power
        answer_ref[block, start : start + state, :] = encode(running * jnp.exp2(power))
        own = decode(message_ref[block, start : start + state, :]) * back
        return running * decay + own, bound * decay + top * back

    def both(block, carry):
        ahead, ahead_bound, behind, behind_bound = carry
        return one(block, 0, 3, 0, ahead, ahead_bound) + one(
            blocks - 1 - block, state, 4, 1, behind, behind_bound
        )

    zero, none = jnp.zeros((state, lanes), F32), jnp.zeros((1, lanes), F32)
    lax.fori_loop(0, blocks, both, (zero, none, zero, none), unroll=4)
    row = lax.broadcasted_iota(jnp.int32, (blocks, META, lanes), 1)
    ahead, behind = powers[0][:, None, :], powers[1][:, None, :]
    meta = jnp.where(row == 0, ahead, jnp.where(row == 1, behind, 0.0))
    answer_ref[:, 2 * state : double, :] = meta.astype(BF16)


def block_kernel(
    head_width,
    scale,
    first_head,
    step_ref,
    cum_ref,
    write_ref,
    read_ref,
    x_ref,
    dy_ref,
    after_ref,
    inner_ref,
    own_ref,
    within_ref,
    maps_ref,
    read_write,
    source,
    cum_rows,
    pair_sum,
    out_flow,
):
    turn = pl.program_id(0)
    rows, lanes = x_ref.shape
    half = rows // 2
    heads = step_ref.shape[1]
    group = lanes // head_width

    @pl.when(turn == 0)
    def _():
        read_write[...] = scale * lax.dot_general(
            write_ref[...], read_ref[...], (((0,), (0,)), ((), ())), preferred_element_type=F32
        )
        source[...] = jnp.log(step_ref[...]) - cum_ref[...]
        cum_rows[...] = cum_ref[...].T
        pair_sum[...] = jnp.zeros_like(pair_sum)
        out_flow[...] = jnp.zeros_like(out_flow)
        own_ref[...] = jnp.zeros_like(own_ref)

    first = first_head + turn * group
    near = pltpu.roll(source[...], lax.rem(heads - first, heads), axis=1)
    near_cum = cum_rows[pl.ds(first, group), :]
    row = lax.broadcasted_iota(jnp.int32, (half, half), 0)
    col = lax.broadcasted_iota(jnp.int32, (half, half), 1)
    ahead = col >= row
    lane = lax.broadcasted_iota(jnp.int32, (half, 2 * head_width), 1)
    first_half = lane < head_width
    head_lane = lax.broadcasted_iota(jnp.int32, (half, heads), 1)
    flow_aa = read_write[0:half, 0:half]
    flow_ab = read_write[0:half, half:rows]
    flow_bb = read_write[half:rows, half:rows]
    sum_aa = jnp.zeros((half, half), F32)
    sum_ab = jnp.zeros((half, half), F32)
    sum_bb = jnp.zeros((half, half), F32)
    own_a = jnp.zeros((half, heads), F32)
    own_b = jnp.zeros((half, heads), F32)
    zero = jnp.zeros((half, 2 * head_width), BF16)
    flows = []
    for pair in range(group // 2):
        span = slice(pair * 2 * head_width, (pair + 1) * 2 * head_width)
        x_a, x_b = x_ref[0:half, span], x_ref[half:rows, span]
        dy_a, dy_b = dy_ref[0:half, span], dy_ref[half:rows, span]
        early_a, late_a = jnp.where(first_half, dy_a, zero), jnp.where(first_half, zero, dy_a)
        early_b, late_b = jnp.where(first_half, dy_b, zero), jnp.where(first_half, zero, dy_b)
        stack = jnp.concatenate([early_a, early_b, late_a, late_b], axis=0)
        stack_b = jnp.concatenate([early_b, late_b], axis=0)
        grad_a = mul_nt(x_a, stack)
        grad_b = mul_nt(x_b, stack_b)
        masks_a, masks_b = [], []
        for side in range(2):
            place = pair * 2 + side
            head = first + place
            from_a = near[0:half, place : place + 1]
            from_b = near[half:rows, place : place + 1]
            to_a = near_cum[place : place + 1, 0:half]
            to_b = near_cum[place : place + 1, half:rows]
            fade_aa = jnp.exp(jnp.where(ahead, to_a + from_a, -1e30))
            fade_ab = jnp.exp(to_b + from_a)
            fade_bb = jnp.exp(jnp.where(ahead, to_b + from_b, -1e30))
            weigh_aa = fade_aa * grad_a[:, side * rows : side * rows + half]
            weigh_ab = fade_ab * grad_a[:, side * rows + half : (side + 1) * rows]
            weigh_bb = fade_bb * grad_b[:, side * half : (side + 1) * half]
            sum_aa += weigh_aa
            sum_ab += weigh_ab
            sum_bb += weigh_bb
            masks_a += [(fade_aa * flow_aa).astype(BF16), (fade_ab * flow_ab).astype(BF16)]
            masks_b += [(fade_bb * flow_bb).astype(BF16)]
            pair_aa = weigh_aa * flow_aa
            pair_ab = weigh_ab * flow_ab
            pair_bb = weigh_bb * flow_bb
            flow_out = jnp.sum(pair_aa + pair_ab, axis=1, keepdims=True)
            own_a = jnp.where(head_lane == head, flow_out, own_a)
            flow_out = jnp.sum(pair_bb, axis=1, keepdims=True)
            own_b = jnp.where(head_lane == head, flow_out, own_b)
            flow_in = [
                jnp.sum(pair_aa, axis=0, keepdims=True),
                jnp.sum(pair_ab, axis=0, keepdims=True) + jnp.sum(pair_bb, axis=0, keepdims=True),
            ]
            flows.append(jnp.concatenate(flow_in, axis=1))
        inner_ref[0:half, span] = mul(jnp.concatenate(masks_a, axis=1), stack).astype(BF16)
        inner_ref[half:rows, span] = mul(jnp.concatenate(masks_b, axis=1), stack_b).astype(BF16)
    out_flow[pl.ds(first, group), :] = jnp.concatenate(flows, axis=0)
    pair_sum[0:half, 0:half] += sum_aa
    pair_sum[0:half, half:rows] += sum_ab
    pair_sum[half:rows, half:rows] += sum_bb
    own_ref[0:half, :] += own_a
    own_ref[half:rows, :] += own_b

    @pl.when(turn == pl.num_programs(0) - 1)
    def _():
        net = own_ref[...] - out_flow[...].T
        within_ref[...] = mul_exact(triangle(rows, lambda r, c: r > c), net)
        weighted = scale * pair_sum[...]
        maps_ref[...] = jnp.concatenate(
            [
                mul_exact(weighted, read_ref[...].astype(F32), ((1,), (1,))),
                mul_exact(weighted, write_ref[...].astype(F32), ((0,), (1,))),
            ],
            axis=1,
        )


def carry_kernel(head_width, scale, first_head, parts, first, last, *refs):
    refs = list(refs)
    take = lambda count: [refs.pop(0) for _ in range(count)]
    raw_ref, bias_ref, decay_ref, step_ref, cum_ref, write_ref, read_ref, skip_ref = take(8)
    x_ref, dy_ref, inner_ref, answer_ref, _ = take(5)
    if not first:
        early_sums, early_through, _ = take(3)
    if last:
        own_refs, within_refs, map_refs = take(parts), take(parts), take(parts)
        grad_ref, table_ref, sums, through, weight_e, weight_s, maps = take(7)
    else:
        grad_ref, sums, through, weight_e, weight_s, maps = take(6)
    turn = pl.program_id(0)
    rows, lanes = x_ref.shape
    heads = step_ref.shape[1]
    state = write_ref.shape[0]
    future, past = slice(0, heads), slice(heads, 2 * heads)
    write_sum = slice(2 * heads, 2 * heads + 2 * state)
    read_sum = slice(2 * heads + 2 * state, 2 * heads + 4 * state)

    @pl.when(turn == 0)
    def _():
        cum = cum_ref[...]
        finish = cum[rows - 1 : rows, :]
        top, low = halves(step_ref[...] * jnp.exp(finish - cum) * scale)
        weight_e[...] = jnp.concatenate([top, low], axis=1)
        top, low = halves(jnp.exp(cum) * scale)
        weight_s[...] = jnp.concatenate([top, low], axis=1)
        write = write_ref[...].astype(F32).T.astype(BF16)
        read = read_ref[...].astype(F32).T.astype(BF16)
        maps[...] = jnp.concatenate([write, write, read, read], axis=1)
        if first:
            sums[...] = jnp.zeros_like(sums)
            through[...] = jnp.zeros_like(through)
        else:
            sums[...] = early_sums[...]
            through[...] = early_through[...]

    pick = head_selector(first_head + turn * (lanes // head_width), heads, lanes, head_width)
    pick_twice = jnp.concatenate([pick, pick], axis=0)
    starts, ends = [], []
    for piece in range(answer_ref.shape[0]):
        back = jnp.exp2(-answer_ref[piece, 2 * state : 2 * state + META, :].astype(F32))
        starts.append(decode(answer_ref[piece, 0:state, :]) * back[0:1])
        ends.append(decode(answer_ref[piece, state : 2 * state, :]) * back[1:2])
    start = jnp.concatenate(starts, axis=1)
    end = jnp.concatenate(ends, axis=1)
    start_parts = jnp.concatenate(halves(start), axis=0)
    end_parts = jnp.concatenate(halves(end), axis=0)
    x = x_ref[...].astype(F32)
    dy = dy_ref[...].astype(F32)
    skip = jnp.concatenate(
        [part.astype(F32) for part in thirds(skip_ref[...])] + [jnp.zeros((13, heads), F32)], axis=0
    )
    skip = jnp.sum(mul(skip.astype(BF16), pick), axis=0, keepdims=True)

    spread_e = mul(weight_e[...], pick_twice)
    carried = mul(maps[:, 0 : 2 * state], end_parts) * spread_e
    grad_ref[...] = (inner_ref[...].astype(F32) + skip * dy + carried).astype(BF16)
    top, low = halves(x * carried)
    sums[:, future] += mul_nt(top, pick) + mul_nt(low, pick)
    top, low = halves(x * spread_e)
    sums[:, write_sum] += mul_nt(top, end_parts) + mul_nt(low, end_parts)

    weighted = dy * mul(weight_s[...], pick_twice)
    top, low = halves(weighted * mul(maps[:, 2 * state : 4 * state], start_parts))
    sums[:, past] += mul_nt(top, pick) + mul_nt(low, pick)
    top, low = halves(weighted)
    sums[:, read_sum] += mul_nt(top, start_parts) + mul_nt(low, start_parts)

    both = jnp.broadcast_to(jnp.sum(start * end, axis=0, keepdims=True), (8, lanes))
    top, low = halves(both)
    through[...] += mul_nt(top, pick) + mul_nt(low, pick)

    if not last:
        return

    @pl.when(turn == pl.num_programs(0) - 1)
    def _():
        rate = -jnp.exp(decay_ref[...])
        step = step_ref[...]
        gate = jax.nn.sigmoid(raw_ref[...].astype(F32) + bias_ref[...])
        finish = cum_ref[rows - 1 : rows, :]
        to_come = sums[:, future]
        decay_grad = (
            sum(ref[...] for ref in within_refs)
            + mul_exact(triangle(rows, lambda r, c: r <= c), sums[:, past])
            + mul_exact(triangle(rows, lambda r, c: r > c), to_come)
            + jnp.exp(finish) * scale * through[0:1, :]
        )
        ratio = jnp.where(step > 1e-30, gate / jnp.maximum(step, 1e-30), 1.0)
        inner = sum(ref[...] for ref in own_refs) + to_come
        raw_grad = inner * ratio + rate * decay_grad * gate
        map_sum = sums[:, 2 * heads :] + 0.0
        write_all = map_sum[:, 0:state] + map_sum[:, state : 2 * state]
        read_all = map_sum[:, 2 * state : 3 * state] + map_sum[:, 3 * state :]
        map_grad = jnp.concatenate([write_all, read_all], axis=1)
        map_grad += sum(ref[...] for ref in map_refs)
        table = jnp.concatenate([raw_grad.T, map_grad.T], axis=0).astype(BF16)
        for copy in range(table_ref.shape[0]):
            table_ref[copy, :, :] = table


def deal_kernel(layer_ref, after_ref, out_ref):
    width = out_ref.shape[3]
    for piece in range(out_ref.shape[0]):
        out_ref[piece, 0, :, :] = layer_ref[:, piece * width : (piece + 1) * width]


def product_kernel(table_ref, layer_ref, out_ref, total):
    turn = pl.program_id(0)
    planes, columns, _ = total.shape

    @pl.when(turn == 0)
    def _():
        total[...] = jnp.zeros_like(total)

    for plane in range(planes):
        total[plane] += mul(table_ref[0], layer_ref[0, plane])

    @pl.when(turn == pl.num_programs(0) - 1)
    def _():
        most = jnp.max(jnp.abs(total[...]), axis=(0, 1), keepdims=True)
        power = power_for(jnp.max(most, axis=2, keepdims=True))
        out_ref[:, 0:columns, :] = encode(total[...] * jnp.exp2(power))
        out_ref[:, columns:, :] = jnp.broadcast_to(power, out_ref[:, columns:, :].shape).astype(BF16)


def gather_kernel(factor, parts_ref, out_ref):
    columns = out_ref.shape[1]
    total = jnp.zeros((columns, out_ref.shape[0]), F32)
    for plane in range(parts_ref.shape[0]):
        power = parts_ref[plane, columns:, :].astype(F32)[0:1]
        total += decode(parts_ref[plane, 0:columns, :]) * jnp.exp2(-power)
    out_ref[...] = (total * factor).T


def whole(shape):
    return pl.BlockSpec(shape, lambda i: (0,) * len(shape))


def call(kernel, steps, in_specs, out, scratch, flops, bytes_accessed, aliases=None):
    return pl.pallas_call(
        kernel,
        grid=(steps,),
        in_specs=in_specs,
        out_specs=[spec for spec, _, _ in out],
        out_shape=[jax.ShapeDtypeStruct(dims, dtype) for _, dims, dtype in out],
        scratch_shapes=[pltpu.VMEM(dims, dtype) for dims, dtype in scratch],
        compiler_params=pltpu.CompilerParams(vmem_limit_bytes=VMEM_LIMIT),
        cost_estimate=pl.CostEstimate(
            flops=flops, bytes_accessed=bytes_accessed, transcendentals=0
        ),
        input_output_aliases=aliases or {},
    )


def body(
    layer_input,
    head_inputs,
    output_grad,
    step_raw,
    state_write,
    state_read,
    decay_log,
    step_bias,
    skip_gain,
):
    rows, channels = head_inputs.shape
    heads = step_raw.shape[1]
    head_width = channels // heads
    state = state_write.shape[1]
    model = layer_input.shape[1]
    columns = heads + 2 * state
    axes = ("wide", "seq")
    wide, planes = lax.axis_size("wide"), lax.axis_size("seq")
    blocks = wide * planes
    own_model = model // blocks
    scale = float(rows * blocks * state) ** -0.5
    parts = HALVES if heads % (HALVES * blocks) == 0 else 1
    part_heads = heads // parts
    part_lanes = channels // parts
    owner_lanes = part_lanes // blocks
    piece_lanes = max(owner_lanes, 128)
    pieces = part_lanes // piece_lanes
    depth = 2 * state + META
    bias = step_bias[None, :]
    decay = decay_log[None, :]
    skip = skip_gain[None, :]
    write_t, read_t = state_write.T, state_read.T

    lanes = CARRY_HEADS * head_width
    steps = part_lanes // lanes
    here = lanes // piece_lanes

    def tokens(part, width):
        first = part * (part_lanes // width)
        return pl.BlockSpec((rows, width), lambda i: (0, first + i))

    message_spec = pl.BlockSpec((here, depth, piece_lanes), lambda i: (i, 0, 0))
    head_spec = whole((rows, heads))
    line_spec = whole((1, heads))
    map_spec = whole((state, rows))
    head_out = (head_spec, (rows, heads), F32)

    def summaries(part):
        return call(
            functools.partial(summary_kernel, head_width, part * part_heads),
            steps,
            [head_spec, line_spec, line_spec, map_spec, map_spec]
            + [tokens(part, lanes), tokens(part, lanes)],
            [(message_spec, (pieces, depth, piece_lanes), BF16), head_out, head_out],
            [((rows, 2 * heads), BF16), ((rows, 2 * heads), BF16), ((META, heads), BF16)],
            8 * rows * part_lanes * state,
            10 * 2**20 // parts,
        )(step_raw, bias, decay, write_t, read_t, head_inputs, output_grad)

    def exchange(array):
        return lax.all_to_all(array, axes, split_axis=0, concat_axis=0, tiled=True)

    def to_owner(array):
        if owner_lanes < piece_lanes:
            split = array.reshape(pieces, depth, piece_lanes // owner_lanes, owner_lanes)
            array = jnp.moveaxis(split, 2, 1).reshape(blocks, depth, owner_lanes)
        return exchange(array)

    def from_owner(array):
        array = exchange(array)
        if owner_lanes < piece_lanes:
            split = array.reshape(pieces, piece_lanes // owner_lanes, depth, owner_lanes)
            array = jnp.moveaxis(split, 1, 2).reshape(pieces, depth, piece_lanes)
        return array

    def scan(message, after):
        spec = whole((blocks, depth, owner_lanes))
        (answer,) = call(
            scan_kernel,
            1,
            [spec, pl.BlockSpec(memory_space=pl.ANY)],
            [(spec, (blocks, depth, owner_lanes), BF16)],
            [((2, blocks, owner_lanes), F32)],
            2**22,
            4 * 2**20 // parts,
        )(message, after)
        return answer

    def own_block(part, step, cum, after):
        width = PAIR_HEADS * head_width
        part_spec = pl.BlockSpec((rows, width), lambda i: (0, i))
        return call(
            functools.partial(block_kernel, head_width, scale, part * part_heads),
            part_lanes // width,
            [head_spec, head_spec, map_spec, map_spec, tokens(part, width), tokens(part, width)]
            + [pl.BlockSpec(memory_space=pl.ANY)],
            [
                (part_spec, (rows, part_lanes), BF16),
                head_out,
                head_out,
                (whole((rows, 2 * state)), (rows, 2 * state), F32),
            ],
            [
                ((rows, rows), F32),
                ((rows, heads), F32),
                ((heads, rows), F32),
                ((rows, rows), F32),
                ((heads, rows), F32),
            ],
            16 * rows * rows * part_lanes,
            12 * 2**20 // parts,
        )(step, cum, write_t, read_t, head_inputs, output_grad, after)

    with jax.named_scope("summaries"):
        summed = [summaries(part) for part in range(parts)]
    step, cum = summed[-1][1:]
    with jax.named_scope("layer"):
        dealt = (wide, planes, rows, own_model)
        (dealt_out,) = call(
            deal_kernel,
            planes,
            [
                pl.BlockSpec((rows, wide * own_model), lambda i: (0, i)),
                pl.BlockSpec(memory_space=pl.ANY),
            ],
            [(pl.BlockSpec((wide, 1, rows, own_model), lambda i: (0, i, 0, 0)), dealt, BF16)],
            [],
            0,
            8 * 2**20,
        )(layer_input, cum)
        layer_parts = lax.all_to_all(dealt_out, "wide", split_axis=0, concat_axis=0, tiled=True)
    with jax.named_scope("own_block"):
        own_parts = [own_block(part, step, cum, dealt_out) for part in range(parts)]
    with jax.named_scope("scan"):
        returned = [
            from_owner(scan(to_owner(one[0]), own[1])) for one, own in zip(summed, own_parts)
        ]

    sums_out = (whole((rows, 2 * heads + 4 * state)), (rows, 2 * heads + 4 * state), F32)
    through_out = (whole((8, heads)), (8, heads), F32)
    early = ()
    with jax.named_scope("carried"):
        for part in range(parts):
            first, last = part == 0, part == parts - 1
            in_specs = [head_spec, line_spec, line_spec, head_spec, head_spec, map_spec, map_spec]
            in_specs += [line_spec, tokens(part, lanes), tokens(part, lanes)]
            in_specs += [pl.BlockSpec((rows, lanes), lambda i: (0, i)), message_spec]
            in_specs += [pl.BlockSpec(memory_space=pl.ANY)]
            operands = [step_raw, bias, decay, step, cum, write_t, read_t, skip]
            operands += [head_inputs, output_grad, own_parts[part][0], returned[part]]
            operands += [layer_parts]
            aliases = {}
            if not first:
                in_specs += [sums_out[0], through_out[0], pl.BlockSpec(memory_space=pl.ANY)]
                operands += [early[1], early[2], early[0]]
                aliases = {len(operands) - 1: 0}
            scratch = [((rows, 2 * heads), BF16)] * 2 + [((rows, 4 * state), BF16)]
            out = [(tokens(part, lanes), (rows, channels), BF16)]
            if last:
                for which in (1, 2, 3):
                    operands += [one[which] for one in own_parts]
                    in_specs += [whole(one[which].shape) for one in own_parts]
                out += [(whole((wide, columns, rows)), (wide, columns, rows), BF16)]
                scratch = [sums_out[1:], through_out[1:]] + scratch
            else:
                out += [sums_out, through_out]
            early = call(
                functools.partial(
                    carry_kernel, head_width, scale, part * part_heads, parts, first, last
                ),
                steps,
                in_specs,
                out,
                scratch,
                32 * rows * part_lanes * state,
                18 * 2**20 // parts,
                aliases,
            )(*operands)
    grad_x, table = early

    with jax.named_scope("projection"):
        tables = lax.all_to_all(table, "wide", split_axis=0, concat_axis=0, tiled=True)
        coded = (planes, columns + META, own_model)
        (product,) = call(
            product_kernel,
            wide,
            [
                pl.BlockSpec((1, columns, rows), lambda i: (i, 0, 0)),
                pl.BlockSpec((1, planes, rows, own_model), lambda i: (i, 0, 0, 0)),
            ],
            [(whole(coded), coded, BF16)],
            [((planes, columns, own_model), F32)],
            2 * rows * model * columns,
            6 * 2**20,
        )(tables, layer_parts)
        coded_parts = lax.all_to_all(product, "seq", split_axis=0, concat_axis=0, tiled=True)
        (weight_grad,) = call(
            functools.partial(gather_kernel, 1.0 / math.sqrt(rows * blocks)),
            1,
            [whole(coded)],
            [(whole((own_model, columns)), (own_model, columns), F32)],
            [],
            2**20,
            2**20,
        )(coded_parts)
    return grad_x, weight_grad


def solution(mesh):
    in_specs = (
        P(("wide", "seq"), None),
        P(("wide", "seq"), None),
        P(("wide", "seq"), None),
        P(("wide", "seq"), None),
        P(("wide", "seq"), None),
        P(("wide", "seq"), None),
        P(),
        P(),
        P(),
    )
    out_specs = (P(("wide", "seq"), None), P(("seq", "wide"), None))
    return jax.shard_map(body, mesh=mesh, in_specs=in_specs, out_specs=out_specs, check_vma=False)
```

```python
import functools
import math

import jax
import jax.numpy as jnp
from jax import lax
from jax.experimental import pallas as pl
from jax.experimental.pallas import tpu as pltpu
from jax.sharding import PartitionSpec as P

F32 = jnp.float32
BF16 = jnp.bfloat16
EXACT = lax.Precision.HIGHEST
VMEM_LIMIT = 56 * 1024 * 1024
TOP_POWER = 30.0
PRODUCT_BOUND = 30.0
CARRY_HEADS = 16
PAIR_HEADS = 8
META = 16
HALVES = 2


def mul(a, b):
    return lax.dot_general(a, b, (((1,), (0,)), ((), ())), preferred_element_type=F32)


def mul_nt(a, b):
    return lax.dot_general(a, b, (((1,), (1,)), ((), ())), preferred_element_type=F32)


def mul_exact(a, b, dims=((1,), (0,))):
    return lax.dot_general(a, b, (dims, ((), ())), preferred_element_type=F32, precision=EXACT)


def halves(value):
    top = value.astype(BF16)
    return top, (value - top.astype(F32)).astype(BF16)


def power_for(bound):
    power = jnp.floor(TOP_POWER - jnp.log2(jnp.maximum(bound, 1e-37)))
    return jnp.clip(power, -100.0, 100.0)


def thirds(value):
    top, rest = value.astype(BF16), value
    rest = rest - top.astype(F32)
    middle = rest.astype(BF16)
    return top, middle, (rest - middle.astype(F32)).astype(BF16)


def encode(value):
    square = value * value
    fourth = square * square
    return jnp.where(value < 0, -fourth, fourth).astype(BF16)


def decode(coded):
    coded = coded.astype(F32)
    size = jnp.maximum(jnp.abs(coded), 1e-37)
    inverse = lax.rsqrt(size)
    return coded * inverse * lax.rsqrt(size * inverse)


def head_selector(first_head, heads, lanes, head_width):
    row = lax.broadcasted_iota(jnp.int32, (heads, lanes), 0)
    lane = lax.broadcasted_iota(jnp.int32, (heads, lanes), 1)
    return jnp.where(row == first_head + lane // head_width, 1.0, 0.0).astype(BF16)


def triangle(length, keep):
    row = lax.broadcasted_iota(jnp.int32, (length, length), 0)
    col = lax.broadcasted_iota(jnp.int32, (length, length), 1)
    return jnp.where(keep(row, col), 1.0, 0.0).astype(F32)


def summary_kernel(
    head_width,
    first_head,
    raw_ref,
    bias_ref,
    decay_ref,
    write_ref,
    read_ref,
    x_ref,
    dy_ref,
    message_ref,
    step_ref,
    cum_ref,
    weight_f,
    weight_b,
    facts,
):
    turn = pl.program_id(0)
    heads = raw_ref.shape[1]
    rows, lanes = x_ref.shape
    state = write_ref.shape[0]

    @pl.when(turn == 0)
    def _():
        step = jax.nn.softplus(raw_ref[...].astype(F32) + bias_ref[...])
        rate = -jnp.exp(decay_ref[...])
        cum = mul_exact(triangle(rows, lambda r, c: r >= c), step * rate)
        finish = cum[rows - 1 : rows, :]
        forward = step * jnp.exp(finish - cum)
        backward = jnp.exp(cum)
        power_f = power_for(PRODUCT_BOUND * jnp.sum(forward, axis=0, keepdims=True))
        power_b = power_for(PRODUCT_BOUND * jnp.sum(backward, axis=0, keepdims=True))
        step_ref[...] = step
        cum_ref[...] = cum
        parts = thirds(jnp.maximum(finish, -1e30))
        facts[...] = jnp.concatenate(
            [part.astype(F32) for part in parts]
            + [power_f, power_b, jnp.zeros((META - 5, heads), F32)],
            axis=0,
        ).astype(BF16)
        top, low = halves(forward * jnp.exp2(power_f))
        weight_f[...] = jnp.concatenate([top, low], axis=1)
        top, low = halves(backward * jnp.exp2(power_b))
        weight_b[...] = jnp.concatenate([top, low], axis=1)

    pick = head_selector(first_head + turn * (lanes // head_width), heads, lanes, head_width)
    pick_twice = jnp.concatenate([pick, pick], axis=0)
    width = message_ref.shape[2]

    def put(start, value):
        for owner in range(message_ref.shape[0]):
            message_ref[owner, start : start + value.shape[0], :] = value[
                :, owner * width : (owner + 1) * width
            ]

    def summed(tokens_ref, weight, rows_t):
        top, low = halves(tokens_ref[...].astype(F32) * mul(weight[...], pick_twice))
        return encode(mul(rows_t[...], top) + mul(rows_t[...], low))

    put(0, summed(x_ref, weight_f, write_ref))
    put(state, summed(dy_ref, weight_b, read_ref))
    put(2 * state, mul(facts[...], pick).astype(BF16))


def scan_kernel(message_ref, after_ref, answer_ref, powers):
    blocks, double, lanes = message_ref.shape
    state = (double - META) // 2
    top = 2.0**TOP_POWER

    def one(block, start, power_row, side, running, bound):
        facts = message_ref[block, 2 * state : double, :].astype(F32)
        decay = jnp.exp(facts[0:1] + facts[1:2] + facts[2:3])
        back = jnp.exp2(-facts[power_row : power_row + 1])
        power = power_for(bound)
        powers[side, pl.ds(block, 1), :] = power
        answer_ref[block, start : start + state, :] = encode(running * jnp.exp2(power))
        own = decode(message_ref[block, start : start + state, :]) * back
        return running * decay + own, bound * decay + top * back

    def both(block, carry):
        ahead, ahead_bound, behind, behind_bound = carry
        return one(block, 0, 3, 0, ahead, ahead_bound) + one(
            blocks - 1 - block, state, 4, 1, behind, behind_bound
        )

    zero, none = jnp.zeros((state, lanes), F32), jnp.zeros((1, lanes), F32)
    lax.fori_loop(0, blocks, both, (zero, none, zero, none), unroll=4)
    row = lax.broadcasted_iota(jnp.int32, (blocks, META, lanes), 1)
    ahead, behind = powers[0][:, None, :], powers[1][:, None, :]
    meta = jnp.where(row == 0, ahead, jnp.where(row == 1, behind, 0.0))
    answer_ref[:, 2 * state : double, :] = meta.astype(BF16)


def block_kernel(
    head_width,
    scale,
    first_head,
    step_ref,
    cum_ref,
    write_ref,
    read_ref,
    x_ref,
    dy_ref,
    after_ref,
    inner_ref,
    own_ref,
    within_ref,
    maps_ref,
    read_write,
    source,
    cum_rows,
    pair_sum,
    out_flow,
):
    turn = pl.program_id(0)
    rows, lanes = x_ref.shape
    half = rows // 2
    heads = step_ref.shape[1]
    group = lanes // head_width

    @pl.when(turn == 0)
    def _():
        read_write[...] = scale * lax.dot_general(
            write_ref[...], read_ref[...], (((0,), (0,)), ((), ())), preferred_element_type=F32
        )
        source[...] = jnp.log(step_ref[...]) - cum_ref[...]
        cum_rows[...] = cum_ref[...].T
        pair_sum[...] = jnp.zeros_like(pair_sum)
        out_flow[...] = jnp.zeros_like(out_flow)
        own_ref[...] = jnp.zeros_like(own_ref)

    first = first_head + turn * group
    near = pltpu.roll(source[...], lax.rem(heads - first, heads), axis=1)
    near_cum = cum_rows[pl.ds(first, group), :]
    row = lax.broadcasted_iota(jnp.int32, (half, half), 0)
    col = lax.broadcasted_iota(jnp.int32, (half, half), 1)
    ahead = col >= row
    lane = lax.broadcasted_iota(jnp.int32, (half, 2 * head_width), 1)
    first_half = lane < head_width
    head_lane = lax.broadcasted_iota(jnp.int32, (half, heads), 1)
    flow_aa = read_write[0:half, 0:half]
    flow_ab = read_write[0:half, half:rows]
    flow_bb = read_write[half:rows, half:rows]
    sum_aa = jnp.zeros((half, half), F32)
    sum_ab = jnp.zeros((half, half), F32)
    sum_bb = jnp.zeros((half, half), F32)
    own_a = jnp.zeros((half, heads), F32)
    own_b = jnp.zeros((half, heads), F32)
    zero = jnp.zeros((half, 2 * head_width), BF16)
    flows = []
    for pair in range(group // 2):
        span = slice(pair * 2 * head_width, (pair + 1) * 2 * head_width)
        x_a, x_b = x_ref[0:half, span], x_ref[half:rows, span]
        dy_a, dy_b = dy_ref[0:half, span], dy_ref[half:rows, span]
        early_a, late_a = jnp.where(first_half, dy_a, zero), jnp.where(first_half, zero, dy_a)
        early_b, late_b = jnp.where(first_half, dy_b, zero), jnp.where(first_half, zero, dy_b)
        stack = jnp.concatenate([early_a, early_b, late_a, late_b], axis=0)
        stack_b = jnp.concatenate([early_b, late_b], axis=0)
        grad_a = mul_nt(x_a, stack)
        grad_b = mul_nt(x_b, stack_b)
        masks_a, masks_b = [], []
        for side in range(2):
            place = pair * 2 + side
            head = first + place
            from_a = near[0:half, place : place + 1]
            from_b = near[half:rows, place : place + 1]
            to_a = near_cum[place : place + 1, 0:half]
            to_b = near_cum[place : place + 1, half:rows]
            fade_aa = jnp.exp(jnp.where(ahead, to_a + from_a, -1e30))
            fade_ab = jnp.exp(to_b + from_a)
            fade_bb = jnp.exp(jnp.where(ahead, to_b + from_b, -1e30))
            weigh_aa = fade_aa * grad_a[:, side * rows : side * rows + half]
            weigh_ab = fade_ab * grad_a[:, side * rows + half : (side + 1) * rows]
            weigh_bb = fade_bb * grad_b[:, side * half : (side + 1) * half]
            sum_aa += weigh_aa
            sum_ab += weigh_ab
            sum_bb += weigh_bb
            masks_a += [(fade_aa * flow_aa).astype(BF16), (fade_ab * flow_ab).astype(BF16)]
            masks_b += [(fade_bb * flow_bb).astype(BF16)]
            pair_aa = weigh_aa * flow_aa
            pair_ab = weigh_ab * flow_ab
            pair_bb = weigh_bb * flow_bb
            flow_out = jnp.sum(pair_aa + pair_ab, axis=1, keepdims=True)
            own_a = jnp.where(head_lane == head, flow_out, own_a)
            flow_out = jnp.sum(pair_bb, axis=1, keepdims=True)
            own_b = jnp.where(head_lane == head, flow_out, own_b)
            flow_in = [
                jnp.sum(pair_aa, axis=0, keepdims=True),
                jnp.sum(pair_ab, axis=0, keepdims=True) + jnp.sum(pair_bb, axis=0, keepdims=True),
            ]
            flows.append(jnp.concatenate(flow_in, axis=1))
        inner_ref[0:half, span] = mul(jnp.concatenate(masks_a, axis=1), stack).astype(BF16)
        inner_ref[half:rows, span] = mul(jnp.concatenate(masks_b, axis=1), stack_b).astype(BF16)
    out_flow[pl.ds(first, group), :] = jnp.concatenate(flows, axis=0)
    pair_sum[0:half, 0:half] += sum_aa
    pair_sum[0:half, half:rows] += sum_ab
    pair_sum[half:rows, half:rows] += sum_bb
    own_ref[0:half, :] += own_a
    own_ref[half:rows, :] += own_b

    @pl.when(turn == pl.num_programs(0) - 1)
    def _():
        net = own_ref[...] - out_flow[...].T
        within_ref[...] = mul_exact(triangle(rows, lambda r, c: r > c), net)
        weighted = scale * pair_sum[...]
        maps_ref[...] = jnp.concatenate(
            [
                mul_exact(weighted, read_ref[...].astype(F32), ((1,), (1,))),
                mul_exact(weighted, write_ref[...].astype(F32), ((0,), (1,))),
            ],
            axis=1,
        )


def carry_kernel(head_width, scale, first_head, parts, waits, first, last, *refs):
    refs = list(refs)
    take = lambda count: [refs.pop(0) for _ in range(count)]
    raw_ref, bias_ref, decay_ref, step_ref, cum_ref, write_ref, read_ref, skip_ref = take(8)
    x_ref, dy_ref, inner_ref, answer_ref = take(4)
    take(waits)
    if not first:
        early_sums, early_through, _ = take(3)
    if last:
        own_refs, within_refs, map_refs = take(parts), take(parts), take(parts)
        grad_ref, table_ref, sums, through, weight_e, weight_s, maps = take(7)
    else:
        grad_ref, sums, through, weight_e, weight_s, maps = take(6)
    turn = pl.program_id(0)
    rows, lanes = x_ref.shape
    heads = step_ref.shape[1]
    state = write_ref.shape[0]
    future, past = slice(0, heads), slice(heads, 2 * heads)
    write_sum = slice(2 * heads, 2 * heads + 2 * state)
    read_sum = slice(2 * heads + 2 * state, 2 * heads + 4 * state)

    @pl.when(turn == 0)
    def _():
        cum = cum_ref[...]
        finish = cum[rows - 1 : rows, :]
        top, low = halves(step_ref[...] * jnp.exp(finish - cum) * scale)
        weight_e[...] = jnp.concatenate([top, low], axis=1)
        top, low = halves(jnp.exp(cum) * scale)
        weight_s[...] = jnp.concatenate([top, low], axis=1)
        write = write_ref[...].astype(F32).T.astype(BF16)
        read = read_ref[...].astype(F32).T.astype(BF16)
        maps[...] = jnp.concatenate([write, write, read, read], axis=1)
        if first:
            sums[...] = jnp.zeros_like(sums)
            through[...] = jnp.zeros_like(through)
        else:
            sums[...] = early_sums[...]
            through[...] = early_through[...]

    pick = head_selector(first_head + turn * (lanes // head_width), heads, lanes, head_width)
    pick_twice = jnp.concatenate([pick, pick], axis=0)
    starts, ends = [], []
    for piece in range(answer_ref.shape[0]):
        back = jnp.exp2(-answer_ref[piece, 2 * state : 2 * state + META, :].astype(F32))
        starts.append(decode(answer_ref[piece, 0:state, :]) * back[0:1])
        ends.append(decode(answer_ref[piece, state : 2 * state, :]) * back[1:2])
    start = jnp.concatenate(starts, axis=1)
    end = jnp.concatenate(ends, axis=1)
    start_parts = jnp.concatenate(halves(start), axis=0)
    end_parts = jnp.concatenate(halves(end), axis=0)
    x = x_ref[...].astype(F32)
    dy = dy_ref[...].astype(F32)
    skip = jnp.concatenate(
        [part.astype(F32) for part in thirds(skip_ref[...])] + [jnp.zeros((13, heads), F32)], axis=0
    )
    skip = jnp.sum(mul(skip.astype(BF16), pick), axis=0, keepdims=True)

    spread_e = mul(weight_e[...], pick_twice)
    carried = mul(maps[:, 0 : 2 * state], end_parts) * spread_e
    grad_ref[...] = (inner_ref[...].astype(F32) + skip * dy + carried).astype(BF16)
    top, low = halves(x * carried)
    sums[:, future] += mul_nt(top, pick) + mul_nt(low, pick)
    top, low = halves(x * spread_e)
    sums[:, write_sum] += mul_nt(top, end_parts) + mul_nt(low, end_parts)

    weighted = dy * mul(weight_s[...], pick_twice)
    top, low = halves(weighted * mul(maps[:, 2 * state : 4 * state], start_parts))
    sums[:, past] += mul_nt(top, pick) + mul_nt(low, pick)
    top, low = halves(weighted)
    sums[:, read_sum] += mul_nt(top, start_parts) + mul_nt(low, start_parts)

    both = jnp.broadcast_to(jnp.sum(start * end, axis=0, keepdims=True), (8, lanes))
    top, low = halves(both)
    through[...] += mul_nt(top, pick) + mul_nt(low, pick)

    if not last:
        return

    @pl.when(turn == pl.num_programs(0) - 1)
    def _():
        rate = -jnp.exp(decay_ref[...])
        step = step_ref[...]
        gate = jax.nn.sigmoid(raw_ref[...].astype(F32) + bias_ref[...])
        finish = cum_ref[rows - 1 : rows, :]
        to_come = sums[:, future]
        decay_grad = (
            sum(ref[...] for ref in within_refs)
            + mul_exact(triangle(rows, lambda r, c: r <= c), sums[:, past])
            + mul_exact(triangle(rows, lambda r, c: r > c), to_come)
            + jnp.exp(finish) * scale * through[0:1, :]
        )
        ratio = jnp.where(step > 1e-30, gate / jnp.maximum(step, 1e-30), 1.0)
        inner = sum(ref[...] for ref in own_refs) + to_come
        raw_grad = inner * ratio + rate * decay_grad * gate
        map_sum = sums[:, 2 * heads :] + 0.0
        write_all = map_sum[:, 0:state] + map_sum[:, state : 2 * state]
        read_all = map_sum[:, 2 * state : 3 * state] + map_sum[:, 3 * state :]
        map_grad = jnp.concatenate([write_all, read_all], axis=1)
        map_grad += sum(ref[...] for ref in map_refs)
        table_ref[...] = jnp.concatenate([raw_grad.T, map_grad.T], axis=0).astype(BF16)


def deal_kernel(place_ref, layer_ref, after_ref, *out_refs):
    width = out_refs[0].shape[2]
    for turn, out_ref in enumerate(out_refs):
        start = pl.multiple_of((place_ref[0] ^ turn) * width, width)
        out_ref[0, :, :] = layer_ref[:, pl.ds(start, width)]


def product_kernel(planes, place_ref, *refs):
    step = pl.program_id(0)
    wide = (len(refs) - planes) // 2
    table_refs, layer_refs, out_refs = refs[:wide], refs[wide : 2 * wide], refs[2 * wide :]
    total = sum(mul(table[...], layer[0]) for table, layer in zip(table_refs, layer_refs))
    columns = total.shape[0]
    most = jnp.max(jnp.abs(total), axis=0, keepdims=True)
    power = power_for(jnp.max(most, axis=1, keepdims=True))
    coded = encode(total * jnp.exp2(power))
    for plane in range(planes):

        @pl.when(step == plane)
        def _(out_ref=out_refs[plane]):
            out_ref[0:columns, :] = coded
            out_ref[columns:, :] = jnp.broadcast_to(power, out_ref[columns:, :].shape).astype(BF16)


def gather_kernel(factor, *refs):
    part_refs, out_ref = refs[:-1], refs[-1]
    columns = out_ref.shape[1]
    total = jnp.zeros((columns, out_ref.shape[0]), F32)
    for part_ref in part_refs:
        power = part_ref[columns:, :].astype(F32)[0:1]
        total += decode(part_ref[0:columns, :]) * jnp.exp2(-power)
    out_ref[...] = (total * factor).T


def swap(array, axis, turn):
    if turn == 0:
        return array
    count = lax.axis_size(axis)
    return lax.ppermute(array, axis, [(one, one ^ turn) for one in range(count)])


def whole(shape):
    return pl.BlockSpec(shape, lambda i: (0,) * len(shape))


def call(kernel, steps, in_specs, out, scratch, flops, bytes_accessed, aliases=None):
    return pl.pallas_call(
        kernel,
        grid=(steps,),
        in_specs=in_specs,
        out_specs=[spec for spec, _, _ in out],
        out_shape=[jax.ShapeDtypeStruct(dims, dtype) for _, dims, dtype in out],
        scratch_shapes=[pltpu.VMEM(dims, dtype) for dims, dtype in scratch],
        compiler_params=pltpu.CompilerParams(vmem_limit_bytes=VMEM_LIMIT),
        cost_estimate=pl.CostEstimate(
            flops=flops, bytes_accessed=bytes_accessed, transcendentals=0
        ),
        input_output_aliases=aliases or {},
    )


def body(
    layer_input,
    head_inputs,
    output_grad,
    step_raw,
    state_write,
    state_read,
    decay_log,
    step_bias,
    skip_gain,
):
    rows, channels = head_inputs.shape
    heads = step_raw.shape[1]
    head_width = channels // heads
    state = state_write.shape[1]
    model = layer_input.shape[1]
    columns = heads + 2 * state
    axes = ("wide", "seq")
    wide, planes = lax.axis_size("wide"), lax.axis_size("seq")
    blocks = wide * planes
    own_model = model // blocks
    scale = float(rows * blocks * state) ** -0.5
    parts = HALVES if heads % (HALVES * blocks) == 0 else 1
    part_heads = heads // parts
    part_lanes = channels // parts
    owner_lanes = part_lanes // blocks
    piece_lanes = max(owner_lanes, 128)
    pieces = part_lanes // piece_lanes
    depth = 2 * state + META
    bias = step_bias[None, :]
    decay = decay_log[None, :]
    skip = skip_gain[None, :]
    write_t, read_t = state_write.T, state_read.T

    lanes = CARRY_HEADS * head_width
    steps = part_lanes // lanes
    here = lanes // piece_lanes

    def tokens(part, width):
        first = part * (part_lanes // width)
        return pl.BlockSpec((rows, width), lambda i: (0, first + i))

    message_spec = pl.BlockSpec((here, depth, piece_lanes), lambda i: (i, 0, 0))
    head_spec = whole((rows, heads))
    line_spec = whole((1, heads))
    map_spec = whole((state, rows))
    head_out = (head_spec, (rows, heads), F32)

    def summaries(part):
        return call(
            functools.partial(summary_kernel, head_width, part * part_heads),
            steps,
            [head_spec, line_spec, line_spec, map_spec, map_spec]
            + [tokens(part, lanes), tokens(part, lanes)],
            [(message_spec, (pieces, depth, piece_lanes), BF16), head_out, head_out],
            [((rows, 2 * heads), BF16), ((rows, 2 * heads), BF16), ((META, heads), BF16)],
            8 * rows * part_lanes * state,
            10 * 2**20 // parts,
        )(step_raw, bias, decay, write_t, read_t, head_inputs, output_grad)

    def exchange(array):
        return lax.all_to_all(array, axes, split_axis=0, concat_axis=0, tiled=True)

    def to_owner(array):
        if owner_lanes < piece_lanes:
            split = array.reshape(pieces, depth, piece_lanes // owner_lanes, owner_lanes)
            array = jnp.moveaxis(split, 2, 1).reshape(blocks, depth, owner_lanes)
        return exchange(array)

    def from_owner(array):
        array = exchange(array)
        if owner_lanes < piece_lanes:
            split = array.reshape(pieces, piece_lanes // owner_lanes, depth, owner_lanes)
            array = jnp.moveaxis(split, 1, 2).reshape(pieces, depth, piece_lanes)
        return array

    def scan(message, after):
        spec = whole((blocks, depth, owner_lanes))
        (answer,) = call(
            scan_kernel,
            1,
            [spec, pl.BlockSpec(memory_space=pl.ANY)],
            [(spec, (blocks, depth, owner_lanes), BF16)],
            [((2, blocks, owner_lanes), F32)],
            2**22,
            4 * 2**20 // parts,
        )(message, after)
        return answer

    def own_block(part, step, cum, after):
        width = PAIR_HEADS * head_width
        part_spec = pl.BlockSpec((rows, width), lambda i: (0, i))
        return call(
            functools.partial(block_kernel, head_width, scale, part * part_heads),
            part_lanes // width,
            [head_spec, head_spec, map_spec, map_spec, tokens(part, width), tokens(part, width)]
            + [pl.BlockSpec(memory_space=pl.ANY)],
            [
                (part_spec, (rows, part_lanes), BF16),
                head_out,
                head_out,
                (whole((rows, 2 * state)), (rows, 2 * state), F32),
            ],
            [
                ((rows, rows), F32),
                ((rows, heads), F32),
                ((heads, rows), F32),
                ((rows, rows), F32),
                ((heads, rows), F32),
            ],
            16 * rows * rows * part_lanes,
            12 * 2**20 // parts,
        )(step, cum, write_t, read_t, head_inputs, output_grad, after)

    with jax.named_scope("summaries"):
        summed = [summaries(part) for part in range(parts)]
    step, cum = summed[-1][1:]
    place = jnp.stack([lax.axis_index("wide"), lax.axis_index("seq")]).astype(jnp.int32)
    with jax.named_scope("layer"):
        if own_model % 128:
            cut = jnp.transpose(layer_input.reshape(rows, planes, wide, own_model), (2, 1, 0, 3))
            dealt = [
                lax.dynamic_index_in_dim(cut, place[0] ^ turn, 0, False) for turn in range(wide)
            ]
        else:
            dealt = pl.pallas_call(
                deal_kernel,
                grid_spec=pltpu.PrefetchScalarGridSpec(
                    num_scalar_prefetch=1,
                    grid=(planes,),
                    in_specs=[
                        pl.BlockSpec((rows, wide * own_model), lambda i, p: (0, i)),
                        pl.BlockSpec(memory_space=pl.ANY),
                    ],
                    out_specs=[pl.BlockSpec((1, rows, own_model), lambda i, p: (i, 0, 0))] * wide,
                ),
                out_shape=[jax.ShapeDtypeStruct((planes, rows, own_model), BF16)] * wide,
                compiler_params=pltpu.CompilerParams(vmem_limit_bytes=VMEM_LIMIT),
                cost_estimate=pl.CostEstimate(flops=0, bytes_accessed=8 * 2**20, transcendentals=0),
            )(place, layer_input, cum)
        layer_parts = [swap(one, "wide", turn) for turn, one in enumerate(dealt)]
    with jax.named_scope("own_block"):
        own_parts = [own_block(part, step, cum, dealt[0]) for part in range(parts)]
    with jax.named_scope("scan"):
        returned = [
            from_owner(scan(to_owner(one[0]), own[1])) for one, own in zip(summed, own_parts)
        ]

    sums_out = (whole((rows, 2 * heads + 4 * state)), (rows, 2 * heads + 4 * state), F32)
    through_out = (whole((8, heads)), (8, heads), F32)
    early = ()
    with jax.named_scope("carried"):
        for part in range(parts):
            first, last = part == 0, part == parts - 1
            in_specs = [head_spec, line_spec, line_spec, head_spec, head_spec, map_spec, map_spec]
            in_specs += [line_spec, tokens(part, lanes), tokens(part, lanes)]
            in_specs += [pl.BlockSpec((rows, lanes), lambda i: (0, i)), message_spec]
            in_specs += [pl.BlockSpec(memory_space=pl.ANY)] * wide
            operands = [step_raw, bias, decay, step, cum, write_t, read_t, skip]
            operands += [head_inputs, output_grad, own_parts[part][0], returned[part]]
            operands += layer_parts
            aliases = {}
            if not first:
                in_specs += [sums_out[0], through_out[0], pl.BlockSpec(memory_space=pl.ANY)]
                operands += [early[1], early[2], early[0]]
                aliases = {len(operands) - 1: 0}
            scratch = [((rows, 2 * heads), BF16)] * 2 + [((rows, 4 * state), BF16)]
            out = [(tokens(part, lanes), (rows, channels), BF16)]
            if last:
                for which in (1, 2, 3):
                    operands += [one[which] for one in own_parts]
                    in_specs += [whole(one[which].shape) for one in own_parts]
                out += [(whole((columns, rows)), (columns, rows), BF16)]
                scratch = [sums_out[1:], through_out[1:]] + scratch
            else:
                out += [sums_out, through_out]
            early = call(
                functools.partial(
                    carry_kernel, head_width, scale, part * part_heads, parts, wide, first, last
                ),
                steps,
                in_specs,
                out,
                scratch,
                32 * rows * part_lanes * state,
                18 * 2**20 // parts,
                aliases,
            )(*operands)
    grad_x, table = early

    with jax.named_scope("projection"):
        tables = [swap(table, "wide", turn) for turn in range(wide)]
        coded = (columns + META, own_model)
        plane_spec = pl.BlockSpec((1, rows, own_model), lambda i, p: (p[1] ^ i, 0, 0))
        products = pl.pallas_call(
            functools.partial(product_kernel, planes),
            grid_spec=pltpu.PrefetchScalarGridSpec(
                num_scalar_prefetch=1,
                grid=(planes,),
                in_specs=[pl.BlockSpec((columns, rows), lambda i, p: (0, 0))] * wide
                + [plane_spec] * wide,
                out_specs=[pl.BlockSpec(coded, lambda i, p: (0, 0))] * planes,
            ),
            out_shape=[jax.ShapeDtypeStruct(coded, BF16)] * planes,
            compiler_params=pltpu.CompilerParams(vmem_limit_bytes=VMEM_LIMIT),
            cost_estimate=pl.CostEstimate(
                flops=2 * rows * model * columns, bytes_accessed=6 * 2**20, transcendentals=0
            ),
        )(place, *tables, *layer_parts)
        sums = [swap(one, "seq", turn) for turn, one in enumerate(products)]
        (weight_grad,) = call(
            functools.partial(gather_kernel, 1.0 / math.sqrt(rows * blocks)),
            1,
            [whole(coded)] * planes,
            [(whole((own_model, columns)), (own_model, columns), F32)],
            [],
            2**20,
            2**20,
        )(*sums)
    return grad_x, weight_grad


def solution(mesh):
    in_specs = (
        P(("wide", "seq"), None),
        P(("wide", "seq"), None),
        P(("wide", "seq"), None),
        P(("wide", "seq"), None),
        P(("wide", "seq"), None),
        P(("wide", "seq"), None),
        P(),
        P(),
        P(),
    )
    out_specs = (P(("wide", "seq"), None), P(("seq", "wide"), None))
    return jax.shard_map(body, mesh=mesh, in_specs=in_specs, out_specs=out_specs, check_vma=False)
```

```python
import functools
import math

import jax
import jax.numpy as jnp
from jax import lax
from jax.experimental import pallas as pl
from jax.experimental.pallas import tpu as pltpu
from jax.sharding import PartitionSpec as P

F32 = jnp.float32
BF16 = jnp.bfloat16
EXACT = lax.Precision.HIGHEST
VMEM_LIMIT = 56 * 1024 * 1024
TOP_POWER = 30.0
PRODUCT_BOUND = 30.0
CARRY_HEADS = 16
PAIR_HEADS = 8
META = 8
HALVES = 2
SHORT = pl.CostEstimate(flops=1000, bytes_accessed=1000, transcendentals=0)


def mul(a, b):
    return lax.dot_general(a, b, (((1,), (0,)), ((), ())), preferred_element_type=F32)


def mul_nt(a, b):
    return lax.dot_general(a, b, (((1,), (1,)), ((), ())), preferred_element_type=F32)


def mul_exact(a, b, dims=((1,), (0,))):
    return lax.dot_general(a, b, (dims, ((), ())), preferred_element_type=F32, precision=EXACT)


def halves(value):
    top = value.astype(BF16)
    return top, (value - top.astype(F32)).astype(BF16)


def power_for(bound):
    power = jnp.floor(TOP_POWER - jnp.log2(jnp.maximum(bound, 1e-37)))
    return jnp.clip(power, -100.0, 100.0)


def thirds(value):
    top, rest = value.astype(BF16), value
    rest = rest - top.astype(F32)
    middle = rest.astype(BF16)
    return top, middle, (rest - middle.astype(F32)).astype(BF16)


def encode(value):
    square = value * value
    fourth = square * square
    return jnp.where(value < 0, -fourth, fourth).astype(BF16)


def decode(coded):
    coded = coded.astype(F32)
    size = jnp.maximum(jnp.abs(coded), 1e-37)
    inverse = lax.rsqrt(size)
    return coded * inverse * lax.rsqrt(size * inverse)


def head_selector(first_head, heads, lanes, head_width):
    row = lax.broadcasted_iota(jnp.int32, (heads, lanes), 0)
    lane = lax.broadcasted_iota(jnp.int32, (heads, lanes), 1)
    return jnp.where(row == first_head + lane // head_width, 1.0, 0.0).astype(BF16)


def triangle(length, keep):
    row = lax.broadcasted_iota(jnp.int32, (length, length), 0)
    col = lax.broadcasted_iota(jnp.int32, (length, length), 1)
    return jnp.where(keep(row, col), 1.0, 0.0).astype(F32)


def summary_kernel(
    head_width,
    raw_ref,
    bias_ref,
    decay_ref,
    write_ref,
    read_ref,
    x_ref,
    dy_ref,
    message_ref,
    step_ref,
    cum_ref,
    weight_f,
    weight_b,
    facts,
):
    turn = pl.program_id(0)
    heads = raw_ref.shape[1]
    rows, lanes = x_ref.shape
    state = write_ref.shape[0]

    @pl.when(turn == 0)
    def _():
        step = jax.nn.softplus(raw_ref[...].astype(F32) + bias_ref[...])
        rate = -jnp.exp(decay_ref[...])
        cum = mul_exact(triangle(rows, lambda r, c: r >= c), step * rate)
        finish = cum[rows - 1 : rows, :]
        forward = step * jnp.exp(finish - cum)
        backward = jnp.exp(cum)
        power_f = power_for(PRODUCT_BOUND * jnp.sum(forward, axis=0, keepdims=True))
        power_b = power_for(PRODUCT_BOUND * jnp.sum(backward, axis=0, keepdims=True))
        step_ref[...] = step
        cum_ref[...] = cum
        parts = thirds(jnp.maximum(finish, -1e30))
        facts[...] = jnp.concatenate(
            [part.astype(F32) for part in parts]
            + [power_f, power_b, jnp.zeros((META - 5, heads), F32)],
            axis=0,
        ).astype(BF16)
        top, low = halves(forward * jnp.exp2(power_f))
        weight_f[...] = jnp.concatenate([top, low], axis=1)
        top, low = halves(backward * jnp.exp2(power_b))
        weight_b[...] = jnp.concatenate([top, low], axis=1)

    pick = head_selector(turn * (lanes // head_width), heads, lanes, head_width)
    pick_twice = jnp.concatenate([pick, pick], axis=0)
    width = message_ref.shape[2]

    def put(start, value):
        for owner in range(message_ref.shape[0]):
            message_ref[owner, start : start + value.shape[0], :] = value[
                :, owner * width : (owner + 1) * width
            ]

    def summed(tokens_ref, weight, rows_t):
        top, low = halves(tokens_ref[...].astype(F32) * mul(weight[...], pick_twice))
        return encode(mul(rows_t[...], top) + mul(rows_t[...], low))

    put(0, summed(x_ref, weight_f, write_ref))
    put(state, summed(dy_ref, weight_b, read_ref))
    put(2 * state, mul(facts[...], pick).astype(BF16))


def scan_kernel(message_ref, after_ref, answer_ref, powers):
    blocks, double, lanes = message_ref.shape
    state = (double - META) // 2
    top = 2.0**TOP_POWER

    def one(block, start, power_row, side, running, bound):
        facts = message_ref[block, 2 * state : double, :].astype(F32)
        decay = jnp.exp(facts[0:1] + facts[1:2] + facts[2:3])
        back = jnp.exp2(-facts[power_row : power_row + 1])
        power = power_for(bound)
        powers[side, pl.ds(block, 1), :] = power
        answer_ref[block, start : start + state, :] = encode(running * jnp.exp2(power))
        own = decode(message_ref[block, start : start + state, :]) * back
        return running * decay + own, bound * decay + top * back

    def both(block, carry):
        ahead, ahead_bound, behind, behind_bound = carry
        return one(block, 0, 3, 0, ahead, ahead_bound) + one(
            blocks - 1 - block, state, 4, 1, behind, behind_bound
        )

    zero, none = jnp.zeros((state, lanes), F32), jnp.zeros((1, lanes), F32)
    lax.fori_loop(0, blocks, both, (zero, none, zero, none), unroll=4)
    row = lax.broadcasted_iota(jnp.int32, (blocks, META, lanes), 1)
    ahead, behind = powers[0][:, None, :], powers[1][:, None, :]
    meta = jnp.where(row == 0, ahead, jnp.where(row == 1, behind, 0.0))
    answer_ref[:, 2 * state : double, :] = meta.astype(BF16)


def block_kernel(
    head_width,
    scale,
    step_ref,
    cum_ref,
    write_ref,
    read_ref,
    x_ref,
    dy_ref,
    after_ref,
    inner_ref,
    own_ref,
    within_ref,
    maps_ref,
    read_write,
    source,
    cum_rows,
    pair_sum,
    out_flow,
):
    turn = pl.program_id(0)
    rows, lanes = x_ref.shape
    half = rows // 2
    heads = step_ref.shape[1]
    group = lanes // head_width

    @pl.when(turn == 0)
    def _():
        read_write[...] = scale * lax.dot_general(
            write_ref[...], read_ref[...], (((0,), (0,)), ((), ())), preferred_element_type=F32
        )
        source[...] = jnp.log(step_ref[...]) - cum_ref[...]
        cum_rows[...] = cum_ref[...].T
        pair_sum[...] = jnp.zeros_like(pair_sum)
        out_flow[...] = jnp.zeros_like(out_flow)
        own_ref[...] = jnp.zeros_like(own_ref)

    first = turn * group
    near = pltpu.roll(source[...], lax.rem(heads - first, heads), axis=1)
    near_cum = cum_rows[pl.ds(first, group), :]
    row = lax.broadcasted_iota(jnp.int32, (half, half), 0)
    col = lax.broadcasted_iota(jnp.int32, (half, half), 1)
    ahead = col >= row
    lane = lax.broadcasted_iota(jnp.int32, (half, 2 * head_width), 1)
    first_half = lane < head_width
    head_lane = lax.broadcasted_iota(jnp.int32, (half, heads), 1)
    flow_aa = read_write[0:half, 0:half]
    flow_ab = read_write[0:half, half:rows]
    flow_bb = read_write[half:rows, half:rows]
    sum_aa = jnp.zeros((half, half), F32)
    sum_ab = jnp.zeros((half, half), F32)
    sum_bb = jnp.zeros((half, half), F32)
    own_a = jnp.zeros((half, heads), F32)
    own_b = jnp.zeros((half, heads), F32)
    zero = jnp.zeros((half, 2 * head_width), BF16)
    flows = []
    for pair in range(group // 2):
        span = slice(pair * 2 * head_width, (pair + 1) * 2 * head_width)
        x_a, x_b = x_ref[0:half, span], x_ref[half:rows, span]
        dy_a, dy_b = dy_ref[0:half, span], dy_ref[half:rows, span]
        early_a, late_a = jnp.where(first_half, dy_a, zero), jnp.where(first_half, zero, dy_a)
        early_b, late_b = jnp.where(first_half, dy_b, zero), jnp.where(first_half, zero, dy_b)
        stack = jnp.concatenate([early_a, early_b, late_a, late_b], axis=0)
        stack_b = jnp.concatenate([early_b, late_b], axis=0)
        grad_a = mul_nt(x_a, stack)
        grad_b = mul_nt(x_b, stack_b)
        masks_a, masks_b = [], []
        for side in range(2):
            place = pair * 2 + side
            head = first + place
            from_a = near[0:half, place : place + 1]
            from_b = near[half:rows, place : place + 1]
            to_a = near_cum[place : place + 1, 0:half]
            to_b = near_cum[place : place + 1, half:rows]
            fade_aa = jnp.exp(jnp.where(ahead, to_a + from_a, -1e30))
            fade_ab = jnp.exp(to_b + from_a)
            fade_bb = jnp.exp(jnp.where(ahead, to_b + from_b, -1e30))
            weigh_aa = fade_aa * grad_a[:, side * rows : side * rows + half]
            weigh_ab = fade_ab * grad_a[:, side * rows + half : (side + 1) * rows]
            weigh_bb = fade_bb * grad_b[:, side * half : (side + 1) * half]
            sum_aa += weigh_aa
            sum_ab += weigh_ab
            sum_bb += weigh_bb
            masks_a += [(fade_aa * flow_aa).astype(BF16), (fade_ab * flow_ab).astype(BF16)]
            masks_b += [(fade_bb * flow_bb).astype(BF16)]
            pair_aa = weigh_aa * flow_aa
            pair_ab = weigh_ab * flow_ab
            pair_bb = weigh_bb * flow_bb
            flow_out = jnp.sum(pair_aa + pair_ab, axis=1, keepdims=True)
            own_a = jnp.where(head_lane == head, flow_out, own_a)
            flow_out = jnp.sum(pair_bb, axis=1, keepdims=True)
            own_b = jnp.where(head_lane == head, flow_out, own_b)
            flow_in = [
                jnp.sum(pair_aa, axis=0, keepdims=True),
                jnp.sum(pair_ab, axis=0, keepdims=True) + jnp.sum(pair_bb, axis=0, keepdims=True),
            ]
            flows.append(jnp.concatenate(flow_in, axis=1))
        inner_ref[0:half, span] = mul(jnp.concatenate(masks_a, axis=1), stack).astype(BF16)
        inner_ref[half:rows, span] = mul(jnp.concatenate(masks_b, axis=1), stack_b).astype(BF16)
    out_flow[pl.ds(first, group), :] = jnp.concatenate(flows, axis=0)
    pair_sum[0:half, 0:half] += sum_aa
    pair_sum[0:half, half:rows] += sum_ab
    pair_sum[half:rows, half:rows] += sum_bb
    own_ref[0:half, :] += own_a
    own_ref[half:rows, :] += own_b

    @pl.when(turn == pl.num_programs(0) - 1)
    def _():
        net = own_ref[...] - out_flow[...].T
        within_ref[...] = mul_exact(triangle(rows, lambda r, c: r > c), net)
        weighted = scale * pair_sum[...]
        maps_ref[...] = jnp.concatenate(
            [
                mul_exact(weighted, read_ref[...].astype(F32), ((1,), (1,))),
                mul_exact(weighted, write_ref[...].astype(F32), ((0,), (1,))),
            ],
            axis=1,
        )


def carry_kernel(head_width, scale, first_head, waits, first, last, *refs):
    refs = list(refs)
    take = lambda count: [refs.pop(0) for _ in range(count)]
    raw_ref, bias_ref, decay_ref, step_ref, cum_ref, write_ref, read_ref, skip_ref = take(8)
    x_ref, dy_ref, inner_ref, answer_ref = take(4)
    take(waits)
    if not first:
        early_sums, early_through, _ = take(3)
    if last:
        own_ref, within_ref, map_ref = take(3)
        grad_ref, table_ref, sums, through, weight_e, weight_s, maps = take(7)
    else:
        grad_ref, sums, through, weight_e, weight_s, maps = take(6)
    turn = pl.program_id(0)
    rows, lanes = x_ref.shape
    heads = step_ref.shape[1]
    state = write_ref.shape[0]
    future, past = slice(0, heads), slice(heads, 2 * heads)
    write_sum = slice(2 * heads, 2 * heads + 2 * state)
    read_sum = slice(2 * heads + 2 * state, 2 * heads + 4 * state)

    @pl.when(turn == 0)
    def _():
        cum = cum_ref[...]
        finish = cum[rows - 1 : rows, :]
        top, low = halves(step_ref[...] * jnp.exp(finish - cum) * scale)
        weight_e[...] = jnp.concatenate([top, low], axis=1)
        top, low = halves(jnp.exp(cum) * scale)
        weight_s[...] = jnp.concatenate([top, low], axis=1)
        write = write_ref[...].astype(F32).T.astype(BF16)
        read = read_ref[...].astype(F32).T.astype(BF16)
        maps[...] = jnp.concatenate([write, write, read, read], axis=1)
        if first:
            sums[...] = jnp.zeros_like(sums)
            through[...] = jnp.zeros_like(through)
        else:
            sums[...] = early_sums[...]
            through[...] = early_through[...]

    pick = head_selector(first_head + turn * (lanes // head_width), heads, lanes, head_width)
    pick_twice = jnp.concatenate([pick, pick], axis=0)
    starts, ends = [], []
    for piece in range(answer_ref.shape[0]):
        back = jnp.exp2(-answer_ref[piece, 2 * state : 2 * state + META, :].astype(F32))
        starts.append(decode(answer_ref[piece, 0:state, :]) * back[0:1])
        ends.append(decode(answer_ref[piece, state : 2 * state, :]) * back[1:2])
    start = jnp.concatenate(starts, axis=1)
    end = jnp.concatenate(ends, axis=1)
    start_parts = jnp.concatenate(halves(start), axis=0)
    end_parts = jnp.concatenate(halves(end), axis=0)
    x = x_ref[...].astype(F32)
    dy = dy_ref[...].astype(F32)
    skip = jnp.concatenate(
        [part.astype(F32) for part in thirds(skip_ref[...])] + [jnp.zeros((13, heads), F32)], axis=0
    )
    skip = jnp.sum(mul(skip.astype(BF16), pick), axis=0, keepdims=True)

    spread_e = mul(weight_e[...], pick_twice)
    carried = mul(maps[:, 0 : 2 * state], end_parts) * spread_e
    grad_ref[...] = (inner_ref[...].astype(F32) + skip * dy + carried).astype(BF16)
    top, low = halves(x * carried)
    sums[:, future] += mul_nt(top, pick) + mul_nt(low, pick)
    top, low = halves(x * spread_e)
    sums[:, write_sum] += mul_nt(top, end_parts) + mul_nt(low, end_parts)

    weighted = dy * mul(weight_s[...], pick_twice)
    top, low = halves(weighted * mul(maps[:, 2 * state : 4 * state], start_parts))
    sums[:, past] += mul_nt(top, pick) + mul_nt(low, pick)
    top, low = halves(weighted)
    sums[:, read_sum] += mul_nt(top, start_parts) + mul_nt(low, start_parts)

    both = jnp.broadcast_to(jnp.sum(start * end, axis=0, keepdims=True), (8, lanes))
    top, low = halves(both)
    through[...] += mul_nt(top, pick) + mul_nt(low, pick)

    if not last:
        return

    @pl.when(turn == pl.num_programs(0) - 1)
    def _():
        rate = -jnp.exp(decay_ref[...])
        step = step_ref[...]
        gate = jax.nn.sigmoid(raw_ref[...].astype(F32) + bias_ref[...])
        finish = cum_ref[rows - 1 : rows, :]
        to_come = sums[:, future]
        decay_grad = (
            within_ref[...]
            + mul_exact(triangle(rows, lambda r, c: r <= c), sums[:, past])
            + mul_exact(triangle(rows, lambda r, c: r > c), to_come)
            + jnp.exp(finish) * scale * through[0:1, :]
        )
        ratio = jnp.where(step > 1e-30, gate / jnp.maximum(step, 1e-30), 1.0)
        inner = own_ref[...] + to_come
        raw_grad = inner * ratio + rate * decay_grad * gate
        map_sum = sums[:, 2 * heads :] + 0.0
        write_all = map_sum[:, 0:state] + map_sum[:, state : 2 * state]
        read_all = map_sum[:, 2 * state : 3 * state] + map_sum[:, 3 * state :]
        map_grad = jnp.concatenate([write_all, read_all], axis=1)
        map_grad += map_ref[...]
        table_ref[...] = jnp.concatenate([raw_grad.T, map_grad.T], axis=0).astype(BF16)


def deal_kernel(place_ref, layer_ref, after_ref, *out_refs):
    width = out_refs[0].shape[2]
    for turn, out_ref in enumerate(out_refs):
        start = pl.multiple_of((place_ref[0] ^ turn) * width, width)
        out_ref[0, :, :] = layer_ref[:, pl.ds(start, width)]


def product_kernel(planes, place_ref, *refs):
    step = pl.program_id(0)
    wide = (len(refs) - planes) // 2
    table_refs, layer_refs, out_refs = refs[:wide], refs[wide : 2 * wide], refs[2 * wide :]
    total = sum(mul(table[...], layer[0]) for table, layer in zip(table_refs, layer_refs))
    columns = total.shape[0]
    most = jnp.max(jnp.abs(total), axis=0, keepdims=True)
    power = power_for(jnp.max(most, axis=1, keepdims=True))
    coded = encode(total * jnp.exp2(power))
    for plane in range(planes):

        @pl.when(step == plane)
        def _(out_ref=out_refs[plane]):
            out_ref[0:columns, :] = coded
            out_ref[columns:, :] = jnp.broadcast_to(power, out_ref[columns:, :].shape).astype(BF16)


def gather_kernel(factor, *refs):
    part_refs, out_ref = refs[:-1], refs[-1]
    columns = out_ref.shape[1]
    total = jnp.zeros((columns, out_ref.shape[0]), F32)
    for part_ref in part_refs:
        power = part_ref[columns:, :].astype(F32)[0:1]
        total += decode(part_ref[0:columns, :]) * jnp.exp2(-power)
    out_ref[...] = (total * factor).T


def swap(array, axis, turn):
    if turn == 0:
        return array
    count = lax.axis_size(axis)
    return lax.ppermute(array, axis, [(one, one ^ turn) for one in range(count)])


def whole(shape):
    return pl.BlockSpec(shape, lambda i: (0,) * len(shape))


def call(kernel, steps, in_specs, out, scratch, aliases=None):
    return pl.pallas_call(
        kernel,
        grid=(steps,),
        in_specs=in_specs,
        out_specs=[spec for spec, _, _ in out],
        out_shape=[jax.ShapeDtypeStruct(dims, dtype) for _, dims, dtype in out],
        scratch_shapes=[pltpu.VMEM(dims, dtype) for dims, dtype in scratch],
        compiler_params=pltpu.CompilerParams(vmem_limit_bytes=VMEM_LIMIT),
        cost_estimate=SHORT,
        input_output_aliases=aliases or {},
    )


def body(
    layer_input,
    head_inputs,
    output_grad,
    step_raw,
    state_write,
    state_read,
    decay_log,
    step_bias,
    skip_gain,
):
    rows, channels = head_inputs.shape
    heads = step_raw.shape[1]
    head_width = channels // heads
    state = state_write.shape[1]
    model = layer_input.shape[1]
    columns = heads + 2 * state
    axes = ("wide", "seq")
    wide, planes = lax.axis_size("wide"), lax.axis_size("seq")
    blocks = wide * planes
    own_model = model // blocks
    scale = float(rows * blocks * state) ** -0.5
    parts = HALVES if heads % (HALVES * blocks) == 0 else 1
    part_heads = heads // parts
    part_lanes = channels // parts
    owner_lanes = part_lanes // blocks
    piece_lanes = max(owner_lanes, 128)
    pieces = part_lanes // piece_lanes
    depth = 2 * state + META
    bias = step_bias[None, :]
    decay = decay_log[None, :]
    skip = skip_gain[None, :]
    write_t, read_t = state_write.T, state_read.T

    lanes = CARRY_HEADS * head_width
    steps = part_lanes // lanes
    here = lanes // piece_lanes

    def tokens(part, width):
        first = part * (part_lanes // width)
        return pl.BlockSpec((rows, width), lambda i: (0, first + i))

    message_spec = pl.BlockSpec((here, depth, piece_lanes), lambda i: (i, 0, 0))
    both_spec = pl.BlockSpec((here, depth, piece_lanes), lambda i: (i % steps, 0, i // steps))
    head_spec = whole((rows, heads))
    line_spec = whole((1, heads))
    map_spec = whole((state, rows))
    head_out = (head_spec, (rows, heads), F32)

    def exchange(array):
        return lax.all_to_all(array, axes, split_axis=0, concat_axis=0, tiled=True)

    def to_owner(array):
        if owner_lanes < piece_lanes:
            split = array.reshape(pieces, depth, piece_lanes // owner_lanes, owner_lanes)
            array = jnp.moveaxis(split, 2, 1).reshape(blocks, depth, owner_lanes)
        return exchange(array)

    def from_owner(array):
        array = exchange(array)
        if owner_lanes < piece_lanes:
            split = array.reshape(pieces, piece_lanes // owner_lanes, depth, owner_lanes)
            array = jnp.moveaxis(split, 1, 2).reshape(pieces, depth, piece_lanes)
        return array

    def scan(part, message):
        dims = (blocks, depth, owner_lanes)
        (answer,) = call(
            scan_kernel,
            1,
            [pl.BlockSpec(dims, lambda i: (0, 0, part)), pl.BlockSpec(memory_space=pl.ANY)],
            [(whole(dims), dims, BF16)],
            [((2, blocks, owner_lanes), F32)],
        )(message, own)
        return answer

    with jax.named_scope("summaries"):
        message, step, cum = call(
            functools.partial(summary_kernel, head_width),
            parts * steps,
            [head_spec, line_spec, line_spec, map_spec, map_spec, tokens(0, lanes), tokens(0, lanes)],
            [(both_spec, (pieces, depth, parts * piece_lanes), BF16), head_out, head_out],
            [((rows, 2 * heads), BF16), ((rows, 2 * heads), BF16), ((META, heads), BF16)],
        )(step_raw, bias, decay, write_t, read_t, head_inputs, output_grad)
    place = jnp.stack([lax.axis_index("wide"), lax.axis_index("seq")]).astype(jnp.int32)
    with jax.named_scope("layer"):
        if own_model % 128:
            cut = jnp.transpose(layer_input.reshape(rows, planes, wide, own_model), (2, 1, 0, 3))
            dealt = [
                lax.dynamic_index_in_dim(cut, place[0] ^ turn, 0, False) for turn in range(wide)
            ]
        else:
            dealt = pl.pallas_call(
                deal_kernel,
                grid_spec=pltpu.PrefetchScalarGridSpec(
                    num_scalar_prefetch=1,
                    grid=(planes,),
                    in_specs=[
                        pl.BlockSpec((rows, wide * own_model), lambda i, p: (0, i)),
                        pl.BlockSpec(memory_space=pl.ANY),
                    ],
                    out_specs=[pl.BlockSpec((1, rows, own_model), lambda i, p: (i, 0, 0))] * wide,
                ),
                out_shape=[jax.ShapeDtypeStruct((planes, rows, own_model), BF16)] * wide,
                compiler_params=pltpu.CompilerParams(vmem_limit_bytes=VMEM_LIMIT),
                cost_estimate=SHORT,
            )(place, layer_input, cum)
        layer_parts = [swap(one, "wide", turn) for turn, one in enumerate(dealt)]
    with jax.named_scope("own_block"):
        width = PAIR_HEADS * head_width
        inner, own, within, maps = call(
            functools.partial(block_kernel, head_width, scale),
            channels // width,
            [head_spec, head_spec, map_spec, map_spec, tokens(0, width), tokens(0, width)]
            + [pl.BlockSpec(memory_space=pl.ANY)],
            [
                (tokens(0, width), (rows, channels), BF16),
                head_out,
                head_out,
                (whole((rows, 2 * state)), (rows, 2 * state), F32),
            ],
            [
                ((rows, rows), F32),
                ((rows, heads), F32),
                ((heads, rows), F32),
                ((rows, rows), F32),
                ((heads, rows), F32),
            ],
        )(step, cum, write_t, read_t, head_inputs, output_grad, dealt[0])
    with jax.named_scope("scan"):
        arrived = to_owner(message)
        returned = [from_owner(scan(part, arrived)) for part in range(parts)]

    sums_out = (whole((rows, 2 * heads + 4 * state)), (rows, 2 * heads + 4 * state), F32)
    through_out = (whole((8, heads)), (8, heads), F32)
    early = ()
    with jax.named_scope("carried"):
        for part in range(parts):
            first, last = part == 0, part == parts - 1
            in_specs = [head_spec, line_spec, line_spec, head_spec, head_spec, map_spec, map_spec]
            in_specs += [line_spec, tokens(part, lanes), tokens(part, lanes)]
            in_specs += [tokens(part, lanes), message_spec]
            in_specs += [pl.BlockSpec(memory_space=pl.ANY)] * wide
            operands = [step_raw, bias, decay, step, cum, write_t, read_t, skip]
            operands += [head_inputs, output_grad, inner, returned[part]]
            operands += layer_parts
            aliases = {}
            if not first:
                in_specs += [sums_out[0], through_out[0], pl.BlockSpec(memory_space=pl.ANY)]
                operands += [early[1], early[2], early[0]]
                aliases = {len(operands) - 1: 0}
            scratch = [((rows, 2 * heads), BF16)] * 2 + [((rows, 4 * state), BF16)]
            out = [(tokens(part, lanes), (rows, channels), BF16)]
            if last:
                operands += [own, within, maps]
                in_specs += [head_spec, head_spec, whole(maps.shape)]
                out += [(whole((columns, rows)), (columns, rows), BF16)]
                scratch = [sums_out[1:], through_out[1:]] + scratch
            else:
                out += [sums_out, through_out]
            early = call(
                functools.partial(
                    carry_kernel, head_width, scale, part * part_heads, wide, first, last
                ),
                steps,
                in_specs,
                out,
                scratch,
                aliases,
            )(*operands)
    grad_x, table = early

    with jax.named_scope("projection"):
        tables = [swap(table, "wide", turn) for turn in range(wide)]
        coded = (columns + META, own_model)
        plane_spec = pl.BlockSpec((1, rows, own_model), lambda i, p: (p[1] ^ i, 0, 0))
        products = pl.pallas_call(
            functools.partial(product_kernel, planes),
            grid_spec=pltpu.PrefetchScalarGridSpec(
                num_scalar_prefetch=1,
                grid=(planes,),
                in_specs=[pl.BlockSpec((columns, rows), lambda i, p: (0, 0))] * wide
                + [plane_spec] * wide,
                out_specs=[pl.BlockSpec(coded, lambda i, p: (0, 0))] * planes,
            ),
            out_shape=[jax.ShapeDtypeStruct(coded, BF16)] * planes,
            compiler_params=pltpu.CompilerParams(vmem_limit_bytes=VMEM_LIMIT),
            cost_estimate=SHORT,
        )(place, *tables, *layer_parts)
        sums = [swap(one, "seq", turn) for turn, one in enumerate(products)]
        (weight_grad,) = call(
            functools.partial(gather_kernel, 1.0 / math.sqrt(rows * blocks)),
            1,
            [whole(coded)] * planes,
            [(whole((own_model, columns)), (own_model, columns), F32)],
            [],
        )(*sums)
    return grad_x, weight_grad


def solution(mesh):
    in_specs = (
        P(("wide", "seq"), None),
        P(("wide", "seq"), None),
        P(("wide", "seq"), None),
        P(("wide", "seq"), None),
        P(("wide", "seq"), None),
        P(("wide", "seq"), None),
        P(),
        P(),
        P(),
    )
    out_specs = (P(("wide", "seq"), None), P(("seq", "wide"), None))
    return jax.shard_map(body, mesh=mesh, in_specs=in_specs, out_specs=out_specs, check_vma=False)
```

```python
import functools
import math

import jax
import jax.numpy as jnp
from jax import lax
from jax.experimental import pallas as pl
from jax.experimental.pallas import tpu as pltpu
from jax.sharding import PartitionSpec as P

F32 = jnp.float32
BF16 = jnp.bfloat16
EXACT = lax.Precision.HIGHEST
VMEM_LIMIT = 56 * 1024 * 1024
TOP_POWER = 30.0
PRODUCT_BOUND = 30.0
CARRY_HEADS = 16
PAIR_HEADS = 8
META = 8
HALVES = 2
TILE = 256
SHORT = pl.CostEstimate(flops=1000, bytes_accessed=1000, transcendentals=0)


def mul(a, b):
    return lax.dot_general(a, b, (((1,), (0,)), ((), ())), preferred_element_type=F32)


def mul_nt(a, b):
    return lax.dot_general(a, b, (((1,), (1,)), ((), ())), preferred_element_type=F32)


def mul_exact(a, b, dims=((1,), (0,))):
    return lax.dot_general(a, b, (dims, ((), ())), preferred_element_type=F32, precision=EXACT)


def halves(value):
    top = value.astype(BF16)
    return top, (value - top.astype(F32)).astype(BF16)


def power_for(bound):
    power = jnp.floor(TOP_POWER - jnp.log2(jnp.maximum(bound, 1e-37)))
    return jnp.clip(power, -100.0, 100.0)


def thirds(value):
    top, rest = value.astype(BF16), value
    rest = rest - top.astype(F32)
    middle = rest.astype(BF16)
    return top, middle, (rest - middle.astype(F32)).astype(BF16)


def encode(value):
    square = value * value
    fourth = square * square
    return jnp.where(value < 0, -fourth, fourth).astype(BF16)


def decode(coded):
    coded = coded.astype(F32)
    size = jnp.maximum(jnp.abs(coded), 1e-37)
    inverse = lax.rsqrt(size)
    return coded * inverse * lax.rsqrt(size * inverse)


def head_selector(first_head, heads, lanes, head_width):
    row = lax.broadcasted_iota(jnp.int32, (heads, lanes), 0)
    lane = lax.broadcasted_iota(jnp.int32, (heads, lanes), 1)
    return jnp.where(row == first_head + lane // head_width, 1.0, 0.0).astype(BF16)


def triangle(length, keep):
    row = lax.broadcasted_iota(jnp.int32, (length, length), 0)
    col = lax.broadcasted_iota(jnp.int32, (length, length), 1)
    return jnp.where(keep(row, col), 1.0, 0.0).astype(F32)


def summary_kernel(
    head_width,
    raw_ref,
    bias_ref,
    decay_ref,
    write_ref,
    read_ref,
    x_ref,
    dy_ref,
    message_ref,
    step_ref,
    cum_ref,
    weight_f,
    weight_b,
    facts,
):
    turn = pl.program_id(0)
    heads = raw_ref.shape[1]
    rows, lanes = x_ref.shape
    state = write_ref.shape[0]

    @pl.when(turn == 0)
    def _():
        step = jax.nn.softplus(raw_ref[...].astype(F32) + bias_ref[...])
        rate = -jnp.exp(decay_ref[...])
        cum = mul_exact(triangle(rows, lambda r, c: r >= c), step * rate)
        finish = cum[rows - 1 : rows, :]
        forward = step * jnp.exp(finish - cum)
        backward = jnp.exp(cum)
        power_f = power_for(PRODUCT_BOUND * jnp.sum(forward, axis=0, keepdims=True))
        power_b = power_for(PRODUCT_BOUND * jnp.sum(backward, axis=0, keepdims=True))
        step_ref[...] = step
        cum_ref[...] = cum
        parts = thirds(jnp.maximum(finish, -1e30))
        facts[...] = jnp.concatenate(
            [part.astype(F32) for part in parts]
            + [power_f, power_b, jnp.zeros((META - 5, heads), F32)],
            axis=0,
        ).astype(BF16)
        top, low = halves(forward * jnp.exp2(power_f))
        weight_f[...] = jnp.concatenate([top, low], axis=1)
        top, low = halves(backward * jnp.exp2(power_b))
        weight_b[...] = jnp.concatenate([top, low], axis=1)

    width = message_ref.shape[2]

    def summed(tokens, weight, pick, rows_t):
        top, low = halves(tokens.astype(F32) * mul(weight[...], pick))
        return encode(mul(rows_t[...], top) + mul(rows_t[...], low))

    for tile in range(lanes // TILE):
        span = slice(tile * TILE, (tile + 1) * TILE)
        first = (turn * lanes + tile * TILE) // head_width
        pick = head_selector(first, heads, TILE, head_width)
        pick_twice = jnp.concatenate([pick, pick], axis=0)
        ahead = summed(x_ref[:, span], weight_f, pick_twice, write_ref)
        behind = summed(dy_ref[:, span], weight_b, pick_twice, read_ref)
        fact = mul(facts[...], pick).astype(BF16)
        for piece in range(TILE // width):
            owner = tile * (TILE // width) + piece
            part = slice(piece * width, (piece + 1) * width)
            message_ref[owner, 0:state, :] = ahead[:, part]
            message_ref[owner, state : 2 * state, :] = behind[:, part]
            message_ref[owner, 2 * state :, :] = fact[:, part]


def scan_kernel(message_ref, *rest):
    answer_ref, powers = rest[-2:]
    blocks, double, lanes = message_ref.shape
    state = (double - META) // 2
    top = 2.0**TOP_POWER

    def one(block, start, power_row, side, running, bound):
        facts = message_ref[block, 2 * state : double, :].astype(F32)
        decay = jnp.exp(facts[0:1] + facts[1:2] + facts[2:3])
        back = jnp.exp2(-facts[power_row : power_row + 1])
        power = power_for(bound)
        powers[side, pl.ds(block, 1), :] = power
        answer_ref[block, start : start + state, :] = encode(running * jnp.exp2(power))
        own = decode(message_ref[block, start : start + state, :]) * back
        return running * decay + own, bound * decay + top * back

    def both(block, carry):
        ahead, ahead_bound, behind, behind_bound = carry
        return one(block, 0, 3, 0, ahead, ahead_bound) + one(
            blocks - 1 - block, state, 4, 1, behind, behind_bound
        )

    zero, none = jnp.zeros((state, lanes), F32), jnp.zeros((1, lanes), F32)
    lax.fori_loop(0, blocks, both, (zero, none, zero, none), unroll=4)
    row = lax.broadcasted_iota(jnp.int32, (blocks, META, lanes), 1)
    ahead, behind = powers[0][:, None, :], powers[1][:, None, :]
    meta = jnp.where(row == 0, ahead, jnp.where(row == 1, behind, 0.0))
    answer_ref[:, 2 * state : double, :] = meta.astype(BF16)


def block_kernel(
    head_width,
    scale,
    first_head,
    waits,
    step_ref,
    cum_ref,
    write_ref,
    read_ref,
    x_ref,
    dy_ref,
    *rest,
):
    inner_ref, own_ref, within_ref, maps_ref = rest[waits : waits + 4]
    read_write, source, cum_rows, pair_sum, out_flow = rest[waits + 4 :]
    turn = pl.program_id(0)
    rows, lanes = x_ref.shape
    half = rows // 2
    heads = step_ref.shape[1]
    group = lanes // head_width

    @pl.when(turn == 0)
    def _():
        read_write[...] = scale * lax.dot_general(
            write_ref[...], read_ref[...], (((0,), (0,)), ((), ())), preferred_element_type=F32
        )
        source[...] = jnp.log(step_ref[...]) - cum_ref[...]
        cum_rows[...] = cum_ref[...].T
        pair_sum[...] = jnp.zeros_like(pair_sum)
        out_flow[...] = jnp.zeros_like(out_flow)
        own_ref[...] = jnp.zeros_like(own_ref)

    first = first_head + turn * group
    near = pltpu.roll(source[...], lax.rem(heads - first, heads), axis=1)
    near_cum = cum_rows[pl.ds(first, group), :]
    row = lax.broadcasted_iota(jnp.int32, (half, half), 0)
    col = lax.broadcasted_iota(jnp.int32, (half, half), 1)
    ahead = col >= row
    lane = lax.broadcasted_iota(jnp.int32, (half, 2 * head_width), 1)
    first_half = lane < head_width
    head_lane = lax.broadcasted_iota(jnp.int32, (half, heads), 1)
    flow_aa = read_write[0:half, 0:half]
    flow_ab = read_write[0:half, half:rows]
    flow_bb = read_write[half:rows, half:rows]
    sum_aa = jnp.zeros((half, half), F32)
    sum_ab = jnp.zeros((half, half), F32)
    sum_bb = jnp.zeros((half, half), F32)
    own_a = jnp.zeros((half, heads), F32)
    own_b = jnp.zeros((half, heads), F32)
    zero = jnp.zeros((half, 2 * head_width), BF16)
    flows = []
    for pair in range(group // 2):
        span = slice(pair * 2 * head_width, (pair + 1) * 2 * head_width)
        x_a, x_b = x_ref[0:half, span], x_ref[half:rows, span]
        dy_a, dy_b = dy_ref[0:half, span], dy_ref[half:rows, span]
        early_a, late_a = jnp.where(first_half, dy_a, zero), jnp.where(first_half, zero, dy_a)
        early_b, late_b = jnp.where(first_half, dy_b, zero), jnp.where(first_half, zero, dy_b)
        stack = jnp.concatenate([early_a, early_b, late_a, late_b], axis=0)
        stack_b = jnp.concatenate([early_b, late_b], axis=0)
        grad_a = mul_nt(x_a, stack)
        grad_b = mul_nt(x_b, stack_b)
        masks_a, masks_b = [], []
        for side in range(2):
            place = pair * 2 + side
            head = first + place
            from_a = near[0:half, place : place + 1]
            from_b = near[half:rows, place : place + 1]
            to_a = near_cum[place : place + 1, 0:half]
            to_b = near_cum[place : place + 1, half:rows]
            fade_aa = jnp.exp(jnp.where(ahead, to_a + from_a, -1e30))
            fade_ab = jnp.exp(to_b + from_a)
            fade_bb = jnp.exp(jnp.where(ahead, to_b + from_b, -1e30))
            weigh_aa = fade_aa * grad_a[:, side * rows : side * rows + half]
            weigh_ab = fade_ab * grad_a[:, side * rows + half : (side + 1) * rows]
            weigh_bb = fade_bb * grad_b[:, side * half : (side + 1) * half]
            sum_aa += weigh_aa
            sum_ab += weigh_ab
            sum_bb += weigh_bb
            masks_a += [(fade_aa * flow_aa).astype(BF16), (fade_ab * flow_ab).astype(BF16)]
            masks_b += [(fade_bb * flow_bb).astype(BF16)]
            pair_aa = weigh_aa * flow_aa
            pair_ab = weigh_ab * flow_ab
            pair_bb = weigh_bb * flow_bb
            flow_out = jnp.sum(pair_aa + pair_ab, axis=1, keepdims=True)
            own_a = jnp.where(head_lane == head, flow_out, own_a)
            flow_out = jnp.sum(pair_bb, axis=1, keepdims=True)
            own_b = jnp.where(head_lane == head, flow_out, own_b)
            flow_in = [
                jnp.sum(pair_aa, axis=0, keepdims=True),
                jnp.sum(pair_ab, axis=0, keepdims=True) + jnp.sum(pair_bb, axis=0, keepdims=True),
            ]
            flows.append(jnp.concatenate(flow_in, axis=1))
        inner_ref[0:half, span] = mul(jnp.concatenate(masks_a, axis=1), stack).astype(BF16)
        inner_ref[half:rows, span] = mul(jnp.concatenate(masks_b, axis=1), stack_b).astype(BF16)
    out_flow[pl.ds(first, group), :] = jnp.concatenate(flows, axis=0)
    pair_sum[0:half, 0:half] += sum_aa
    pair_sum[0:half, half:rows] += sum_ab
    pair_sum[half:rows, half:rows] += sum_bb
    own_ref[0:half, :] += own_a
    own_ref[half:rows, :] += own_b

    @pl.when(turn == pl.num_programs(0) - 1)
    def _():
        net = own_ref[...] - out_flow[...].T
        within_ref[...] = mul_exact(triangle(rows, lambda r, c: r > c), net)
        weighted = scale * pair_sum[...]
        maps_ref[...] = jnp.concatenate(
            [
                mul_exact(weighted, read_ref[...].astype(F32), ((1,), (1,))),
                mul_exact(weighted, write_ref[...].astype(F32), ((0,), (1,))),
            ],
            axis=1,
        )


def carry_kernel(head_width, scale, first_head, parts, first, last, *refs):
    refs = list(refs)
    take = lambda count: [refs.pop(0) for _ in range(count)]
    raw_ref, bias_ref, decay_ref, step_ref, cum_ref, write_ref, read_ref, skip_ref = take(8)
    x_ref, dy_ref, inner_ref, answer_ref = take(4)
    if not first:
        early_sums, early_through, _ = take(3)
    if last:
        own_refs, within_refs, map_refs = take(parts), take(parts), take(parts)
        grad_ref, table_ref, sums, through, weight_e, weight_s, maps = take(7)
    else:
        grad_ref, sums, through, weight_e, weight_s, maps = take(6)
    turn = pl.program_id(0)
    rows, lanes = x_ref.shape
    heads = step_ref.shape[1]
    state = write_ref.shape[0]
    future, past = slice(0, heads), slice(heads, 2 * heads)
    write_sum = slice(2 * heads, 2 * heads + 2 * state)
    read_sum = slice(2 * heads + 2 * state, 2 * heads + 4 * state)

    @pl.when(turn == 0)
    def _():
        cum = cum_ref[...]
        finish = cum[rows - 1 : rows, :]
        top, low = halves(step_ref[...] * jnp.exp(finish - cum) * scale)
        weight_e[...] = jnp.concatenate([top, low], axis=1)
        top, low = halves(jnp.exp(cum) * scale)
        weight_s[...] = jnp.concatenate([top, low], axis=1)
        write = write_ref[...].astype(F32).T.astype(BF16)
        read = read_ref[...].astype(F32).T.astype(BF16)
        maps[...] = jnp.concatenate([write, write, read, read], axis=1)
        if first:
            sums[...] = jnp.zeros_like(sums)
            through[...] = jnp.zeros_like(through)
        else:
            sums[...] = early_sums[...]
            through[...] = early_through[...]

    width = answer_ref.shape[2]
    skips = jnp.concatenate(
        [part.astype(F32) for part in thirds(skip_ref[...])] + [jnp.zeros((13, heads), F32)], axis=0
    ).astype(BF16)
    future_sum = past_sum = write_total = read_total = through_sum = 0.0
    for tile in range(lanes // TILE):
        span = slice(tile * TILE, (tile + 1) * TILE)
        first_of = first_head + (turn * lanes + tile * TILE) // head_width
        pick = head_selector(first_of, heads, TILE, head_width)
        pick_twice = jnp.concatenate([pick, pick], axis=0)
        starts, ends = [], []
        for piece in range(tile * (TILE // width), (tile + 1) * (TILE // width)):
            back = jnp.exp2(-answer_ref[piece, 2 * state :, :].astype(F32))
            starts.append(decode(answer_ref[piece, 0:state, :]) * back[0:1])
            ends.append(decode(answer_ref[piece, state : 2 * state, :]) * back[1:2])
        start = jnp.concatenate(starts, axis=1)
        end = jnp.concatenate(ends, axis=1)
        start_parts = jnp.concatenate(halves(start), axis=0)
        end_parts = jnp.concatenate(halves(end), axis=0)
        x = x_ref[:, span].astype(F32)
        dy = dy_ref[:, span].astype(F32)
        skip = jnp.sum(mul(skips, pick), axis=0, keepdims=True)

        spread = mul(weight_e[...], pick_twice)
        carried = mul(maps[:, 0 : 2 * state], end_parts) * spread
        grad_ref[:, span] = (inner_ref[:, span].astype(F32) + skip * dy + carried).astype(BF16)
        top, low = halves(x * carried)
        future_sum += mul_nt(top, pick) + mul_nt(low, pick)
        top, low = halves(x * spread)
        write_total += mul_nt(top, end_parts) + mul_nt(low, end_parts)

        weighted = dy * mul(weight_s[...], pick_twice)
        top, low = halves(weighted * mul(maps[:, 2 * state : 4 * state], start_parts))
        past_sum += mul_nt(top, pick) + mul_nt(low, pick)
        top, low = halves(weighted)
        read_total += mul_nt(top, start_parts) + mul_nt(low, start_parts)

        both = jnp.broadcast_to(jnp.sum(start * end, axis=0, keepdims=True), (8, TILE))
        top, low = halves(both)
        through_sum += mul_nt(top, pick) + mul_nt(low, pick)
    sums[:, future] += future_sum
    sums[:, past] += past_sum
    sums[:, write_sum] += write_total
    sums[:, read_sum] += read_total
    through[...] += through_sum

    if not last:
        return

    @pl.when(turn == pl.num_programs(0) - 1)
    def _():
        rate = -jnp.exp(decay_ref[...])
        step = step_ref[...]
        gate = jax.nn.sigmoid(raw_ref[...].astype(F32) + bias_ref[...])
        finish = cum_ref[rows - 1 : rows, :]
        to_come = sums[:, future]
        decay_grad = (
            sum(ref[...] for ref in within_refs)
            + mul_exact(triangle(rows, lambda r, c: r <= c), sums[:, past])
            + mul_exact(triangle(rows, lambda r, c: r > c), to_come)
            + jnp.exp(finish) * scale * through[0:1, :]
        )
        ratio = jnp.where(step > 1e-30, gate / jnp.maximum(step, 1e-30), 1.0)
        inner = sum(ref[...] for ref in own_refs) + to_come
        raw_grad = inner * ratio + rate * decay_grad * gate
        map_sum = sums[:, 2 * heads :] + 0.0
        write_all = map_sum[:, 0:state] + map_sum[:, state : 2 * state]
        read_all = map_sum[:, 2 * state : 3 * state] + map_sum[:, 3 * state :]
        map_grad = jnp.concatenate([write_all, read_all], axis=1)
        map_grad += sum(ref[...] for ref in map_refs)
        table_ref[...] = jnp.concatenate([raw_grad.T, map_grad.T], axis=0).astype(BF16)


def deal_kernel(place_ref, layer_ref, after_ref, *out_refs):
    width = out_refs[0].shape[2]
    for turn, out_ref in enumerate(out_refs):
        start = pl.multiple_of((place_ref[0] ^ turn) * width, width)
        out_ref[0, :, :] = layer_ref[:, pl.ds(start, width)]


def product_kernel(planes, place_ref, *refs):
    step = pl.program_id(0)
    wide = (len(refs) - planes) // 2
    table_refs, layer_refs, out_refs = refs[:wide], refs[wide : 2 * wide], refs[2 * wide :]
    total = sum(mul(table[...], layer[0]) for table, layer in zip(table_refs, layer_refs))
    columns = total.shape[0]
    most = jnp.max(jnp.abs(total), axis=0, keepdims=True)
    power = power_for(jnp.max(most, axis=1, keepdims=True))
    coded = encode(total * jnp.exp2(power))
    for plane in range(planes):

        @pl.when(step == plane)
        def _(out_ref=out_refs[plane]):
            out_ref[0:columns, :] = coded
            out_ref[columns:, :] = jnp.broadcast_to(power, out_ref[columns:, :].shape).astype(BF16)


def gather_kernel(factor, *refs):
    part_refs, out_ref = refs[:-1], refs[-1]
    columns = out_ref.shape[1]
    total = jnp.zeros((columns, out_ref.shape[0]), F32)
    for part_ref in part_refs:
        power = part_ref[columns:, :].astype(F32)[0:1]
        total += decode(part_ref[0:columns, :]) * jnp.exp2(-power)
    out_ref[...] = (total * factor).T


def swap(array, axis, turn):
    if turn == 0:
        return array
    count = lax.axis_size(axis)
    return lax.ppermute(array, axis, [(one, one ^ turn) for one in range(count)])


def whole(shape):
    return pl.BlockSpec(shape, lambda i: (0,) * len(shape))


def call(kernel, steps, in_specs, out, scratch, aliases=None):
    return pl.pallas_call(
        kernel,
        grid=(steps,),
        in_specs=in_specs,
        out_specs=[spec for spec, _, _ in out],
        out_shape=[jax.ShapeDtypeStruct(dims, dtype) for _, dims, dtype in out],
        scratch_shapes=[pltpu.VMEM(dims, dtype) for dims, dtype in scratch],
        compiler_params=pltpu.CompilerParams(vmem_limit_bytes=VMEM_LIMIT),
        cost_estimate=SHORT,
        input_output_aliases=aliases or {},
    )


def body(
    layer_input,
    head_inputs,
    output_grad,
    step_raw,
    state_write,
    state_read,
    decay_log,
    step_bias,
    skip_gain,
):
    rows, channels = head_inputs.shape
    heads = step_raw.shape[1]
    head_width = channels // heads
    state = state_write.shape[1]
    model = layer_input.shape[1]
    columns = heads + 2 * state
    axes = ("wide", "seq")
    wide, planes = lax.axis_size("wide"), lax.axis_size("seq")
    blocks = wide * planes
    own_model = model // blocks
    scale = float(rows * blocks * state) ** -0.5
    parts = HALVES if heads % (HALVES * blocks) == 0 else 1
    part_heads = heads // parts
    part_lanes = channels // parts
    owner_lanes = part_lanes // blocks
    piece_lanes = max(owner_lanes, 128)
    pieces = part_lanes // piece_lanes
    depth = 2 * state + META
    bias = step_bias[None, :]
    decay = decay_log[None, :]
    skip = skip_gain[None, :]
    write_t, read_t = state_write.T, state_read.T

    lanes = CARRY_HEADS * head_width
    steps = part_lanes // lanes
    here = lanes // piece_lanes

    def tokens(part, width):
        first = part * (part_lanes // width)
        return pl.BlockSpec((rows, width), lambda i: (0, first + i))

    message_spec = pl.BlockSpec((here, depth, piece_lanes), lambda i: (i, 0, 0))
    both_spec = pl.BlockSpec((here, depth, piece_lanes), lambda i: (i % steps, 0, i // steps))
    head_spec = whole((rows, heads))
    line_spec = whole((1, heads))
    map_spec = whole((state, rows))
    head_out = (head_spec, (rows, heads), F32)

    def exchange(array):
        return lax.all_to_all(array, axes, split_axis=0, concat_axis=0, tiled=True)

    def to_owner(array):
        if owner_lanes < piece_lanes:
            split = array.reshape(pieces, depth, piece_lanes // owner_lanes, owner_lanes)
            array = jnp.moveaxis(split, 2, 1).reshape(blocks, depth, owner_lanes)
        return exchange(array)

    def from_owner(array):
        array = exchange(array)
        if owner_lanes < piece_lanes:
            split = array.reshape(pieces, piece_lanes // owner_lanes, depth, owner_lanes)
            array = jnp.moveaxis(split, 1, 2).reshape(pieces, depth, piece_lanes)
        return array

    def scan(part, message, after):
        dims = (blocks, depth, owner_lanes)
        (answer,) = call(
            scan_kernel,
            1,
            [pl.BlockSpec(dims, lambda i: (0, 0, part))] + [anywhere] * len(after),
            [(whole(dims), dims, BF16)],
            [((2, blocks, owner_lanes), F32)],
        )(message, *after)
        return answer

    with jax.named_scope("summaries"):
        message, step, cum = call(
            functools.partial(summary_kernel, head_width),
            parts * steps,
            [head_spec, line_spec, line_spec, map_spec, map_spec, tokens(0, lanes), tokens(0, lanes)],
            [(both_spec, (pieces, depth, parts * piece_lanes), BF16), head_out, head_out],
            [((rows, 2 * heads), BF16), ((rows, 2 * heads), BF16), ((META, heads), BF16)],
        )(step_raw, bias, decay, write_t, read_t, head_inputs, output_grad)
    place = jnp.stack([lax.axis_index("wide"), lax.axis_index("seq")]).astype(jnp.int32)
    with jax.named_scope("layer"):
        if own_model % 128:
            cut = jnp.transpose(layer_input.reshape(rows, planes, wide, own_model), (2, 1, 0, 3))
            dealt = [
                lax.dynamic_index_in_dim(cut, place[0] ^ turn, 0, False) for turn in range(wide)
            ]
        else:
            dealt = pl.pallas_call(
                deal_kernel,
                grid_spec=pltpu.PrefetchScalarGridSpec(
                    num_scalar_prefetch=1,
                    grid=(planes,),
                    in_specs=[
                        pl.BlockSpec((rows, wide * own_model), lambda i, p: (0, i)),
                        pl.BlockSpec(memory_space=pl.ANY),
                    ],
                    out_specs=[pl.BlockSpec((1, rows, own_model), lambda i, p: (i, 0, 0))] * wide,
                ),
                out_shape=[jax.ShapeDtypeStruct((planes, rows, own_model), BF16)] * wide,
                compiler_params=pltpu.CompilerParams(vmem_limit_bytes=VMEM_LIMIT),
                cost_estimate=SHORT,
            )(place, layer_input, cum)
        layer_parts = [swap(one, "wide", turn) for turn, one in enumerate(dealt)]
    anywhere = pl.BlockSpec(memory_space=pl.ANY)

    def own_block(part, after):
        width = PAIR_HEADS * head_width
        here_spec = pl.BlockSpec((rows, width), lambda i: (0, i))
        return call(
            functools.partial(block_kernel, head_width, scale, part * part_heads, len(after)),
            part_lanes // width,
            [head_spec, head_spec, map_spec, map_spec, tokens(part, width), tokens(part, width)]
            + [anywhere] * len(after),
            [
                (here_spec, (rows, part_lanes), BF16),
                head_out,
                head_out,
                (whole((rows, 2 * state)), (rows, 2 * state), F32),
            ],
            [
                ((rows, rows), F32),
                ((rows, heads), F32),
                ((heads, rows), F32),
                ((rows, rows), F32),
                ((heads, rows), F32),
            ],
        )(step, cum, write_t, read_t, head_inputs, output_grad, *after)

    cuts = [0, wide // 2, 3 * wide // 4, wide]
    with jax.named_scope("own_block"):
        own_parts = [own_block(0, dealt[:1])]
        if parts > 1:
            own_parts.append(own_block(1, layer_parts[1 : cuts[1]]))
    with jax.named_scope("scan"):
        arrived = to_owner(message)
        returned = []
        for part in range(parts):
            after = [own_parts[-1][1]] + layer_parts[cuts[part + 1] : cuts[part + 2]]
            returned.append(from_owner(scan(part, arrived, after)))

    sums_out = (whole((rows, 2 * heads + 4 * state)), (rows, 2 * heads + 4 * state), F32)
    through_out = (whole((8, heads)), (8, heads), F32)
    early = ()
    with jax.named_scope("carried"):
        for part in range(parts):
            first, last = part == 0, part == parts - 1
            in_specs = [head_spec, line_spec, line_spec, head_spec, head_spec, map_spec, map_spec]
            in_specs += [line_spec, tokens(part, lanes), tokens(part, lanes)]
            in_specs += [pl.BlockSpec((rows, lanes), lambda i: (0, i)), message_spec]
            operands = [step_raw, bias, decay, step, cum, write_t, read_t, skip]
            operands += [head_inputs, output_grad, own_parts[part][0], returned[part]]
            aliases = {}
            if not first:
                in_specs += [sums_out[0], through_out[0], pl.BlockSpec(memory_space=pl.ANY)]
                operands += [early[1], early[2], early[0]]
                aliases = {len(operands) - 1: 0}
            scratch = [((rows, 2 * heads), BF16)] * 2 + [((rows, 4 * state), BF16)]
            out = [(tokens(part, lanes), (rows, channels), BF16)]
            if last:
                for which in (1, 2, 3):
                    operands += [one[which] for one in own_parts]
                    in_specs += [whole(one[which].shape) for one in own_parts]
                out += [(whole((columns, rows)), (columns, rows), BF16)]
                scratch = [sums_out[1:], through_out[1:]] + scratch
            else:
                out += [sums_out, through_out]
            early = call(
                functools.partial(
                    carry_kernel, head_width, scale, part * part_heads, parts, first, last
                ),
                steps,
                in_specs,
                out,
                scratch,
                aliases,
            )(*operands)
    grad_x, table = early

    with jax.named_scope("projection"):
        tables = [swap(table, "wide", turn) for turn in range(wide)]
        coded = (columns + META, own_model)
        plane_spec = pl.BlockSpec((1, rows, own_model), lambda i, p: (p[1] ^ i, 0, 0))
        products = pl.pallas_call(
            functools.partial(product_kernel, planes),
            grid_spec=pltpu.PrefetchScalarGridSpec(
                num_scalar_prefetch=1,
                grid=(planes,),
                in_specs=[pl.BlockSpec((columns, rows), lambda i, p: (0, 0))] * wide
                + [plane_spec] * wide,
                out_specs=[pl.BlockSpec(coded, lambda i, p: (0, 0))] * planes,
            ),
            out_shape=[jax.ShapeDtypeStruct(coded, BF16)] * planes,
            compiler_params=pltpu.CompilerParams(vmem_limit_bytes=VMEM_LIMIT),
            cost_estimate=SHORT,
        )(place, *tables, *layer_parts)
        sums = [swap(one, "seq", turn) for turn, one in enumerate(products)]
        (weight_grad,) = call(
            functools.partial(gather_kernel, 1.0 / math.sqrt(rows * blocks)),
            1,
            [whole(coded)] * planes,
            [(whole((own_model, columns)), (own_model, columns), F32)],
            [],
        )(*sums)
    return grad_x, weight_grad


def solution(mesh):
    in_specs = (
        P(("wide", "seq"), None),
        P(("wide", "seq"), None),
        P(("wide", "seq"), None),
        P(("wide", "seq"), None),
        P(("wide", "seq"), None),
        P(("wide", "seq"), None),
        P(),
        P(),
        P(),
    )
    out_specs = (P(("wide", "seq"), None), P(("seq", "wide"), None))
    return jax.shard_map(body, mesh=mesh, in_specs=in_specs, out_specs=out_specs, check_vma=False)
```

```python
import functools
import math

import jax
import jax.numpy as jnp
from jax import lax
from jax.experimental import pallas as pl
from jax.experimental.pallas import tpu as pltpu
from jax.sharding import PartitionSpec as P

F32 = jnp.float32
BF16 = jnp.bfloat16
EXACT = lax.Precision.HIGHEST
VMEM_LIMIT = 56 * 1024 * 1024
TOP_POWER = 30.0
PRODUCT_BOUND = 30.0
CARRY_HEADS = 16
PAIR_HEADS = 8
META = 8
HALVES = 2
SHORT = pl.CostEstimate(flops=1000, bytes_accessed=1000, transcendentals=0)


def mul(a, b):
    return lax.dot_general(a, b, (((1,), (0,)), ((), ())), preferred_element_type=F32)


def mul_nt(a, b):
    return lax.dot_general(a, b, (((1,), (1,)), ((), ())), preferred_element_type=F32)


def mul_exact(a, b, dims=((1,), (0,))):
    return lax.dot_general(a, b, (dims, ((), ())), preferred_element_type=F32, precision=EXACT)


def halves(value):
    top = value.astype(BF16)
    return top, (value - top.astype(F32)).astype(BF16)


def power_for(bound):
    power = jnp.floor(TOP_POWER - jnp.log2(jnp.maximum(bound, 1e-37)))
    return jnp.clip(power, -100.0, 100.0)


def thirds(value):
    top, rest = value.astype(BF16), value
    rest = rest - top.astype(F32)
    middle = rest.astype(BF16)
    return top, middle, (rest - middle.astype(F32)).astype(BF16)


def encode(value):
    square = value * value
    fourth = square * square
    return jnp.where(value < 0, -fourth, fourth).astype(BF16)


def decode(coded):
    coded = coded.astype(F32)
    size = jnp.maximum(jnp.abs(coded), 1e-37)
    inverse = lax.rsqrt(size)
    return coded * inverse * lax.rsqrt(size * inverse)


def head_selector(first_head, heads, lanes, head_width):
    row = lax.broadcasted_iota(jnp.int32, (heads, lanes), 0)
    lane = lax.broadcasted_iota(jnp.int32, (heads, lanes), 1)
    return jnp.where(row == first_head + lane // head_width, 1.0, 0.0).astype(BF16)


def triangle(length, keep):
    row = lax.broadcasted_iota(jnp.int32, (length, length), 0)
    col = lax.broadcasted_iota(jnp.int32, (length, length), 1)
    return jnp.where(keep(row, col), 1.0, 0.0).astype(F32)


def summary_kernel(
    head_width,
    raw_ref,
    bias_ref,
    decay_ref,
    write_ref,
    read_ref,
    x_ref,
    dy_ref,
    message_ref,
    step_ref,
    cum_ref,
    weight_f,
    weight_b,
    facts,
):
    turn = pl.program_id(0)
    heads = raw_ref.shape[1]
    rows, lanes = x_ref.shape
    state = write_ref.shape[0]

    @pl.when(turn == 0)
    def _():
        step = jax.nn.softplus(raw_ref[...].astype(F32) + bias_ref[...])
        rate = -jnp.exp(decay_ref[...])
        cum = mul_exact(triangle(rows, lambda r, c: r >= c), step * rate)
        finish = cum[rows - 1 : rows, :]
        forward = step * jnp.exp(finish - cum)
        backward = jnp.exp(cum)
        power_f = power_for(PRODUCT_BOUND * jnp.sum(forward, axis=0, keepdims=True))
        power_b = power_for(PRODUCT_BOUND * jnp.sum(backward, axis=0, keepdims=True))
        step_ref[...] = step
        cum_ref[...] = cum
        parts = thirds(jnp.maximum(finish, -1e30))
        facts[...] = jnp.concatenate(
            [part.astype(F32) for part in parts]
            + [power_f, power_b, jnp.zeros((META - 5, heads), F32)],
            axis=0,
        ).astype(BF16)
        weight_f[...] = (forward * jnp.exp2(power_f)).T
        weight_b[...] = (backward * jnp.exp2(power_b)).T

    group = lanes // head_width
    pair_lanes = 2 * head_width
    width = message_ref.shape[2]
    near = pl.ds(turn * group, group)
    pick = head_selector(turn * group, heads, lanes, head_width)
    fact = mul(facts[...], pick).astype(BF16)
    lane = lax.broadcasted_iota(jnp.int32, (state, pair_lanes), 1)
    ahead = (x_ref, write_ref[...].astype(F32), weight_f[near, :], 0)
    behind = (dy_ref, read_ref[...].astype(F32), weight_b[near, :], state)
    for pair in range(group // 2):
        span = slice(pair * pair_lanes, (pair + 1) * pair_lanes)
        owner, offset = pair * pair_lanes // width, pair * pair_lanes % width
        here = slice(offset, offset + pair_lanes)
        for tokens_ref, rows_t, weights, start in (ahead, behind):
            scaled = []
            for head in (2 * pair, 2 * pair + 1):
                scaled += halves(rows_t * weights[head : head + 1, :])
            product = mul(jnp.concatenate(scaled, axis=0), tokens_ref[:, span])
            early = product[0:state] + product[state : 2 * state]
            late = product[2 * state : 3 * state] + product[3 * state :]
            total = jnp.where(lane < head_width, early, late)
            message_ref[owner, start : start + state, here] = encode(total)
        message_ref[owner, 2 * state :, here] = fact[:, span]


def scan_kernel(message_ref, *rest):
    answer_ref, powers = rest[-2:]
    blocks, double, lanes = message_ref.shape
    state = (double - META) // 2
    top = 2.0**TOP_POWER

    def one(block, start, power_row, side, running, bound):
        facts = message_ref[block, 2 * state : double, :].astype(F32)
        decay = jnp.exp(facts[0:1] + facts[1:2] + facts[2:3])
        back = jnp.exp2(-facts[power_row : power_row + 1])
        power = power_for(bound)
        powers[side, pl.ds(block, 1), :] = power
        answer_ref[block, start : start + state, :] = encode(running * jnp.exp2(power))
        own = decode(message_ref[block, start : start + state, :]) * back
        return running * decay + own, bound * decay + top * back

    def both(block, carry):
        ahead, ahead_bound, behind, behind_bound = carry
        return one(block, 0, 3, 0, ahead, ahead_bound) + one(
            blocks - 1 - block, state, 4, 1, behind, behind_bound
        )

    zero, none = jnp.zeros((state, lanes), F32), jnp.zeros((1, lanes), F32)
    lax.fori_loop(0, blocks, both, (zero, none, zero, none), unroll=4)
    row = lax.broadcasted_iota(jnp.int32, (blocks, META, lanes), 1)
    ahead, behind = powers[0][:, None, :], powers[1][:, None, :]
    meta = jnp.where(row == 0, ahead, jnp.where(row == 1, behind, 0.0))
    answer_ref[:, 2 * state : double, :] = meta.astype(BF16)


def block_kernel(
    head_width,
    scale,
    first_head,
    waits,
    step_ref,
    cum_ref,
    write_ref,
    read_ref,
    x_ref,
    dy_ref,
    *rest,
):
    inner_ref, own_ref, within_ref, maps_ref = rest[waits : waits + 4]
    read_write, source, cum_rows, pair_sum, out_flow = rest[waits + 4 :]
    turn = pl.program_id(0)
    rows, lanes = x_ref.shape
    half = rows // 2
    heads = step_ref.shape[1]
    group = lanes // head_width

    @pl.when(turn == 0)
    def _():
        read_write[...] = scale * lax.dot_general(
            write_ref[...], read_ref[...], (((0,), (0,)), ((), ())), preferred_element_type=F32
        )
        source[...] = jnp.log(step_ref[...]) - cum_ref[...]
        cum_rows[...] = cum_ref[...].T
        pair_sum[...] = jnp.zeros_like(pair_sum)
        out_flow[...] = jnp.zeros_like(out_flow)
        own_ref[...] = jnp.zeros_like(own_ref)

    first = first_head + turn * group
    near = pltpu.roll(source[...], lax.rem(heads - first, heads), axis=1)
    near_cum = cum_rows[pl.ds(first, group), :]
    row = lax.broadcasted_iota(jnp.int32, (half, half), 0)
    col = lax.broadcasted_iota(jnp.int32, (half, half), 1)
    ahead = col >= row
    lane = lax.broadcasted_iota(jnp.int32, (half, 2 * head_width), 1)
    first_half = lane < head_width
    head_lane = lax.broadcasted_iota(jnp.int32, (half, heads), 1)
    flow_aa = read_write[0:half, 0:half]
    flow_ab = read_write[0:half, half:rows]
    flow_bb = read_write[half:rows, half:rows]
    sum_aa = jnp.zeros((half, half), F32)
    sum_ab = jnp.zeros((half, half), F32)
    sum_bb = jnp.zeros((half, half), F32)
    own_a = jnp.zeros((half, heads), F32)
    own_b = jnp.zeros((half, heads), F32)
    zero = jnp.zeros((half, 2 * head_width), BF16)
    flows = []
    for pair in range(group // 2):
        span = slice(pair * 2 * head_width, (pair + 1) * 2 * head_width)
        x_a, x_b = x_ref[0:half, span], x_ref[half:rows, span]
        dy_a, dy_b = dy_ref[0:half, span], dy_ref[half:rows, span]
        early_a, late_a = jnp.where(first_half, dy_a, zero), jnp.where(first_half, zero, dy_a)
        early_b, late_b = jnp.where(first_half, dy_b, zero), jnp.where(first_half, zero, dy_b)
        stack = jnp.concatenate([early_a, early_b, late_a, late_b], axis=0)
        stack_b = jnp.concatenate([early_b, late_b], axis=0)
        grad_a = mul_nt(x_a, stack)
        grad_b = mul_nt(x_b, stack_b)
        masks_a, masks_b = [], []
        for side in range(2):
            place = pair * 2 + side
            head = first + place
            from_a = near[0:half, place : place + 1]
            from_b = near[half:rows, place : place + 1]
            to_a = near_cum[place : place + 1, 0:half]
            to_b = near_cum[place : place + 1, half:rows]
            fade_aa = jnp.exp(jnp.where(ahead, to_a + from_a, -1e30))
            fade_ab = jnp.exp(to_b + from_a)
            fade_bb = jnp.exp(jnp.where(ahead, to_b + from_b, -1e30))
            weigh_aa = fade_aa * grad_a[:, side * rows : side * rows + half]
            weigh_ab = fade_ab * grad_a[:, side * rows + half : (side + 1) * rows]
            weigh_bb = fade_bb * grad_b[:, side * half : (side + 1) * half]
            sum_aa += weigh_aa
            sum_ab += weigh_ab
            sum_bb += weigh_bb
            masks_a += [(fade_aa * flow_aa).astype(BF16), (fade_ab * flow_ab).astype(BF16)]
            masks_b += [(fade_bb * flow_bb).astype(BF16)]
            pair_aa = weigh_aa * flow_aa
            pair_ab = weigh_ab * flow_ab
            pair_bb = weigh_bb * flow_bb
            flow_out = jnp.sum(pair_aa + pair_ab, axis=1, keepdims=True)
            own_a = jnp.where(head_lane == head, flow_out, own_a)
            flow_out = jnp.sum(pair_bb, axis=1, keepdims=True)
            own_b = jnp.where(head_lane == head, flow_out, own_b)
            flow_in = [
                jnp.sum(pair_aa, axis=0, keepdims=True),
                jnp.sum(pair_ab, axis=0, keepdims=True) + jnp.sum(pair_bb, axis=0, keepdims=True),
            ]
            flows.append(jnp.concatenate(flow_in, axis=1))
        inner_ref[0:half, span] = mul(jnp.concatenate(masks_a, axis=1), stack).astype(BF16)
        inner_ref[half:rows, span] = mul(jnp.concatenate(masks_b, axis=1), stack_b).astype(BF16)
    out_flow[pl.ds(first, group), :] = jnp.concatenate(flows, axis=0)
    pair_sum[0:half, 0:half] += sum_aa
    pair_sum[0:half, half:rows] += sum_ab
    pair_sum[half:rows, half:rows] += sum_bb
    own_ref[0:half, :] += own_a
    own_ref[half:rows, :] += own_b

    @pl.when(turn == pl.num_programs(0) - 1)
    def _():
        net = own_ref[...] - out_flow[...].T
        within_ref[...] = mul_exact(triangle(rows, lambda r, c: r > c), net)
        weighted = scale * pair_sum[...]
        maps_ref[...] = jnp.concatenate(
            [
                mul_exact(weighted, read_ref[...].astype(F32), ((1,), (1,))),
                mul_exact(weighted, write_ref[...].astype(F32), ((0,), (1,))),
            ],
            axis=1,
        )


def carry_kernel(head_width, scale, first_head, parts, first, last, *refs):
    refs = list(refs)
    take = lambda count: [refs.pop(0) for _ in range(count)]
    raw_ref, bias_ref, decay_ref, step_ref, cum_ref, write_ref, read_ref, skip_ref = take(8)
    x_ref, dy_ref, inner_ref, answer_ref = take(4)
    if not first:
        early_sums, early_through, _ = take(3)
    if last:
        own_refs, within_refs, map_refs = take(parts), take(parts), take(parts)
        grad_ref, table_ref, sums, through, weight_e, weight_s, maps = take(7)
    else:
        grad_ref, sums, through, weight_e, weight_s, maps = take(6)
    turn = pl.program_id(0)
    rows, lanes = x_ref.shape
    heads = step_ref.shape[1]
    state = write_ref.shape[0]
    future, past = slice(0, heads), slice(heads, 2 * heads)
    write_sum = slice(2 * heads, 2 * heads + 2 * state)
    read_sum = slice(2 * heads + 2 * state, 2 * heads + 4 * state)

    @pl.when(turn == 0)
    def _():
        cum = cum_ref[...]
        finish = cum[rows - 1 : rows, :]
        top, low = halves(step_ref[...] * jnp.exp(finish - cum) * scale)
        weight_e[...] = jnp.concatenate([top, low], axis=1)
        top, low = halves(jnp.exp(cum) * scale)
        weight_s[...] = jnp.concatenate([top, low], axis=1)
        write = write_ref[...].astype(F32).T.astype(BF16)
        read = read_ref[...].astype(F32).T.astype(BF16)
        maps[...] = jnp.concatenate([write, write, read, read], axis=1)
        if first:
            sums[...] = jnp.zeros_like(sums)
            through[...] = jnp.zeros_like(through)
        else:
            sums[...] = early_sums[...]
            through[...] = early_through[...]

    pick = head_selector(first_head + turn * (lanes // head_width), heads, lanes, head_width)
    pick_twice = jnp.concatenate([pick, pick], axis=0)
    starts, ends = [], []
    for piece in range(answer_ref.shape[0]):
        back = jnp.exp2(-answer_ref[piece, 2 * state : 2 * state + META, :].astype(F32))
        starts.append(decode(answer_ref[piece, 0:state, :]) * back[0:1])
        ends.append(decode(answer_ref[piece, state : 2 * state, :]) * back[1:2])
    start = jnp.concatenate(starts, axis=1)
    end = jnp.concatenate(ends, axis=1)
    start_parts = jnp.concatenate(halves(start), axis=0)
    end_parts = jnp.concatenate(halves(end), axis=0)
    x = x_ref[...].astype(F32)
    dy = dy_ref[...].astype(F32)
    skip = jnp.concatenate(
        [part.astype(F32) for part in thirds(skip_ref[...])] + [jnp.zeros((13, heads), F32)], axis=0
    )
    skip = jnp.sum(mul(skip.astype(BF16), pick), axis=0, keepdims=True)

    spread_e = mul(weight_e[...], pick_twice)
    carried = mul(maps[:, 0 : 2 * state], end_parts) * spread_e
    grad_ref[...] = (inner_ref[...].astype(F32) + skip * dy + carried).astype(BF16)
    top, low = halves(x * carried)
    sums[:, future] += mul_nt(top, pick) + mul_nt(low, pick)
    top, low = halves(x * spread_e)
    sums[:, write_sum] += mul_nt(top, end_parts) + mul_nt(low, end_parts)

    weighted = dy * mul(weight_s[...], pick_twice)
    top, low = halves(weighted * mul(maps[:, 2 * state : 4 * state], start_parts))
    sums[:, past] += mul_nt(top, pick) + mul_nt(low, pick)
    top, low = halves(weighted)
    sums[:, read_sum] += mul_nt(top, start_parts) + mul_nt(low, start_parts)

    both = jnp.broadcast_to(jnp.sum(start * end, axis=0, keepdims=True), (8, lanes))
    top, low = halves(both)
    through[...] += mul_nt(top, pick) + mul_nt(low, pick)

    if not last:
        return

    @pl.when(turn == pl.num_programs(0) - 1)
    def _():
        rate = -jnp.exp(decay_ref[...])
        step = step_ref[...]
        gate = jax.nn.sigmoid(raw_ref[...].astype(F32) + bias_ref[...])
        finish = cum_ref[rows - 1 : rows, :]
        to_come = sums[:, future]
        decay_grad = (
            sum(ref[...] for ref in within_refs)
            + mul_exact(triangle(rows, lambda r, c: r <= c), sums[:, past])
            + mul_exact(triangle(rows, lambda r, c: r > c), to_come)
            + jnp.exp(finish) * scale * through[0:1, :]
        )
        ratio = jnp.where(step > 1e-30, gate / jnp.maximum(step, 1e-30), 1.0)
        inner = sum(ref[...] for ref in own_refs) + to_come
        raw_grad = inner * ratio + rate * decay_grad * gate
        map_sum = sums[:, 2 * heads :] + 0.0
        write_all = map_sum[:, 0:state] + map_sum[:, state : 2 * state]
        read_all = map_sum[:, 2 * state : 3 * state] + map_sum[:, 3 * state :]
        map_grad = jnp.concatenate([write_all, read_all], axis=1)
        map_grad += sum(ref[...] for ref in map_refs)
        table_ref[...] = jnp.concatenate([raw_grad.T, map_grad.T], axis=0).astype(BF16)


def deal_kernel(place_ref, layer_ref, after_ref, *out_refs):
    width = out_refs[0].shape[2]
    for turn, out_ref in enumerate(out_refs):
        start = pl.multiple_of((place_ref[0] ^ turn) * width, width)
        out_ref[0, :, :] = layer_ref[:, pl.ds(start, width)]


def product_kernel(planes, place_ref, *refs):
    step = pl.program_id(0)
    wide = (len(refs) - planes) // 2
    table_refs, layer_refs, out_refs = refs[:wide], refs[wide : 2 * wide], refs[2 * wide :]
    total = sum(mul(table[...], layer[0]) for table, layer in zip(table_refs, layer_refs))
    columns = total.shape[0]
    most = jnp.max(jnp.abs(total), axis=0, keepdims=True)
    power = power_for(jnp.max(most, axis=1, keepdims=True))
    coded = encode(total * jnp.exp2(power))
    for plane in range(planes):

        @pl.when(step == plane)
        def _(out_ref=out_refs[plane]):
            out_ref[0:columns, :] = coded
            out_ref[columns:, :] = jnp.broadcast_to(power, out_ref[columns:, :].shape).astype(BF16)


def gather_kernel(factor, *refs):
    part_refs, out_ref = refs[:-1], refs[-1]
    columns = out_ref.shape[1]
    total = jnp.zeros((columns, out_ref.shape[0]), F32)
    for part_ref in part_refs:
        power = part_ref[columns:, :].astype(F32)[0:1]
        total += decode(part_ref[0:columns, :]) * jnp.exp2(-power)
    out_ref[...] = (total * factor).T


def swap(array, axis, turn):
    if turn == 0:
        return array
    count = lax.axis_size(axis)
    return lax.ppermute(array, axis, [(one, one ^ turn) for one in range(count)])


def whole(shape):
    return pl.BlockSpec(shape, lambda i: (0,) * len(shape))


def call(kernel, steps, in_specs, out, scratch, aliases=None):
    return pl.pallas_call(
        kernel,
        grid=(steps,),
        in_specs=in_specs,
        out_specs=[spec for spec, _, _ in out],
        out_shape=[jax.ShapeDtypeStruct(dims, dtype) for _, dims, dtype in out],
        scratch_shapes=[pltpu.VMEM(dims, dtype) for dims, dtype in scratch],
        compiler_params=pltpu.CompilerParams(vmem_limit_bytes=VMEM_LIMIT),
        cost_estimate=SHORT,
        input_output_aliases=aliases or {},
    )


def body(
    layer_input,
    head_inputs,
    output_grad,
    step_raw,
    state_write,
    state_read,
    decay_log,
    step_bias,
    skip_gain,
):
    rows, channels = head_inputs.shape
    heads = step_raw.shape[1]
    head_width = channels // heads
    state = state_write.shape[1]
    model = layer_input.shape[1]
    columns = heads + 2 * state
    axes = ("wide", "seq")
    wide, planes = lax.axis_size("wide"), lax.axis_size("seq")
    blocks = wide * planes
    own_model = model // blocks
    scale = float(rows * blocks * state) ** -0.5
    parts = HALVES if heads % (HALVES * blocks) == 0 else 1
    part_heads = heads // parts
    part_lanes = channels // parts
    owner_lanes = part_lanes // blocks
    piece_lanes = max(owner_lanes, 128)
    pieces = part_lanes // piece_lanes
    depth = 2 * state + META
    bias = step_bias[None, :]
    decay = decay_log[None, :]
    skip = skip_gain[None, :]
    write_t, read_t = state_write.T, state_read.T

    lanes = CARRY_HEADS * head_width
    steps = part_lanes // lanes
    here = lanes // piece_lanes

    def tokens(part, width):
        first = part * (part_lanes // width)
        return pl.BlockSpec((rows, width), lambda i: (0, first + i))

    message_spec = pl.BlockSpec((here, depth, piece_lanes), lambda i: (i, 0, 0))
    both_spec = pl.BlockSpec((here, depth, piece_lanes), lambda i: (i % steps, 0, i // steps))
    head_spec = whole((rows, heads))
    line_spec = whole((1, heads))
    map_spec = whole((state, rows))
    head_out = (head_spec, (rows, heads), F32)

    def exchange(array):
        return lax.all_to_all(array, axes, split_axis=0, concat_axis=0, tiled=True)

    def to_owner(array):
        if owner_lanes < piece_lanes:
            split = array.reshape(pieces, depth, piece_lanes // owner_lanes, owner_lanes)
            array = jnp.moveaxis(split, 2, 1).reshape(blocks, depth, owner_lanes)
        return exchange(array)

    def from_owner(array):
        array = exchange(array)
        if owner_lanes < piece_lanes:
            split = array.reshape(pieces, piece_lanes // owner_lanes, depth, owner_lanes)
            array = jnp.moveaxis(split, 1, 2).reshape(pieces, depth, piece_lanes)
        return array

    def scan(part, message, after):
        dims = (blocks, depth, owner_lanes)
        (answer,) = call(
            scan_kernel,
            1,
            [pl.BlockSpec(dims, lambda i: (0, 0, part))] + [anywhere] * len(after),
            [(whole(dims), dims, BF16)],
            [((2, blocks, owner_lanes), F32)],
        )(message, *after)
        return answer

    with jax.named_scope("summaries"):
        message, step, cum = call(
            functools.partial(summary_kernel, head_width),
            parts * steps,
            [head_spec, line_spec, line_spec, map_spec, map_spec, tokens(0, lanes), tokens(0, lanes)],
            [(both_spec, (pieces, depth, parts * piece_lanes), BF16), head_out, head_out],
            [((heads, rows), F32), ((heads, rows), F32), ((META, heads), BF16)],
        )(step_raw, bias, decay, write_t, read_t, head_inputs, output_grad)
    place = jnp.stack([lax.axis_index("wide"), lax.axis_index("seq")]).astype(jnp.int32)
    with jax.named_scope("layer"):
        if own_model % 128:
            cut = jnp.transpose(layer_input.reshape(rows, planes, wide, own_model), (2, 1, 0, 3))
            dealt = [
                lax.dynamic_index_in_dim(cut, place[0] ^ turn, 0, False) for turn in range(wide)
            ]
        else:
            dealt = pl.pallas_call(
                deal_kernel,
                grid_spec=pltpu.PrefetchScalarGridSpec(
                    num_scalar_prefetch=1,
                    grid=(planes,),
                    in_specs=[
                        pl.BlockSpec((rows, wide * own_model), lambda i, p: (0, i)),
                        pl.BlockSpec(memory_space=pl.ANY),
                    ],
                    out_specs=[pl.BlockSpec((1, rows, own_model), lambda i, p: (i, 0, 0))] * wide,
                ),
                out_shape=[jax.ShapeDtypeStruct((planes, rows, own_model), BF16)] * wide,
                compiler_params=pltpu.CompilerParams(vmem_limit_bytes=VMEM_LIMIT),
                cost_estimate=SHORT,
            )(place, layer_input, cum)
        layer_parts = [swap(one, "wide", turn) for turn, one in enumerate(dealt)]
    anywhere = pl.BlockSpec(memory_space=pl.ANY)

    def own_block(part, after):
        width = PAIR_HEADS * head_width
        here_spec = pl.BlockSpec((rows, width), lambda i: (0, i))
        return call(
            functools.partial(block_kernel, head_width, scale, part * part_heads, len(after)),
            part_lanes // width,
            [head_spec, head_spec, map_spec, map_spec, tokens(part, width), tokens(part, width)]
            + [anywhere] * len(after),
            [
                (here_spec, (rows, part_lanes), BF16),
                head_out,
                head_out,
                (whole((rows, 2 * state)), (rows, 2 * state), F32),
            ],
            [
                ((rows, rows), F32),
                ((rows, heads), F32),
                ((heads, rows), F32),
                ((rows, rows), F32),
                ((heads, rows), F32),
            ],
        )(step, cum, write_t, read_t, head_inputs, output_grad, *after)

    single = [turn for turn in (1, 2, 4) if turn < wide]
    double = [turn for turn in (3, 5) if turn < wide]
    others = [turn for turn in range(1, wide) if turn not in single + double]
    with jax.named_scope("own_block"):
        own_parts = [own_block(0, dealt[:1])]
        if parts > 1:
            after = [own_parts[0][1]] + [layer_parts[turn] for turn in single]
            own_parts.append(own_block(1, after))
    with jax.named_scope("scan"):
        arrived = to_owner(message)
        returned = []
        for part in range(parts):
            after = [layer_parts[turn] for turn in (double, others)[part]]
            returned.append(from_owner(scan(part, arrived, [own_parts[-1][1]] + after)))

    sums_out = (whole((rows, 2 * heads + 4 * state)), (rows, 2 * heads + 4 * state), F32)
    through_out = (whole((8, heads)), (8, heads), F32)
    early = ()
    with jax.named_scope("carried"):
        for part in range(parts):
            first, last = part == 0, part == parts - 1
            in_specs = [head_spec, line_spec, line_spec, head_spec, head_spec, map_spec, map_spec]
            in_specs += [line_spec, tokens(part, lanes), tokens(part, lanes)]
            in_specs += [pl.BlockSpec((rows, lanes), lambda i: (0, i)), message_spec]
            operands = [step_raw, bias, decay, step, cum, write_t, read_t, skip]
            operands += [head_inputs, output_grad, own_parts[part][0], returned[part]]
            aliases = {}
            if not first:
                in_specs += [sums_out[0], through_out[0], pl.BlockSpec(memory_space=pl.ANY)]
                operands += [early[1], early[2], early[0]]
                aliases = {len(operands) - 1: 0}
            scratch = [((rows, 2 * heads), BF16)] * 2 + [((rows, 4 * state), BF16)]
            out = [(tokens(part, lanes), (rows, channels), BF16)]
            if last:
                for which in (1, 2, 3):
                    operands += [one[which] for one in own_parts]
                    in_specs += [whole(one[which].shape) for one in own_parts]
                out += [(whole((columns, rows)), (columns, rows), BF16)]
                scratch = [sums_out[1:], through_out[1:]] + scratch
            else:
                out += [sums_out, through_out]
            early = call(
                functools.partial(
                    carry_kernel, head_width, scale, part * part_heads, parts, first, last
                ),
                steps,
                in_specs,
                out,
                scratch,
                aliases,
            )(*operands)
    grad_x, table = early

    with jax.named_scope("projection"):
        tables = [swap(table, "wide", turn) for turn in range(wide)]
        coded = (columns + META, own_model)
        plane_spec = pl.BlockSpec((1, rows, own_model), lambda i, p: (p[1] ^ i, 0, 0))
        products = pl.pallas_call(
            functools.partial(product_kernel, planes),
            grid_spec=pltpu.PrefetchScalarGridSpec(
                num_scalar_prefetch=1,
                grid=(planes,),
                in_specs=[pl.BlockSpec((columns, rows), lambda i, p: (0, 0))] * wide
                + [plane_spec] * wide,
                out_specs=[pl.BlockSpec(coded, lambda i, p: (0, 0))] * planes,
            ),
            out_shape=[jax.ShapeDtypeStruct(coded, BF16)] * planes,
            compiler_params=pltpu.CompilerParams(vmem_limit_bytes=VMEM_LIMIT),
            cost_estimate=SHORT,
        )(place, *tables, *layer_parts)
        sums = [swap(one, "seq", turn) for turn, one in enumerate(products)]
        (weight_grad,) = call(
            functools.partial(gather_kernel, 1.0 / math.sqrt(rows * blocks)),
            1,
            [whole(coded)] * planes,
            [(whole((own_model, columns)), (own_model, columns), F32)],
            [],
        )(*sums)
    return grad_x, weight_grad


def solution(mesh):
    in_specs = (
        P(("wide", "seq"), None),
        P(("wide", "seq"), None),
        P(("wide", "seq"), None),
        P(("wide", "seq"), None),
        P(("wide", "seq"), None),
        P(("wide", "seq"), None),
        P(),
        P(),
        P(),
    )
    out_specs = (P(("wide", "seq"), None), P(("seq", "wide"), None))
    return jax.shard_map(body, mesh=mesh, in_specs=in_specs, out_specs=out_specs, check_vma=False)
```

```python
import functools
import math

import jax
import jax.numpy as jnp
from jax import lax
from jax.experimental import pallas as pl
from jax.experimental.pallas import tpu as pltpu
from jax.sharding import PartitionSpec as P

F32 = jnp.float32
BF16 = jnp.bfloat16
EXACT = lax.Precision.HIGHEST
VMEM_LIMIT = 56 * 1024 * 1024
TOP_POWER = 30.0
PRODUCT_BOUND = 30.0
CARRY_HEADS = 16
PAIR_HEADS = 8
META = 8
HALVES = 2
SHORT = pl.CostEstimate(flops=1000, bytes_accessed=1000, transcendentals=0)


def mul(a, b):
    return lax.dot_general(a, b, (((1,), (0,)), ((), ())), preferred_element_type=F32)


def mul_nt(a, b):
    return lax.dot_general(a, b, (((1,), (1,)), ((), ())), preferred_element_type=F32)


def mul_exact(a, b, dims=((1,), (0,))):
    return lax.dot_general(a, b, (dims, ((), ())), preferred_element_type=F32, precision=EXACT)


def halves(value):
    top = value.astype(BF16)
    return top, (value - top.astype(F32)).astype(BF16)


def power_for(bound):
    power = jnp.floor(TOP_POWER - jnp.log2(jnp.maximum(bound, 1e-37)))
    return jnp.clip(power, -100.0, 100.0)


def thirds(value):
    top, rest = value.astype(BF16), value
    rest = rest - top.astype(F32)
    middle = rest.astype(BF16)
    return top, middle, (rest - middle.astype(F32)).astype(BF16)


def encode(value):
    square = value * value
    fourth = square * square
    return jnp.where(value < 0, -fourth, fourth).astype(BF16)


def decode(coded):
    coded = coded.astype(F32)
    size = jnp.maximum(jnp.abs(coded), 1e-37)
    inverse = lax.rsqrt(size)
    return coded * inverse * lax.rsqrt(size * inverse)


def head_selector(first_head, heads, lanes, head_width):
    row = lax.broadcasted_iota(jnp.int32, (heads, lanes), 0)
    lane = lax.broadcasted_iota(jnp.int32, (heads, lanes), 1)
    return jnp.where(row == first_head + lane // head_width, 1.0, 0.0).astype(BF16)


def triangle(length, keep):
    row = lax.broadcasted_iota(jnp.int32, (length, length), 0)
    col = lax.broadcasted_iota(jnp.int32, (length, length), 1)
    return jnp.where(keep(row, col), 1.0, 0.0).astype(F32)


def summary_kernel(
    head_width,
    raw_ref,
    bias_ref,
    decay_ref,
    write_ref,
    read_ref,
    x_ref,
    dy_ref,
    message_ref,
    step_ref,
    cum_ref,
    weight_f,
    weight_b,
    facts,
):
    turn = pl.program_id(0)
    heads = raw_ref.shape[1]
    rows, lanes = x_ref.shape
    state = write_ref.shape[0]

    @pl.when(turn == 0)
    def _():
        step = jax.nn.softplus(raw_ref[...].astype(F32) + bias_ref[...])
        rate = -jnp.exp(decay_ref[...])
        cum = mul_exact(triangle(rows, lambda r, c: r >= c), step * rate)
        finish = cum[rows - 1 : rows, :]
        forward = step * jnp.exp(finish - cum)
        backward = jnp.exp(cum)
        power_f = power_for(PRODUCT_BOUND * jnp.sum(forward, axis=0, keepdims=True))
        power_b = power_for(PRODUCT_BOUND * jnp.sum(backward, axis=0, keepdims=True))
        step_ref[...] = step
        cum_ref[...] = cum
        parts = thirds(jnp.maximum(finish, -1e30))
        facts[...] = jnp.concatenate(
            [part.astype(F32) for part in parts]
            + [power_f, power_b, jnp.zeros((META - 5, heads), F32)],
            axis=0,
        ).astype(BF16)
        weight_f[...] = (forward * jnp.exp2(power_f)).T
        weight_b[...] = (backward * jnp.exp2(power_b)).T

    group = lanes // head_width
    pair_lanes = 2 * head_width
    width = message_ref.shape[2]
    near = pl.ds(turn * group, group)
    pick = head_selector(turn * group, heads, lanes, head_width)
    fact = mul(facts[...], pick).astype(BF16)
    lane = lax.broadcasted_iota(jnp.int32, (state, pair_lanes), 1)
    ahead = (x_ref, write_ref[...].astype(F32), weight_f[near, :], 0)
    behind = (dy_ref, read_ref[...].astype(F32), weight_b[near, :], state)
    for pair in range(group // 2):
        span = slice(pair * pair_lanes, (pair + 1) * pair_lanes)
        owner, offset = pair * pair_lanes // width, pair * pair_lanes % width
        here = slice(offset, offset + pair_lanes)
        for tokens_ref, rows_t, weights, start in (ahead, behind):
            scaled = []
            for head in (2 * pair, 2 * pair + 1):
                scaled += halves(rows_t * weights[head : head + 1, :])
            product = mul(jnp.concatenate(scaled, axis=0), tokens_ref[:, span])
            early = product[0:state] + product[state : 2 * state]
            late = product[2 * state : 3 * state] + product[3 * state :]
            total = jnp.where(lane < head_width, early, late)
            message_ref[owner, start : start + state, here] = encode(total)
        message_ref[owner, 2 * state :, here] = fact[:, span]


def scan_kernel(message_ref, *rest):
    answer_ref, powers = rest[-2:]
    blocks, double, lanes = message_ref.shape
    state = (double - META) // 2
    top = 2.0**TOP_POWER

    def one(block, start, power_row, side, running, bound):
        facts = message_ref[block, 2 * state : double, :].astype(F32)
        decay = jnp.exp(facts[0:1] + facts[1:2] + facts[2:3])
        back = jnp.exp2(-facts[power_row : power_row + 1])
        power = power_for(bound)
        powers[side, pl.ds(block, 1), :] = power
        answer_ref[block, start : start + state, :] = encode(running * jnp.exp2(power))
        own = decode(message_ref[block, start : start + state, :]) * back
        return running * decay + own, bound * decay + top * back

    def both(block, carry):
        ahead, ahead_bound, behind, behind_bound = carry
        return one(block, 0, 3, 0, ahead, ahead_bound) + one(
            blocks - 1 - block, state, 4, 1, behind, behind_bound
        )

    zero, none = jnp.zeros((state, lanes), F32), jnp.zeros((1, lanes), F32)
    lax.fori_loop(0, blocks, both, (zero, none, zero, none), unroll=4)
    row = lax.broadcasted_iota(jnp.int32, (blocks, META, lanes), 1)
    ahead, behind = powers[0][:, None, :], powers[1][:, None, :]
    meta = jnp.where(row == 0, ahead, jnp.where(row == 1, behind, 0.0))
    answer_ref[:, 2 * state : double, :] = meta.astype(BF16)


def block_kernel(
    head_width,
    scale,
    first_head,
    waits,
    step_ref,
    cum_ref,
    write_ref,
    read_ref,
    x_ref,
    dy_ref,
    *rest,
):
    inner_ref, own_ref, within_ref, maps_ref = rest[waits : waits + 4]
    read_write, source, cum_rows, pair_sum, out_flow = rest[waits + 4 :]
    turn = pl.program_id(0)
    rows, lanes = x_ref.shape
    half = rows // 2
    heads = step_ref.shape[1]
    group = lanes // head_width

    @pl.when(turn == 0)
    def _():
        read_write[...] = scale * lax.dot_general(
            write_ref[...], read_ref[...], (((0,), (0,)), ((), ())), preferred_element_type=F32
        )
        source[...] = jnp.log(step_ref[...]) - cum_ref[...]
        cum_rows[...] = cum_ref[...].T
        pair_sum[...] = jnp.zeros_like(pair_sum)
        out_flow[...] = jnp.zeros_like(out_flow)
        own_ref[...] = jnp.zeros_like(own_ref)

    first = first_head + turn * group
    near = pltpu.roll(source[...], lax.rem(heads - first, heads), axis=1)
    near_cum = cum_rows[pl.ds(first, group), :]
    row = lax.broadcasted_iota(jnp.int32, (half, half), 0)
    col = lax.broadcasted_iota(jnp.int32, (half, half), 1)
    ahead = col >= row
    lane = lax.broadcasted_iota(jnp.int32, (half, 2 * head_width), 1)
    first_half = lane < head_width
    head_lane = lax.broadcasted_iota(jnp.int32, (half, heads), 1)
    flow_aa = read_write[0:half, 0:half]
    flow_ab = read_write[0:half, half:rows]
    flow_bb = read_write[half:rows, half:rows]
    sum_aa = jnp.zeros((half, half), F32)
    sum_ab = jnp.zeros((half, half), F32)
    sum_bb = jnp.zeros((half, half), F32)
    own_a = jnp.zeros((half, heads), F32)
    own_b = jnp.zeros((half, heads), F32)
    zero = jnp.zeros((half, 2 * head_width), BF16)
    flows = []
    for pair in range(group // 2):
        span = slice(pair * 2 * head_width, (pair + 1) * 2 * head_width)
        x_a, x_b = x_ref[0:half, span], x_ref[half:rows, span]
        dy_a, dy_b = dy_ref[0:half, span], dy_ref[half:rows, span]
        early_a, late_a = jnp.where(first_half, dy_a, zero), jnp.where(first_half, zero, dy_a)
        early_b, late_b = jnp.where(first_half, dy_b, zero), jnp.where(first_half, zero, dy_b)
        stack = jnp.concatenate([early_a, early_b, late_a, late_b], axis=0)
        stack_b = jnp.concatenate([early_b, late_b], axis=0)
        grad_a = mul_nt(x_a, stack)
        grad_b = mul_nt(x_b, stack_b)
        masks_a, masks_b = [], []
        for side in range(2):
            place = pair * 2 + side
            head = first + place
            from_a = near[0:half, place : place + 1]
            from_b = near[half:rows, place : place + 1]
            to_a = near_cum[place : place + 1, 0:half]
            to_b = near_cum[place : place + 1, half:rows]
            fade_aa = jnp.exp(jnp.where(ahead, to_a + from_a, -1e30))
            fade_ab = jnp.exp(to_b + from_a)
            fade_bb = jnp.exp(jnp.where(ahead, to_b + from_b, -1e30))
            weigh_aa = fade_aa * grad_a[:, side * rows : side * rows + half]
            weigh_ab = fade_ab * grad_a[:, side * rows + half : (side + 1) * rows]
            weigh_bb = fade_bb * grad_b[:, side * half : (side + 1) * half]
            sum_aa += weigh_aa
            sum_ab += weigh_ab
            sum_bb += weigh_bb
            masks_a += [(fade_aa * flow_aa).astype(BF16), (fade_ab * flow_ab).astype(BF16)]
            masks_b += [(fade_bb * flow_bb).astype(BF16)]
            pair_aa = weigh_aa * flow_aa
            pair_ab = weigh_ab * flow_ab
            pair_bb = weigh_bb * flow_bb
            flow_out = jnp.sum(pair_aa + pair_ab, axis=1, keepdims=True)
            own_a = jnp.where(head_lane == head, flow_out, own_a)
            flow_out = jnp.sum(pair_bb, axis=1, keepdims=True)
            own_b = jnp.where(head_lane == head, flow_out, own_b)
            flow_in = [
                jnp.sum(pair_aa, axis=0, keepdims=True),
                jnp.sum(pair_ab, axis=0, keepdims=True) + jnp.sum(pair_bb, axis=0, keepdims=True),
            ]
            flows.append(jnp.concatenate(flow_in, axis=1))
        inner_ref[0:half, span] = mul(jnp.concatenate(masks_a, axis=1), stack).astype(BF16)
        inner_ref[half:rows, span] = mul(jnp.concatenate(masks_b, axis=1), stack_b).astype(BF16)
    out_flow[pl.ds(first, group), :] = jnp.concatenate(flows, axis=0)
    pair_sum[0:half, 0:half] += sum_aa
    pair_sum[0:half, half:rows] += sum_ab
    pair_sum[half:rows, half:rows] += sum_bb
    own_ref[0:half, :] += own_a
    own_ref[half:rows, :] += own_b

    @pl.when(turn == pl.num_programs(0) - 1)
    def _():
        net = own_ref[...] - out_flow[...].T
        within_ref[...] = mul_exact(triangle(rows, lambda r, c: r > c), net)
        weighted = scale * pair_sum[...]
        maps_ref[...] = jnp.concatenate(
            [
                mul_exact(weighted, read_ref[...].astype(F32), ((1,), (1,))),
                mul_exact(weighted, write_ref[...].astype(F32), ((0,), (1,))),
            ],
            axis=1,
        )


def carry_kernel(head_width, scale, first_head, parts, first, last, *refs):
    refs = list(refs)
    take = lambda count: [refs.pop(0) for _ in range(count)]
    raw_ref, bias_ref, decay_ref, step_ref, cum_ref, write_ref, read_ref, skip_ref = take(8)
    x_ref, dy_ref, inner_ref, answer_ref = take(4)
    if not first:
        early_sums, early_through, _ = take(3)
    if last:
        own_refs, within_refs, map_refs = take(parts), take(parts), take(parts)
        grad_ref, table_ref, sums, through, weight_e, weight_s, maps, picks = take(8)
    else:
        grad_ref, sums, through, weight_e, weight_s, maps, picks = take(7)
    turn = pl.program_id(0)
    rows, lanes = x_ref.shape
    heads = step_ref.shape[1]
    state = write_ref.shape[0]
    future, past = slice(0, heads), slice(heads, 2 * heads)
    write_sum = slice(2 * heads, 2 * heads + 2 * state)
    read_sum = slice(2 * heads + 2 * state, 2 * heads + 4 * state)

    @pl.when(turn == 0)
    def _():
        cum = cum_ref[...]
        finish = cum[rows - 1 : rows, :]
        weight_e[...] = step_ref[...] * jnp.exp(finish - cum) * scale
        weight_s[...] = jnp.exp(cum) * scale
        pick = head_selector(0, heads, lanes, head_width)
        picks[...] = jnp.concatenate([pick, pick], axis=0)
        write = write_ref[...].astype(F32).T.astype(BF16)
        read = read_ref[...].astype(F32).T.astype(BF16)
        maps[...] = jnp.concatenate([write, write, read, read], axis=1)
        if first:
            sums[...] = jnp.zeros_like(sums)
            through[...] = jnp.zeros_like(through)
        else:
            sums[...] = early_sums[...]
            through[...] = early_through[...]

    first_here = first_head + turn * (lanes // head_width)
    pick = picks[0:heads, :]

    def rolled(value, shift):
        return pltpu.roll(value, lax.rem(shift, heads), axis=1)

    def spread_of(weight):
        near = rolled(weight[...], heads - first_here)
        return mul(jnp.concatenate(halves(near), axis=1), picks[...])

    starts, ends = [], []
    for piece in range(answer_ref.shape[0]):
        back = jnp.exp2(-answer_ref[piece, 2 * state : 2 * state + META, :].astype(F32))
        starts.append(decode(answer_ref[piece, 0:state, :]) * back[0:1])
        ends.append(decode(answer_ref[piece, state : 2 * state, :]) * back[1:2])
    start = jnp.concatenate(starts, axis=1)
    end = jnp.concatenate(ends, axis=1)
    start_parts = jnp.concatenate(halves(start), axis=0)
    end_parts = jnp.concatenate(halves(end), axis=0)
    x = x_ref[...].astype(F32)
    dy = dy_ref[...].astype(F32)
    skip = jnp.concatenate(
        [part.astype(F32) for part in thirds(skip_ref[...])] + [jnp.zeros((5, heads), F32)], axis=0
    )
    skip = rolled(skip, heads - first_here).astype(BF16)
    skip = jnp.sum(mul(skip, pick), axis=0, keepdims=True)

    spread_e = spread_of(weight_e)
    carried = mul(maps[:, 0 : 2 * state], end_parts) * spread_e
    grad_ref[...] = (inner_ref[...].astype(F32) + skip * dy + carried).astype(BF16)
    top, low = halves(x * carried)
    sums[:, future] += rolled(mul_nt(top, pick) + mul_nt(low, pick), first_here)
    top, low = halves(x * spread_e)
    sums[:, write_sum] += mul_nt(top, end_parts) + mul_nt(low, end_parts)

    weighted = dy * spread_of(weight_s)
    top = (weighted * mul(maps[:, 2 * state : 4 * state], start_parts)).astype(BF16)
    sums[:, past] += rolled(mul_nt(top, pick), first_here)
    top, low = halves(weighted)
    sums[:, read_sum] += mul_nt(top, start_parts) + mul_nt(low, start_parts)

    both = jnp.broadcast_to(jnp.sum(start * end, axis=0, keepdims=True), (8, lanes))
    top, low = halves(both)
    through[...] += rolled(mul_nt(top, pick) + mul_nt(low, pick), first_here)

    if not last:
        return

    @pl.when(turn == pl.num_programs(0) - 1)
    def _():
        rate = -jnp.exp(decay_ref[...])
        step = step_ref[...]
        gate = jax.nn.sigmoid(raw_ref[...].astype(F32) + bias_ref[...])
        finish = cum_ref[rows - 1 : rows, :]
        to_come = sums[:, future]
        decay_grad = (
            sum(ref[...] for ref in within_refs)
            + mul_exact(triangle(rows, lambda r, c: r <= c), sums[:, past])
            + mul_exact(triangle(rows, lambda r, c: r > c), to_come)
            + jnp.exp(finish) * scale * through[0:1, :]
        )
        ratio = jnp.where(step > 1e-30, gate / jnp.maximum(step, 1e-30), 1.0)
        inner = sum(ref[...] for ref in own_refs) + to_come
        raw_grad = inner * ratio + rate * decay_grad * gate
        map_sum = sums[:, 2 * heads :] + 0.0
        write_all = map_sum[:, 0:state] + map_sum[:, state : 2 * state]
        read_all = map_sum[:, 2 * state : 3 * state] + map_sum[:, 3 * state :]
        map_grad = jnp.concatenate([write_all, read_all], axis=1)
        map_grad += sum(ref[...] for ref in map_refs)
        table_ref[...] = jnp.concatenate([raw_grad.T, map_grad.T], axis=0).astype(BF16)


def deal_kernel(place_ref, layer_ref, after_ref, *out_refs):
    width = out_refs[0].shape[2]
    for turn, out_ref in enumerate(out_refs):
        start = pl.multiple_of((place_ref[0] ^ turn) * width, width)
        out_ref[0, :, :] = layer_ref[:, pl.ds(start, width)]


def product_kernel(planes, place_ref, *refs):
    wide = (len(refs) - planes) // 2
    table_refs, layer_refs, out_refs = refs[:wide], refs[wide : 2 * wide], refs[2 * wide :]
    table = jnp.concatenate([ref[...] for ref in table_refs], axis=1)
    columns = table.shape[0]
    for plane, out_ref in enumerate(out_refs):
        source = place_ref[1] ^ plane
        total = mul(table, jnp.concatenate([ref[source] for ref in layer_refs], axis=0))
        most = jnp.max(jnp.abs(total), axis=0, keepdims=True)
        power = power_for(jnp.max(most, axis=1, keepdims=True))
        out_ref[0:columns, :] = encode(total * jnp.exp2(power))
        out_ref[columns:, :] = jnp.broadcast_to(power, out_ref[columns:, :].shape).astype(BF16)


def gather_kernel(factor, *refs):
    part_refs, out_ref = refs[:-1], refs[-1]
    columns = out_ref.shape[1]
    total = jnp.zeros((columns, out_ref.shape[0]), F32)
    for part_ref in part_refs:
        power = part_ref[columns:, :].astype(F32)[0:1]
        total += decode(part_ref[0:columns, :]) * jnp.exp2(-power)
    out_ref[...] = (total * factor).T


def swap(array, axis, turn):
    if turn == 0:
        return array
    count = lax.axis_size(axis)
    return lax.ppermute(array, axis, [(one, one ^ turn) for one in range(count)])


def whole(shape):
    return pl.BlockSpec(shape, lambda i: (0,) * len(shape))


def call(kernel, steps, in_specs, out, scratch, aliases=None):
    return pl.pallas_call(
        kernel,
        grid=(steps,),
        in_specs=in_specs,
        out_specs=[spec for spec, _, _ in out],
        out_shape=[jax.ShapeDtypeStruct(dims, dtype) for _, dims, dtype in out],
        scratch_shapes=[pltpu.VMEM(dims, dtype) for dims, dtype in scratch],
        compiler_params=pltpu.CompilerParams(vmem_limit_bytes=VMEM_LIMIT),
        cost_estimate=SHORT,
        input_output_aliases=aliases or {},
    )


def body(
    layer_input,
    head_inputs,
    output_grad,
    step_raw,
    state_write,
    state_read,
    decay_log,
    step_bias,
    skip_gain,
):
    rows, channels = head_inputs.shape
    heads = step_raw.shape[1]
    head_width = channels // heads
    state = state_write.shape[1]
    model = layer_input.shape[1]
    columns = heads + 2 * state
    axes = ("wide", "seq")
    wide, planes = lax.axis_size("wide"), lax.axis_size("seq")
    blocks = wide * planes
    own_model = model // blocks
    scale = float(rows * blocks * state) ** -0.5
    parts = HALVES if heads % (HALVES * blocks) == 0 else 1
    part_heads = heads // parts
    part_lanes = channels // parts
    owner_lanes = part_lanes // blocks
    piece_lanes = max(owner_lanes, 128)
    pieces = part_lanes // piece_lanes
    depth = 2 * state + META
    bias = step_bias[None, :]
    decay = decay_log[None, :]
    skip = skip_gain[None, :]
    write_t, read_t = state_write.T, state_read.T

    lanes = CARRY_HEADS * head_width
    steps = part_lanes // lanes
    here = lanes // piece_lanes

    def tokens(part, width):
        first = part * (part_lanes // width)
        return pl.BlockSpec((rows, width), lambda i: (0, first + i))

    message_spec = pl.BlockSpec((here, depth, piece_lanes), lambda i: (i, 0, 0))
    both_spec = pl.BlockSpec((here, depth, piece_lanes), lambda i: (i % steps, 0, i // steps))
    head_spec = whole((rows, heads))
    line_spec = whole((1, heads))
    map_spec = whole((state, rows))
    head_out = (head_spec, (rows, heads), F32)

    def exchange(array):
        return lax.all_to_all(array, axes, split_axis=0, concat_axis=0, tiled=True)

    def to_owner(array):
        if owner_lanes < piece_lanes:
            split = array.reshape(pieces, depth, piece_lanes // owner_lanes, owner_lanes)
            array = jnp.moveaxis(split, 2, 1).reshape(blocks, depth, owner_lanes)
        return exchange(array)

    def from_owner(array):
        array = exchange(array)
        if owner_lanes < piece_lanes:
            split = array.reshape(pieces, piece_lanes // owner_lanes, depth, owner_lanes)
            array = jnp.moveaxis(split, 1, 2).reshape(pieces, depth, piece_lanes)
        return array

    def scan(part, message, after):
        dims = (blocks, depth, owner_lanes)
        (answer,) = call(
            scan_kernel,
            1,
            [pl.BlockSpec(dims, lambda i: (0, 0, part))] + [anywhere] * len(after),
            [(whole(dims), dims, BF16)],
            [((2, blocks, owner_lanes), F32)],
        )(message, *after)
        return answer

    with jax.named_scope("summaries"):
        message, step, cum = call(
            functools.partial(summary_kernel, head_width),
            parts * steps,
            [head_spec, line_spec, line_spec, map_spec, map_spec, tokens(0, lanes), tokens(0, lanes)],
            [(both_spec, (pieces, depth, parts * piece_lanes), BF16), head_out, head_out],
            [((heads, rows), F32), ((heads, rows), F32), ((META, heads), BF16)],
        )(step_raw, bias, decay, write_t, read_t, head_inputs, output_grad)
    place = jnp.stack([lax.axis_index("wide"), lax.axis_index("seq")]).astype(jnp.int32)
    with jax.named_scope("layer"):
        if own_model % 128:
            cut = jnp.transpose(layer_input.reshape(rows, planes, wide, own_model), (2, 1, 0, 3))
            dealt = [
                lax.dynamic_index_in_dim(cut, place[0] ^ turn, 0, False) for turn in range(wide)
            ]
        else:
            dealt = pl.pallas_call(
                deal_kernel,
                grid_spec=pltpu.PrefetchScalarGridSpec(
                    num_scalar_prefetch=1,
                    grid=(planes,),
                    in_specs=[
                        pl.BlockSpec((rows, wide * own_model), lambda i, p: (0, i)),
                        pl.BlockSpec(memory_space=pl.ANY),
                    ],
                    out_specs=[pl.BlockSpec((1, rows, own_model), lambda i, p: (i, 0, 0))] * wide,
                ),
                out_shape=[jax.ShapeDtypeStruct((planes, rows, own_model), BF16)] * wide,
                compiler_params=pltpu.CompilerParams(vmem_limit_bytes=VMEM_LIMIT),
                cost_estimate=SHORT,
            )(place, layer_input, cum)
        layer_parts = [swap(one, "wide", turn) for turn, one in enumerate(dealt)]
    anywhere = pl.BlockSpec(memory_space=pl.ANY)

    def own_block(part, after):
        width = PAIR_HEADS * head_width
        here_spec = pl.BlockSpec((rows, width), lambda i: (0, i))
        return call(
            functools.partial(block_kernel, head_width, scale, part * part_heads, len(after)),
            part_lanes // width,
            [head_spec, head_spec, map_spec, map_spec, tokens(part, width), tokens(part, width)]
            + [anywhere] * len(after),
            [
                (here_spec, (rows, part_lanes), BF16),
                head_out,
                head_out,
                (whole((rows, 2 * state)), (rows, 2 * state), F32),
            ],
            [
                ((rows, rows), F32),
                ((rows, heads), F32),
                ((heads, rows), F32),
                ((rows, rows), F32),
                ((heads, rows), F32),
            ],
        )(step, cum, write_t, read_t, head_inputs, output_grad, *after)

    others = [turn for turn in (3, 5) if turn < wide] + list(range(8, wide))
    firsts = [turn for turn in (6, 7, 2, 4) if turn < wide]
    with jax.named_scope("own_block"):
        own_parts = [own_block(0, dealt[:1])]
        if parts > 1:
            own_parts.append(own_block(1, [own_parts[0][1], layer_parts[1]]))
    with jax.named_scope("scan"):
        arrived = to_owner(message)
        returned, before = [], own_parts[-1][1]
        for part in range(parts):
            after = [layer_parts[turn] for turn in (firsts, others)[part]]
            before = scan(part, arrived, [before] + after)
            returned.append(from_owner(before))

    sums_out = (whole((rows, 2 * heads + 4 * state)), (rows, 2 * heads + 4 * state), F32)
    through_out = (whole((8, heads)), (8, heads), F32)
    early = ()
    with jax.named_scope("carried"):
        for part in range(parts):
            first, last = part == 0, part == parts - 1
            in_specs = [head_spec, line_spec, line_spec, head_spec, head_spec, map_spec, map_spec]
            in_specs += [line_spec, tokens(part, lanes), tokens(part, lanes)]
            in_specs += [pl.BlockSpec((rows, lanes), lambda i: (0, i)), message_spec]
            operands = [step_raw, bias, decay, step, cum, write_t, read_t, skip]
            operands += [head_inputs, output_grad, own_parts[part][0], returned[part]]
            aliases = {}
            if not first:
                in_specs += [sums_out[0], through_out[0], pl.BlockSpec(memory_space=pl.ANY)]
                operands += [early[1], early[2], early[0]]
                aliases = {len(operands) - 1: 0}
            scratch = [((rows, heads), F32)] * 2 + [((rows, 4 * state), BF16)]
            scratch += [((2 * heads, lanes), BF16)]
            out = [(tokens(part, lanes), (rows, channels), BF16)]
            if last:
                for which in (1, 2, 3):
                    operands += [one[which] for one in own_parts]
                    in_specs += [whole(one[which].shape) for one in own_parts]
                out += [(whole((columns, rows)), (columns, rows), BF16)]
                scratch = [sums_out[1:], through_out[1:]] + scratch
            else:
                out += [sums_out, through_out]
            early = call(
                functools.partial(
                    carry_kernel, head_width, scale, part * part_heads, parts, first, last
                ),
                steps,
                in_specs,
                out,
                scratch,
                aliases,
            )(*operands)
    grad_x, table = early

    with jax.named_scope("projection"):
        tables = [swap(table, "wide", turn) for turn in range(wide)]
        coded = (columns + META, own_model)
        products = pl.pallas_call(
            functools.partial(product_kernel, planes),
            in_specs=[pl.BlockSpec(memory_space=pltpu.SMEM)]
            + [pl.BlockSpec(memory_space=pltpu.VMEM)] * (2 * wide),
            out_specs=[pl.BlockSpec(memory_space=pltpu.VMEM)] * planes,
            out_shape=[jax.ShapeDtypeStruct(coded, BF16)] * planes,
            compiler_params=pltpu.CompilerParams(vmem_limit_bytes=VMEM_LIMIT),
            cost_estimate=SHORT,
        )(place, *tables, *layer_parts)
        sums = [swap(one, "seq", turn) for turn, one in enumerate(products)]
        (weight_grad,) = call(
            functools.partial(gather_kernel, 1.0 / math.sqrt(rows * blocks)),
            1,
            [whole(coded)] * planes,
            [(whole((own_model, columns)), (own_model, columns), F32)],
            [],
        )(*sums)
    return grad_x, weight_grad


def solution(mesh):
    in_specs = (
        P(("wide", "seq"), None),
        P(("wide", "seq"), None),
        P(("wide", "seq"), None),
        P(("wide", "seq"), None),
        P(("wide", "seq"), None),
        P(("wide", "seq"), None),
        P(),
        P(),
        P(),
    )
    out_specs = (P(("wide", "seq"), None), P(("seq", "wide"), None))
    return jax.shard_map(body, mesh=mesh, in_specs=in_specs, out_specs=out_specs, check_vma=False)
```

```python
import functools
import math

import jax
import jax.numpy as jnp
from jax import lax
from jax.experimental import pallas as pl
from jax.experimental.pallas import tpu as pltpu
from jax.sharding import PartitionSpec as P

F32 = jnp.float32
BF16 = jnp.bfloat16
EXACT = lax.Precision.HIGHEST
VMEM_LIMIT = 64 * 1024 * 1024
TOP_POWER = 30.0
PRODUCT_BOUND = 30.0
CARRY_HEADS = 16
PAIR_HEADS = 8
META = 8
HALVES = 2
SHORT = pl.CostEstimate(flops=1000, bytes_accessed=1000, transcendentals=0)


def mul(a, b):
    return lax.dot_general(a, b, (((1,), (0,)), ((), ())), preferred_element_type=F32)


def mul_nt(a, b):
    return lax.dot_general(a, b, (((1,), (1,)), ((), ())), preferred_element_type=F32)


def mul_exact(a, b, dims=((1,), (0,))):
    return lax.dot_general(a, b, (dims, ((), ())), preferred_element_type=F32, precision=EXACT)


def halves(value):
    top = value.astype(BF16)
    return top, (value - top.astype(F32)).astype(BF16)


def power_for(bound):
    power = jnp.floor(TOP_POWER - jnp.log2(jnp.maximum(bound, 1e-37)))
    return jnp.clip(power, -100.0, 100.0)


def thirds(value):
    top, rest = value.astype(BF16), value
    rest = rest - top.astype(F32)
    middle = rest.astype(BF16)
    return top, middle, (rest - middle.astype(F32)).astype(BF16)


def encode(value):
    square = value * value
    fourth = square * square
    return jnp.where(value < 0, -fourth, fourth).astype(BF16)


def decode(coded):
    coded = coded.astype(F32)
    size = jnp.maximum(jnp.abs(coded), 1e-37)
    inverse = lax.rsqrt(size)
    return coded * inverse * lax.rsqrt(size * inverse)


def head_selector(first_head, heads, lanes, head_width):
    row = lax.broadcasted_iota(jnp.int32, (heads, lanes), 0)
    lane = lax.broadcasted_iota(jnp.int32, (heads, lanes), 1)
    return jnp.where(row == first_head + lane // head_width, 1.0, 0.0).astype(BF16)


def triangle(length, keep):
    row = lax.broadcasted_iota(jnp.int32, (length, length), 0)
    col = lax.broadcasted_iota(jnp.int32, (length, length), 1)
    return jnp.where(keep(row, col), 1.0, 0.0).astype(F32)


def summary_kernel(
    head_width,
    raw_ref,
    bias_ref,
    decay_ref,
    write_ref,
    read_ref,
    x_ref,
    dy_ref,
    message_ref,
    step_ref,
    cum_ref,
    weight_f,
    weight_b,
    facts,
):
    turn = pl.program_id(0)
    heads = raw_ref.shape[1]
    rows, lanes = x_ref.shape
    state = write_ref.shape[0]

    @pl.when(turn == 0)
    def _():
        step = jax.nn.softplus(raw_ref[...].astype(F32) + bias_ref[...])
        rate = -jnp.exp(decay_ref[...])
        cum = mul_exact(triangle(rows, lambda r, c: r >= c), step * rate)
        finish = cum[rows - 1 : rows, :]
        forward = step * jnp.exp(finish - cum)
        backward = jnp.exp(cum)
        power_f = power_for(PRODUCT_BOUND * jnp.sum(forward, axis=0, keepdims=True))
        power_b = power_for(PRODUCT_BOUND * jnp.sum(backward, axis=0, keepdims=True))
        step_ref[...] = step
        cum_ref[...] = cum
        parts = thirds(jnp.maximum(finish, -1e30))
        facts[...] = jnp.concatenate(
            [part.astype(F32) for part in parts]
            + [power_f, power_b, jnp.zeros((META - 5, heads), F32)],
            axis=0,
        ).astype(BF16)
        weight_f[...] = (forward * jnp.exp2(power_f)).T
        weight_b[...] = (backward * jnp.exp2(power_b)).T

    group = lanes // head_width
    pair_lanes = 2 * head_width
    width = message_ref.shape[2]
    near = pl.ds(turn * group, group)
    pick = head_selector(turn * group, heads, lanes, head_width)
    fact = mul(facts[...], pick).astype(BF16)
    lane = lax.broadcasted_iota(jnp.int32, (state, pair_lanes), 1)
    ahead = (x_ref, write_ref[...].astype(F32), weight_f[near, :], 0)
    behind = (dy_ref, read_ref[...].astype(F32), weight_b[near, :], state)
    for pair in range(group // 2):
        span = slice(pair * pair_lanes, (pair + 1) * pair_lanes)
        owner, offset = pair * pair_lanes // width, pair * pair_lanes % width
        here = slice(offset, offset + pair_lanes)
        for tokens_ref, rows_t, weights, start in (ahead, behind):
            scaled = []
            for head in (2 * pair, 2 * pair + 1):
                scaled += halves(rows_t * weights[head : head + 1, :])
            product = mul(jnp.concatenate(scaled, axis=0), tokens_ref[:, span])
            early = product[0:state] + product[state : 2 * state]
            late = product[2 * state : 3 * state] + product[3 * state :]
            total = jnp.where(lane < head_width, early, late)
            message_ref[owner, start : start + state, here] = encode(total)
        message_ref[owner, 2 * state :, here] = fact[:, span]


def scan_kernel(message_ref, *rest):
    answer_ref, powers = rest[-2:]
    blocks, double, lanes = message_ref.shape
    state = (double - META) // 2
    top = 2.0**TOP_POWER

    def one(block, start, power_row, side, running, bound):
        facts = message_ref[block, 2 * state : double, :].astype(F32)
        decay = jnp.exp(facts[0:1] + facts[1:2] + facts[2:3])
        back = jnp.exp2(-facts[power_row : power_row + 1])
        power = power_for(bound)
        powers[side, pl.ds(block, 1), :] = power
        answer_ref[block, start : start + state, :] = encode(running * jnp.exp2(power))
        own = decode(message_ref[block, start : start + state, :]) * back
        return running * decay + own, bound * decay + top * back

    def both(block, carry):
        ahead, ahead_bound, behind, behind_bound = carry
        return one(block, 0, 3, 0, ahead, ahead_bound) + one(
            blocks - 1 - block, state, 4, 1, behind, behind_bound
        )

    zero, none = jnp.zeros((state, lanes), F32), jnp.zeros((1, lanes), F32)
    lax.fori_loop(0, blocks, both, (zero, none, zero, none), unroll=4)
    row = lax.broadcasted_iota(jnp.int32, (blocks, META, lanes), 1)
    ahead, behind = powers[0][:, None, :], powers[1][:, None, :]
    meta = jnp.where(row == 0, ahead, jnp.where(row == 1, behind, 0.0))
    answer_ref[:, 2 * state : double, :] = meta.astype(BF16)


def block_kernel(
    head_width,
    scale,
    first_head,
    waits,
    step_ref,
    cum_ref,
    write_ref,
    read_ref,
    x_ref,
    dy_ref,
    *rest,
):
    inner_ref, own_ref, within_ref, maps_ref = rest[waits : waits + 4]
    read_write, source, cum_rows, pair_sum, out_flow = rest[waits + 4 :]
    turn = pl.program_id(0)
    rows, lanes = x_ref.shape
    half = rows // 2
    heads = step_ref.shape[1]
    group = lanes // head_width

    @pl.when(turn == 0)
    def _():
        read_write[...] = scale * lax.dot_general(
            write_ref[...], read_ref[...], (((0,), (0,)), ((), ())), preferred_element_type=F32
        )
        source[...] = jnp.log(step_ref[...]) - cum_ref[...]
        cum_rows[...] = cum_ref[...].T
        pair_sum[...] = jnp.zeros_like(pair_sum)
        out_flow[...] = jnp.zeros_like(out_flow)
        own_ref[...] = jnp.zeros_like(own_ref)

    first = first_head + turn * group
    near = pltpu.roll(source[...], lax.rem(heads - first, heads), axis=1)
    near_cum = cum_rows[pl.ds(first, group), :]
    row = lax.broadcasted_iota(jnp.int32, (half, half), 0)
    col = lax.broadcasted_iota(jnp.int32, (half, half), 1)
    ahead = col >= row
    lane = lax.broadcasted_iota(jnp.int32, (half, 2 * head_width), 1)
    first_half = lane < head_width
    head_lane = lax.broadcasted_iota(jnp.int32, (half, heads), 1)
    flow_aa = read_write[0:half, 0:half]
    flow_ab = read_write[0:half, half:rows]
    flow_bb = read_write[half:rows, half:rows]
    sum_aa = jnp.zeros((half, half), F32)
    sum_ab = jnp.zeros((half, half), F32)
    sum_bb = jnp.zeros((half, half), F32)
    own_a = jnp.zeros((half, heads), F32)
    own_b = jnp.zeros((half, heads), F32)
    zero = jnp.zeros((half, 2 * head_width), BF16)
    flows = []
    for pair in range(group // 2):
        span = slice(pair * 2 * head_width, (pair + 1) * 2 * head_width)
        x_a, x_b = x_ref[0:half, span], x_ref[half:rows, span]
        dy_a, dy_b = dy_ref[0:half, span], dy_ref[half:rows, span]
        early_a, late_a = jnp.where(first_half, dy_a, zero), jnp.where(first_half, zero, dy_a)
        early_b, late_b = jnp.where(first_half, dy_b, zero), jnp.where(first_half, zero, dy_b)
        stack = jnp.concatenate([early_a, early_b, late_a, late_b], axis=0)
        stack_b = jnp.concatenate([early_b, late_b], axis=0)
        grad_a = mul_nt(x_a, stack)
        grad_b = mul_nt(x_b, stack_b)
        masks_a, masks_b = [], []
        for side in range(2):
            place = pair * 2 + side
            head = first + place
            from_a = near[0:half, place : place + 1]
            from_b = near[half:rows, place : place + 1]
            to_a = near_cum[place : place + 1, 0:half]
            to_b = near_cum[place : place + 1, half:rows]
            fade_aa = jnp.exp(jnp.where(ahead, to_a + from_a, -1e30))
            fade_ab = jnp.exp(to_b + from_a)
            fade_bb = jnp.exp(jnp.where(ahead, to_b + from_b, -1e30))
            weigh_aa = fade_aa * grad_a[:, side * rows : side * rows + half]
            weigh_ab = fade_ab * grad_a[:, side * rows + half : (side + 1) * rows]
            weigh_bb = fade_bb * grad_b[:, side * half : (side + 1) * half]
            sum_aa += weigh_aa
            sum_ab += weigh_ab
            sum_bb += weigh_bb
            masks_a += [(fade_aa * flow_aa).astype(BF16), (fade_ab * flow_ab).astype(BF16)]
            masks_b += [(fade_bb * flow_bb).astype(BF16)]
            pair_aa = weigh_aa * flow_aa
            pair_ab = weigh_ab * flow_ab
            pair_bb = weigh_bb * flow_bb
            flow_out = jnp.sum(pair_aa + pair_ab, axis=1, keepdims=True)
            own_a = jnp.where(head_lane == head, flow_out, own_a)
            flow_out = jnp.sum(pair_bb, axis=1, keepdims=True)
            own_b = jnp.where(head_lane == head, flow_out, own_b)
            flow_in = [
                jnp.sum(pair_aa, axis=0, keepdims=True),
                jnp.sum(pair_ab, axis=0, keepdims=True) + jnp.sum(pair_bb, axis=0, keepdims=True),
            ]
            flows.append(jnp.concatenate(flow_in, axis=1))
        inner_ref[0:half, span] = mul(jnp.concatenate(masks_a, axis=1), stack).astype(BF16)
        inner_ref[half:rows, span] = mul(jnp.concatenate(masks_b, axis=1), stack_b).astype(BF16)
    out_flow[pl.ds(first, group), :] = jnp.concatenate(flows, axis=0)
    pair_sum[0:half, 0:half] += sum_aa
    pair_sum[0:half, half:rows] += sum_ab
    pair_sum[half:rows, half:rows] += sum_bb
    own_ref[0:half, :] += own_a
    own_ref[half:rows, :] += own_b

    @pl.when(turn == pl.num_programs(0) - 1)
    def _():
        net = own_ref[...] - out_flow[...].T
        within_ref[...] = mul_exact(triangle(rows, lambda r, c: r > c), net)
        weighted = scale * pair_sum[...]
        maps_ref[...] = jnp.concatenate(
            [
                mul_exact(weighted, read_ref[...].astype(F32), ((1,), (1,))),
                mul_exact(weighted, write_ref[...].astype(F32), ((0,), (1,))),
            ],
            axis=1,
        )


def carry_kernel(head_width, scale, first_head, parts, waits, first, last, *refs):
    refs = list(refs)
    take = lambda count: [refs.pop(0) for _ in range(count)]
    raw_ref, bias_ref, decay_ref, step_ref, cum_ref, write_ref, read_ref, skip_ref = take(8)
    x_ref, dy_ref, inner_ref, answer_ref = take(4)
    take(waits)
    if not first:
        early_sums, early_through, _ = take(3)
    if last:
        own_refs, within_refs, map_refs = take(parts), take(parts), take(parts)
        grad_ref, table_ref, sums, through, weight_e, weight_s, maps, picks = take(8)
    else:
        grad_ref, sums, through, weight_e, weight_s, maps, picks = take(7)
    turn = pl.program_id(0)
    rows, lanes = x_ref.shape
    heads = step_ref.shape[1]
    state = write_ref.shape[0]
    future, past = slice(0, heads), slice(heads, 2 * heads)
    write_sum = slice(2 * heads, 2 * heads + 2 * state)
    read_sum = slice(2 * heads + 2 * state, 2 * heads + 4 * state)

    @pl.when(turn == 0)
    def _():
        cum = cum_ref[...]
        finish = cum[rows - 1 : rows, :]
        weight_e[...] = step_ref[...] * jnp.exp(finish - cum) * scale
        weight_s[...] = jnp.exp(cum) * scale
        pick = head_selector(0, heads, lanes, head_width)
        picks[...] = jnp.concatenate([pick, pick], axis=0)
        write = write_ref[...].astype(F32).T.astype(BF16)
        read = read_ref[...].astype(F32).T.astype(BF16)
        maps[...] = jnp.concatenate([write, write, read, read], axis=1)
        if first:
            sums[...] = jnp.zeros_like(sums)
            through[...] = jnp.zeros_like(through)
        else:
            sums[...] = early_sums[...]
            through[...] = early_through[...]

    first_here = first_head + turn * (lanes // head_width)
    pick = picks[0:heads, :]

    def rolled(value, shift):
        return pltpu.roll(value, lax.rem(shift, heads), axis=1)

    def spread_of(weight):
        near = rolled(weight[...], heads - first_here)
        return mul(jnp.concatenate(halves(near), axis=1), picks[...])

    starts, ends = [], []
    for piece in range(answer_ref.shape[0]):
        back = jnp.exp2(-answer_ref[piece, 2 * state : 2 * state + META, :].astype(F32))
        starts.append(decode(answer_ref[piece, 0:state, :]) * back[0:1])
        ends.append(decode(answer_ref[piece, state : 2 * state, :]) * back[1:2])
    start = jnp.concatenate(starts, axis=1)
    end = jnp.concatenate(ends, axis=1)
    start_parts = jnp.concatenate(halves(start), axis=0)
    end_parts = jnp.concatenate(halves(end), axis=0)
    x = x_ref[...].astype(F32)
    dy = dy_ref[...].astype(F32)
    skip = jnp.concatenate(
        [part.astype(F32) for part in thirds(skip_ref[...])] + [jnp.zeros((5, heads), F32)], axis=0
    )
    skip = rolled(skip, heads - first_here).astype(BF16)
    skip = jnp.sum(mul(skip, pick), axis=0, keepdims=True)

    spread_e = spread_of(weight_e)
    carried = mul(maps[:, 0 : 2 * state], end_parts) * spread_e
    grad_ref[...] = (inner_ref[...].astype(F32) + skip * dy + carried).astype(BF16)
    top, low = halves(x * carried)
    sums[:, future] += rolled(mul_nt(top, pick) + mul_nt(low, pick), first_here)
    top, low = halves(x * spread_e)
    sums[:, write_sum] += mul_nt(top, end_parts) + mul_nt(low, end_parts)

    weighted = dy * spread_of(weight_s)
    top = (weighted * mul(maps[:, 2 * state : 4 * state], start_parts)).astype(BF16)
    sums[:, past] += rolled(mul_nt(top, pick), first_here)
    top, low = halves(weighted)
    sums[:, read_sum] += mul_nt(top, start_parts) + mul_nt(low, start_parts)

    both = jnp.broadcast_to(jnp.sum(start * end, axis=0, keepdims=True), (8, lanes))
    top, low = halves(both)
    through[...] += rolled(mul_nt(top, pick) + mul_nt(low, pick), first_here)

    if not last:
        return

    @pl.when(turn == pl.num_programs(0) - 1)
    def _():
        rate = -jnp.exp(decay_ref[...])
        step = step_ref[...]
        gate = jax.nn.sigmoid(raw_ref[...].astype(F32) + bias_ref[...])
        finish = cum_ref[rows - 1 : rows, :]
        to_come = sums[:, future]
        decay_grad = (
            sum(ref[...] for ref in within_refs)
            + mul_exact(triangle(rows, lambda r, c: r <= c), sums[:, past])
            + mul_exact(triangle(rows, lambda r, c: r > c), to_come)
            + jnp.exp(finish) * scale * through[0:1, :]
        )
        ratio = jnp.where(step > 1e-30, gate / jnp.maximum(step, 1e-30), 1.0)
        inner = sum(ref[...] for ref in own_refs) + to_come
        raw_grad = inner * ratio + rate * decay_grad * gate
        map_sum = sums[:, 2 * heads :] + 0.0
        write_all = map_sum[:, 0:state] + map_sum[:, state : 2 * state]
        read_all = map_sum[:, 2 * state : 3 * state] + map_sum[:, 3 * state :]
        map_grad = jnp.concatenate([write_all, read_all], axis=1)
        map_grad += sum(ref[...] for ref in map_refs)
        table_ref[...] = jnp.concatenate([raw_grad.T, map_grad.T], axis=0).astype(BF16)


def deal_kernel(place_ref, layer_ref, after_ref, *out_refs):
    width = out_refs[0].shape[2]
    for turn, out_ref in enumerate(out_refs):
        start = pl.multiple_of((place_ref[0] ^ turn) * width, width)
        out_ref[0, :, :] = layer_ref[:, pl.ds(start, width)]


def product_kernel(planes, place_ref, *refs):
    table_all, layer_all, sems = refs[-3:]
    wide = (len(refs) - 3 - planes) // 2
    table_refs, layer_refs = refs[:wide], refs[wide : 2 * wide]
    out_refs = refs[2 * wide : 2 * wide + planes]
    columns, rows = table_refs[0].shape
    copies = []
    for plane in range(planes):
        source = place_ref[1] ^ plane
        copies += [
            pltpu.make_async_copy(
                ref.at[source], layer_all.at[plane, pl.ds(turn * rows, rows)], sems.at[plane, turn]
            )
            for turn, ref in enumerate(layer_refs)
        ]
    for copy in copies:
        copy.start()
    for turn, ref in enumerate(table_refs):
        table_all[:, turn * rows : (turn + 1) * rows] = ref[...]
    for plane, out_ref in enumerate(out_refs):
        for turn in range(wide):
            copies[plane * wide + turn].wait()
        total = mul(table_all[...], layer_all[plane])
        most = jnp.max(jnp.abs(total), axis=0, keepdims=True)
        power = power_for(jnp.max(most, axis=1, keepdims=True))
        out_ref[0:columns, :] = encode(total * jnp.exp2(power))
        out_ref[columns:, :] = jnp.broadcast_to(power, out_ref[columns:, :].shape).astype(BF16)


def gather_kernel(factor, *refs):
    part_refs, out_ref = refs[:-1], refs[-1]
    columns = out_ref.shape[1]
    total = jnp.zeros((columns, out_ref.shape[0]), F32)
    for part_ref in part_refs:
        power = part_ref[columns:, :].astype(F32)[0:1]
        total += decode(part_ref[0:columns, :]) * jnp.exp2(-power)
    out_ref[...] = (total * factor).T


def swap(array, axis, turn):
    if turn == 0:
        return array
    count = lax.axis_size(axis)
    return lax.ppermute(array, axis, [(one, one ^ turn) for one in range(count)])


def whole(shape):
    return pl.BlockSpec(shape, lambda i: (0,) * len(shape))


def call(kernel, steps, in_specs, out, scratch, aliases=None):
    return pl.pallas_call(
        kernel,
        grid=(steps,),
        in_specs=in_specs,
        out_specs=[spec for spec, _, _ in out],
        out_shape=[jax.ShapeDtypeStruct(dims, dtype) for _, dims, dtype in out],
        scratch_shapes=[pltpu.VMEM(dims, dtype) for dims, dtype in scratch],
        compiler_params=pltpu.CompilerParams(vmem_limit_bytes=VMEM_LIMIT),
        cost_estimate=SHORT,
        input_output_aliases=aliases or {},
    )


def body(
    layer_input,
    head_inputs,
    output_grad,
    step_raw,
    state_write,
    state_read,
    decay_log,
    step_bias,
    skip_gain,
):
    rows, channels = head_inputs.shape
    heads = step_raw.shape[1]
    head_width = channels // heads
    state = state_write.shape[1]
    model = layer_input.shape[1]
    columns = heads + 2 * state
    axes = ("wide", "seq")
    wide, planes = lax.axis_size("wide"), lax.axis_size("seq")
    blocks = wide * planes
    own_model = model // blocks
    scale = float(rows * blocks * state) ** -0.5
    parts = HALVES if heads % (HALVES * blocks) == 0 else 1
    part_heads = heads // parts
    part_lanes = channels // parts
    owner_lanes = part_lanes // blocks
    piece_lanes = max(owner_lanes, 128)
    pieces = part_lanes // piece_lanes
    depth = 2 * state + META
    bias = step_bias[None, :]
    decay = decay_log[None, :]
    skip = skip_gain[None, :]
    write_t, read_t = state_write.T, state_read.T

    lanes = CARRY_HEADS * head_width
    steps = part_lanes // lanes
    here = lanes // piece_lanes

    def tokens(part, width):
        first = part * (part_lanes // width)
        return pl.BlockSpec((rows, width), lambda i: (0, first + i))

    message_spec = pl.BlockSpec((here, depth, piece_lanes), lambda i: (i, 0, 0))
    both_spec = pl.BlockSpec((here, depth, piece_lanes), lambda i: (i % steps, 0, i // steps))
    head_spec = whole((rows, heads))
    line_spec = whole((1, heads))
    map_spec = whole((state, rows))
    head_out = (head_spec, (rows, heads), F32)

    def exchange(array):
        return lax.all_to_all(array, axes, split_axis=0, concat_axis=0, tiled=True)

    def to_owner(array):
        if owner_lanes < piece_lanes:
            split = array.reshape(pieces, depth, piece_lanes // owner_lanes, owner_lanes)
            array = jnp.moveaxis(split, 2, 1).reshape(blocks, depth, owner_lanes)
        return exchange(array)

    def from_owner(array):
        array = exchange(array)
        if owner_lanes < piece_lanes:
            split = array.reshape(pieces, piece_lanes // owner_lanes, depth, owner_lanes)
            array = jnp.moveaxis(split, 1, 2).reshape(pieces, depth, piece_lanes)
        return array

    def scan(part, message, after):
        dims = (blocks, depth, owner_lanes)
        (answer,) = call(
            scan_kernel,
            1,
            [pl.BlockSpec(dims, lambda i: (0, 0, part))] + [anywhere] * len(after),
            [(whole(dims), dims, BF16)],
            [((2, blocks, owner_lanes), F32)],
        )(message, *after)
        return answer

    with jax.named_scope("summaries"):
        message, step, cum = call(
            functools.partial(summary_kernel, head_width),
            parts * steps,
            [head_spec, line_spec, line_spec, map_spec, map_spec, tokens(0, lanes), tokens(0, lanes)],
            [(both_spec, (pieces, depth, parts * piece_lanes), BF16), head_out, head_out],
            [((heads, rows), F32), ((heads, rows), F32), ((META, heads), BF16)],
        )(step_raw, bias, decay, write_t, read_t, head_inputs, output_grad)
    place = jnp.stack([lax.axis_index("wide"), lax.axis_index("seq")]).astype(jnp.int32)
    with jax.named_scope("layer"):
        if own_model % 128:
            cut = jnp.transpose(layer_input.reshape(rows, planes, wide, own_model), (2, 1, 0, 3))
            dealt = [
                lax.dynamic_index_in_dim(cut, place[0] ^ turn, 0, False) for turn in range(wide)
            ]
        else:
            dealt = pl.pallas_call(
                deal_kernel,
                grid_spec=pltpu.PrefetchScalarGridSpec(
                    num_scalar_prefetch=1,
                    grid=(planes,),
                    in_specs=[
                        pl.BlockSpec((rows, wide * own_model), lambda i, p: (0, i)),
                        pl.BlockSpec(memory_space=pl.ANY),
                    ],
                    out_specs=[pl.BlockSpec((1, rows, own_model), lambda i, p: (i, 0, 0))] * wide,
                ),
                out_shape=[jax.ShapeDtypeStruct((planes, rows, own_model), BF16)] * wide,
                compiler_params=pltpu.CompilerParams(vmem_limit_bytes=VMEM_LIMIT),
                cost_estimate=SHORT,
            )(place, layer_input, cum)
        layer_parts = [swap(one, "wide", turn) for turn, one in enumerate(dealt)]

    anywhere = pl.BlockSpec(memory_space=pltpu.HBM)

    def own_block(part, after):
        width = PAIR_HEADS * head_width
        here_spec = pl.BlockSpec((rows, width), lambda i: (0, i))
        return call(
            functools.partial(block_kernel, head_width, scale, part * part_heads, len(after)),
            part_lanes // width,
            [head_spec, head_spec, map_spec, map_spec, tokens(part, width), tokens(part, width)]
            + [anywhere] * len(after),
            [
                (here_spec, (rows, part_lanes), BF16),
                head_out,
                head_out,
                (whole((rows, 2 * state)), (rows, 2 * state), F32),
            ],
            [
                ((rows, rows), F32),
                ((rows, heads), F32),
                ((heads, rows), F32),
                ((rows, rows), F32),
                ((heads, rows), F32),
            ],
        )(step, cum, write_t, read_t, head_inputs, output_grad, *after)

    firsts = [turn for turn in (2, 4, 3, 5) if turn < wide]
    middle = [turn for turn in (6,) if turn < wide]
    with jax.named_scope("own_block"):
        own_parts = [own_block(0, dealt[:1])]
        if parts > 1:
            own_parts.append(own_block(1, [own_parts[0][1], layer_parts[1]]))
    with jax.named_scope("scan"):
        arrived = to_owner(message)
        returned, before = [], own_parts[-1][1]
        for part in range(parts):
            after = [layer_parts[turn] for turn in (firsts, middle)[part]]
            before = scan(part, arrived, [before] + after)
            returned.append(from_owner(before))

    sums_out = (whole((rows, 2 * heads + 4 * state)), (rows, 2 * heads + 4 * state), F32)
    through_out = (whole((8, heads)), (8, heads), F32)
    early = ()
    with jax.named_scope("carried"):
        for part in range(parts):
            first, last = part == 0, part == parts - 1
            in_specs = [head_spec, line_spec, line_spec, head_spec, head_spec, map_spec, map_spec]
            in_specs += [line_spec, tokens(part, lanes), tokens(part, lanes)]
            in_specs += [pl.BlockSpec((rows, lanes), lambda i: (0, i)), message_spec]
            operands = [step_raw, bias, decay, step, cum, write_t, read_t, skip]
            operands += [head_inputs, output_grad, own_parts[part][0], returned[part]]
            after = layer_parts[7:] if last else []
            operands += after
            in_specs += [anywhere] * len(after)
            aliases = {}
            if not first:
                in_specs += [sums_out[0], through_out[0], pl.BlockSpec(memory_space=pl.ANY)]
                operands += [early[1], early[2], early[0]]
                aliases = {len(operands) - 1: 0}
            scratch = [((rows, heads), F32)] * 2 + [((rows, 4 * state), BF16)]
            scratch += [((2 * heads, lanes), BF16)]
            out = [(tokens(part, lanes), (rows, channels), BF16)]
            if last:
                for which in (1, 2, 3):
                    operands += [one[which] for one in own_parts]
                    in_specs += [whole(one[which].shape) for one in own_parts]
                out += [(whole((columns, rows)), (columns, rows), BF16)]
                scratch = [sums_out[1:], through_out[1:]] + scratch
            else:
                out += [sums_out, through_out]
            early = call(
                functools.partial(
                    carry_kernel, head_width, scale, part * part_heads, parts, len(after), first, last
                ),
                steps,
                in_specs,
                out,
                scratch,
                aliases,
            )(*operands)
    grad_x, table = early

    with jax.named_scope("projection"):
        tables = [swap(table, "wide", turn) for turn in range(wide)]
        coded = (columns + META, own_model)
        products = pl.pallas_call(
            functools.partial(product_kernel, planes),
            in_specs=[pl.BlockSpec(memory_space=pltpu.SMEM)]
            + [pl.BlockSpec(memory_space=pltpu.VMEM)] * wide
            + [anywhere] * wide,
            out_specs=[pl.BlockSpec(memory_space=pltpu.VMEM)] * planes,
            out_shape=[jax.ShapeDtypeStruct(coded, BF16)] * planes,
            scratch_shapes=[
                pltpu.VMEM((columns, wide * rows), BF16),
                pltpu.VMEM((planes, wide * rows, own_model), BF16),
                pltpu.SemaphoreType.DMA((planes, wide)),
            ],
            compiler_params=pltpu.CompilerParams(vmem_limit_bytes=VMEM_LIMIT),
            cost_estimate=SHORT,
        )(place, *tables, *layer_parts)
        sums = [swap(one, "seq", turn) for turn, one in enumerate(products)]
        (weight_grad,) = call(
            functools.partial(gather_kernel, 1.0 / math.sqrt(rows * blocks)),
            1,
            [whole(coded)] * planes,
            [(whole((own_model, columns)), (own_model, columns), F32)],
            [],
        )(*sums)
    return grad_x, weight_grad


def solution(mesh):
    in_specs = (
        P(("wide", "seq"), None),
        P(("wide", "seq"), None),
        P(("wide", "seq"), None),
        P(("wide", "seq"), None),
        P(("wide", "seq"), None),
        P(("wide", "seq"), None),
        P(),
        P(),
        P(),
    )
    out_specs = (P(("wide", "seq"), None), P(("seq", "wide"), None))
    return jax.shard_map(body, mesh=mesh, in_specs=in_specs, out_specs=out_specs, check_vma=False)
```

```python
import functools
import math

import jax
import jax.numpy as jnp
from jax import lax
from jax.experimental import pallas as pl
from jax.experimental.pallas import tpu as pltpu
from jax.sharding import PartitionSpec as P

F32 = jnp.float32
BF16 = jnp.bfloat16
EXACT = lax.Precision.HIGHEST
VMEM_LIMIT = 64 * 1024 * 1024
TOP_POWER = 30.0
PRODUCT_BOUND = 30.0
CARRY_HEADS = 16
PAIR_HEADS = 8
META = 8
SHORT = pl.CostEstimate(flops=1000, bytes_accessed=1000, transcendentals=0)


def mul(a, b):
    return lax.dot_general(a, b, (((1,), (0,)), ((), ())), preferred_element_type=F32)


def mul_nt(a, b):
    return lax.dot_general(a, b, (((1,), (1,)), ((), ())), preferred_element_type=F32)


def mul_exact(a, b, dims=((1,), (0,))):
    return lax.dot_general(a, b, (dims, ((), ())), preferred_element_type=F32, precision=EXACT)


def halves(value):
    top = value.astype(BF16)
    return top, (value - top.astype(F32)).astype(BF16)


def power_for(bound):
    power = jnp.floor(TOP_POWER - jnp.log2(jnp.maximum(bound, 1e-37)))
    return jnp.clip(power, -100.0, 100.0)


def thirds(value):
    top, rest = value.astype(BF16), value
    rest = rest - top.astype(F32)
    middle = rest.astype(BF16)
    return top, middle, (rest - middle.astype(F32)).astype(BF16)


def encode(value):
    square = value * value
    fourth = square * square
    return jnp.where(value < 0, -fourth, fourth).astype(BF16)


def decode(coded):
    coded = coded.astype(F32)
    size = jnp.maximum(jnp.abs(coded), 1e-37)
    inverse = lax.rsqrt(size)
    return coded * inverse * lax.rsqrt(size * inverse)


def head_selector(first_head, heads, lanes, head_width):
    row = lax.broadcasted_iota(jnp.int32, (heads, lanes), 0)
    lane = lax.broadcasted_iota(jnp.int32, (heads, lanes), 1)
    return jnp.where(row == first_head + lane // head_width, 1.0, 0.0).astype(BF16)


def triangle(length, keep):
    row = lax.broadcasted_iota(jnp.int32, (length, length), 0)
    col = lax.broadcasted_iota(jnp.int32, (length, length), 1)
    return jnp.where(keep(row, col), 1.0, 0.0).astype(F32)


def summary_kernel(
    head_width,
    raw_ref,
    bias_ref,
    decay_ref,
    write_ref,
    read_ref,
    x_ref,
    dy_ref,
    message_ref,
    step_ref,
    cum_ref,
    weight_f,
    weight_b,
    facts,
):
    turn = pl.program_id(0)
    heads = raw_ref.shape[1]
    rows, lanes = x_ref.shape
    state = write_ref.shape[0]

    @pl.when(turn == 0)
    def _():
        step = jax.nn.softplus(raw_ref[...].astype(F32) + bias_ref[...])
        rate = -jnp.exp(decay_ref[...])
        cum = mul_exact(triangle(rows, lambda r, c: r >= c), step * rate)
        finish = cum[rows - 1 : rows, :]
        forward = step * jnp.exp(finish - cum)
        backward = jnp.exp(cum)
        power_f = power_for(PRODUCT_BOUND * jnp.sum(forward, axis=0, keepdims=True))
        power_b = power_for(PRODUCT_BOUND * jnp.sum(backward, axis=0, keepdims=True))
        step_ref[...] = step
        cum_ref[...] = cum
        parts = thirds(jnp.maximum(finish, -1e30))
        facts[...] = jnp.concatenate(
            [part.astype(F32) for part in parts]
            + [power_f, power_b, jnp.zeros((META - 5, heads), F32)],
            axis=0,
        ).astype(BF16)
        weight_f[...] = (forward * jnp.exp2(power_f)).T
        weight_b[...] = (backward * jnp.exp2(power_b)).T

    group = lanes // head_width
    pair_lanes = 2 * head_width
    width = message_ref.shape[2]
    near = pl.ds(turn * group, group)
    pick = head_selector(turn * group, heads, lanes, head_width)
    fact = mul(facts[...], pick).astype(BF16)
    lane = lax.broadcasted_iota(jnp.int32, (state, pair_lanes), 1)
    ahead = (x_ref, write_ref[...].astype(F32), weight_f[near, :], 0)
    behind = (dy_ref, read_ref[...].astype(F32), weight_b[near, :], state)
    for pair in range(group // 2):
        span = slice(pair * pair_lanes, (pair + 1) * pair_lanes)
        owner, offset = pair * pair_lanes // width, pair * pair_lanes % width
        here = slice(offset, offset + pair_lanes)
        for tokens_ref, rows_t, weights, start in (ahead, behind):
            scaled = []
            for head in (2 * pair, 2 * pair + 1):
                scaled += halves(rows_t * weights[head : head + 1, :])
            product = mul(jnp.concatenate(scaled, axis=0), tokens_ref[:, span])
            early = product[0:state] + product[state : 2 * state]
            late = product[2 * state : 3 * state] + product[3 * state :]
            total = jnp.where(lane < head_width, early, late)
            message_ref[owner, start : start + state, here] = encode(total)
        message_ref[owner, 2 * state :, here] = fact[:, span]


def scan_kernel(message_ref, *rest):
    answer_ref, powers = rest[-2:]
    blocks, double, lanes = message_ref.shape
    state = (double - META) // 2
    top = 2.0**TOP_POWER

    def one(block, start, power_row, side, running, bound):
        facts = message_ref[block, 2 * state : double, :].astype(F32)
        decay = jnp.exp(facts[0:1] + facts[1:2] + facts[2:3])
        back = jnp.exp2(-facts[power_row : power_row + 1])
        power = power_for(bound)
        powers[side, pl.ds(block, 1), :] = power
        answer_ref[block, start : start + state, :] = encode(running * jnp.exp2(power))
        own = decode(message_ref[block, start : start + state, :]) * back
        return running * decay + own, bound * decay + top * back

    def both(block, carry):
        ahead, ahead_bound, behind, behind_bound = carry
        return one(block, 0, 3, 0, ahead, ahead_bound) + one(
            blocks - 1 - block, state, 4, 1, behind, behind_bound
        )

    zero, none = jnp.zeros((state, lanes), F32), jnp.zeros((1, lanes), F32)
    lax.fori_loop(0, blocks, both, (zero, none, zero, none), unroll=4)
    row = lax.broadcasted_iota(jnp.int32, (blocks, META, lanes), 1)
    ahead, behind = powers[0][:, None, :], powers[1][:, None, :]
    meta = jnp.where(row == 0, ahead, jnp.where(row == 1, behind, 0.0))
    answer_ref[:, 2 * state : double, :] = meta.astype(BF16)


def block_kernel(
    head_width,
    scale,
    first_head,
    waits,
    step_ref,
    cum_ref,
    write_ref,
    read_ref,
    x_ref,
    dy_ref,
    *rest,
):
    inner_ref, own_ref, within_ref, maps_ref = rest[waits : waits + 4]
    read_write, source, cum_rows, pair_sum, out_flow = rest[waits + 4 :]
    turn = pl.program_id(0)
    rows, lanes = x_ref.shape
    half = rows // 2
    heads = step_ref.shape[1]
    group = lanes // head_width

    @pl.when(turn == 0)
    def _():
        read_write[...] = scale * lax.dot_general(
            write_ref[...], read_ref[...], (((0,), (0,)), ((), ())), preferred_element_type=F32
        )
        source[...] = jnp.log(step_ref[...]) - cum_ref[...]
        cum_rows[...] = cum_ref[...].T
        pair_sum[...] = jnp.zeros_like(pair_sum)
        out_flow[...] = jnp.zeros_like(out_flow)
        own_ref[...] = jnp.zeros_like(own_ref)

    first = first_head + turn * group
    near = pltpu.roll(source[...], lax.rem(heads - first, heads), axis=1)
    near_cum = cum_rows[pl.ds(first, group), :]
    row = lax.broadcasted_iota(jnp.int32, (half, half), 0)
    col = lax.broadcasted_iota(jnp.int32, (half, half), 1)
    ahead = col >= row
    lane = lax.broadcasted_iota(jnp.int32, (half, 2 * head_width), 1)
    first_half = lane < head_width
    head_lane = lax.broadcasted_iota(jnp.int32, (half, heads), 1)
    flow_aa = read_write[0:half, 0:half]
    flow_ab = read_write[0:half, half:rows]
    flow_bb = read_write[half:rows, half:rows]
    sum_aa = jnp.zeros((half, half), F32)
    sum_ab = jnp.zeros((half, half), F32)
    sum_bb = jnp.zeros((half, half), F32)
    own_a = jnp.zeros((half, heads), F32)
    own_b = jnp.zeros((half, heads), F32)
    zero = jnp.zeros((half, 2 * head_width), BF16)
    flows = []
    for pair in range(group // 2):
        span = slice(pair * 2 * head_width, (pair + 1) * 2 * head_width)
        x_a, x_b = x_ref[0:half, span], x_ref[half:rows, span]
        dy_a, dy_b = dy_ref[0:half, span], dy_ref[half:rows, span]
        early_a, late_a = jnp.where(first_half, dy_a, zero), jnp.where(first_half, zero, dy_a)
        early_b, late_b = jnp.where(first_half, dy_b, zero), jnp.where(first_half, zero, dy_b)
        stack = jnp.concatenate([early_a, early_b, late_a, late_b], axis=0)
        stack_b = jnp.concatenate([early_b, late_b], axis=0)
        grad_a = mul_nt(x_a, stack)
        grad_b = mul_nt(x_b, stack_b)
        masks_a, masks_b = [], []
        for side in range(2):
            place = pair * 2 + side
            head = first + place
            from_a = near[0:half, place : place + 1]
            from_b = near[half:rows, place : place + 1]
            to_a = near_cum[place : place + 1, 0:half]
            to_b = near_cum[place : place + 1, half:rows]
            fade_aa = jnp.exp(jnp.where(ahead, to_a + from_a, -1e30))
            fade_ab = jnp.exp(to_b + from_a)
            fade_bb = jnp.exp(jnp.where(ahead, to_b + from_b, -1e30))
            weigh_aa = fade_aa * grad_a[:, side * rows : side * rows + half]
            weigh_ab = fade_ab * grad_a[:, side * rows + half : (side + 1) * rows]
            weigh_bb = fade_bb * grad_b[:, side * half : (side + 1) * half]
            sum_aa += weigh_aa
            sum_ab += weigh_ab
            sum_bb += weigh_bb
            masks_a += [(fade_aa * flow_aa).astype(BF16), (fade_ab * flow_ab).astype(BF16)]
            masks_b += [(fade_bb * flow_bb).astype(BF16)]
            pair_aa = weigh_aa * flow_aa
            pair_ab = weigh_ab * flow_ab
            pair_bb = weigh_bb * flow_bb
            flow_out = jnp.sum(pair_aa + pair_ab, axis=1, keepdims=True)
            own_a = jnp.where(head_lane == head, flow_out, own_a)
            flow_out = jnp.sum(pair_bb, axis=1, keepdims=True)
            own_b = jnp.where(head_lane == head, flow_out, own_b)
            flow_in = [
                jnp.sum(pair_aa, axis=0, keepdims=True),
                jnp.sum(pair_ab, axis=0, keepdims=True) + jnp.sum(pair_bb, axis=0, keepdims=True),
            ]
            flows.append(jnp.concatenate(flow_in, axis=1))
        inner_ref[0:half, span] = mul(jnp.concatenate(masks_a, axis=1), stack).astype(BF16)
        inner_ref[half:rows, span] = mul(jnp.concatenate(masks_b, axis=1), stack_b).astype(BF16)
    out_flow[pl.ds(first, group), :] = jnp.concatenate(flows, axis=0)
    pair_sum[0:half, 0:half] += sum_aa
    pair_sum[0:half, half:rows] += sum_ab
    pair_sum[half:rows, half:rows] += sum_bb
    own_ref[0:half, :] += own_a
    own_ref[half:rows, :] += own_b

    @pl.when(turn == pl.num_programs(0) - 1)
    def _():
        net = own_ref[...] - out_flow[...].T
        within_ref[...] = mul_exact(triangle(rows, lambda r, c: r > c), net)
        weighted = scale * pair_sum[...]
        maps_ref[...] = jnp.concatenate(
            [
                mul_exact(weighted, read_ref[...].astype(F32), ((1,), (1,))),
                mul_exact(weighted, write_ref[...].astype(F32), ((0,), (1,))),
            ],
            axis=1,
        )


def spread_heads(weight, first_head, picks, group):
    heads = weight.shape[1]
    near = pltpu.roll(weight, lax.rem(heads - first_head, heads), axis=1)
    top = near.astype(BF16).astype(F32)
    low = pltpu.roll(near - top, group, axis=1)
    lane = lax.broadcasted_iota(jnp.int32, near.shape, 1)
    return mul(jnp.where(lane < group, top, low).astype(BF16), picks)


def spread_picks(group, heads, lanes, head_width):
    row = lax.broadcasted_iota(jnp.int32, (heads, lanes), 0)
    lane = lax.broadcasted_iota(jnp.int32, (heads, lanes), 1)
    match = jnp.where(row < group, row, row - group) == lane // head_width
    return jnp.where(match, 1.0, 0.0).astype(BF16)


def read_answer(answer_ref, state, power_row):
    found = []
    start = power_row * state
    for piece in range(answer_ref.shape[0]):
        facts = answer_ref[piece, 2 * state :, :].astype(F32)
        back = jnp.exp2(-facts[power_row : power_row + 1])
        found.append(decode(answer_ref[piece, start : start + state, :]) * back)
    return jnp.concatenate(found, axis=1)


def carry_kernel(head_width, scale, waits, *refs):
    raw_ref, bias_ref, decay_ref, step_ref, cum_ref, write_ref, read_ref = refs[:7]
    own_ref, within_ref, map_ref, x_ref, dy_ref, answer_ref = refs[7:13]
    table_ref, sums, through, weight_e, weight_s, maps, picks = refs[13 + waits :]
    turn = pl.program_id(0)
    rows, lanes = x_ref.shape
    heads = step_ref.shape[1]
    state = write_ref.shape[0]
    group = lanes // head_width
    pair_lanes = 2 * head_width
    future, past = slice(0, heads), slice(heads, 2 * heads)
    write_sum = slice(2 * heads, 2 * heads + 2 * state)
    read_sum = slice(2 * heads + 2 * state, 2 * heads + 4 * state)

    @pl.when(turn == 0)
    def _():
        cum = cum_ref[...]
        finish = cum[rows - 1 : rows, :]
        weight_e[...] = step_ref[...] * jnp.exp(finish - cum) * scale
        weight_s[...] = jnp.exp(cum) * scale
        write, read = write_ref[...].astype(F32).T, read_ref[...].astype(F32).T
        maps[...] = jnp.concatenate([write, write, read, read], axis=1)
        picks[0:heads, :] = spread_picks(group, heads, lanes, head_width)
        picks[heads:, :] = head_selector(0, heads, lanes, head_width)
        sums[...] = jnp.zeros_like(sums)
        through[...] = jnp.zeros_like(through)

    first_here = turn * group
    pick = picks[heads:, :]
    early = lax.broadcasted_iota(jnp.int32, (state, pair_lanes), 1) < head_width
    none = jnp.zeros((state, pair_lanes), BF16)
    start = read_answer(answer_ref, state, 0)
    end = read_answer(answer_ref, state, 1)

    def products(tokens_ref, states, weight, map_columns):
        spread = spread_heads(weight[...], first_here, picks[0:heads, :], group)
        parts = halves(states)
        total, mapped = 0.0, []
        for pair in range(group // 2):
            span = slice(pair * pair_lanes, (pair + 1) * pair_lanes)
            blocks = [
                jnp.concatenate(
                    [jnp.where(early, part[:, span], none), jnp.where(early, none, part[:, span])],
                    axis=0,
                )
                for part in parts
            ]
            twice = jnp.concatenate([tokens_ref[:, span], tokens_ref[:, span]], axis=1)
            weighted = mul_nt(twice, jnp.concatenate(blocks, axis=1)) * spread[:, span]
            total += weighted
            mapped.append(weighted * map_columns)
        return total, mapped

    def summed(parts):
        return mul_nt(jnp.concatenate(parts, axis=1), pick)

    def placed(value):
        return pltpu.roll(value, first_here, axis=1)

    total, mapped = products(x_ref, end, weight_e, maps[:, 0 : 2 * state])
    sums[:, write_sum] += total
    mapped = [halves(one) for one in mapped]
    to_come = summed([one[0] for one in mapped]) + summed([one[1] for one in mapped])
    sums[:, future] += placed(to_come)

    total, mapped = products(dy_ref, start, weight_s, maps[:, 2 * state : 4 * state])
    sums[:, read_sum] += total
    sums[:, past] += placed(summed([one.astype(BF16) for one in mapped]))

    both = jnp.broadcast_to(jnp.sum(start * end, axis=0, keepdims=True), (8, lanes))
    top, low = halves(both)
    through[...] += placed(mul_nt(top, pick) + mul_nt(low, pick))

    @pl.when(turn == pl.num_programs(0) - 1)
    def _():
        rate = -jnp.exp(decay_ref[...])
        step = step_ref[...]
        gate = jax.nn.sigmoid(raw_ref[...].astype(F32) + bias_ref[...])
        finish = cum_ref[rows - 1 : rows, :]
        ahead = sums[:, future]
        decay_grad = (
            within_ref[...]
            + mul_exact(triangle(rows, lambda r, c: r <= c), sums[:, past])
            + mul_exact(triangle(rows, lambda r, c: r > c), ahead)
            + jnp.exp(finish) * scale * through[0:1, :]
        )
        ratio = jnp.where(step > 1e-30, gate / jnp.maximum(step, 1e-30), 1.0)
        raw_grad = (own_ref[...] + ahead) * ratio + rate * decay_grad * gate
        map_sum = sums[:, 2 * heads :]
        write_all = map_sum[:, 0:state] + map_sum[:, state : 2 * state]
        read_all = map_sum[:, 2 * state : 3 * state] + map_sum[:, 3 * state :]
        map_grad = jnp.concatenate([write_all, read_all], axis=1) + map_ref[...]
        table_ref[...] = jnp.concatenate([raw_grad.T, map_grad.T], axis=0).astype(BF16)


def grad_kernel(head_width, scale, first_head, waits, *refs):
    step_ref, cum_ref, write_ref, skip_ref, dy_ref, inner_ref, answer_ref = refs[:7]
    grad_ref, weight_e, maps, picks = refs[7 + waits :]
    turn = pl.program_id(0)
    rows, lanes = dy_ref.shape
    heads = step_ref.shape[1]
    state = write_ref.shape[0]
    group = lanes // head_width

    @pl.when(turn == 0)
    def _():
        cum = cum_ref[...]
        finish = cum[rows - 1 : rows, :]
        weight_e[...] = step_ref[...] * jnp.exp(finish - cum) * scale
        write = write_ref[...].astype(F32).T.astype(BF16)
        maps[...] = jnp.concatenate([write, write], axis=1)
        picks[...] = spread_picks(group, heads, lanes, head_width)

    first_here = first_head + turn * group
    end_parts = jnp.concatenate(halves(read_answer(answer_ref, state, 1)), axis=0)
    skip = jnp.broadcast_to(skip_ref[...], (16, heads))
    skip = spread_heads(skip, first_here, picks[...], group)[0:1]
    carried = mul(maps[...], end_parts) * spread_heads(weight_e[...], first_here, picks[...], group)
    inner = inner_ref[...].astype(F32)
    grad_ref[...] = (inner + skip * dy_ref[...].astype(F32) + carried).astype(BF16)


def deal_kernel(place_ref, layer_ref, after_ref, *out_refs):
    width = out_refs[0].shape[2]
    for turn, out_ref in enumerate(out_refs):
        start = pl.multiple_of((place_ref[0] ^ turn) * width, width)
        out_ref[0, :, :] = layer_ref[:, pl.ds(start, width)]


def product_kernel(planes, wide, place_ref, *refs):
    table_refs, layer_refs = refs[:wide], refs[wide : 2 * wide]
    out_refs = refs[-3 - planes : -3]
    table_all, layer_all, sems = refs[-3:]
    columns, rows = table_refs[0].shape
    loads = [
        pltpu.make_async_copy(ref, table_all.at[turn], sems.at[planes, turn])
        for turn, ref in enumerate(table_refs)
    ]
    for plane in range(planes):
        source = place_ref[1] ^ plane
        loads += [
            pltpu.make_async_copy(
                ref.at[source], layer_all.at[plane, pl.ds(turn * rows, rows)], sems.at[plane, turn]
            )
            for turn, ref in enumerate(layer_refs)
        ]
    for load in loads:
        load.start()
    for load in loads[:wide]:
        load.wait()
    table = jnp.concatenate([table_all[turn] for turn in range(wide)], axis=1)
    for plane, out_ref in enumerate(out_refs):
        for load in loads[(plane + 1) * wide : (plane + 2) * wide]:
            load.wait()
        total = mul(table, layer_all[plane])
        most = jnp.max(jnp.abs(total), axis=0, keepdims=True)
        power = power_for(jnp.max(most, axis=1, keepdims=True))
        out_ref[0:columns, :] = encode(total * jnp.exp2(power))
        out_ref[columns:, :] = jnp.broadcast_to(power, out_ref[columns:, :].shape).astype(BF16)


def gather_kernel(factor, planes, *refs):
    part_refs, out_ref = refs[:planes], refs[-1]
    columns = out_ref.shape[1]
    total = jnp.zeros((columns, out_ref.shape[0]), F32)
    for part_ref in part_refs:
        power = part_ref[columns:, :].astype(F32)[0:1]
        total += decode(part_ref[0:columns, :]) * jnp.exp2(-power)
    out_ref[...] = (total * factor).T


def swap(array, axis, turn):
    if turn == 0:
        return array
    count = lax.axis_size(axis)
    return lax.ppermute(array, axis, [(one, one ^ turn) for one in range(count)])


def whole(shape):
    return pl.BlockSpec(shape, lambda i: (0,) * len(shape))


def call(kernel, steps, in_specs, out, scratch, aliases=None):
    return pl.pallas_call(
        kernel,
        grid=(steps,),
        in_specs=in_specs,
        out_specs=[spec for spec, _, _ in out],
        out_shape=[jax.ShapeDtypeStruct(dims, dtype) for _, dims, dtype in out],
        scratch_shapes=[pltpu.VMEM(dims, dtype) for dims, dtype in scratch],
        compiler_params=pltpu.CompilerParams(vmem_limit_bytes=VMEM_LIMIT),
        cost_estimate=SHORT,
        input_output_aliases=aliases or {},
    )


def body(
    layer_input,
    head_inputs,
    output_grad,
    step_raw,
    state_write,
    state_read,
    decay_log,
    step_bias,
    skip_gain,
):
    rows, channels = head_inputs.shape
    heads = step_raw.shape[1]
    head_width = channels // heads
    state = state_write.shape[1]
    model = layer_input.shape[1]
    columns = heads + 2 * state
    axes = ("wide", "seq")
    wide, planes = lax.axis_size("wide"), lax.axis_size("seq")
    blocks = wide * planes
    own_model = model // blocks
    scale = float(rows * blocks * state) ** -0.5
    owner_lanes = channels // blocks
    piece_lanes = max(owner_lanes, 128)
    pieces = channels // piece_lanes
    depth = 2 * state + META
    bias = step_bias[None, :]
    decay = decay_log[None, :]
    skip = skip_gain[None, :]
    write_t, read_t = state_write.T, state_read.T

    lanes = CARRY_HEADS * head_width
    steps = channels // lanes
    here = lanes // piece_lanes

    def tokens(width, first=0):
        return pl.BlockSpec((rows, width), lambda i: (0, first + i))

    message_spec = pl.BlockSpec((here, depth, piece_lanes), lambda i: (i, 0, 0))
    head_spec = whole((rows, heads))
    line_spec = whole((1, heads))
    map_spec = whole((state, rows))
    head_out = (head_spec, (rows, heads), F32)

    def exchange(array):
        return lax.all_to_all(array, axes, split_axis=0, concat_axis=0, tiled=True)

    def to_owner(array):
        if owner_lanes < piece_lanes:
            split = array.reshape(pieces, depth, piece_lanes // owner_lanes, owner_lanes)
            array = jnp.moveaxis(split, 2, 1).reshape(blocks, depth, owner_lanes)
        return exchange(array)

    def from_owner(array):
        array = exchange(array)
        if owner_lanes < piece_lanes:
            split = array.reshape(pieces, piece_lanes // owner_lanes, depth, owner_lanes)
            array = jnp.moveaxis(split, 1, 2).reshape(pieces, depth, piece_lanes)
        return array

    with jax.named_scope("summaries"):
        message, step, cum = call(
            functools.partial(summary_kernel, head_width),
            steps,
            [head_spec, line_spec, line_spec, map_spec, map_spec, tokens(lanes), tokens(lanes)],
            [(message_spec, (pieces, depth, piece_lanes), BF16), head_out, head_out],
            [((heads, rows), F32), ((heads, rows), F32), ((META, heads), BF16)],
        )(step_raw, bias, decay, write_t, read_t, head_inputs, output_grad)
    place = jnp.stack([lax.axis_index("wide"), lax.axis_index("seq")]).astype(jnp.int32)
    with jax.named_scope("layer"):
        if own_model % 128:
            cut = jnp.transpose(layer_input.reshape(rows, planes, wide, own_model), (2, 1, 0, 3))
            dealt = [
                lax.dynamic_index_in_dim(cut, place[0] ^ turn, 0, False) for turn in range(wide)
            ]
        else:
            dealt = pl.pallas_call(
                deal_kernel,
                grid_spec=pltpu.PrefetchScalarGridSpec(
                    num_scalar_prefetch=1,
                    grid=(planes,),
                    in_specs=[
                        pl.BlockSpec((rows, wide * own_model), lambda i, p: (0, i)),
                        pl.BlockSpec(memory_space=pl.ANY),
                    ],
                    out_specs=[pl.BlockSpec((1, rows, own_model), lambda i, p: (i, 0, 0))] * wide,
                ),
                out_shape=[jax.ShapeDtypeStruct((planes, rows, own_model), BF16)] * wide,
                compiler_params=pltpu.CompilerParams(vmem_limit_bytes=VMEM_LIMIT),
                cost_estimate=SHORT,
            )(place, layer_input, cum)
        layer_parts = [swap(one, "wide", turn) for turn, one in enumerate(dealt)]

    anywhere = pl.BlockSpec(memory_space=pltpu.HBM)
    firsts = [turn for turn in (1, 2, 4, 3, 5) if turn < wide]
    lasts = [layer_parts[turn] for turn in range(1, wide) if turn not in firsts]
    with jax.named_scope("own_block"):
        width = PAIR_HEADS * head_width
        inner, own, within, maps = call(
            functools.partial(block_kernel, head_width, scale, 0, 1),
            channels // width,
            [head_spec, head_spec, map_spec, map_spec, tokens(width), tokens(width), anywhere],
            [
                (tokens(width), (rows, channels), BF16),
                head_out,
                head_out,
                (whole((rows, 2 * state)), (rows, 2 * state), F32),
            ],
            [
                ((rows, rows), F32),
                ((rows, heads), F32),
                ((heads, rows), F32),
                ((rows, rows), F32),
                ((heads, rows), F32),
            ],
        )(step, cum, write_t, read_t, head_inputs, output_grad, dealt[0])
    with jax.named_scope("scan"):
        after = [own] + [layer_parts[turn] for turn in firsts]
        dims = (blocks, depth, owner_lanes)
        (answer,) = call(
            scan_kernel,
            1,
            [whole(dims)] + [anywhere] * len(after),
            [(whole(dims), dims, BF16)],
            [((2, blocks, owner_lanes), F32)],
        )(to_owner(message), *after)
        returned = from_owner(answer)

    with jax.named_scope("carried"):
        (table,) = call(
            functools.partial(carry_kernel, head_width, scale, len(lasts)),
            steps,
            [head_spec, line_spec, line_spec, head_spec, head_spec, map_spec, map_spec]
            + [head_spec, head_spec, whole((rows, 2 * state))]
            + [tokens(lanes), tokens(lanes), message_spec]
            + [anywhere] * len(lasts),
            [(whole((columns, rows)), (columns, rows), BF16)],
            [
                ((rows, 2 * heads + 4 * state), F32),
                ((8, heads), F32),
                ((rows, heads), F32),
                ((rows, heads), F32),
                ((rows, 4 * state), F32),
                ((2 * heads, lanes), BF16),
            ],
        )(
            *(step_raw, bias, decay, step, cum, write_t, read_t, own, within, maps),
            *(head_inputs, output_grad, returned, *lasts),
        )

    def grad_half(half, grad):
        first = half * (steps // 2)
        in_specs = [head_spec, head_spec, map_spec, line_spec]
        in_specs += [tokens(lanes, first), tokens(lanes, first)]
        in_specs += [pl.BlockSpec((here, depth, piece_lanes), lambda i: (first + i, 0, 0))]
        in_specs += [anywhere] * len(grad)
        (grad,) = call(
            functools.partial(grad_kernel, head_width, scale, first * CARRY_HEADS, len(grad)),
            steps // 2,
            in_specs,
            [(tokens(lanes, first), (rows, channels), BF16)],
            [((rows, heads), F32), ((rows, 2 * state), BF16), ((heads, lanes), BF16)],
            {len(in_specs) - 1: 0} if half else {},
        )(step, cum, write_t, skip, output_grad, inner, returned, *grad)
        return grad

    with jax.named_scope("grad_x"):
        grad_part = grad_half(0, [table])
        grad_x = grad_half(1, [grad_part])

    with jax.named_scope("projection"):
        tables = [swap(table, "wide", turn) for turn in range(wide)]
        coded = (columns + META, own_model)
        products = pl.pallas_call(
            functools.partial(product_kernel, planes, wide),
            in_specs=[pl.BlockSpec(memory_space=pltpu.SMEM)] + [anywhere] * (2 * wide + 1),
            out_specs=[pl.BlockSpec(memory_space=pltpu.VMEM)] * planes,
            out_shape=[jax.ShapeDtypeStruct(coded, BF16)] * planes,
            scratch_shapes=[
                pltpu.VMEM((wide, columns, rows), BF16),
                pltpu.VMEM((planes, wide * rows, own_model), BF16),
                pltpu.SemaphoreType.DMA((planes + 1, wide)),
            ],
            compiler_params=pltpu.CompilerParams(vmem_limit_bytes=VMEM_LIMIT),
            cost_estimate=SHORT,
        )(place, *tables, *layer_parts, grad_part)
        sums = [swap(one, "seq", turn) for turn, one in enumerate(products)]
        (weight_grad,) = call(
            functools.partial(gather_kernel, 1.0 / math.sqrt(rows * blocks), planes),
            1,
            [whole(coded)] * planes + [anywhere],
            [(whole((own_model, columns)), (own_model, columns), F32)],
            [],
        )(*sums, grad_x)
    return grad_x, weight_grad


def solution(mesh):
    in_specs = (
        P(("wide", "seq"), None),
        P(("wide", "seq"), None),
        P(("wide", "seq"), None),
        P(("wide", "seq"), None),
        P(("wide", "seq"), None),
        P(("wide", "seq"), None),
        P(),
        P(),
        P(),
    )
    out_specs = (P(("wide", "seq"), None), P(("seq", "wide"), None))
    return jax.shard_map(body, mesh=mesh, in_specs=in_specs, out_specs=out_specs, check_vma=False)
```

```python
import functools
import math

import jax
import jax.numpy as jnp
from jax import lax
from jax.experimental import pallas as pl
from jax.experimental.pallas import tpu as pltpu
from jax.sharding import PartitionSpec as P

F32 = jnp.float32
BF16 = jnp.bfloat16
EXACT = lax.Precision.HIGHEST
VMEM_LIMIT = 64 * 1024 * 1024
TOP_POWER = 30.0
PRODUCT_BOUND = 30.0
SUMMARY_HEADS = 8
CARRY_HEADS = 32
GRAD_HEADS = 16
PAIR_HEADS = 8
META = 8
SHORT = pl.CostEstimate(flops=1000, bytes_accessed=1000, transcendentals=0)


def mul(a, b):
    return lax.dot_general(a, b, (((1,), (0,)), ((), ())), preferred_element_type=F32)


def mul_nt(a, b):
    return lax.dot_general(a, b, (((1,), (1,)), ((), ())), preferred_element_type=F32)


def mul_exact(a, b, dims=((1,), (0,))):
    return lax.dot_general(a, b, (dims, ((), ())), preferred_element_type=F32, precision=EXACT)


def halves(value):
    top = value.astype(BF16)
    return top, (value - top.astype(F32)).astype(BF16)


def power_for(bound):
    power = jnp.floor(TOP_POWER - jnp.log2(jnp.maximum(bound, 1e-37)))
    return jnp.clip(power, -100.0, 100.0)


def thirds(value):
    top, rest = value.astype(BF16), value
    rest = rest - top.astype(F32)
    middle = rest.astype(BF16)
    return top, middle, (rest - middle.astype(F32)).astype(BF16)


def encode(value):
    square = value * value
    fourth = square * square
    return jnp.where(value < 0, -fourth, fourth).astype(BF16)


def decode(coded):
    coded = coded.astype(F32)
    size = jnp.maximum(jnp.abs(coded), 1e-37)
    inverse = lax.rsqrt(size)
    return coded * inverse * lax.rsqrt(size * inverse)


def head_selector(first_head, heads, lanes, head_width):
    row = lax.broadcasted_iota(jnp.int32, (heads, lanes), 0)
    lane = lax.broadcasted_iota(jnp.int32, (heads, lanes), 1)
    return jnp.where(row == first_head + lane // head_width, 1.0, 0.0).astype(BF16)


def triangle(length, keep):
    row = lax.broadcasted_iota(jnp.int32, (length, length), 0)
    col = lax.broadcasted_iota(jnp.int32, (length, length), 1)
    return jnp.where(keep(row, col), 1.0, 0.0).astype(F32)


def summary_kernel(
    head_width,
    raw_ref,
    bias_ref,
    decay_ref,
    write_ref,
    read_ref,
    x_ref,
    dy_ref,
    message_ref,
    step_ref,
    cum_ref,
    weight_f,
    weight_b,
    facts,
):
    turn = pl.program_id(0)
    heads = raw_ref.shape[1]
    rows, lanes = x_ref.shape
    state = write_ref.shape[0]

    @pl.when(turn == 0)
    def _():
        step = jax.nn.softplus(raw_ref[...].astype(F32) + bias_ref[...])
        rate = -jnp.exp(decay_ref[...])
        cum = mul_exact(triangle(rows, lambda r, c: r >= c), step * rate)
        finish = cum[rows - 1 : rows, :]
        forward = step * jnp.exp(finish - cum)
        backward = jnp.exp(cum)
        power_f = power_for(PRODUCT_BOUND * jnp.sum(forward, axis=0, keepdims=True))
        power_b = power_for(PRODUCT_BOUND * jnp.sum(backward, axis=0, keepdims=True))
        step_ref[...] = step
        cum_ref[...] = cum
        parts = thirds(jnp.maximum(finish, -1e30))
        facts[...] = jnp.concatenate(
            [part.astype(F32) for part in parts]
            + [power_f, power_b, jnp.zeros((META - 5, heads), F32)],
            axis=0,
        ).astype(BF16)
        weight_f[...] = (forward * jnp.exp2(power_f)).T
        weight_b[...] = (backward * jnp.exp2(power_b)).T

    group = lanes // head_width
    pair_lanes = 2 * head_width
    width = message_ref.shape[2]
    near = pl.ds(turn * group, group)
    pick = head_selector(turn * group, heads, lanes, head_width)
    fact = mul(facts[...], pick).astype(BF16)
    lane = lax.broadcasted_iota(jnp.int32, (state, pair_lanes), 1)
    ahead = (x_ref, write_ref[...].astype(F32), weight_f[near, :], 0)
    behind = (dy_ref, read_ref[...].astype(F32), weight_b[near, :], state)
    for pair in range(group // 2):
        span = slice(pair * pair_lanes, (pair + 1) * pair_lanes)
        owner, offset = pair * pair_lanes // width, pair * pair_lanes % width
        here = slice(offset, offset + pair_lanes)
        for tokens_ref, rows_t, weights, start in (ahead, behind):
            scaled = []
            for head in (2 * pair, 2 * pair + 1):
                scaled += halves(rows_t * weights[head : head + 1, :])
            product = mul(jnp.concatenate(scaled, axis=0), tokens_ref[:, span])
            early = product[0:state] + product[state : 2 * state]
            late = product[2 * state : 3 * state] + product[3 * state :]
            total = jnp.where(lane < head_width, early, late)
            message_ref[owner, start : start + state, here] = encode(total)
        message_ref[owner, 2 * state :, here] = fact[:, span]


def scan_kernel(message_ref, *rest):
    answer_ref, powers = rest[-2:]
    blocks, double, lanes = message_ref.shape
    state = (double - META) // 2
    top = 2.0**TOP_POWER

    def one(block, start, power_row, side, running, bound):
        facts = message_ref[block, 2 * state : double, :].astype(F32)
        decay = jnp.exp(facts[0:1] + facts[1:2] + facts[2:3])
        back = jnp.exp2(-facts[power_row : power_row + 1])
        power = power_for(bound)
        powers[side, pl.ds(block, 1), :] = power
        answer_ref[block, start : start + state, :] = encode(running * jnp.exp2(power))
        own = decode(message_ref[block, start : start + state, :]) * back
        return running * decay + own, bound * decay + top * back

    def both(block, carry):
        ahead, ahead_bound, behind, behind_bound = carry
        return one(block, 0, 3, 0, ahead, ahead_bound) + one(
            blocks - 1 - block, state, 4, 1, behind, behind_bound
        )

    zero, none = jnp.zeros((state, lanes), F32), jnp.zeros((1, lanes), F32)
    lax.fori_loop(0, blocks, both, (zero, none, zero, none), unroll=4)
    row = lax.broadcasted_iota(jnp.int32, (blocks, META, lanes), 1)
    ahead, behind = powers[0][:, None, :], powers[1][:, None, :]
    meta = jnp.where(row == 0, ahead, jnp.where(row == 1, behind, 0.0))
    answer_ref[:, 2 * state : double, :] = meta.astype(BF16)


def block_kernel(
    head_width,
    scale,
    first_head,
    waits,
    step_ref,
    cum_ref,
    write_ref,
    read_ref,
    x_ref,
    dy_ref,
    *rest,
):
    inner_ref, own_ref, within_ref, maps_ref = rest[waits : waits + 4]
    read_write, source, cum_rows, pair_sum, out_flow = rest[waits + 4 :]
    turn = pl.program_id(0)
    rows, lanes = x_ref.shape
    half = rows // 2
    heads = step_ref.shape[1]
    group = lanes // head_width

    @pl.when(turn == 0)
    def _():
        read_write[...] = scale * lax.dot_general(
            write_ref[...], read_ref[...], (((0,), (0,)), ((), ())), preferred_element_type=F32
        )
        source[...] = jnp.log(step_ref[...]) - cum_ref[...]
        cum_rows[...] = cum_ref[...].T
        pair_sum[...] = jnp.zeros_like(pair_sum)
        out_flow[...] = jnp.zeros_like(out_flow)
        own_ref[...] = jnp.zeros_like(own_ref)

    first = first_head + turn * group
    near = pltpu.roll(source[...], lax.rem(heads - first, heads), axis=1)
    near_cum = cum_rows[pl.ds(first, group), :]
    row = lax.broadcasted_iota(jnp.int32, (half, half), 0)
    col = lax.broadcasted_iota(jnp.int32, (half, half), 1)
    ahead = col >= row
    lane = lax.broadcasted_iota(jnp.int32, (half, 2 * head_width), 1)
    first_half = lane < head_width
    head_lane = lax.broadcasted_iota(jnp.int32, (half, heads), 1)
    flow_aa = read_write[0:half, 0:half]
    flow_ab = read_write[0:half, half:rows]
    flow_bb = read_write[half:rows, half:rows]
    sum_aa = jnp.zeros((half, half), F32)
    sum_ab = jnp.zeros((half, half), F32)
    sum_bb = jnp.zeros((half, half), F32)
    own_a = jnp.zeros((half, heads), F32)
    own_b = jnp.zeros((half, heads), F32)
    zero = jnp.zeros((half, 2 * head_width), BF16)
    flows = []
    for pair in range(group // 2):
        span = slice(pair * 2 * head_width, (pair + 1) * 2 * head_width)
        x_a, x_b = x_ref[0:half, span], x_ref[half:rows, span]
        dy_a, dy_b = dy_ref[0:half, span], dy_ref[half:rows, span]
        early_a, late_a = jnp.where(first_half, dy_a, zero), jnp.where(first_half, zero, dy_a)
        early_b, late_b = jnp.where(first_half, dy_b, zero), jnp.where(first_half, zero, dy_b)
        stack = jnp.concatenate([early_a, early_b, late_a, late_b], axis=0)
        stack_b = jnp.concatenate([early_b, late_b], axis=0)
        grad_a = mul_nt(x_a, stack)
        grad_b = mul_nt(x_b, stack_b)
        masks_a, masks_b = [], []
        for side in range(2):
            place = pair * 2 + side
            head = first + place
            from_a = near[0:half, place : place + 1]
            from_b = near[half:rows, place : place + 1]
            to_a = near_cum[place : place + 1, 0:half]
            to_b = near_cum[place : place + 1, half:rows]
            fade_aa = jnp.exp(jnp.where(ahead, to_a + from_a, -1e30))
            fade_ab = jnp.exp(to_b + from_a)
            fade_bb = jnp.exp(jnp.where(ahead, to_b + from_b, -1e30))
            weigh_aa = fade_aa * grad_a[:, side * rows : side * rows + half]
            weigh_ab = fade_ab * grad_a[:, side * rows + half : (side + 1) * rows]
            weigh_bb = fade_bb * grad_b[:, side * half : (side + 1) * half]
            sum_aa += weigh_aa
            sum_ab += weigh_ab
            sum_bb += weigh_bb
            masks_a += [(fade_aa * flow_aa).astype(BF16), (fade_ab * flow_ab).astype(BF16)]
            masks_b += [(fade_bb * flow_bb).astype(BF16)]
            pair_aa = weigh_aa * flow_aa
            pair_ab = weigh_ab * flow_ab
            pair_bb = weigh_bb * flow_bb
            flow_out = jnp.sum(pair_aa + pair_ab, axis=1, keepdims=True)
            own_a = jnp.where(head_lane == head, flow_out, own_a)
            flow_out = jnp.sum(pair_bb, axis=1, keepdims=True)
            own_b = jnp.where(head_lane == head, flow_out, own_b)
            flow_in = [
                jnp.sum(pair_aa, axis=0, keepdims=True),
                jnp.sum(pair_ab, axis=0, keepdims=True) + jnp.sum(pair_bb, axis=0, keepdims=True),
            ]
            flows.append(jnp.concatenate(flow_in, axis=1))
        inner_ref[0:half, span] = mul(jnp.concatenate(masks_a, axis=1), stack).astype(BF16)
        inner_ref[half:rows, span] = mul(jnp.concatenate(masks_b, axis=1), stack_b).astype(BF16)
    out_flow[pl.ds(first, group), :] = jnp.concatenate(flows, axis=0)
    pair_sum[0:half, 0:half] += sum_aa
    pair_sum[0:half, half:rows] += sum_ab
    pair_sum[half:rows, half:rows] += sum_bb
    own_ref[0:half, :] += own_a
    own_ref[half:rows, :] += own_b

    @pl.when(turn == pl.num_programs(0) - 1)
    def _():
        net = own_ref[...] - out_flow[...].T
        within_ref[...] = mul_exact(triangle(rows, lambda r, c: r > c), net)
        weighted = scale * pair_sum[...]
        maps_ref[...] = jnp.concatenate(
            [
                mul_exact(weighted, read_ref[...].astype(F32), ((1,), (1,))),
                mul_exact(weighted, write_ref[...].astype(F32), ((0,), (1,))),
            ],
            axis=1,
        )


def spread_heads(weight, first_head, picks, group):
    heads = weight.shape[1]
    near = pltpu.roll(weight, lax.rem(heads - first_head, heads), axis=1)
    top = near.astype(BF16).astype(F32)
    low = pltpu.roll(near - top, group, axis=1)
    lane = lax.broadcasted_iota(jnp.int32, near.shape, 1)
    return mul(jnp.where(lane < group, top, low).astype(BF16), picks)


def spread_picks(group, heads, lanes, head_width):
    row = lax.broadcasted_iota(jnp.int32, (heads, lanes), 0)
    lane = lax.broadcasted_iota(jnp.int32, (heads, lanes), 1)
    match = jnp.where(row < group, row, row - group) == lane // head_width
    return jnp.where(match, 1.0, 0.0).astype(BF16)


def read_answer(answer_ref, state, power_row):
    found = []
    start = power_row * state
    for piece in range(answer_ref.shape[0]):
        facts = answer_ref[piece, 2 * state :, :].astype(F32)
        back = jnp.exp2(-facts[power_row : power_row + 1])
        found.append(decode(answer_ref[piece, start : start + state, :]) * back)
    return jnp.concatenate(found, axis=1)


def carry_kernel(head_width, scale, waits, *refs):
    raw_ref, bias_ref, decay_ref, step_ref, cum_ref, write_ref, read_ref = refs[:7]
    own_ref, within_ref, map_ref, x_ref, dy_ref, answer_ref = refs[7:13]
    table_ref, sums, through, weight_e, weight_s, maps, picks = refs[13 + waits :]
    turn = pl.program_id(0)
    rows, lanes = x_ref.shape
    heads = step_ref.shape[1]
    state = write_ref.shape[0]
    group = lanes // head_width
    pair_lanes = 2 * head_width
    future, past = slice(0, heads), slice(heads, 2 * heads)
    write_sum = slice(2 * heads, 2 * heads + 2 * state)
    read_sum = slice(2 * heads + 2 * state, 2 * heads + 4 * state)

    @pl.when(turn == 0)
    def _():
        cum = cum_ref[...]
        finish = cum[rows - 1 : rows, :]
        weight_e[...] = step_ref[...] * jnp.exp(finish - cum) * scale
        weight_s[...] = jnp.exp(cum) * scale
        write, read = write_ref[...].astype(F32).T, read_ref[...].astype(F32).T
        maps[...] = jnp.concatenate([write, write, read, read], axis=1)
        picks[0:heads, :] = spread_picks(group, heads, lanes, head_width)
        picks[heads:, :] = head_selector(0, heads, lanes, head_width)
        sums[...] = jnp.zeros_like(sums)
        through[...] = jnp.zeros_like(through)

    first_here = turn * group
    pick = picks[heads:, :]
    early = lax.broadcasted_iota(jnp.int32, (state, pair_lanes), 1) < head_width
    none = jnp.zeros((state, pair_lanes), BF16)
    start = read_answer(answer_ref, state, 0)
    end = read_answer(answer_ref, state, 1)

    def products(tokens_ref, states, weight, map_columns):
        spread = spread_heads(weight[...], first_here, picks[0:heads, :], group)
        parts = halves(states)
        total, mapped = 0.0, []
        for pair in range(group // 2):
            span = slice(pair * pair_lanes, (pair + 1) * pair_lanes)
            blocks = [
                jnp.concatenate(
                    [jnp.where(early, part[:, span], none), jnp.where(early, none, part[:, span])],
                    axis=0,
                )
                for part in parts
            ]
            twice = jnp.concatenate([tokens_ref[:, span], tokens_ref[:, span]], axis=1)
            weighted = mul_nt(twice, jnp.concatenate(blocks, axis=1)) * spread[:, span]
            total += weighted
            mapped.append((weighted * map_columns).astype(BF16))
        return total, mapped

    def summed(parts):
        return mul_nt(jnp.concatenate(parts, axis=1), pick)

    def placed(value):
        return pltpu.roll(value, first_here, axis=1)

    total, mapped = products(x_ref, end, weight_e, maps[:, 0 : 2 * state])
    sums[:, write_sum] += total
    sums[:, future] += placed(summed(mapped))

    total, mapped = products(dy_ref, start, weight_s, maps[:, 2 * state : 4 * state])
    sums[:, read_sum] += total
    sums[:, past] += placed(summed(mapped))

    both = jnp.broadcast_to(jnp.sum(start * end, axis=0, keepdims=True), (8, lanes))
    top, low = halves(both)
    through[...] += placed(mul_nt(top, pick) + mul_nt(low, pick))

    @pl.when(turn == pl.num_programs(0) - 1)
    def _():
        rate = -jnp.exp(decay_ref[...])
        step = step_ref[...]
        gate = jax.nn.sigmoid(raw_ref[...].astype(F32) + bias_ref[...])
        finish = cum_ref[rows - 1 : rows, :]
        ahead = sums[:, future]
        decay_grad = (
            within_ref[...]
            + mul_exact(triangle(rows, lambda r, c: r <= c), sums[:, past])
            + mul_exact(triangle(rows, lambda r, c: r > c), ahead)
            + jnp.exp(finish) * scale * through[0:1, :]
        )
        ratio = jnp.where(step > 1e-30, gate / jnp.maximum(step, 1e-30), 1.0)
        raw_grad = (own_ref[...] + ahead) * ratio + rate * decay_grad * gate
        map_sum = sums[:, 2 * heads :]
        write_all = map_sum[:, 0:state] + map_sum[:, state : 2 * state]
        read_all = map_sum[:, 2 * state : 3 * state] + map_sum[:, 3 * state :]
        map_grad = jnp.concatenate([write_all, read_all], axis=1) + map_ref[...]
        table_ref[...] = jnp.concatenate([raw_grad.T, map_grad.T], axis=0).astype(BF16)


def grad_kernel(head_width, scale, first_head, waits, *refs):
    step_ref, cum_ref, write_ref, skip_ref, dy_ref, inner_ref, answer_ref = refs[:7]
    grad_ref, weight_e, maps, picks = refs[7 + waits :]
    turn = pl.program_id(0)
    rows, lanes = dy_ref.shape
    heads = step_ref.shape[1]
    state = write_ref.shape[0]
    group = lanes // head_width

    @pl.when(turn == 0)
    def _():
        cum = cum_ref[...]
        finish = cum[rows - 1 : rows, :]
        weight_e[...] = step_ref[...] * jnp.exp(finish - cum) * scale
        write = write_ref[...].astype(F32).T.astype(BF16)
        maps[...] = jnp.concatenate([write, write], axis=1)
        picks[...] = spread_picks(group, heads, lanes, head_width)

    first_here = first_head + turn * group
    end_parts = jnp.concatenate(halves(read_answer(answer_ref, state, 1)), axis=0)
    skip = jnp.broadcast_to(skip_ref[...], (16, heads))
    skip = spread_heads(skip, first_here, picks[...], group)[0:1]
    carried = mul(maps[...], end_parts) * spread_heads(weight_e[...], first_here, picks[...], group)
    inner = inner_ref[...].astype(F32)
    grad_ref[...] = (inner + skip * dy_ref[...].astype(F32) + carried).astype(BF16)


def deal_kernel(place_ref, layer_ref, after_ref, *out_refs):
    width = out_refs[0].shape[2]
    for turn, out_ref in enumerate(out_refs):
        start = pl.multiple_of((place_ref[0] ^ turn) * width, width)
        out_ref[0, :, :] = layer_ref[:, pl.ds(start, width)]


def product_kernel(turns, wide, place_ref, *refs):
    planes = len(turns)
    table_refs, layer_refs = refs[:wide], refs[wide : 2 * wide]
    out_refs = refs[-3 - planes : -3]
    table_all, layer_all, sems = refs[-3:]
    columns, rows = table_refs[0].shape
    loads = [
        pltpu.make_async_copy(ref, table_all.at[turn], sems.at[planes, turn])
        for turn, ref in enumerate(table_refs)
    ]
    for plane, turn_of in enumerate(turns):
        source = place_ref[1] ^ turn_of
        loads += [
            pltpu.make_async_copy(
                ref.at[source], layer_all.at[plane, pl.ds(turn * rows, rows)], sems.at[plane, turn]
            )
            for turn, ref in enumerate(layer_refs)
        ]
    for load in loads:
        load.start()
    for load in loads[:wide]:
        load.wait()
    table = jnp.concatenate([table_all[turn] for turn in range(wide)], axis=1)
    for plane, out_ref in enumerate(out_refs):
        for load in loads[(plane + 1) * wide : (plane + 2) * wide]:
            load.wait()
        total = mul(table, layer_all[plane])
        most = jnp.max(jnp.abs(total), axis=0, keepdims=True)
        power = power_for(jnp.max(most, axis=1, keepdims=True))
        out_ref[0:columns, :] = encode(total * jnp.exp2(power))
        out_ref[columns:, :] = jnp.broadcast_to(power, out_ref[columns:, :].shape).astype(BF16)


def gather_kernel(factor, planes, *refs):
    part_refs, out_ref = refs[:planes], refs[-1]
    columns = out_ref.shape[1]
    total = jnp.zeros((columns, out_ref.shape[0]), F32)
    for part_ref in part_refs:
        power = part_ref[columns:, :].astype(F32)[0:1]
        total += decode(part_ref[0:columns, :]) * jnp.exp2(-power)
    out_ref[...] = (total * factor).T


def swap(array, axis, turn):
    if turn == 0:
        return array
    count = lax.axis_size(axis)
    return lax.ppermute(array, axis, [(one, one ^ turn) for one in range(count)])


def whole(shape):
    return pl.BlockSpec(shape, lambda i: (0,) * len(shape))


def call(kernel, steps, in_specs, out, scratch, aliases=None):
    return pl.pallas_call(
        kernel,
        grid=(steps,),
        in_specs=in_specs,
        out_specs=[spec for spec, _, _ in out],
        out_shape=[jax.ShapeDtypeStruct(dims, dtype) for _, dims, dtype in out],
        scratch_shapes=[pltpu.VMEM(dims, dtype) for dims, dtype in scratch],
        compiler_params=pltpu.CompilerParams(vmem_limit_bytes=VMEM_LIMIT),
        cost_estimate=SHORT,
        input_output_aliases=aliases or {},
    )


def body(
    layer_input,
    head_inputs,
    output_grad,
    step_raw,
    state_write,
    state_read,
    decay_log,
    step_bias,
    skip_gain,
):
    rows, channels = head_inputs.shape
    heads = step_raw.shape[1]
    head_width = channels // heads
    state = state_write.shape[1]
    model = layer_input.shape[1]
    columns = heads + 2 * state
    axes = ("wide", "seq")
    wide, planes = lax.axis_size("wide"), lax.axis_size("seq")
    blocks = wide * planes
    own_model = model // blocks
    scale = float(rows * blocks * state) ** -0.5
    owner_lanes = channels // blocks
    piece_lanes = max(owner_lanes, 128)
    pieces = channels // piece_lanes
    depth = 2 * state + META
    bias = step_bias[None, :]
    decay = decay_log[None, :]
    skip = skip_gain[None, :]
    write_t, read_t = state_write.T, state_read.T

    summary_lanes = SUMMARY_HEADS * head_width
    carry_lanes = CARRY_HEADS * head_width
    grad_lanes = GRAD_HEADS * head_width

    def tokens(width, first=0):
        return pl.BlockSpec((rows, width), lambda i: (0, first + i))

    def messages(width, first=0):
        return pl.BlockSpec((width // piece_lanes, depth, piece_lanes), lambda i: (first + i, 0, 0))

    head_spec = whole((rows, heads))
    line_spec = whole((1, heads))
    map_spec = whole((state, rows))
    head_out = (head_spec, (rows, heads), F32)

    def exchange(array):
        return lax.all_to_all(array, axes, split_axis=0, concat_axis=0, tiled=True)

    def to_owner(array):
        if owner_lanes < piece_lanes:
            split = array.reshape(pieces, depth, piece_lanes // owner_lanes, owner_lanes)
            array = jnp.moveaxis(split, 2, 1).reshape(blocks, depth, owner_lanes)
        return exchange(array)

    def from_owner(array):
        array = exchange(array)
        if owner_lanes < piece_lanes:
            split = array.reshape(pieces, piece_lanes // owner_lanes, depth, owner_lanes)
            array = jnp.moveaxis(split, 1, 2).reshape(pieces, depth, piece_lanes)
        return array

    with jax.named_scope("summaries"):
        message, step, cum = call(
            functools.partial(summary_kernel, head_width),
            channels // summary_lanes,
            [head_spec, line_spec, line_spec, map_spec, map_spec]
            + [tokens(summary_lanes), tokens(summary_lanes)],
            [
                (messages(summary_lanes), (pieces, depth, piece_lanes), BF16),
                head_out,
                head_out,
            ],
            [((heads, rows), F32), ((heads, rows), F32), ((META, heads), BF16)],
        )(step_raw, bias, decay, write_t, read_t, head_inputs, output_grad)
    place = jnp.stack([lax.axis_index("wide"), lax.axis_index("seq")]).astype(jnp.int32)
    with jax.named_scope("layer"):
        if own_model % 128:
            cut = jnp.transpose(layer_input.reshape(rows, planes, wide, own_model), (2, 1, 0, 3))
            dealt = [
                lax.dynamic_index_in_dim(cut, place[0] ^ turn, 0, False) for turn in range(wide)
            ]
        else:
            dealt = pl.pallas_call(
                deal_kernel,
                grid_spec=pltpu.PrefetchScalarGridSpec(
                    num_scalar_prefetch=1,
                    grid=(planes,),
                    in_specs=[
                        pl.BlockSpec((rows, wide * own_model), lambda i, p: (0, i)),
                        pl.BlockSpec(memory_space=pl.ANY),
                    ],
                    out_specs=[pl.BlockSpec((1, rows, own_model), lambda i, p: (i, 0, 0))] * wide,
                ),
                out_shape=[jax.ShapeDtypeStruct((planes, rows, own_model), BF16)] * wide,
                compiler_params=pltpu.CompilerParams(vmem_limit_bytes=VMEM_LIMIT),
                cost_estimate=SHORT,
            )(place, layer_input, cum)
        layer_parts = [swap(one, "wide", turn) for turn, one in enumerate(dealt)]

    anywhere = pl.BlockSpec(memory_space=pltpu.HBM)
    firsts = [turn for turn in (1, 2, 4, 3, 5) if turn < wide]
    lasts = [layer_parts[turn] for turn in range(1, wide) if turn not in firsts]
    with jax.named_scope("own_block"):
        width = PAIR_HEADS * head_width
        inner, own, within, maps = call(
            functools.partial(block_kernel, head_width, scale, 0, 1),
            channels // width,
            [head_spec, head_spec, map_spec, map_spec, tokens(width), tokens(width), anywhere],
            [
                (tokens(width), (rows, channels), BF16),
                head_out,
                head_out,
                (whole((rows, 2 * state)), (rows, 2 * state), F32),
            ],
            [
                ((rows, rows), F32),
                ((rows, heads), F32),
                ((heads, rows), F32),
                ((rows, rows), F32),
                ((heads, rows), F32),
            ],
        )(step, cum, write_t, read_t, head_inputs, output_grad, dealt[0])
    with jax.named_scope("scan"):
        after = [own] + [layer_parts[turn] for turn in firsts]
        dims = (blocks, depth, owner_lanes)
        (answer,) = call(
            scan_kernel,
            1,
            [whole(dims)] + [anywhere] * len(after),
            [(whole(dims), dims, BF16)],
            [((2, blocks, owner_lanes), F32)],
        )(to_owner(message), *after)
        returned = from_owner(answer)

    with jax.named_scope("carried"):
        (table,) = call(
            functools.partial(carry_kernel, head_width, scale, len(lasts)),
            channels // carry_lanes,
            [head_spec, line_spec, line_spec, head_spec, head_spec, map_spec, map_spec]
            + [head_spec, head_spec, whole((rows, 2 * state))]
            + [tokens(carry_lanes), tokens(carry_lanes), messages(carry_lanes)]
            + [anywhere] * len(lasts),
            [(whole((columns, rows)), (columns, rows), BF16)],
            [
                ((rows, 2 * heads + 4 * state), F32),
                ((8, heads), F32),
                ((rows, heads), F32),
                ((rows, heads), F32),
                ((rows, 4 * state), F32),
                ((2 * heads, carry_lanes), BF16),
            ],
        )(
            *(step_raw, bias, decay, step, cum, write_t, read_t, own, within, maps),
            *(head_inputs, output_grad, returned, *lasts),
        )

    def grad_half(half, grad):
        steps = channels // grad_lanes // 2
        first = half * steps
        in_specs = [head_spec, head_spec, map_spec, line_spec]
        in_specs += [tokens(grad_lanes, first), tokens(grad_lanes, first)]
        in_specs += [messages(grad_lanes, first)]
        in_specs += [anywhere] * len(grad)
        (grad,) = call(
            functools.partial(grad_kernel, head_width, scale, first * GRAD_HEADS, len(grad)),
            steps,
            in_specs,
            [(tokens(grad_lanes, first), (rows, channels), BF16)],
            [((rows, heads), F32), ((rows, 2 * state), BF16), ((heads, grad_lanes), BF16)],
            {len(in_specs) - 1: 0} if half else {},
        )(step, cum, write_t, skip, output_grad, inner, returned, *grad)
        return grad

    with jax.named_scope("grad_x"):
        grad_part = grad_half(0, [table])
        grad_x = grad_half(1, [grad_part])

    with jax.named_scope("projection"):
        tables = [swap(table, "wide", turn) for turn in range(wide)]
        coded = (columns + META, own_model)

        def product(turns, after):
            count = len(turns)
            return pl.pallas_call(
                functools.partial(product_kernel, turns, wide),
                in_specs=[pl.BlockSpec(memory_space=pltpu.SMEM)] + [anywhere] * (2 * wide + 1),
                out_specs=[pl.BlockSpec(memory_space=pltpu.VMEM)] * count,
                out_shape=[jax.ShapeDtypeStruct(coded, BF16)] * count,
                scratch_shapes=[
                    pltpu.VMEM((wide, columns, rows), BF16),
                    pltpu.VMEM((count, wide * rows, own_model), BF16),
                    pltpu.SemaphoreType.DMA((count + 1, wide)),
                ],
                compiler_params=pltpu.CompilerParams(vmem_limit_bytes=VMEM_LIMIT),
                cost_estimate=SHORT,
            )(place, *tables, *layer_parts, after)

        far = tuple(range(planes // 2, planes))
        near = tuple(range(planes // 2))
        far_parts = product(far, grad_part)
        sums = [swap(one, "seq", turn) for turn, one in zip(far, far_parts)]
        near_parts = product(near, far_parts[0])
        sums += [swap(one, "seq", turn) for turn, one in zip(near, near_parts)]
        (weight_grad,) = call(
            functools.partial(gather_kernel, 1.0 / math.sqrt(rows * blocks), planes),
            1,
            [whole(coded)] * planes + [anywhere],
            [(whole((own_model, columns)), (own_model, columns), F32)],
            [],
        )(*sums, grad_x)
    return grad_x, weight_grad


def solution(mesh):
    in_specs = (
        P(("wide", "seq"), None),
        P(("wide", "seq"), None),
        P(("wide", "seq"), None),
        P(("wide", "seq"), None),
        P(("wide", "seq"), None),
        P(("wide", "seq"), None),
        P(),
        P(),
        P(),
    )
    out_specs = (P(("wide", "seq"), None), P(("seq", "wide"), None))
    return jax.shard_map(body, mesh=mesh, in_specs=in_specs, out_specs=out_specs, check_vma=False)
```

```python
import functools
import math

import jax
import jax.numpy as jnp
from jax import lax
from jax.experimental import pallas as pl
from jax.experimental.pallas import tpu as pltpu
from jax.sharding import PartitionSpec as P

F32 = jnp.float32
BF16 = jnp.bfloat16
EXACT = lax.Precision.HIGHEST
VMEM_LIMIT = 64 * 1024 * 1024
TOP_POWER = 30.0
PRODUCT_BOUND = 30.0
SUMMARY_HEADS = 32
CARRY_HEADS = 32
GRAD_HEADS = 32
PAIR_HEADS = 8
META = 8
SHORT = pl.CostEstimate(flops=1000, bytes_accessed=1000, transcendentals=0)


def mul(a, b):
    return lax.dot_general(a, b, (((1,), (0,)), ((), ())), preferred_element_type=F32)


def mul_nt(a, b):
    return lax.dot_general(a, b, (((1,), (1,)), ((), ())), preferred_element_type=F32)


def mul_exact(a, b, dims=((1,), (0,))):
    return lax.dot_general(a, b, (dims, ((), ())), preferred_element_type=F32, precision=EXACT)


def halves(value):
    top = value.astype(BF16)
    return top, (value - top.astype(F32)).astype(BF16)


def power_for(bound):
    power = jnp.floor(TOP_POWER - jnp.log2(jnp.maximum(bound, 1e-37)))
    return jnp.clip(power, -100.0, 100.0)


def thirds(value):
    top, rest = value.astype(BF16), value
    rest = rest - top.astype(F32)
    middle = rest.astype(BF16)
    return top, middle, (rest - middle.astype(F32)).astype(BF16)


def encode(value):
    square = value * value
    fourth = square * square
    return jnp.where(value < 0, -fourth, fourth).astype(BF16)


def decode(coded):
    coded = coded.astype(F32)
    size = jnp.maximum(jnp.abs(coded), 1e-37)
    inverse = lax.rsqrt(size)
    return coded * inverse * lax.rsqrt(size * inverse)


def head_selector(first_head, heads, lanes, head_width):
    row = lax.broadcasted_iota(jnp.int32, (heads, lanes), 0)
    lane = lax.broadcasted_iota(jnp.int32, (heads, lanes), 1)
    return jnp.where(row == first_head + lane // head_width, 1.0, 0.0).astype(BF16)


def triangle(length, keep):
    row = lax.broadcasted_iota(jnp.int32, (length, length), 0)
    col = lax.broadcasted_iota(jnp.int32, (length, length), 1)
    return jnp.where(keep(row, col), 1.0, 0.0).astype(F32)


def summary_kernel(
    head_width,
    raw_ref,
    bias_ref,
    decay_ref,
    write_ref,
    read_ref,
    x_ref,
    dy_ref,
    message_ref,
    step_ref,
    cum_ref,
    weight_f,
    weight_b,
    facts,
):
    turn = pl.program_id(0)
    heads = raw_ref.shape[1]
    rows, lanes = x_ref.shape
    state = write_ref.shape[0]

    @pl.when(turn == 0)
    def _():
        step = jax.nn.softplus(raw_ref[...].astype(F32) + bias_ref[...])
        rate = -jnp.exp(decay_ref[...])
        cum = mul_exact(triangle(rows, lambda r, c: r >= c), step * rate)
        finish = cum[rows - 1 : rows, :]
        forward = step * jnp.exp(finish - cum)
        backward = jnp.exp(cum)
        power_f = power_for(PRODUCT_BOUND * jnp.sum(forward, axis=0, keepdims=True))
        power_b = power_for(PRODUCT_BOUND * jnp.sum(backward, axis=0, keepdims=True))
        step_ref[...] = step
        cum_ref[...] = cum
        parts = thirds(jnp.maximum(finish, -1e30))
        facts[...] = jnp.concatenate(
            [part.astype(F32) for part in parts]
            + [power_f, power_b, jnp.zeros((META - 5, heads), F32)],
            axis=0,
        ).astype(BF16)
        weight_f[...] = (forward * jnp.exp2(power_f)).T
        weight_b[...] = (backward * jnp.exp2(power_b)).T

    group = lanes // head_width
    pair_lanes = 2 * head_width
    width = message_ref.shape[2]
    near = pl.ds(turn * group, group)
    pick = head_selector(turn * group, heads, lanes, head_width)
    fact = mul(facts[...], pick).astype(BF16)
    lane = lax.broadcasted_iota(jnp.int32, (state, pair_lanes), 1)
    ahead = (x_ref, write_ref[...].astype(F32), weight_f[near, :], 0)
    behind = (dy_ref, read_ref[...].astype(F32), weight_b[near, :], state)
    for pair in range(group // 2):
        span = slice(pair * pair_lanes, (pair + 1) * pair_lanes)
        owner, offset = pair * pair_lanes // width, pair * pair_lanes % width
        here = slice(offset, offset + pair_lanes)
        for tokens_ref, rows_t, weights, start in (ahead, behind):
            scaled = []
            for head in (2 * pair, 2 * pair + 1):
                scaled += halves(rows_t * weights[head : head + 1, :])
            product = mul(jnp.concatenate(scaled, axis=0), tokens_ref[:, span])
            early = product[0:state] + product[state : 2 * state]
            late = product[2 * state : 3 * state] + product[3 * state :]
            total = jnp.where(lane < head_width, early, late)
            message_ref[owner, start : start + state, here] = encode(total)
        message_ref[owner, 2 * state :, here] = fact[:, span]


def scan_kernel(message_ref, *rest):
    answer_ref, powers = rest[-2:]
    blocks, double, lanes = message_ref.shape
    state = (double - META) // 2
    top = 2.0**TOP_POWER

    def one(block, start, power_row, side, running, bound):
        facts = message_ref[block, 2 * state : double, :].astype(F32)
        decay = jnp.exp(facts[0:1] + facts[1:2] + facts[2:3])
        back = jnp.exp2(-facts[power_row : power_row + 1])
        power = power_for(bound)
        powers[side, pl.ds(block, 1), :] = power
        answer_ref[block, start : start + state, :] = encode(running * jnp.exp2(power))
        own = decode(message_ref[block, start : start + state, :]) * back
        return running * decay + own, bound * decay + top * back

    def both(block, carry):
        ahead, ahead_bound, behind, behind_bound = carry
        return one(block, 0, 3, 0, ahead, ahead_bound) + one(
            blocks - 1 - block, state, 4, 1, behind, behind_bound
        )

    zero, none = jnp.zeros((state, lanes), F32), jnp.zeros((1, lanes), F32)
    lax.fori_loop(0, blocks, both, (zero, none, zero, none), unroll=4)
    row = lax.broadcasted_iota(jnp.int32, (blocks, META, lanes), 1)
    ahead, behind = powers[0][:, None, :], powers[1][:, None, :]
    meta = jnp.where(row == 0, ahead, jnp.where(row == 1, behind, 0.0))
    answer_ref[:, 2 * state : double, :] = meta.astype(BF16)


def block_kernel(
    head_width,
    scale,
    first_head,
    waits,
    step_ref,
    cum_ref,
    write_ref,
    read_ref,
    x_ref,
    dy_ref,
    *rest,
):
    inner_ref, own_ref, within_ref, maps_ref = rest[waits : waits + 4]
    read_write, source, cum_rows, pair_sum, out_flow = rest[waits + 4 :]
    turn = pl.program_id(0)
    rows, lanes = x_ref.shape
    half = rows // 2
    heads = step_ref.shape[1]
    group = lanes // head_width

    @pl.when(turn == 0)
    def _():
        read_write[...] = scale * lax.dot_general(
            write_ref[...], read_ref[...], (((0,), (0,)), ((), ())), preferred_element_type=F32
        )
        source[...] = jnp.log(step_ref[...]) - cum_ref[...]
        cum_rows[...] = cum_ref[...].T
        pair_sum[...] = jnp.zeros_like(pair_sum)
        out_flow[...] = jnp.zeros_like(out_flow)
        own_ref[...] = jnp.zeros_like(own_ref)

    first = first_head + turn * group
    near = pltpu.roll(source[...], lax.rem(heads - first, heads), axis=1)
    near_cum = cum_rows[pl.ds(first, group), :]
    row = lax.broadcasted_iota(jnp.int32, (half, half), 0)
    col = lax.broadcasted_iota(jnp.int32, (half, half), 1)
    ahead = col >= row
    lane = lax.broadcasted_iota(jnp.int32, (half, 2 * head_width), 1)
    first_half = lane < head_width
    head_lane = lax.broadcasted_iota(jnp.int32, (half, heads), 1)
    flow_aa = read_write[0:half, 0:half]
    flow_ab = read_write[0:half, half:rows]
    flow_bb = read_write[half:rows, half:rows]
    sum_aa = jnp.zeros((half, half), F32)
    sum_ab = jnp.zeros((half, half), F32)
    sum_bb = jnp.zeros((half, half), F32)
    own_a = jnp.zeros((half, heads), F32)
    own_b = jnp.zeros((half, heads), F32)
    zero = jnp.zeros((half, 2 * head_width), BF16)
    flows = []
    for pair in range(group // 2):
        span = slice(pair * 2 * head_width, (pair + 1) * 2 * head_width)
        x_a, x_b = x_ref[0:half, span], x_ref[half:rows, span]
        dy_a, dy_b = dy_ref[0:half, span], dy_ref[half:rows, span]
        early_a, late_a = jnp.where(first_half, dy_a, zero), jnp.where(first_half, zero, dy_a)
        early_b, late_b = jnp.where(first_half, dy_b, zero), jnp.where(first_half, zero, dy_b)
        stack = jnp.concatenate([early_a, early_b, late_a, late_b], axis=0)
        stack_b = jnp.concatenate([early_b, late_b], axis=0)
        grad_a = mul_nt(x_a, stack)
        grad_b = mul_nt(x_b, stack_b)
        masks_a, masks_b = [], []
        for side in range(2):
            place = pair * 2 + side
            head = first + place
            from_a = near[0:half, place : place + 1]
            from_b = near[half:rows, place : place + 1]
            to_a = near_cum[place : place + 1, 0:half]
            to_b = near_cum[place : place + 1, half:rows]
            fade_aa = jnp.exp(jnp.where(ahead, to_a + from_a, -1e30))
            fade_ab = jnp.exp(to_b + from_a)
            fade_bb = jnp.exp(jnp.where(ahead, to_b + from_b, -1e30))
            weigh_aa = fade_aa * grad_a[:, side * rows : side * rows + half]
            weigh_ab = fade_ab * grad_a[:, side * rows + half : (side + 1) * rows]
            weigh_bb = fade_bb * grad_b[:, side * half : (side + 1) * half]
            sum_aa += weigh_aa
            sum_ab += weigh_ab
            sum_bb += weigh_bb
            masks_a += [(fade_aa * flow_aa).astype(BF16), (fade_ab * flow_ab).astype(BF16)]
            masks_b += [(fade_bb * flow_bb).astype(BF16)]
            pair_aa = weigh_aa * flow_aa
            pair_ab = weigh_ab * flow_ab
            pair_bb = weigh_bb * flow_bb
            flow_out = jnp.sum(pair_aa + pair_ab, axis=1, keepdims=True)
            own_a = jnp.where(head_lane == head, flow_out, own_a)
            flow_out = jnp.sum(pair_bb, axis=1, keepdims=True)
            own_b = jnp.where(head_lane == head, flow_out, own_b)
            flow_in = [
                jnp.sum(pair_aa, axis=0, keepdims=True),
                jnp.sum(pair_ab, axis=0, keepdims=True) + jnp.sum(pair_bb, axis=0, keepdims=True),
            ]
            flows.append(jnp.concatenate(flow_in, axis=1))
        inner_ref[0:half, span] = mul(jnp.concatenate(masks_a, axis=1), stack).astype(BF16)
        inner_ref[half:rows, span] = mul(jnp.concatenate(masks_b, axis=1), stack_b).astype(BF16)
    out_flow[pl.ds(first, group), :] = jnp.concatenate(flows, axis=0)
    pair_sum[0:half, 0:half] += sum_aa
    pair_sum[0:half, half:rows] += sum_ab
    pair_sum[half:rows, half:rows] += sum_bb
    own_ref[0:half, :] += own_a
    own_ref[half:rows, :] += own_b

    @pl.when(turn == pl.num_programs(0) - 1)
    def _():
        net = own_ref[...] - out_flow[...].T
        within_ref[...] = mul_exact(triangle(rows, lambda r, c: r > c), net)
        weighted = scale * pair_sum[...]
        maps_ref[...] = jnp.concatenate(
            [
                mul_exact(weighted, read_ref[...].astype(F32), ((1,), (1,))),
                mul_exact(weighted, write_ref[...].astype(F32), ((0,), (1,))),
            ],
            axis=1,
        )


def spread_heads(weight, first_head, picks, group):
    heads = weight.shape[1]
    near = pltpu.roll(weight, lax.rem(heads - first_head, heads), axis=1)
    top = near.astype(BF16).astype(F32)
    low = pltpu.roll(near - top, group, axis=1)
    lane = lax.broadcasted_iota(jnp.int32, near.shape, 1)
    return mul(jnp.where(lane < group, top, low).astype(BF16), picks)


def spread_picks(group, heads, lanes, head_width):
    row = lax.broadcasted_iota(jnp.int32, (heads, lanes), 0)
    lane = lax.broadcasted_iota(jnp.int32, (heads, lanes), 1)
    match = jnp.where(row < group, row, row - group) == lane // head_width
    return jnp.where(match, 1.0, 0.0).astype(BF16)


def read_answer(answer_ref, state, power_row):
    found = []
    start = power_row * state
    for piece in range(answer_ref.shape[0]):
        facts = answer_ref[piece, 2 * state :, :].astype(F32)
        back = jnp.exp2(-facts[power_row : power_row + 1])
        found.append(decode(answer_ref[piece, start : start + state, :]) * back)
    return jnp.concatenate(found, axis=1)


def carry_kernel(head_width, scale, waits, *refs):
    raw_ref, bias_ref, decay_ref, step_ref, cum_ref, write_ref, read_ref = refs[:7]
    own_ref, within_ref, map_ref, x_ref, dy_ref, answer_ref = refs[7:13]
    table_ref, sums, through, weight_e, weight_s, maps, picks = refs[13 + waits :]
    turn = pl.program_id(0)
    rows, lanes = x_ref.shape
    heads = step_ref.shape[1]
    state = write_ref.shape[0]
    group = lanes // head_width
    pair_lanes = 2 * head_width
    future, past = slice(0, heads), slice(heads, 2 * heads)
    write_sum = slice(2 * heads, 2 * heads + 2 * state)
    read_sum = slice(2 * heads + 2 * state, 2 * heads + 4 * state)

    @pl.when(turn == 0)
    def _():
        cum = cum_ref[...]
        finish = cum[rows - 1 : rows, :]
        weight_e[...] = step_ref[...] * jnp.exp(finish - cum) * scale
        weight_s[...] = jnp.exp(cum) * scale
        write, read = write_ref[...].astype(F32).T, read_ref[...].astype(F32).T
        maps[...] = jnp.concatenate([write, write, read, read], axis=1)
        picks[0:heads, :] = spread_picks(group, heads, lanes, head_width)
        picks[heads:, :] = head_selector(0, heads, lanes, head_width)
        sums[...] = jnp.zeros_like(sums)
        through[...] = jnp.zeros_like(through)

    first_here = turn * group
    pick = picks[heads:, :]
    early = lax.broadcasted_iota(jnp.int32, (state, pair_lanes), 1) < head_width
    none = jnp.zeros((state, pair_lanes), BF16)
    start = read_answer(answer_ref, state, 0)
    end = read_answer(answer_ref, state, 1)

    def products(tokens_ref, states, weight, map_columns):
        spread = spread_heads(weight[...], first_here, picks[0:heads, :], group)
        parts = halves(states)
        total, mapped = 0.0, []
        for pair in range(group // 2):
            span = slice(pair * pair_lanes, (pair + 1) * pair_lanes)
            blocks = [
                jnp.concatenate(
                    [jnp.where(early, part[:, span], none), jnp.where(early, none, part[:, span])],
                    axis=0,
                )
                for part in parts
            ]
            twice = jnp.concatenate([tokens_ref[:, span], tokens_ref[:, span]], axis=1)
            weighted = mul_nt(twice, jnp.concatenate(blocks, axis=1)) * spread[:, span]
            total += weighted
            mapped.append((weighted * map_columns).astype(BF16))
        return total, mapped

    def summed(parts):
        return mul_nt(jnp.concatenate(parts, axis=1), pick)

    def placed(value):
        return pltpu.roll(value, first_here, axis=1)

    total, mapped = products(x_ref, end, weight_e, maps[:, 0 : 2 * state])
    sums[:, write_sum] += total
    sums[:, future] += placed(summed(mapped))

    total, mapped = products(dy_ref, start, weight_s, maps[:, 2 * state : 4 * state])
    sums[:, read_sum] += total
    sums[:, past] += placed(summed(mapped))

    both = jnp.broadcast_to(jnp.sum(start * end, axis=0, keepdims=True), (8, lanes))
    top, low = halves(both)
    through[...] += placed(mul_nt(top, pick) + mul_nt(low, pick))

    @pl.when(turn == pl.num_programs(0) - 1)
    def _():
        rate = -jnp.exp(decay_ref[...])
        step = step_ref[...]
        gate = jax.nn.sigmoid(raw_ref[...].astype(F32) + bias_ref[...])
        finish = cum_ref[rows - 1 : rows, :]
        ahead = sums[:, future]
        decay_grad = (
            within_ref[...]
            + mul_exact(triangle(rows, lambda r, c: r <= c), sums[:, past])
            + mul_exact(triangle(rows, lambda r, c: r > c), ahead)
            + jnp.exp(finish) * scale * through[0:1, :]
        )
        ratio = jnp.where(step > 1e-30, gate / jnp.maximum(step, 1e-30), 1.0)
        raw_grad = (own_ref[...] + ahead) * ratio + rate * decay_grad * gate
        map_sum = sums[:, 2 * heads :]
        write_all = map_sum[:, 0:state] + map_sum[:, state : 2 * state]
        read_all = map_sum[:, 2 * state : 3 * state] + map_sum[:, 3 * state :]
        map_grad = jnp.concatenate([write_all, read_all], axis=1) + map_ref[...]
        table_ref[...] = jnp.concatenate([raw_grad.T, map_grad.T], axis=0).astype(BF16)


def grad_kernel(head_width, scale, first_head, waits, *refs):
    step_ref, cum_ref, write_ref, skip_ref, dy_ref, inner_ref, answer_ref = refs[:7]
    grad_ref, weight_e, maps, picks = refs[7 + waits :]
    turn = pl.program_id(0)
    rows, lanes = dy_ref.shape
    heads = step_ref.shape[1]
    state = write_ref.shape[0]
    group = lanes // head_width

    @pl.when(turn == 0)
    def _():
        cum = cum_ref[...]
        finish = cum[rows - 1 : rows, :]
        weight_e[...] = step_ref[...] * jnp.exp(finish - cum) * scale
        write = write_ref[...].astype(F32).T.astype(BF16)
        maps[...] = jnp.concatenate([write, write], axis=1)
        picks[...] = spread_picks(group, heads, lanes, head_width)

    first_here = first_head + turn * group
    end_parts = jnp.concatenate(halves(read_answer(answer_ref, state, 1)), axis=0)
    skip = jnp.broadcast_to(skip_ref[...], (16, heads))
    skip = spread_heads(skip, first_here, picks[...], group)[0:1]
    carried = mul(maps[...], end_parts) * spread_heads(weight_e[...], first_here, picks[...], group)
    inner = inner_ref[...].astype(F32)
    grad_ref[...] = (inner + skip * dy_ref[...].astype(F32) + carried).astype(BF16)


def deal_kernel(place_ref, layer_ref, after_ref, *out_refs):
    width = out_refs[0].shape[2]
    for turn, out_ref in enumerate(out_refs):
        start = pl.multiple_of((place_ref[0] ^ turn) * width, width)
        out_ref[0, :, :] = layer_ref[:, pl.ds(start, width)]


def product_kernel(planes, wide, place_ref, *refs):
    table_refs, layer_refs = refs[:wide], refs[wide : 2 * wide]
    out_refs = refs[-3 - planes : -3]
    table_all, layer_all, sems = refs[-3:]
    columns, rows = table_refs[0].shape
    loads = [
        pltpu.make_async_copy(ref, table_all.at[turn], sems.at[planes, turn])
        for turn, ref in enumerate(table_refs)
    ]
    for plane in range(planes):
        source = place_ref[1] ^ plane
        loads += [
            pltpu.make_async_copy(
                ref.at[source], layer_all.at[plane, pl.ds(turn * rows, rows)], sems.at[plane, turn]
            )
            for turn, ref in enumerate(layer_refs)
        ]
    for load in loads:
        load.start()
    for load in loads[:wide]:
        load.wait()
    table = jnp.concatenate([table_all[turn] for turn in range(wide)], axis=1)
    for plane, out_ref in enumerate(out_refs):
        for load in loads[(plane + 1) * wide : (plane + 2) * wide]:
            load.wait()
        total = mul(table, layer_all[plane])
        most = jnp.max(jnp.abs(total), axis=0, keepdims=True)
        power = power_for(jnp.max(most, axis=1, keepdims=True))
        out_ref[0:columns, :] = encode(total * jnp.exp2(power))
        out_ref[columns:, :] = jnp.broadcast_to(power, out_ref[columns:, :].shape).astype(BF16)


def gather_kernel(factor, planes, *refs):
    part_refs, out_ref = refs[:planes], refs[-1]
    columns = out_ref.shape[1]
    total = jnp.zeros((columns, out_ref.shape[0]), F32)
    for part_ref in part_refs:
        power = part_ref[columns:, :].astype(F32)[0:1]
        total += decode(part_ref[0:columns, :]) * jnp.exp2(-power)
    out_ref[...] = (total * factor).T


def swap(array, axis, turn):
    if turn == 0:
        return array
    count = lax.axis_size(axis)
    return lax.ppermute(array, axis, [(one, one ^ turn) for one in range(count)])


def whole(shape):
    return pl.BlockSpec(shape, lambda i: (0,) * len(shape))


def call(kernel, steps, in_specs, out, scratch, aliases=None):
    return pl.pallas_call(
        kernel,
        grid=(steps,),
        in_specs=in_specs,
        out_specs=[spec for spec, _, _ in out],
        out_shape=[jax.ShapeDtypeStruct(dims, dtype) for _, dims, dtype in out],
        scratch_shapes=[pltpu.VMEM(dims, dtype) for dims, dtype in scratch],
        compiler_params=pltpu.CompilerParams(vmem_limit_bytes=VMEM_LIMIT),
        cost_estimate=SHORT,
        input_output_aliases=aliases or {},
    )


def body(
    layer_input,
    head_inputs,
    output_grad,
    step_raw,
    state_write,
    state_read,
    decay_log,
    step_bias,
    skip_gain,
):
    rows, channels = head_inputs.shape
    heads = step_raw.shape[1]
    head_width = channels // heads
    state = state_write.shape[1]
    model = layer_input.shape[1]
    columns = heads + 2 * state
    axes = ("wide", "seq")
    wide, planes = lax.axis_size("wide"), lax.axis_size("seq")
    blocks = wide * planes
    own_model = model // blocks
    scale = float(rows * blocks * state) ** -0.5
    owner_lanes = channels // blocks
    piece_lanes = max(owner_lanes, 128)
    pieces = channels // piece_lanes
    depth = 2 * state + META
    bias = step_bias[None, :]
    decay = decay_log[None, :]
    skip = skip_gain[None, :]
    write_t, read_t = state_write.T, state_read.T

    summary_lanes = SUMMARY_HEADS * head_width
    carry_lanes = CARRY_HEADS * head_width
    grad_lanes = GRAD_HEADS * head_width

    def tokens(width, first=0):
        return pl.BlockSpec((rows, width), lambda i: (0, first + i))

    def messages(width, first=0):
        return pl.BlockSpec((width // piece_lanes, depth, piece_lanes), lambda i: (first + i, 0, 0))

    head_spec = whole((rows, heads))
    line_spec = whole((1, heads))
    map_spec = whole((state, rows))
    head_out = (head_spec, (rows, heads), F32)

    def exchange(array):
        return lax.all_to_all(array, axes, split_axis=0, concat_axis=0, tiled=True)

    def to_owner(array):
        if owner_lanes < piece_lanes:
            split = array.reshape(pieces, depth, piece_lanes // owner_lanes, owner_lanes)
            array = jnp.moveaxis(split, 2, 1).reshape(blocks, depth, owner_lanes)
        return exchange(array)

    def from_owner(array):
        array = exchange(array)
        if owner_lanes < piece_lanes:
            split = array.reshape(pieces, piece_lanes // owner_lanes, depth, owner_lanes)
            array = jnp.moveaxis(split, 1, 2).reshape(pieces, depth, piece_lanes)
        return array

    with jax.named_scope("summaries"):
        message, step, cum = call(
            functools.partial(summary_kernel, head_width),
            channels // summary_lanes,
            [head_spec, line_spec, line_spec, map_spec, map_spec]
            + [tokens(summary_lanes), tokens(summary_lanes)],
            [
                (messages(summary_lanes), (pieces, depth, piece_lanes), BF16),
                head_out,
                head_out,
            ],
            [((heads, rows), F32), ((heads, rows), F32), ((META, heads), BF16)],
        )(step_raw, bias, decay, write_t, read_t, head_inputs, output_grad)
    place = jnp.stack([lax.axis_index("wide"), lax.axis_index("seq")]).astype(jnp.int32)
    with jax.named_scope("layer"):
        if own_model % 128:
            cut = jnp.transpose(layer_input.reshape(rows, planes, wide, own_model), (2, 1, 0, 3))
            dealt = [
                lax.dynamic_index_in_dim(cut, place[0] ^ turn, 0, False) for turn in range(wide)
            ]
        else:
            dealt = pl.pallas_call(
                deal_kernel,
                grid_spec=pltpu.PrefetchScalarGridSpec(
                    num_scalar_prefetch=1,
                    grid=(planes,),
                    in_specs=[
                        pl.BlockSpec((rows, wide * own_model), lambda i, p: (0, i)),
                        pl.BlockSpec(memory_space=pl.ANY),
                    ],
                    out_specs=[pl.BlockSpec((1, rows, own_model), lambda i, p: (i, 0, 0))] * wide,
                ),
                out_shape=[jax.ShapeDtypeStruct((planes, rows, own_model), BF16)] * wide,
                compiler_params=pltpu.CompilerParams(vmem_limit_bytes=VMEM_LIMIT),
                cost_estimate=SHORT,
            )(place, layer_input, cum)
        layer_parts = [swap(one, "wide", turn) for turn, one in enumerate(dealt)]

    anywhere = pl.BlockSpec(memory_space=pltpu.HBM)
    firsts = [turn for turn in (1, 2, 4, 3, 5) if turn < wide]
    lasts = [layer_parts[turn] for turn in range(1, wide) if turn not in firsts]
    with jax.named_scope("own_block"):
        width = PAIR_HEADS * head_width
        inner, own, within, maps = call(
            functools.partial(block_kernel, head_width, scale, 0, 1),
            channels // width,
            [head_spec, head_spec, map_spec, map_spec, tokens(width), tokens(width), anywhere],
            [
                (tokens(width), (rows, channels), BF16),
                head_out,
                head_out,
                (whole((rows, 2 * state)), (rows, 2 * state), F32),
            ],
            [
                ((rows, rows), F32),
                ((rows, heads), F32),
                ((heads, rows), F32),
                ((rows, rows), F32),
                ((heads, rows), F32),
            ],
        )(step, cum, write_t, read_t, head_inputs, output_grad, dealt[0])
    with jax.named_scope("scan"):
        after = [own] + [layer_parts[turn] for turn in firsts]
        scan_lanes = min(owner_lanes, 128)
        scan_spec = pl.BlockSpec((blocks, depth, scan_lanes), lambda i: (0, 0, i))
        (answer,) = call(
            scan_kernel,
            owner_lanes // scan_lanes,
            [scan_spec] + [anywhere] * len(after),
            [(scan_spec, (blocks, depth, owner_lanes), BF16)],
            [((2, blocks, scan_lanes), F32)],
        )(to_owner(message), *after)
        returned = from_owner(answer)

    with jax.named_scope("carried"):
        (table,) = call(
            functools.partial(carry_kernel, head_width, scale, len(lasts)),
            channels // carry_lanes,
            [head_spec, line_spec, line_spec, head_spec, head_spec, map_spec, map_spec]
            + [head_spec, head_spec, whole((rows, 2 * state))]
            + [tokens(carry_lanes), tokens(carry_lanes), messages(carry_lanes)]
            + [anywhere] * len(lasts),
            [(whole((columns, rows)), (columns, rows), BF16)],
            [
                ((rows, 2 * heads + 4 * state), F32),
                ((8, heads), F32),
                ((rows, heads), F32),
                ((rows, heads), F32),
                ((rows, 4 * state), F32),
                ((2 * heads, carry_lanes), BF16),
            ],
        )(
            *(step_raw, bias, decay, step, cum, write_t, read_t, own, within, maps),
            *(head_inputs, output_grad, returned, *lasts),
        )

    def grad_half(half, grad):
        steps = channels // grad_lanes // 2
        first = half * steps
        in_specs = [head_spec, head_spec, map_spec, line_spec]
        in_specs += [tokens(grad_lanes, first), tokens(grad_lanes, first)]
        in_specs += [messages(grad_lanes, first)]
        in_specs += [anywhere] * len(grad)
        (grad,) = call(
            functools.partial(grad_kernel, head_width, scale, first * GRAD_HEADS, len(grad)),
            steps,
            in_specs,
            [(tokens(grad_lanes, first), (rows, channels), BF16)],
            [((rows, heads), F32), ((rows, 2 * state), BF16), ((heads, grad_lanes), BF16)],
            {len(in_specs) - 1: 0} if half else {},
        )(step, cum, write_t, skip, output_grad, inner, returned, *grad)
        return grad

    with jax.named_scope("grad_x"):
        grad_part = grad_half(0, [table])
        grad_x = grad_half(1, [grad_part])

    with jax.named_scope("projection"):
        tables = [swap(table, "wide", turn) for turn in range(wide)]
        coded = (columns + META, own_model)
        products = pl.pallas_call(
            functools.partial(product_kernel, planes, wide),
            in_specs=[pl.BlockSpec(memory_space=pltpu.SMEM)] + [anywhere] * (2 * wide + 1),
            out_specs=[pl.BlockSpec(memory_space=pltpu.VMEM)] * planes,
            out_shape=[jax.ShapeDtypeStruct(coded, BF16)] * planes,
            scratch_shapes=[
                pltpu.VMEM((wide, columns, rows), BF16),
                pltpu.VMEM((planes, wide * rows, own_model), BF16),
                pltpu.SemaphoreType.DMA((planes + 1, wide)),
            ],
            compiler_params=pltpu.CompilerParams(vmem_limit_bytes=VMEM_LIMIT),
            cost_estimate=SHORT,
        )(place, *tables, *layer_parts, grad_part)
        sums = [swap(one, "seq", turn) for turn, one in enumerate(products)]
        (weight_grad,) = call(
            functools.partial(gather_kernel, 1.0 / math.sqrt(rows * blocks), planes),
            1,
            [whole(coded)] * planes + [anywhere],
            [(whole((own_model, columns)), (own_model, columns), F32)],
            [],
        )(*sums, grad_x)
    return grad_x, weight_grad


def solution(mesh):
    in_specs = (
        P(("wide", "seq"), None),
        P(("wide", "seq"), None),
        P(("wide", "seq"), None),
        P(("wide", "seq"), None),
        P(("wide", "seq"), None),
        P(("wide", "seq"), None),
        P(),
        P(),
        P(),
    )
    out_specs = (P(("wide", "seq"), None), P(("seq", "wide"), None))
    return jax.shard_map(body, mesh=mesh, in_specs=in_specs, out_specs=out_specs, check_vma=False)
```

```python
import functools
import math

import jax
import jax.numpy as jnp
from jax import lax
from jax.experimental import pallas as pl
from jax.experimental.pallas import tpu as pltpu
from jax.sharding import PartitionSpec as P

F32 = jnp.float32
BF16 = jnp.bfloat16
EXACT = lax.Precision.HIGHEST
VMEM_LIMIT = 64 * 1024 * 1024
TOP_POWER = 30.0
PRODUCT_BOUND = 30.0
LAYER_BOUND = 24.0
SUMMARY_HEADS = 32
CARRY_HEADS = 32
GRAD_HEADS = 32
PAIR_HEADS = 8
META = 8
SHORT = pl.CostEstimate(flops=1000, bytes_accessed=1000, transcendentals=0)


def mul(a, b):
    return lax.dot_general(a, b, (((1,), (0,)), ((), ())), preferred_element_type=F32)


def mul_nt(a, b):
    return lax.dot_general(a, b, (((1,), (1,)), ((), ())), preferred_element_type=F32)


def mul_exact(a, b, dims=((1,), (0,))):
    return lax.dot_general(a, b, (dims, ((), ())), preferred_element_type=F32, precision=EXACT)


def halves(value):
    top = value.astype(BF16)
    return top, (value - top.astype(F32)).astype(BF16)


def power_for(bound):
    power = jnp.floor(TOP_POWER - jnp.log2(jnp.maximum(bound, 1e-37)))
    return jnp.clip(power, -100.0, 100.0)


def thirds(value):
    top, rest = value.astype(BF16), value
    rest = rest - top.astype(F32)
    middle = rest.astype(BF16)
    return top, middle, (rest - middle.astype(F32)).astype(BF16)


def encode(value):
    square = value * value
    fourth = square * square
    return jnp.where(value < 0, -fourth, fourth).astype(BF16)


def decode(coded):
    coded = coded.astype(F32)
    size = jnp.maximum(jnp.abs(coded), 1e-37)
    inverse = lax.rsqrt(size)
    return coded * inverse * lax.rsqrt(size * inverse)


def head_selector(first_head, heads, lanes, head_width):
    row = lax.broadcasted_iota(jnp.int32, (heads, lanes), 0)
    lane = lax.broadcasted_iota(jnp.int32, (heads, lanes), 1)
    return jnp.where(row == first_head + lane // head_width, 1.0, 0.0).astype(BF16)


def triangle(length, keep):
    row = lax.broadcasted_iota(jnp.int32, (length, length), 0)
    col = lax.broadcasted_iota(jnp.int32, (length, length), 1)
    return jnp.where(keep(row, col), 1.0, 0.0).astype(F32)


def summary_kernel(
    head_width,
    raw_ref,
    bias_ref,
    decay_ref,
    write_ref,
    read_ref,
    x_ref,
    dy_ref,
    message_ref,
    step_ref,
    cum_ref,
    weight_f,
    weight_b,
    facts,
):
    turn = pl.program_id(0)
    heads = raw_ref.shape[1]
    rows, lanes = x_ref.shape
    state = write_ref.shape[0]

    @pl.when(turn == 0)
    def _():
        step = jax.nn.softplus(raw_ref[...].astype(F32) + bias_ref[...])
        rate = -jnp.exp(decay_ref[...])
        cum = mul_exact(triangle(rows, lambda r, c: r >= c), step * rate)
        finish = cum[rows - 1 : rows, :]
        forward = step * jnp.exp(finish - cum)
        backward = jnp.exp(cum)
        power_f = power_for(PRODUCT_BOUND * jnp.sum(forward, axis=0, keepdims=True))
        power_b = power_for(PRODUCT_BOUND * jnp.sum(backward, axis=0, keepdims=True))
        step_ref[...] = step
        cum_ref[...] = cum
        parts = thirds(jnp.maximum(finish, -1e30))
        facts[...] = jnp.concatenate(
            [part.astype(F32) for part in parts]
            + [power_f, power_b, jnp.zeros((META - 5, heads), F32)],
            axis=0,
        ).astype(BF16)
        weight_f[...] = (forward * jnp.exp2(power_f)).T
        weight_b[...] = (backward * jnp.exp2(power_b)).T

    group = lanes // head_width
    pair_lanes = 2 * head_width
    width = message_ref.shape[2]
    near = pl.ds(turn * group, group)
    pick = head_selector(turn * group, heads, lanes, head_width)
    fact = mul(facts[...], pick).astype(BF16)
    lane = lax.broadcasted_iota(jnp.int32, (state, pair_lanes), 1)
    ahead = (x_ref, write_ref[...].astype(F32), weight_f[near, :], 0)
    behind = (dy_ref, read_ref[...].astype(F32), weight_b[near, :], state)
    for pair in range(group // 2):
        span = slice(pair * pair_lanes, (pair + 1) * pair_lanes)
        owner, offset = pair * pair_lanes // width, pair * pair_lanes % width
        here = slice(offset, offset + pair_lanes)
        for tokens_ref, rows_t, weights, start in (ahead, behind):
            scaled = []
            for head in (2 * pair, 2 * pair + 1):
                scaled += halves(rows_t * weights[head : head + 1, :])
            product = mul(jnp.concatenate(scaled, axis=0), tokens_ref[:, span])
            early = product[0:state] + product[state : 2 * state]
            late = product[2 * state : 3 * state] + product[3 * state :]
            total = jnp.where(lane < head_width, early, late)
            message_ref[owner, start : start + state, here] = encode(total)
        message_ref[owner, 2 * state :, here] = fact[:, span]


def scan_kernel(message_ref, *rest):
    answer_ref, powers = rest[-2:]
    blocks, double, lanes = message_ref.shape
    state = (double - META) // 2
    top = 2.0**TOP_POWER

    def one(block, start, power_row, side, running, bound):
        facts = message_ref[block, 2 * state : double, :].astype(F32)
        decay = jnp.exp(facts[0:1] + facts[1:2] + facts[2:3])
        back = jnp.exp2(-facts[power_row : power_row + 1])
        power = power_for(bound)
        powers[side, pl.ds(block, 1), :] = power
        answer_ref[block, start : start + state, :] = encode(running * jnp.exp2(power))
        own = decode(message_ref[block, start : start + state, :]) * back
        return running * decay + own, bound * decay + top * back

    def both(block, carry):
        ahead, ahead_bound, behind, behind_bound = carry
        return one(block, 0, 3, 0, ahead, ahead_bound) + one(
            blocks - 1 - block, state, 4, 1, behind, behind_bound
        )

    zero, none = jnp.zeros((state, lanes), F32), jnp.zeros((1, lanes), F32)
    lax.fori_loop(0, blocks, both, (zero, none, zero, none), unroll=4)
    row = lax.broadcasted_iota(jnp.int32, (blocks, META, lanes), 1)
    ahead, behind = powers[0][:, None, :], powers[1][:, None, :]
    meta = jnp.where(row == 0, ahead, jnp.where(row == 1, behind, 0.0))
    answer_ref[:, 2 * state : double, :] = meta.astype(BF16)


def block_kernel(
    head_width,
    scale,
    first_head,
    waits,
    step_ref,
    cum_ref,
    write_ref,
    read_ref,
    x_ref,
    dy_ref,
    *rest,
):
    inner_ref, own_ref, within_ref, maps_ref = rest[waits : waits + 4]
    read_write, source, cum_rows, pair_sum, out_flow = rest[waits + 4 :]
    turn = pl.program_id(0)
    rows, lanes = x_ref.shape
    half = rows // 2
    heads = step_ref.shape[1]
    group = lanes // head_width

    @pl.when(turn == 0)
    def _():
        read_write[...] = scale * lax.dot_general(
            write_ref[...], read_ref[...], (((0,), (0,)), ((), ())), preferred_element_type=F32
        )
        source[...] = jnp.log(step_ref[...]) - cum_ref[...]
        cum_rows[...] = cum_ref[...].T
        pair_sum[...] = jnp.zeros_like(pair_sum)
        out_flow[...] = jnp.zeros_like(out_flow)
        own_ref[...] = jnp.zeros_like(own_ref)

    first = first_head + turn * group
    near = pltpu.roll(source[...], lax.rem(heads - first, heads), axis=1)
    near_cum = cum_rows[pl.ds(first, group), :]
    row = lax.broadcasted_iota(jnp.int32, (half, half), 0)
    col = lax.broadcasted_iota(jnp.int32, (half, half), 1)
    ahead = col >= row
    lane = lax.broadcasted_iota(jnp.int32, (half, 2 * head_width), 1)
    first_half = lane < head_width
    head_lane = lax.broadcasted_iota(jnp.int32, (half, heads), 1)
    flow_aa = read_write[0:half, 0:half]
    flow_ab = read_write[0:half, half:rows]
    flow_bb = read_write[half:rows, half:rows]
    sum_aa = jnp.zeros((half, half), F32)
    sum_ab = jnp.zeros((half, half), F32)
    sum_bb = jnp.zeros((half, half), F32)
    own_a = jnp.zeros((half, heads), F32)
    own_b = jnp.zeros((half, heads), F32)
    zero = jnp.zeros((half, 2 * head_width), BF16)
    flows = []
    for pair in range(group // 2):
        span = slice(pair * 2 * head_width, (pair + 1) * 2 * head_width)
        x_a, x_b = x_ref[0:half, span], x_ref[half:rows, span]
        dy_a, dy_b = dy_ref[0:half, span], dy_ref[half:rows, span]
        early_a, late_a = jnp.where(first_half, dy_a, zero), jnp.where(first_half, zero, dy_a)
        early_b, late_b = jnp.where(first_half, dy_b, zero), jnp.where(first_half, zero, dy_b)
        stack = jnp.concatenate([early_a, early_b, late_a, late_b], axis=0)
        stack_b = jnp.concatenate([early_b, late_b], axis=0)
        grad_a = mul_nt(x_a, stack)
        grad_b = mul_nt(x_b, stack_b)
        masks_a, masks_b = [], []
        for side in range(2):
            place = pair * 2 + side
            head = first + place
            from_a = near[0:half, place : place + 1]
            from_b = near[half:rows, place : place + 1]
            to_a = near_cum[place : place + 1, 0:half]
            to_b = near_cum[place : place + 1, half:rows]
            fade_aa = jnp.exp(jnp.where(ahead, to_a + from_a, -1e30))
            fade_ab = jnp.exp(to_b + from_a)
            fade_bb = jnp.exp(jnp.where(ahead, to_b + from_b, -1e30))
            weigh_aa = fade_aa * grad_a[:, side * rows : side * rows + half]
            weigh_ab = fade_ab * grad_a[:, side * rows + half : (side + 1) * rows]
            weigh_bb = fade_bb * grad_b[:, side * half : (side + 1) * half]
            sum_aa += weigh_aa
            sum_ab += weigh_ab
            sum_bb += weigh_bb
            masks_a += [(fade_aa * flow_aa).astype(BF16), (fade_ab * flow_ab).astype(BF16)]
            masks_b += [(fade_bb * flow_bb).astype(BF16)]
            pair_aa = weigh_aa * flow_aa
            pair_ab = weigh_ab * flow_ab
            pair_bb = weigh_bb * flow_bb
            flow_out = jnp.sum(pair_aa + pair_ab, axis=1, keepdims=True)
            own_a = jnp.where(head_lane == head, flow_out, own_a)
            flow_out = jnp.sum(pair_bb, axis=1, keepdims=True)
            own_b = jnp.where(head_lane == head, flow_out, own_b)
            flow_in = [
                jnp.sum(pair_aa, axis=0, keepdims=True),
                jnp.sum(pair_ab, axis=0, keepdims=True) + jnp.sum(pair_bb, axis=0, keepdims=True),
            ]
            flows.append(jnp.concatenate(flow_in, axis=1))
        inner_ref[0:half, span] = mul(jnp.concatenate(masks_a, axis=1), stack).astype(BF16)
        inner_ref[half:rows, span] = mul(jnp.concatenate(masks_b, axis=1), stack_b).astype(BF16)
    out_flow[pl.ds(first, group), :] = jnp.concatenate(flows, axis=0)
    pair_sum[0:half, 0:half] += sum_aa
    pair_sum[0:half, half:rows] += sum_ab
    pair_sum[half:rows, half:rows] += sum_bb
    own_ref[0:half, :] += own_a
    own_ref[half:rows, :] += own_b

    @pl.when(turn == pl.num_programs(0) - 1)
    def _():
        net = own_ref[...] - out_flow[...].T
        within_ref[...] = mul_exact(triangle(rows, lambda r, c: r > c), net)
        weighted = scale * pair_sum[...]
        maps_ref[...] = jnp.concatenate(
            [
                mul_exact(weighted, read_ref[...].astype(F32), ((1,), (1,))),
                mul_exact(weighted, write_ref[...].astype(F32), ((0,), (1,))),
            ],
            axis=1,
        )


def spread_heads(weight, first_head, picks, group):
    heads = weight.shape[1]
    near = pltpu.roll(weight, lax.rem(heads - first_head, heads), axis=1)
    top = near.astype(BF16).astype(F32)
    low = pltpu.roll(near - top, group, axis=1)
    lane = lax.broadcasted_iota(jnp.int32, near.shape, 1)
    return mul(jnp.where(lane < group, top, low).astype(BF16), picks)


def spread_picks(group, heads, lanes, head_width):
    row = lax.broadcasted_iota(jnp.int32, (heads, lanes), 0)
    lane = lax.broadcasted_iota(jnp.int32, (heads, lanes), 1)
    match = jnp.where(row < group, row, row - group) == lane // head_width
    return jnp.where(match, 1.0, 0.0).astype(BF16)


def read_answer(answer_ref, state, power_row):
    found = []
    start = power_row * state
    for piece in range(answer_ref.shape[0]):
        facts = answer_ref[piece, 2 * state :, :].astype(F32)
        back = jnp.exp2(-facts[power_row : power_row + 1])
        found.append(decode(answer_ref[piece, start : start + state, :]) * back)
    return jnp.concatenate(found, axis=1)


def carry_kernel(head_width, scale, waits, *refs):
    raw_ref, bias_ref, decay_ref, step_ref, cum_ref, write_ref, read_ref = refs[:7]
    own_ref, within_ref, map_ref, x_ref, dy_ref, answer_ref = refs[7:13]
    table_ref, sums, through, weight_e, weight_s, maps, picks = refs[13 + waits :]
    turn = pl.program_id(0)
    rows, lanes = x_ref.shape
    heads = step_ref.shape[1]
    state = write_ref.shape[0]
    group = lanes // head_width
    pair_lanes = 2 * head_width
    future, past = slice(0, heads), slice(heads, 2 * heads)
    write_sum = slice(2 * heads, 2 * heads + 2 * state)
    read_sum = slice(2 * heads + 2 * state, 2 * heads + 4 * state)

    @pl.when(turn == 0)
    def _():
        cum = cum_ref[...]
        finish = cum[rows - 1 : rows, :]
        weight_e[...] = step_ref[...] * jnp.exp(finish - cum) * scale
        weight_s[...] = jnp.exp(cum) * scale
        write, read = write_ref[...].astype(F32).T, read_ref[...].astype(F32).T
        maps[...] = jnp.concatenate([write, write, read, read], axis=1)
        picks[0:heads, :] = spread_picks(group, heads, lanes, head_width)
        picks[heads:, :] = head_selector(0, heads, lanes, head_width)
        sums[...] = jnp.zeros_like(sums)
        through[...] = jnp.zeros_like(through)

    first_here = turn * group
    pick = picks[heads:, :]
    early = lax.broadcasted_iota(jnp.int32, (state, pair_lanes), 1) < head_width
    none = jnp.zeros((state, pair_lanes), BF16)
    start = read_answer(answer_ref, state, 0)
    end = read_answer(answer_ref, state, 1)

    def products(tokens_ref, states, weight, map_columns):
        spread = spread_heads(weight[...], first_here, picks[0:heads, :], group)
        parts = halves(states)
        total, mapped = 0.0, []
        for pair in range(group // 2):
            span = slice(pair * pair_lanes, (pair + 1) * pair_lanes)
            blocks = [
                jnp.concatenate(
                    [jnp.where(early, part[:, span], none), jnp.where(early, none, part[:, span])],
                    axis=0,
                )
                for part in parts
            ]
            twice = jnp.concatenate([tokens_ref[:, span], tokens_ref[:, span]], axis=1)
            weighted = mul_nt(twice, jnp.concatenate(blocks, axis=1)) * spread[:, span]
            total += weighted
            mapped.append((weighted * map_columns).astype(BF16))
        return total, mapped

    def summed(parts):
        return mul_nt(jnp.concatenate(parts, axis=1), pick)

    def placed(value):
        return pltpu.roll(value, first_here, axis=1)

    total, mapped = products(x_ref, end, weight_e, maps[:, 0 : 2 * state])
    sums[:, write_sum] += total
    sums[:, future] += placed(summed(mapped))

    total, mapped = products(dy_ref, start, weight_s, maps[:, 2 * state : 4 * state])
    sums[:, read_sum] += total
    sums[:, past] += placed(summed(mapped))

    both = jnp.broadcast_to(jnp.sum(start * end, axis=0, keepdims=True), (8, lanes))
    top, low = halves(both)
    through[...] += placed(mul_nt(top, pick) + mul_nt(low, pick))

    @pl.when(turn == pl.num_programs(0) - 1)
    def _():
        rate = -jnp.exp(decay_ref[...])
        step = step_ref[...]
        gate = jax.nn.sigmoid(raw_ref[...].astype(F32) + bias_ref[...])
        finish = cum_ref[rows - 1 : rows, :]
        ahead = sums[:, future]
        decay_grad = (
            within_ref[...]
            + mul_exact(triangle(rows, lambda r, c: r <= c), sums[:, past])
            + mul_exact(triangle(rows, lambda r, c: r > c), ahead)
            + jnp.exp(finish) * scale * through[0:1, :]
        )
        ratio = jnp.where(step > 1e-30, gate / jnp.maximum(step, 1e-30), 1.0)
        raw_grad = (own_ref[...] + ahead) * ratio + rate * decay_grad * gate
        map_sum = sums[:, 2 * heads :]
        write_all = map_sum[:, 0:state] + map_sum[:, state : 2 * state]
        read_all = map_sum[:, 2 * state : 3 * state] + map_sum[:, 3 * state :]
        map_grad = jnp.concatenate([write_all, read_all], axis=1) + map_ref[...]
        table_ref[...] = jnp.concatenate([raw_grad.T, map_grad.T], axis=0).astype(BF16)


def grad_kernel(head_width, scale, first_head, waits, *refs):
    step_ref, cum_ref, write_ref, skip_ref, dy_ref, inner_ref, answer_ref = refs[:7]
    grad_ref, weight_e, maps, picks = refs[7 + waits :]
    turn = pl.program_id(0)
    rows, lanes = dy_ref.shape
    heads = step_ref.shape[1]
    state = write_ref.shape[0]
    group = lanes // head_width

    @pl.when(turn == 0)
    def _():
        cum = cum_ref[...]
        finish = cum[rows - 1 : rows, :]
        weight_e[...] = step_ref[...] * jnp.exp(finish - cum) * scale
        write = write_ref[...].astype(F32).T.astype(BF16)
        maps[...] = jnp.concatenate([write, write], axis=1)
        picks[...] = spread_picks(group, heads, lanes, head_width)

    first_here = first_head + turn * group
    end_parts = jnp.concatenate(halves(read_answer(answer_ref, state, 1)), axis=0)
    skip = jnp.broadcast_to(skip_ref[...], (16, heads))
    skip = spread_heads(skip, first_here, picks[...], group)[0:1]
    carried = mul(maps[...], end_parts) * spread_heads(weight_e[...], first_here, picks[...], group)
    inner = inner_ref[...].astype(F32)
    grad_ref[...] = (inner + skip * dy_ref[...].astype(F32) + carried).astype(BF16)


def deal_kernel(place_ref, layer_ref, after_ref, *out_refs):
    width = out_refs[0].shape[2]
    for turn, out_ref in enumerate(out_refs):
        start = pl.multiple_of((place_ref[0] ^ turn) * width, width)
        out_ref[0, :, :] = layer_ref[:, pl.ds(start, width)]


def product_kernel(planes, wide, place_ref, *refs):
    table_refs, layer_refs = refs[:wide], refs[wide : 2 * wide]
    out_refs = refs[-3 - planes : -3]
    table_all, layer_all, sems = refs[-3:]
    columns, rows = table_refs[0].shape
    loads = [
        pltpu.make_async_copy(ref, table_all.at[turn], sems.at[planes, turn])
        for turn, ref in enumerate(table_refs)
    ]
    for plane in range(planes):
        source = place_ref[1] ^ plane
        loads += [
            pltpu.make_async_copy(
                ref.at[source], layer_all.at[plane, pl.ds(turn * rows, rows)], sems.at[plane, turn]
            )
            for turn, ref in enumerate(layer_refs)
        ]
    for load in loads:
        load.start()
    for load in loads[:wide]:
        load.wait()
    table = jnp.concatenate([table_all[turn] for turn in range(wide)], axis=1)
    most = jnp.max(jnp.abs(table.astype(F32)), axis=0, keepdims=True)
    most = jnp.max(most, axis=1, keepdims=True)
    power = power_for(LAYER_BOUND * wide * rows * most)
    forth = jnp.exp2(power)
    for plane, out_ref in enumerate(out_refs):
        for load in loads[(plane + 1) * wide : (plane + 2) * wide]:
            load.wait()
        out_ref[0:columns, :] = encode(mul(table, layer_all[plane]) * forth)
        out_ref[columns:, :] = jnp.broadcast_to(power, out_ref[columns:, :].shape).astype(BF16)


def gather_kernel(factor, planes, *refs):
    part_refs, out_ref = refs[:planes], refs[-1]
    columns = out_ref.shape[1]
    total = jnp.zeros((columns, out_ref.shape[0]), F32)
    for part_ref in part_refs:
        power = part_ref[columns:, :].astype(F32)[0:1]
        total += decode(part_ref[0:columns, :]) * jnp.exp2(-power)
    out_ref[...] = (total * factor).T


def swap(array, axis, turn):
    if turn == 0:
        return array
    count = lax.axis_size(axis)
    return lax.ppermute(array, axis, [(one, one ^ turn) for one in range(count)])


def whole(shape):
    return pl.BlockSpec(shape, lambda i: (0,) * len(shape))


def call(kernel, steps, in_specs, out, scratch, aliases=None):
    return pl.pallas_call(
        kernel,
        grid=(steps,),
        in_specs=in_specs,
        out_specs=[spec for spec, _, _ in out],
        out_shape=[jax.ShapeDtypeStruct(dims, dtype) for _, dims, dtype in out],
        scratch_shapes=[pltpu.VMEM(dims, dtype) for dims, dtype in scratch],
        compiler_params=pltpu.CompilerParams(vmem_limit_bytes=VMEM_LIMIT),
        cost_estimate=SHORT,
        input_output_aliases=aliases or {},
    )


def body(
    layer_input,
    head_inputs,
    output_grad,
    step_raw,
    state_write,
    state_read,
    decay_log,
    step_bias,
    skip_gain,
):
    rows, channels = head_inputs.shape
    heads = step_raw.shape[1]
    head_width = channels // heads
    state = state_write.shape[1]
    model = layer_input.shape[1]
    columns = heads + 2 * state
    axes = ("wide", "seq")
    wide, planes = lax.axis_size("wide"), lax.axis_size("seq")
    blocks = wide * planes
    own_model = model // blocks
    scale = float(rows * blocks * state) ** -0.5
    owner_lanes = channels // blocks
    piece_lanes = max(owner_lanes, 128)
    pieces = channels // piece_lanes
    depth = 2 * state + META
    bias = step_bias[None, :]
    decay = decay_log[None, :]
    skip = skip_gain[None, :]
    write_t, read_t = state_write.T, state_read.T

    summary_lanes = SUMMARY_HEADS * head_width
    carry_lanes = CARRY_HEADS * head_width
    grad_lanes = GRAD_HEADS * head_width

    def tokens(width, first=0):
        return pl.BlockSpec((rows, width), lambda i: (0, first + i))

    def messages(width, first=0):
        return pl.BlockSpec((width // piece_lanes, depth, piece_lanes), lambda i: (first + i, 0, 0))

    head_spec = whole((rows, heads))
    line_spec = whole((1, heads))
    map_spec = whole((state, rows))
    head_out = (head_spec, (rows, heads), F32)

    def exchange(array):
        return lax.all_to_all(array, axes, split_axis=0, concat_axis=0, tiled=True)

    def to_owner(array):
        if owner_lanes < piece_lanes:
            split = array.reshape(pieces, depth, piece_lanes // owner_lanes, owner_lanes)
            array = jnp.moveaxis(split, 2, 1).reshape(blocks, depth, owner_lanes)
        return exchange(array)

    def from_owner(array):
        array = exchange(array)
        if owner_lanes < piece_lanes:
            split = array.reshape(pieces, piece_lanes // owner_lanes, depth, owner_lanes)
            array = jnp.moveaxis(split, 1, 2).reshape(pieces, depth, piece_lanes)
        return array

    with jax.named_scope("summaries"):
        message, step, cum = call(
            functools.partial(summary_kernel, head_width),
            channels // summary_lanes,
            [head_spec, line_spec, line_spec, map_spec, map_spec]
            + [tokens(summary_lanes), tokens(summary_lanes)],
            [
                (messages(summary_lanes), (pieces, depth, piece_lanes), BF16),
                head_out,
                head_out,
            ],
            [((heads, rows), F32), ((heads, rows), F32), ((META, heads), BF16)],
        )(step_raw, bias, decay, write_t, read_t, head_inputs, output_grad)
    place = jnp.stack([lax.axis_index("wide"), lax.axis_index("seq")]).astype(jnp.int32)
    with jax.named_scope("layer"):
        if own_model % 128:
            cut = jnp.transpose(layer_input.reshape(rows, planes, wide, own_model), (2, 1, 0, 3))
            dealt = [
                lax.dynamic_index_in_dim(cut, place[0] ^ turn, 0, False) for turn in range(wide)
            ]
        else:
            dealt = pl.pallas_call(
                deal_kernel,
                grid_spec=pltpu.PrefetchScalarGridSpec(
                    num_scalar_prefetch=1,
                    grid=(planes,),
                    in_specs=[
                        pl.BlockSpec((rows, wide * own_model), lambda i, p: (0, i)),
                        pl.BlockSpec(memory_space=pl.ANY),
                    ],
                    out_specs=[pl.BlockSpec((1, rows, own_model), lambda i, p: (i, 0, 0))] * wide,
                ),
                out_shape=[jax.ShapeDtypeStruct((planes, rows, own_model), BF16)] * wide,
                compiler_params=pltpu.CompilerParams(vmem_limit_bytes=VMEM_LIMIT),
                cost_estimate=SHORT,
            )(place, layer_input, cum)
        layer_parts = [swap(one, "wide", turn) for turn, one in enumerate(dealt)]

    anywhere = pl.BlockSpec(memory_space=pltpu.HBM)
    firsts = [turn for turn in (1, 2, 4, 3, 5) if turn < wide]
    lasts = [layer_parts[turn] for turn in range(1, wide) if turn not in firsts]
    lasts, latest = lasts[:-1], lasts[-1:]
    with jax.named_scope("own_block"):
        width = PAIR_HEADS * head_width
        inner, own, within, maps = call(
            functools.partial(block_kernel, head_width, scale, 0, 1),
            channels // width,
            [head_spec, head_spec, map_spec, map_spec, tokens(width), tokens(width), anywhere],
            [
                (tokens(width), (rows, channels), BF16),
                head_out,
                head_out,
                (whole((rows, 2 * state)), (rows, 2 * state), F32),
            ],
            [
                ((rows, rows), F32),
                ((rows, heads), F32),
                ((heads, rows), F32),
                ((rows, rows), F32),
                ((heads, rows), F32),
            ],
        )(step, cum, write_t, read_t, head_inputs, output_grad, dealt[0])
    with jax.named_scope("scan"):
        after = [own] + [layer_parts[turn] for turn in firsts]
        scan_lanes = min(owner_lanes, 128)
        scan_spec = pl.BlockSpec((blocks, depth, scan_lanes), lambda i: (0, 0, i))
        (answer,) = call(
            scan_kernel,
            owner_lanes // scan_lanes,
            [scan_spec] + [anywhere] * len(after),
            [(scan_spec, (blocks, depth, owner_lanes), BF16)],
            [((2, blocks, scan_lanes), F32)],
        )(to_owner(message), *after)
        returned = from_owner(answer)

    with jax.named_scope("carried"):
        (table,) = call(
            functools.partial(carry_kernel, head_width, scale, len(lasts)),
            channels // carry_lanes,
            [head_spec, line_spec, line_spec, head_spec, head_spec, map_spec, map_spec]
            + [head_spec, head_spec, whole((rows, 2 * state))]
            + [tokens(carry_lanes), tokens(carry_lanes), messages(carry_lanes)]
            + [anywhere] * len(lasts),
            [(whole((columns, rows)), (columns, rows), BF16)],
            [
                ((rows, 2 * heads + 4 * state), F32),
                ((8, heads), F32),
                ((rows, heads), F32),
                ((rows, heads), F32),
                ((rows, 4 * state), F32),
                ((2 * heads, carry_lanes), BF16),
            ],
        )(
            *(step_raw, bias, decay, step, cum, write_t, read_t, own, within, maps),
            *(head_inputs, output_grad, returned, *lasts),
        )

    def grad_half(half, grad):
        steps = channels // grad_lanes // 2
        first = half * steps
        in_specs = [head_spec, head_spec, map_spec, line_spec]
        in_specs += [tokens(grad_lanes, first), tokens(grad_lanes, first)]
        in_specs += [messages(grad_lanes, first)]
        in_specs += [anywhere] * len(grad)
        (grad,) = call(
            functools.partial(grad_kernel, head_width, scale, first * GRAD_HEADS, len(grad)),
            steps,
            in_specs,
            [(tokens(grad_lanes, first), (rows, channels), BF16)],
            [((rows, heads), F32), ((rows, 2 * state), BF16), ((heads, grad_lanes), BF16)],
            {len(in_specs) - 1: 0} if half else {},
        )(step, cum, write_t, skip, output_grad, inner, returned, *grad)
        return grad

    with jax.named_scope("grad_x"):
        grad_part = grad_half(0, [table] + latest)
        grad_x = grad_half(1, [grad_part])

    with jax.named_scope("projection"):
        tables = [table]
        for turn in range(1, wide):
            tables.append(swap(tables[turn - 1], "wide", 1) if turn % 2 else swap(table, "wide", turn))
        coded = (columns + META, own_model)
        products = pl.pallas_call(
            functools.partial(product_kernel, planes, wide),
            in_specs=[pl.BlockSpec(memory_space=pltpu.SMEM)] + [anywhere] * (2 * wide + 1),
            out_specs=[pl.BlockSpec(memory_space=pltpu.VMEM)] * planes,
            out_shape=[jax.ShapeDtypeStruct(coded, BF16)] * planes,
            scratch_shapes=[
                pltpu.VMEM((wide, columns, rows), BF16),
                pltpu.VMEM((planes, wide * rows, own_model), BF16),
                pltpu.SemaphoreType.DMA((planes + 1, wide)),
            ],
            compiler_params=pltpu.CompilerParams(vmem_limit_bytes=VMEM_LIMIT),
            cost_estimate=SHORT,
        )(place, *tables, *layer_parts, grad_part)
        sums = [swap(one, "seq", turn) for turn, one in enumerate(products)]
        (weight_grad,) = call(
            functools.partial(gather_kernel, 1.0 / math.sqrt(rows * blocks), planes),
            1,
            [whole(coded)] * planes + [anywhere],
            [(whole((own_model, columns)), (own_model, columns), F32)],
            [],
        )(*sums, grad_x)
    return grad_x, weight_grad


def solution(mesh):
    in_specs = (
        P(("wide", "seq"), None),
        P(("wide", "seq"), None),
        P(("wide", "seq"), None),
        P(("wide", "seq"), None),
        P(("wide", "seq"), None),
        P(("wide", "seq"), None),
        P(),
        P(),
        P(),
    )
    out_specs = (P(("wide", "seq"), None), P(("seq", "wide"), None))
    return jax.shard_map(body, mesh=mesh, in_specs=in_specs, out_specs=out_specs, check_vma=False)
```

```python
import functools
import math

import jax
import jax.numpy as jnp
from jax import lax
from jax.experimental import pallas as pl
from jax.experimental.pallas import tpu as pltpu
from jax.sharding import PartitionSpec as P

F32 = jnp.float32
BF16 = jnp.bfloat16
EXACT = lax.Precision.HIGHEST
VMEM_LIMIT = 64 * 1024 * 1024
PRODUCT_LIMIT = 32 * 1024 * 1024
TOP_POWER = 30.0
PRODUCT_BOUND = 30.0
LAYER_BOUND = 24.0
SUMMARY_HEADS = 32
CARRY_HEADS = 32
GRAD_HEADS = 32
PAIR_HEADS = 8
META = 8
SHORT = pl.CostEstimate(flops=1000, bytes_accessed=1000, transcendentals=0)


def mul(a, b):
    return lax.dot_general(a, b, (((1,), (0,)), ((), ())), preferred_element_type=F32)


def mul_nt(a, b):
    return lax.dot_general(a, b, (((1,), (1,)), ((), ())), preferred_element_type=F32)


def mul_exact(a, b, dims=((1,), (0,))):
    return lax.dot_general(a, b, (dims, ((), ())), preferred_element_type=F32, precision=EXACT)


def halves(value):
    top = value.astype(BF16)
    return top, (value - top.astype(F32)).astype(BF16)


def power_for(bound):
    power = jnp.floor(TOP_POWER - jnp.log2(jnp.maximum(bound, 1e-37)))
    return jnp.clip(power, -100.0, 100.0)


def thirds(value):
    top, rest = value.astype(BF16), value
    rest = rest - top.astype(F32)
    middle = rest.astype(BF16)
    return top, middle, (rest - middle.astype(F32)).astype(BF16)


def encode(value):
    square = value * value
    fourth = square * square
    return jnp.where(value < 0, -fourth, fourth).astype(BF16)


def decode(coded):
    coded = coded.astype(F32)
    size = jnp.maximum(jnp.abs(coded), 1e-37)
    inverse = lax.rsqrt(size)
    return coded * inverse * lax.rsqrt(size * inverse)


def head_selector(first_head, heads, lanes, head_width):
    row = lax.broadcasted_iota(jnp.int32, (heads, lanes), 0)
    lane = lax.broadcasted_iota(jnp.int32, (heads, lanes), 1)
    return jnp.where(row == first_head + lane // head_width, 1.0, 0.0).astype(BF16)


def triangle(length, keep):
    row = lax.broadcasted_iota(jnp.int32, (length, length), 0)
    col = lax.broadcasted_iota(jnp.int32, (length, length), 1)
    return jnp.where(keep(row, col), 1.0, 0.0).astype(F32)


def summary_kernel(
    head_width,
    raw_ref,
    bias_ref,
    decay_ref,
    write_ref,
    read_ref,
    x_ref,
    dy_ref,
    message_ref,
    step_ref,
    cum_ref,
    weight_f,
    weight_b,
    facts,
    x_all,
    dy_all,
    message_all,
    in_sems,
    out_sems,
):
    heads = raw_ref.shape[1]
    chunks, rows, lanes = x_all.shape
    state = write_ref.shape[0]
    group = lanes // head_width
    pair_lanes = 2 * head_width
    width = message_all.shape[2]
    here = lanes // width

    def loads(chunk):
        span = pl.ds(chunk * lanes, lanes)
        return (
            pltpu.make_async_copy(x_ref.at[:, span], x_all.at[chunk], in_sems.at[0, chunk]),
            pltpu.make_async_copy(dy_ref.at[:, span], dy_all.at[chunk], in_sems.at[1, chunk]),
        )

    def send(chunk):
        span = pl.ds(chunk * here, here)
        return pltpu.make_async_copy(
            message_all.at[span], message_ref.at[span], out_sems.at[chunk]
        )

    for chunk in range(chunks):
        for load in loads(chunk):
            load.start()

    step = jax.nn.softplus(raw_ref[...].astype(F32) + bias_ref[...])
    rate = -jnp.exp(decay_ref[...])
    cum = mul_exact(triangle(rows, lambda r, c: r >= c), step * rate)
    finish = cum[rows - 1 : rows, :]
    forward = step * jnp.exp(finish - cum)
    backward = jnp.exp(cum)
    power_f = power_for(PRODUCT_BOUND * jnp.sum(forward, axis=0, keepdims=True))
    power_b = power_for(PRODUCT_BOUND * jnp.sum(backward, axis=0, keepdims=True))
    step_ref[...] = step
    cum_ref[...] = cum
    parts = thirds(jnp.maximum(finish, -1e30))
    facts[...] = jnp.concatenate(
        [part.astype(F32) for part in parts]
        + [power_f, power_b, jnp.zeros((META - 5, heads), F32)],
        axis=0,
    ).astype(BF16)
    weight_f[...] = (forward * jnp.exp2(power_f)).T
    weight_b[...] = (backward * jnp.exp2(power_b)).T
    lane = lax.broadcasted_iota(jnp.int32, (state, pair_lanes), 1)

    def one(chunk, carry):
        for load in loads(chunk):
            load.wait()
        near = pl.ds(chunk * group, group)
        pick = head_selector(chunk * group, heads, lanes, head_width)
        fact = mul(facts[...], pick).astype(BF16)
        ahead = (x_all, write_ref[...].astype(F32), weight_f[near, :], 0)
        behind = (dy_all, read_ref[...].astype(F32), weight_b[near, :], state)
        for pair in range(group // 2):
            span = slice(pair * pair_lanes, (pair + 1) * pair_lanes)
            owner, offset = pair * pair_lanes // width, pair * pair_lanes % width
            part = slice(offset, offset + pair_lanes)
            owner = chunk * here + owner
            for tokens, rows_t, weights, start in (ahead, behind):
                scaled = []
                for head in (2 * pair, 2 * pair + 1):
                    scaled += halves(rows_t * weights[head : head + 1, :])
                product = mul(jnp.concatenate(scaled, axis=0), tokens[chunk, :, span])
                early = product[0:state] + product[state : 2 * state]
                late = product[2 * state : 3 * state] + product[3 * state :]
                total = jnp.where(lane < head_width, early, late)
                message_all[owner, start : start + state, part] = encode(total)
            message_all[owner, 2 * state :, part] = fact[:, span]
        send(chunk).start()
        return carry

    lax.fori_loop(0, chunks, one, 0)
    for chunk in range(chunks):
        send(chunk).wait()


def scan_kernel(message_ref, *rest):
    answer_ref, powers = rest[-2:]
    blocks, double, lanes = message_ref.shape
    state = (double - META) // 2
    top = 2.0**TOP_POWER

    def one(block, start, power_row, side, running, bound):
        facts = message_ref[block, 2 * state : double, :].astype(F32)
        decay = jnp.exp(facts[0:1] + facts[1:2] + facts[2:3])
        back = jnp.exp2(-facts[power_row : power_row + 1])
        power = power_for(bound)
        powers[side, pl.ds(block, 1), :] = power
        answer_ref[block, start : start + state, :] = encode(running * jnp.exp2(power))
        own = decode(message_ref[block, start : start + state, :]) * back
        return running * decay + own, bound * decay + top * back

    def both(block, carry):
        ahead, ahead_bound, behind, behind_bound = carry
        return one(block, 0, 3, 0, ahead, ahead_bound) + one(
            blocks - 1 - block, state, 4, 1, behind, behind_bound
        )

    zero, none = jnp.zeros((state, lanes), F32), jnp.zeros((1, lanes), F32)
    lax.fori_loop(0, blocks, both, (zero, none, zero, none), unroll=4)
    row = lax.broadcasted_iota(jnp.int32, (blocks, META, lanes), 1)
    ahead, behind = powers[0][:, None, :], powers[1][:, None, :]
    meta = jnp.where(row == 0, ahead, jnp.where(row == 1, behind, 0.0))
    answer_ref[:, 2 * state : double, :] = meta.astype(BF16)


def block_kernel(
    head_width,
    scale,
    first_head,
    waits,
    step_ref,
    cum_ref,
    write_ref,
    read_ref,
    x_ref,
    dy_ref,
    *rest,
):
    inner_ref, own_ref, within_ref, maps_ref = rest[waits : waits + 4]
    read_write, source, cum_rows, pair_sum, out_flow = rest[waits + 4 :]
    turn = pl.program_id(0)
    rows, lanes = x_ref.shape
    half = rows // 2
    heads = step_ref.shape[1]
    group = lanes // head_width

    @pl.when(turn == 0)
    def _():
        read_write[...] = scale * lax.dot_general(
            write_ref[...], read_ref[...], (((0,), (0,)), ((), ())), preferred_element_type=F32
        )
        source[...] = jnp.log(step_ref[...]) - cum_ref[...]
        cum_rows[...] = cum_ref[...].T
        pair_sum[...] = jnp.zeros_like(pair_sum)
        out_flow[...] = jnp.zeros_like(out_flow)
        own_ref[...] = jnp.zeros_like(own_ref)

    first = first_head + turn * group
    near = pltpu.roll(source[...], lax.rem(heads - first, heads), axis=1)
    near_cum = cum_rows[pl.ds(first, group), :]
    row = lax.broadcasted_iota(jnp.int32, (half, half), 0)
    col = lax.broadcasted_iota(jnp.int32, (half, half), 1)
    ahead = col >= row
    lane = lax.broadcasted_iota(jnp.int32, (half, 2 * head_width), 1)
    first_half = lane < head_width
    head_lane = lax.broadcasted_iota(jnp.int32, (half, heads), 1)
    flow_aa = read_write[0:half, 0:half]
    flow_ab = read_write[0:half, half:rows]
    flow_bb = read_write[half:rows, half:rows]
    sum_aa = jnp.zeros((half, half), F32)
    sum_ab = jnp.zeros((half, half), F32)
    sum_bb = jnp.zeros((half, half), F32)
    own_a = jnp.zeros((half, heads), F32)
    own_b = jnp.zeros((half, heads), F32)
    zero = jnp.zeros((half, 2 * head_width), BF16)
    flows = []
    for pair in range(group // 2):
        span = slice(pair * 2 * head_width, (pair + 1) * 2 * head_width)
        x_a, x_b = x_ref[0:half, span], x_ref[half:rows, span]
        dy_a, dy_b = dy_ref[0:half, span], dy_ref[half:rows, span]
        early_a, late_a = jnp.where(first_half, dy_a, zero), jnp.where(first_half, zero, dy_a)
        early_b, late_b = jnp.where(first_half, dy_b, zero), jnp.where(first_half, zero, dy_b)
        stack = jnp.concatenate([early_a, early_b, late_a, late_b], axis=0)
        stack_b = jnp.concatenate([early_b, late_b], axis=0)
        grad_a = mul_nt(x_a, stack)
        grad_b = mul_nt(x_b, stack_b)
        masks_a, masks_b = [], []
        for side in range(2):
            place = pair * 2 + side
            head = first + place
            from_a = near[0:half, place : place + 1]
            from_b = near[half:rows, place : place + 1]
            to_a = near_cum[place : place + 1, 0:half]
            to_b = near_cum[place : place + 1, half:rows]
            fade_aa = jnp.exp(jnp.where(ahead, to_a + from_a, -1e30))
            fade_ab = jnp.exp(to_b + from_a)
            fade_bb = jnp.exp(jnp.where(ahead, to_b + from_b, -1e30))
            weigh_aa = fade_aa * grad_a[:, side * rows : side * rows + half]
            weigh_ab = fade_ab * grad_a[:, side * rows + half : (side + 1) * rows]
            weigh_bb = fade_bb * grad_b[:, side * half : (side + 1) * half]
            sum_aa += weigh_aa
            sum_ab += weigh_ab
            sum_bb += weigh_bb
            masks_a += [(fade_aa * flow_aa).astype(BF16), (fade_ab * flow_ab).astype(BF16)]
            masks_b += [(fade_bb * flow_bb).astype(BF16)]
            pair_aa = weigh_aa * flow_aa
            pair_ab = weigh_ab * flow_ab
            pair_bb = weigh_bb * flow_bb
            flow_out = jnp.sum(pair_aa + pair_ab, axis=1, keepdims=True)
            own_a = jnp.where(head_lane == head, flow_out, own_a)
            flow_out = jnp.sum(pair_bb, axis=1, keepdims=True)
            own_b = jnp.where(head_lane == head, flow_out, own_b)
            flow_in = [
                jnp.sum(pair_aa, axis=0, keepdims=True),
                jnp.sum(pair_ab, axis=0, keepdims=True) + jnp.sum(pair_bb, axis=0, keepdims=True),
            ]
            flows.append(jnp.concatenate(flow_in, axis=1))
        inner_ref[0:half, span] = mul(jnp.concatenate(masks_a, axis=1), stack).astype(BF16)
        inner_ref[half:rows, span] = mul(jnp.concatenate(masks_b, axis=1), stack_b).astype(BF16)
    out_flow[pl.ds(first, group), :] = jnp.concatenate(flows, axis=0)
    pair_sum[0:half, 0:half] += sum_aa
    pair_sum[0:half, half:rows] += sum_ab
    pair_sum[half:rows, half:rows] += sum_bb
    own_ref[0:half, :] += own_a
    own_ref[half:rows, :] += own_b

    @pl.when(turn == pl.num_programs(0) - 1)
    def _():
        net = own_ref[...] - out_flow[...].T
        within_ref[...] = mul_exact(triangle(rows, lambda r, c: r > c), net)
        weighted = scale * pair_sum[...]
        maps_ref[...] = jnp.concatenate(
            [
                mul_exact(weighted, read_ref[...].astype(F32), ((1,), (1,))),
                mul_exact(weighted, write_ref[...].astype(F32), ((0,), (1,))),
            ],
            axis=1,
        )


def spread_heads(weight, first_head, picks, group):
    heads = weight.shape[1]
    near = pltpu.roll(weight, lax.rem(heads - first_head, heads), axis=1)
    top = near.astype(BF16).astype(F32)
    low = pltpu.roll(near - top, group, axis=1)
    lane = lax.broadcasted_iota(jnp.int32, near.shape, 1)
    return mul(jnp.where(lane < group, top, low).astype(BF16), picks)


def spread_picks(group, heads, lanes, head_width):
    row = lax.broadcasted_iota(jnp.int32, (heads, lanes), 0)
    lane = lax.broadcasted_iota(jnp.int32, (heads, lanes), 1)
    match = jnp.where(row < group, row, row - group) == lane // head_width
    return jnp.where(match, 1.0, 0.0).astype(BF16)


def read_answer(answer_ref, state, power_row):
    found = []
    start = power_row * state
    for piece in range(answer_ref.shape[0]):
        facts = answer_ref[piece, 2 * state :, :].astype(F32)
        back = jnp.exp2(-facts[power_row : power_row + 1])
        found.append(decode(answer_ref[piece, start : start + state, :]) * back)
    return jnp.concatenate(found, axis=1)


def carry_kernel(head_width, scale, waits, *refs):
    raw_ref, bias_ref, decay_ref, step_ref, cum_ref, write_ref, read_ref = refs[:7]
    own_ref, within_ref, map_ref, x_ref, dy_ref, answer_ref = refs[7:13]
    table_ref, sums, through, weight_e, weight_s, maps, picks = refs[13 + waits :]
    turn = pl.program_id(0)
    rows, lanes = x_ref.shape
    heads = step_ref.shape[1]
    state = write_ref.shape[0]
    group = lanes // head_width
    pair_lanes = 2 * head_width
    future, past = slice(0, heads), slice(heads, 2 * heads)
    write_sum = slice(2 * heads, 2 * heads + 2 * state)
    read_sum = slice(2 * heads + 2 * state, 2 * heads + 4 * state)

    @pl.when(turn == 0)
    def _():
        cum = cum_ref[...]
        finish = cum[rows - 1 : rows, :]
        weight_e[...] = step_ref[...] * jnp.exp(finish - cum) * scale
        weight_s[...] = jnp.exp(cum) * scale
        write, read = write_ref[...].astype(F32).T, read_ref[...].astype(F32).T
        maps[...] = jnp.concatenate([write, write, read, read], axis=1)
        picks[0:heads, :] = spread_picks(group, heads, lanes, head_width)
        picks[heads:, :] = head_selector(0, heads, lanes, head_width)
        sums[...] = jnp.zeros_like(sums)
        through[...] = jnp.zeros_like(through)

    first_here = turn * group
    pick = picks[heads:, :]
    early = lax.broadcasted_iota(jnp.int32, (state, pair_lanes), 1) < head_width
    none = jnp.zeros((state, pair_lanes), BF16)
    start = read_answer(answer_ref, state, 0)
    end = read_answer(answer_ref, state, 1)

    def products(tokens_ref, states, weight, map_columns):
        spread = spread_heads(weight[...], first_here, picks[0:heads, :], group)
        parts = halves(states)
        total, mapped = 0.0, []
        for pair in range(group // 2):
            span = slice(pair * pair_lanes, (pair + 1) * pair_lanes)
            blocks = [
                jnp.concatenate(
                    [jnp.where(early, part[:, span], none), jnp.where(early, none, part[:, span])],
                    axis=0,
                )
                for part in parts
            ]
            twice = jnp.concatenate([tokens_ref[:, span], tokens_ref[:, span]], axis=1)
            weighted = mul_nt(twice, jnp.concatenate(blocks, axis=1)) * spread[:, span]
            total += weighted
            mapped.append((weighted * map_columns).astype(BF16))
        return total, mapped

    def summed(parts):
        return mul_nt(jnp.concatenate(parts, axis=1), pick)

    def placed(value):
        return pltpu.roll(value, first_here, axis=1)

    total, mapped = products(x_ref, end, weight_e, maps[:, 0 : 2 * state])
    sums[:, write_sum] += total
    sums[:, future] += placed(summed(mapped))

    total, mapped = products(dy_ref, start, weight_s, maps[:, 2 * state : 4 * state])
    sums[:, read_sum] += total
    sums[:, past] += placed(summed(mapped))

    both = jnp.broadcast_to(jnp.sum(start * end, axis=0, keepdims=True), (8, lanes))
    top, low = halves(both)
    through[...] += placed(mul_nt(top, pick) + mul_nt(low, pick))

    @pl.when(turn == pl.num_programs(0) - 1)
    def _():
        rate = -jnp.exp(decay_ref[...])
        step = step_ref[...]
        gate = jax.nn.sigmoid(raw_ref[...].astype(F32) + bias_ref[...])
        finish = cum_ref[rows - 1 : rows, :]
        ahead = sums[:, future]
        decay_grad = (
            within_ref[...]
            + mul_exact(triangle(rows, lambda r, c: r <= c), sums[:, past])
            + mul_exact(triangle(rows, lambda r, c: r > c), ahead)
            + jnp.exp(finish) * scale * through[0:1, :]
        )
        ratio = jnp.where(step > 1e-30, gate / jnp.maximum(step, 1e-30), 1.0)
        raw_grad = (own_ref[...] + ahead) * ratio + rate * decay_grad * gate
        map_sum = sums[:, 2 * heads :]
        write_all = map_sum[:, 0:state] + map_sum[:, state : 2 * state]
        read_all = map_sum[:, 2 * state : 3 * state] + map_sum[:, 3 * state :]
        map_grad = jnp.concatenate([write_all, read_all], axis=1) + map_ref[...]
        table_ref[...] = jnp.concatenate([raw_grad.T, map_grad.T], axis=0).astype(BF16)


def grad_kernel(head_width, scale, *refs):
    step_ref, cum_ref, write_ref, skip_ref, dy_ref, inner_ref, answer_ref = refs[:7]
    grad_ref, weight_e, maps, picks = refs[8:]
    turn = pl.program_id(0)
    rows, lanes = dy_ref.shape
    heads = step_ref.shape[1]
    state = write_ref.shape[0]
    group = lanes // head_width

    @pl.when(turn == 0)
    def _():
        cum = cum_ref[...]
        finish = cum[rows - 1 : rows, :]
        weight_e[...] = step_ref[...] * jnp.exp(finish - cum) * scale
        write = write_ref[...].astype(F32).T.astype(BF16)
        maps[...] = jnp.concatenate([write, write], axis=1)
        picks[...] = spread_picks(group, heads, lanes, head_width)

    first_here = turn * group
    end_parts = jnp.concatenate(halves(read_answer(answer_ref, state, 1)), axis=0)
    skip = jnp.broadcast_to(skip_ref[...], (16, heads))
    skip = spread_heads(skip, first_here, picks[...], group)[0:1]
    carried = mul(maps[...], end_parts) * spread_heads(weight_e[...], first_here, picks[...], group)
    inner = inner_ref[...].astype(F32)
    grad_ref[...] = (inner + skip * dy_ref[...].astype(F32) + carried).astype(BF16)


def deal_kernel(place_ref, layer_ref, after_ref, *out_refs):
    width = out_refs[0].shape[2]
    for turn, out_ref in enumerate(out_refs):
        start = pl.multiple_of((place_ref[0] ^ turn) * width, width)
        out_ref[0, :, :] = layer_ref[:, pl.ds(start, width)]


def product_kernel(planes, wide, place_ref, *refs):
    table_refs, layer_refs = refs[:wide], refs[wide : 2 * wide]
    out_refs = refs[-3 - planes : -3]
    table_all, layer_all, sems = refs[-3:]
    columns, rows = table_refs[0].shape
    loads = [
        pltpu.make_async_copy(ref, table_all.at[turn], sems.at[planes, turn])
        for turn, ref in enumerate(table_refs)
    ]
    for plane in range(planes):
        source = place_ref[1] ^ plane
        loads += [
            pltpu.make_async_copy(
                ref.at[source], layer_all.at[plane, pl.ds(turn * rows, rows)], sems.at[plane, turn]
            )
            for turn, ref in enumerate(layer_refs)
        ]
    for load in loads:
        load.start()
    for load in loads[:wide]:
        load.wait()
    table = jnp.concatenate([table_all[turn] for turn in range(wide)], axis=1)
    most = jnp.max(jnp.abs(table.astype(F32)), axis=0, keepdims=True)
    most = jnp.max(most, axis=1, keepdims=True)
    power = power_for(LAYER_BOUND * wide * rows * most)
    forth = jnp.exp2(power)
    for plane, out_ref in enumerate(out_refs):
        for load in loads[(plane + 1) * wide : (plane + 2) * wide]:
            load.wait()
        out_ref[0:columns, :] = encode(mul(table, layer_all[plane]) * forth)
        out_ref[columns:, :] = jnp.broadcast_to(power, out_ref[columns:, :].shape).astype(BF16)


def gather_kernel(factor, planes, *refs):
    part_refs, out_ref = refs[:planes], refs[-1]
    columns = out_ref.shape[1]
    total = jnp.zeros((columns, out_ref.shape[0]), F32)
    for part_ref in part_refs:
        power = part_ref[columns:, :].astype(F32)[0:1]
        total += decode(part_ref[0:columns, :]) * jnp.exp2(-power)
    out_ref[...] = (total * factor).T


def swap(array, axis, turn):
    if turn == 0:
        return array
    count = lax.axis_size(axis)
    return lax.ppermute(array, axis, [(one, one ^ turn) for one in range(count)])


def whole(shape):
    return pl.BlockSpec(shape, lambda i: (0,) * len(shape))


def call(kernel, steps, in_specs, out, scratch, aliases=None):
    return pl.pallas_call(
        kernel,
        grid=(steps,),
        in_specs=in_specs,
        out_specs=[spec for spec, _, _ in out],
        out_shape=[jax.ShapeDtypeStruct(dims, dtype) for _, dims, dtype in out],
        scratch_shapes=[
            pltpu.VMEM(*one) if isinstance(one, tuple) else one for one in scratch
        ],
        compiler_params=pltpu.CompilerParams(vmem_limit_bytes=VMEM_LIMIT),
        cost_estimate=SHORT,
        input_output_aliases=aliases or {},
    )


def body(
    layer_input,
    head_inputs,
    output_grad,
    step_raw,
    state_write,
    state_read,
    decay_log,
    step_bias,
    skip_gain,
):
    rows, channels = head_inputs.shape
    heads = step_raw.shape[1]
    head_width = channels // heads
    state = state_write.shape[1]
    model = layer_input.shape[1]
    columns = heads + 2 * state
    axes = ("wide", "seq")
    wide, planes = lax.axis_size("wide"), lax.axis_size("seq")
    blocks = wide * planes
    own_model = model // blocks
    scale = float(rows * blocks * state) ** -0.5
    owner_lanes = channels // blocks
    piece_lanes = max(owner_lanes, 128)
    pieces = channels // piece_lanes
    depth = 2 * state + META
    bias = step_bias[None, :]
    decay = decay_log[None, :]
    skip = skip_gain[None, :]
    write_t, read_t = state_write.T, state_read.T

    summary_lanes = SUMMARY_HEADS * head_width
    carry_lanes = CARRY_HEADS * head_width
    grad_lanes = GRAD_HEADS * head_width

    def tokens(width):
        return pl.BlockSpec((rows, width), lambda i: (0, i))

    def messages(width):
        return pl.BlockSpec((width // piece_lanes, depth, piece_lanes), lambda i: (i, 0, 0))

    head_spec = whole((rows, heads))
    line_spec = whole((1, heads))
    map_spec = whole((state, rows))
    head_out = (head_spec, (rows, heads), F32)

    def exchange(array):
        return lax.all_to_all(array, axes, split_axis=0, concat_axis=0, tiled=True)

    def to_owner(array):
        if owner_lanes < piece_lanes:
            split = array.reshape(pieces, depth, piece_lanes // owner_lanes, owner_lanes)
            array = jnp.moveaxis(split, 2, 1).reshape(blocks, depth, owner_lanes)
        return exchange(array)

    def from_owner(array):
        array = exchange(array)
        if owner_lanes < piece_lanes:
            split = array.reshape(pieces, piece_lanes // owner_lanes, depth, owner_lanes)
            array = jnp.moveaxis(split, 1, 2).reshape(pieces, depth, piece_lanes)
        return array

    anywhere = pl.BlockSpec(memory_space=pltpu.HBM)
    message_dims = (pieces, depth, piece_lanes)
    chunks = heads // SUMMARY_HEADS
    with jax.named_scope("summaries"):
        message, step, cum = call(
            functools.partial(summary_kernel, head_width),
            1,
            [head_spec, line_spec, line_spec, map_spec, map_spec, anywhere, anywhere],
            [(anywhere, message_dims, BF16), head_out, head_out],
            [
                ((heads, rows), F32),
                ((heads, rows), F32),
                ((META, heads), BF16),
                ((chunks, rows, summary_lanes), BF16),
                ((chunks, rows, summary_lanes), BF16),
                (message_dims, BF16),
                pltpu.SemaphoreType.DMA((2, chunks)),
                pltpu.SemaphoreType.DMA((chunks,)),
            ],
        )(step_raw, bias, decay, write_t, read_t, head_inputs, output_grad)

    place = jnp.stack([lax.axis_index("wide"), lax.axis_index("seq")]).astype(jnp.int32)
    with jax.named_scope("layer"):
        if own_model % 128:
            cut = jnp.transpose(layer_input.reshape(rows, planes, wide, own_model), (2, 1, 0, 3))
            dealt = [
                lax.dynamic_index_in_dim(cut, place[0] ^ turn, 0, False) for turn in range(wide)
            ]
        else:
            dealt = pl.pallas_call(
                deal_kernel,
                grid_spec=pltpu.PrefetchScalarGridSpec(
                    num_scalar_prefetch=1,
                    grid=(planes,),
                    in_specs=[
                        pl.BlockSpec((rows, wide * own_model), lambda i, p: (0, i)),
                        pl.BlockSpec(memory_space=pl.ANY),
                    ],
                    out_specs=[pl.BlockSpec((1, rows, own_model), lambda i, p: (i, 0, 0))] * wide,
                ),
                out_shape=[jax.ShapeDtypeStruct((planes, rows, own_model), BF16)] * wide,
                compiler_params=pltpu.CompilerParams(vmem_limit_bytes=VMEM_LIMIT),
                cost_estimate=SHORT,
            )(place, layer_input, cum)
        layer_parts = [swap(one, "wide", turn) for turn, one in enumerate(dealt)]

    firsts = [turn for turn in (1, 2, 4, 3, 5) if turn < wide]
    lasts = [layer_parts[turn] for turn in range(1, wide) if turn not in firsts]
    lasts = lasts[:-1]
    with jax.named_scope("own_block"):
        width = PAIR_HEADS * head_width
        inner, own, within, maps = call(
            functools.partial(block_kernel, head_width, scale, 0, 1),
            channels // width,
            [head_spec, head_spec, map_spec, map_spec, tokens(width), tokens(width), anywhere],
            [
                (tokens(width), (rows, channels), BF16),
                head_out,
                head_out,
                (whole((rows, 2 * state)), (rows, 2 * state), F32),
            ],
            [
                ((rows, rows), F32),
                ((rows, heads), F32),
                ((heads, rows), F32),
                ((rows, rows), F32),
                ((heads, rows), F32),
            ],
        )(step, cum, write_t, read_t, head_inputs, output_grad, dealt[0])
    with jax.named_scope("scan"):
        after = [own] + [layer_parts[turn] for turn in firsts]
        scan_lanes = min(owner_lanes, 128)
        scan_spec = pl.BlockSpec((blocks, depth, scan_lanes), lambda i: (0, 0, i))
        (answer,) = call(
            scan_kernel,
            owner_lanes // scan_lanes,
            [scan_spec] + [anywhere] * len(after),
            [(scan_spec, (blocks, depth, owner_lanes), BF16)],
            [((2, blocks, scan_lanes), F32)],
        )(to_owner(message), *after)
        returned = from_owner(answer)

    with jax.named_scope("carried"):
        (table,) = call(
            functools.partial(carry_kernel, head_width, scale, len(lasts)),
            channels // carry_lanes,
            [head_spec, line_spec, line_spec, head_spec, head_spec, map_spec, map_spec]
            + [head_spec, head_spec, whole((rows, 2 * state))]
            + [tokens(carry_lanes), tokens(carry_lanes), messages(carry_lanes)]
            + [anywhere] * len(lasts),
            [(whole((columns, rows)), (columns, rows), BF16)],
            [
                ((rows, 2 * heads + 4 * state), F32),
                ((8, heads), F32),
                ((rows, heads), F32),
                ((rows, heads), F32),
                ((rows, 4 * state), F32),
                ((2 * heads, carry_lanes), BF16),
            ],
        )(
            *(step_raw, bias, decay, step, cum, write_t, read_t, own, within, maps),
            *(head_inputs, output_grad, returned, *lasts),
        )

    with jax.named_scope("projection"):
        tables = [table]
        for turn in range(1, wide):
            tables.append(swap(tables[turn - 1], "wide", 1) if turn % 2 else swap(table, "wide", turn))
        coded = (columns + META, own_model)
        products = pl.pallas_call(
            functools.partial(product_kernel, planes, wide),
            in_specs=[pl.BlockSpec(memory_space=pltpu.SMEM)]
            + [pl.BlockSpec(memory_space=pl.ANY)] * wide
            + [anywhere] * wide,
            out_specs=[pl.BlockSpec(memory_space=pltpu.VMEM)] * planes,
            out_shape=[jax.ShapeDtypeStruct(coded, BF16)] * planes,
            scratch_shapes=[
                pltpu.VMEM((wide, columns, rows), BF16),
                pltpu.VMEM((planes, wide * rows, own_model), BF16),
                pltpu.SemaphoreType.DMA((planes + 1, wide)),
            ],
            compiler_params=pltpu.CompilerParams(vmem_limit_bytes=PRODUCT_LIMIT),
            cost_estimate=SHORT,
        )(place, *tables, *layer_parts)
        (grad_x,) = call(
            functools.partial(grad_kernel, head_width, scale),
            channels // grad_lanes,
            [head_spec, head_spec, map_spec, line_spec]
            + [tokens(grad_lanes), tokens(grad_lanes), messages(grad_lanes), anywhere],
            [(tokens(grad_lanes), (rows, channels), BF16)],
            [((rows, heads), F32), ((rows, 2 * state), BF16), ((heads, grad_lanes), BF16)],
        )(step, cum, write_t, skip, output_grad, inner, returned, products[0])
        sums = [swap(one, "seq", turn) for turn, one in enumerate(products)]
        (weight_grad,) = call(
            functools.partial(gather_kernel, 1.0 / math.sqrt(rows * blocks), planes),
            1,
            [whole(coded)] * planes + [anywhere],
            [(whole((own_model, columns)), (own_model, columns), F32)],
            [],
        )(*sums, grad_x)
    return grad_x, weight_grad


def solution(mesh):
    in_specs = (
        P(("wide", "seq"), None),
        P(("wide", "seq"), None),
        P(("wide", "seq"), None),
        P(("wide", "seq"), None),
        P(("wide", "seq"), None),
        P(("wide", "seq"), None),
        P(),
        P(),
        P(),
    )
    out_specs = (P(("wide", "seq"), None), P(("seq", "wide"), None))
    return jax.shard_map(body, mesh=mesh, in_specs=in_specs, out_specs=out_specs, check_vma=False)
```

```python
import functools
import math

import jax
import jax.numpy as jnp
from jax import lax
from jax.experimental import pallas as pl
from jax.experimental.pallas import tpu as pltpu
from jax.sharding import PartitionSpec as P

F32 = jnp.float32
BF16 = jnp.bfloat16
EXACT = lax.Precision.HIGHEST
VMEM_LIMIT = 64 * 1024 * 1024
TOP_POWER = 30.0
PRODUCT_BOUND = 30.0
LAYER_BOUND = 24.0
SUMMARY_HEADS = 32
CARRY_HEADS = 32
GRAD_HEADS = 32
PAIR_HEADS = 8
META = 8
SHORT = pl.CostEstimate(flops=1000, bytes_accessed=1000, transcendentals=0)


def mul(a, b):
    return lax.dot_general(a, b, (((1,), (0,)), ((), ())), preferred_element_type=F32)


def mul_nt(a, b):
    return lax.dot_general(a, b, (((1,), (1,)), ((), ())), preferred_element_type=F32)


def mul_exact(a, b, dims=((1,), (0,))):
    return lax.dot_general(a, b, (dims, ((), ())), preferred_element_type=F32, precision=EXACT)


def halves(value):
    top = value.astype(BF16)
    return top, (value - top.astype(F32)).astype(BF16)


def power_for(bound):
    power = jnp.floor(TOP_POWER - jnp.log2(jnp.maximum(bound, 1e-37)))
    return jnp.clip(power, -100.0, 100.0)


def thirds(value):
    top, rest = value.astype(BF16), value
    rest = rest - top.astype(F32)
    middle = rest.astype(BF16)
    return top, middle, (rest - middle.astype(F32)).astype(BF16)


def encode(value):
    square = value * value
    fourth = square * square
    return jnp.where(value < 0, -fourth, fourth).astype(BF16)


def decode(coded):
    coded = coded.astype(F32)
    size = jnp.maximum(jnp.abs(coded), 1e-37)
    inverse = lax.rsqrt(size)
    return coded * inverse * lax.rsqrt(size * inverse)


def head_selector(first_head, heads, lanes, head_width):
    row = lax.broadcasted_iota(jnp.int32, (heads, lanes), 0)
    lane = lax.broadcasted_iota(jnp.int32, (heads, lanes), 1)
    return jnp.where(row == first_head + lane // head_width, 1.0, 0.0).astype(BF16)


def triangle(length, keep):
    row = lax.broadcasted_iota(jnp.int32, (length, length), 0)
    col = lax.broadcasted_iota(jnp.int32, (length, length), 1)
    return jnp.where(keep(row, col), 1.0, 0.0).astype(F32)


def summary_kernel(
    head_width,
    raw_ref,
    bias_ref,
    decay_ref,
    write_ref,
    read_ref,
    x_ref,
    dy_ref,
    message_ref,
    step_ref,
    cum_ref,
    weight_f,
    weight_b,
    facts,
):
    turn = pl.program_id(0)
    heads = raw_ref.shape[1]
    rows, lanes = x_ref.shape
    state = write_ref.shape[0]

    @pl.when(turn == 0)
    def _():
        step = jax.nn.softplus(raw_ref[...].astype(F32) + bias_ref[...])
        rate = -jnp.exp(decay_ref[...])
        cum = mul_exact(triangle(rows, lambda r, c: r >= c), step * rate)
        finish = cum[rows - 1 : rows, :]
        forward = step * jnp.exp(finish - cum)
        backward = jnp.exp(cum)
        power_f = power_for(PRODUCT_BOUND * jnp.sum(forward, axis=0, keepdims=True))
        power_b = power_for(PRODUCT_BOUND * jnp.sum(backward, axis=0, keepdims=True))
        step_ref[...] = step
        cum_ref[...] = cum
        parts = thirds(jnp.maximum(finish, -1e30))
        facts[...] = jnp.concatenate(
            [part.astype(F32) for part in parts]
            + [power_f, power_b, jnp.zeros((META - 5, heads), F32)],
            axis=0,
        ).astype(BF16)
        weight_f[...] = (forward * jnp.exp2(power_f)).T
        weight_b[...] = (backward * jnp.exp2(power_b)).T

    group = lanes // head_width
    pair_lanes = 2 * head_width
    width = message_ref.shape[2]
    near = pl.ds(turn * group, group)
    pick = head_selector(turn * group, heads, lanes, head_width)
    fact = mul(facts[...], pick).astype(BF16)
    lane = lax.broadcasted_iota(jnp.int32, (state, pair_lanes), 1)
    ahead = (x_ref, write_ref[...].astype(F32), weight_f[near, :], 0)
    behind = (dy_ref, read_ref[...].astype(F32), weight_b[near, :], state)
    for pair in range(group // 2):
        span = slice(pair * pair_lanes, (pair + 1) * pair_lanes)
        owner, offset = pair * pair_lanes // width, pair * pair_lanes % width
        here = slice(offset, offset + pair_lanes)
        for tokens_ref, rows_t, weights, start in (ahead, behind):
            scaled = []
            for head in (2 * pair, 2 * pair + 1):
                scaled += halves(rows_t * weights[head : head + 1, :])
            product = mul(jnp.concatenate(scaled, axis=0), tokens_ref[:, span])
            early = product[0:state] + product[state : 2 * state]
            late = product[2 * state : 3 * state] + product[3 * state :]
            total = jnp.where(lane < head_width, early, late)
            message_ref[owner, start : start + state, here] = encode(total)
        message_ref[owner, 2 * state :, here] = fact[:, span]


def scan_kernel(message_ref, *rest):
    answer_ref, powers = rest[-2:]
    blocks, double, lanes = message_ref.shape
    state = (double - META) // 2
    top = 2.0**TOP_POWER

    def one(block, start, power_row, side, running, bound):
        facts = message_ref[block, 2 * state : double, :].astype(F32)
        decay = jnp.exp(facts[0:1] + facts[1:2] + facts[2:3])
        back = jnp.exp2(-facts[power_row : power_row + 1])
        power = power_for(bound)
        powers[side, pl.ds(block, 1), :] = power
        answer_ref[block, start : start + state, :] = encode(running * jnp.exp2(power))
        own = decode(message_ref[block, start : start + state, :]) * back
        return running * decay + own, bound * decay + top * back

    def both(block, carry):
        ahead, ahead_bound, behind, behind_bound = carry
        return one(block, 0, 3, 0, ahead, ahead_bound) + one(
            blocks - 1 - block, state, 4, 1, behind, behind_bound
        )

    zero, none = jnp.zeros((state, lanes), F32), jnp.zeros((1, lanes), F32)
    lax.fori_loop(0, blocks, both, (zero, none, zero, none), unroll=8)
    row = lax.broadcasted_iota(jnp.int32, (blocks, META, lanes), 1)
    ahead, behind = powers[0][:, None, :], powers[1][:, None, :]
    meta = jnp.where(row == 0, ahead, jnp.where(row == 1, behind, 0.0))
    answer_ref[:, 2 * state : double, :] = meta.astype(BF16)


def block_kernel(
    head_width,
    scale,
    first_head,
    waits,
    step_ref,
    cum_ref,
    write_ref,
    read_ref,
    x_ref,
    dy_ref,
    *rest,
):
    inner_ref, own_ref, within_ref, maps_ref = rest[waits : waits + 4]
    read_write, source, cum_rows, pair_sum, out_flow = rest[waits + 4 :]
    turn = pl.program_id(0)
    rows, lanes = x_ref.shape
    half = rows // 2
    heads = step_ref.shape[1]
    group = lanes // head_width

    @pl.when(turn == 0)
    def _():
        read_write[...] = scale * lax.dot_general(
            write_ref[...], read_ref[...], (((0,), (0,)), ((), ())), preferred_element_type=F32
        )
        source[...] = jnp.log(step_ref[...]) - cum_ref[...]
        cum_rows[...] = cum_ref[...].T
        pair_sum[...] = jnp.zeros_like(pair_sum)
        out_flow[...] = jnp.zeros_like(out_flow)
        own_ref[...] = jnp.zeros_like(own_ref)

    first = first_head + turn * group
    near = pltpu.roll(source[...], lax.rem(heads - first, heads), axis=1)
    near_cum = cum_rows[pl.ds(first, group), :]
    row = lax.broadcasted_iota(jnp.int32, (half, half), 0)
    col = lax.broadcasted_iota(jnp.int32, (half, half), 1)
    ahead = col >= row
    lane = lax.broadcasted_iota(jnp.int32, (half, 2 * head_width), 1)
    first_half = lane < head_width
    head_lane = lax.broadcasted_iota(jnp.int32, (half, heads), 1)
    flow_aa = read_write[0:half, 0:half]
    flow_ab = read_write[0:half, half:rows]
    flow_bb = read_write[half:rows, half:rows]
    sum_aa = jnp.zeros((half, half), F32)
    sum_ab = jnp.zeros((half, half), F32)
    sum_bb = jnp.zeros((half, half), F32)
    own_a = jnp.zeros((half, heads), F32)
    own_b = jnp.zeros((half, heads), F32)
    zero = jnp.zeros((half, 2 * head_width), BF16)
    flows = []
    for pair in range(group // 2):
        span = slice(pair * 2 * head_width, (pair + 1) * 2 * head_width)
        x_a, x_b = x_ref[0:half, span], x_ref[half:rows, span]
        dy_a, dy_b = dy_ref[0:half, span], dy_ref[half:rows, span]
        early_a, late_a = jnp.where(first_half, dy_a, zero), jnp.where(first_half, zero, dy_a)
        early_b, late_b = jnp.where(first_half, dy_b, zero), jnp.where(first_half, zero, dy_b)
        stack = jnp.concatenate([early_a, early_b, late_a, late_b], axis=0)
        stack_b = jnp.concatenate([early_b, late_b], axis=0)
        grad_a = mul_nt(x_a, stack)
        grad_b = mul_nt(x_b, stack_b)
        masks_a, masks_b = [], []
        for side in range(2):
            place = pair * 2 + side
            head = first + place
            from_a = near[0:half, place : place + 1]
            from_b = near[half:rows, place : place + 1]
            to_a = near_cum[place : place + 1, 0:half]
            to_b = near_cum[place : place + 1, half:rows]
            fade_aa = jnp.exp(jnp.where(ahead, to_a + from_a, -1e30))
            fade_ab = jnp.exp(to_b + from_a)
            fade_bb = jnp.exp(jnp.where(ahead, to_b + from_b, -1e30))
            weigh_aa = fade_aa * grad_a[:, side * rows : side * rows + half]
            weigh_ab = fade_ab * grad_a[:, side * rows + half : (side + 1) * rows]
            weigh_bb = fade_bb * grad_b[:, side * half : (side + 1) * half]
            sum_aa += weigh_aa
            sum_ab += weigh_ab
            sum_bb += weigh_bb
            masks_a += [(fade_aa * flow_aa).astype(BF16), (fade_ab * flow_ab).astype(BF16)]
            masks_b += [(fade_bb * flow_bb).astype(BF16)]
            pair_aa = weigh_aa * flow_aa
            pair_ab = weigh_ab * flow_ab
            pair_bb = weigh_bb * flow_bb
            flow_out = jnp.sum(pair_aa + pair_ab, axis=1, keepdims=True)
            own_a = jnp.where(head_lane == head, flow_out, own_a)
            flow_out = jnp.sum(pair_bb, axis=1, keepdims=True)
            own_b = jnp.where(head_lane == head, flow_out, own_b)
            flow_in = [
                jnp.sum(pair_aa, axis=0, keepdims=True),
                jnp.sum(pair_ab, axis=0, keepdims=True) + jnp.sum(pair_bb, axis=0, keepdims=True),
            ]
            flows.append(jnp.concatenate(flow_in, axis=1))
        inner_ref[0:half, span] = mul(jnp.concatenate(masks_a, axis=1), stack).astype(BF16)
        inner_ref[half:rows, span] = mul(jnp.concatenate(masks_b, axis=1), stack_b).astype(BF16)
    out_flow[pl.ds(first, group), :] = jnp.concatenate(flows, axis=0)
    pair_sum[0:half, 0:half] += sum_aa
    pair_sum[0:half, half:rows] += sum_ab
    pair_sum[half:rows, half:rows] += sum_bb
    own_ref[0:half, :] += own_a
    own_ref[half:rows, :] += own_b

    @pl.when(turn == pl.num_programs(0) - 1)
    def _():
        net = own_ref[...] - out_flow[...].T
        within_ref[...] = mul_exact(triangle(rows, lambda r, c: r > c), net)
        weighted = scale * pair_sum[...]
        maps_ref[...] = jnp.concatenate(
            [
                mul_exact(weighted, read_ref[...].astype(F32), ((1,), (1,))),
                mul_exact(weighted, write_ref[...].astype(F32), ((0,), (1,))),
            ],
            axis=1,
        )


def spread_heads(weight, first_head, picks, group):
    heads = weight.shape[1]
    near = pltpu.roll(weight, lax.rem(heads - first_head, heads), axis=1)
    top = near.astype(BF16).astype(F32)
    low = pltpu.roll(near - top, group, axis=1)
    lane = lax.broadcasted_iota(jnp.int32, near.shape, 1)
    return mul(jnp.where(lane < group, top, low).astype(BF16), picks)


def spread_picks(group, heads, lanes, head_width):
    row = lax.broadcasted_iota(jnp.int32, (heads, lanes), 0)
    lane = lax.broadcasted_iota(jnp.int32, (heads, lanes), 1)
    match = jnp.where(row < group, row, row - group) == lane // head_width
    return jnp.where(match, 1.0, 0.0).astype(BF16)


def read_answer(answer_ref, state, power_row):
    found = []
    start = power_row * state
    for piece in range(answer_ref.shape[0]):
        facts = answer_ref[piece, 2 * state :, :].astype(F32)
        back = jnp.exp2(-facts[power_row : power_row + 1])
        found.append(decode(answer_ref[piece, start : start + state, :]) * back)
    return jnp.concatenate(found, axis=1)


def carry_kernel(head_width, scale, waits, *refs):
    raw_ref, bias_ref, decay_ref, step_ref, cum_ref, write_ref, read_ref = refs[:7]
    own_ref, within_ref, map_ref, x_ref, dy_ref, answer_ref = refs[7:13]
    table_ref, sums, through, weight_e, weight_s, maps, picks = refs[13 + waits :]
    turn = pl.program_id(0)
    rows, lanes = x_ref.shape
    heads = step_ref.shape[1]
    state = write_ref.shape[0]
    group = lanes // head_width
    pair_lanes = 2 * head_width
    future, past = slice(0, heads), slice(heads, 2 * heads)
    write_sum = slice(2 * heads, 2 * heads + 2 * state)
    read_sum = slice(2 * heads + 2 * state, 2 * heads + 4 * state)

    @pl.when(turn == 0)
    def _():
        cum = cum_ref[...]
        finish = cum[rows - 1 : rows, :]
        weight_e[...] = step_ref[...] * jnp.exp(finish - cum) * scale
        weight_s[...] = jnp.exp(cum) * scale
        write, read = write_ref[...].astype(F32).T, read_ref[...].astype(F32).T
        maps[...] = jnp.concatenate([write, write, read, read], axis=1)
        picks[0:heads, :] = spread_picks(group, heads, lanes, head_width)
        picks[heads:, :] = head_selector(0, heads, lanes, head_width)
        sums[...] = jnp.zeros_like(sums)
        through[...] = jnp.zeros_like(through)

    first_here = turn * group
    pick = picks[heads:, :]
    early = lax.broadcasted_iota(jnp.int32, (state, pair_lanes), 1) < head_width
    none = jnp.zeros((state, pair_lanes), BF16)
    start = read_answer(answer_ref, state, 0)
    end = read_answer(answer_ref, state, 1)

    def products(tokens_ref, states, weight, map_columns):
        spread = spread_heads(weight[...], first_here, picks[0:heads, :], group)
        parts = halves(states)
        total, mapped = 0.0, []
        for pair in range(group // 2):
            span = slice(pair * pair_lanes, (pair + 1) * pair_lanes)
            blocks = [
                jnp.concatenate(
                    [jnp.where(early, part[:, span], none), jnp.where(early, none, part[:, span])],
                    axis=0,
                )
                for part in parts
            ]
            twice = jnp.concatenate([tokens_ref[:, span], tokens_ref[:, span]], axis=1)
            weighted = mul_nt(twice, jnp.concatenate(blocks, axis=1)) * spread[:, span]
            total += weighted
            mapped.append((weighted * map_columns).astype(BF16))
        return total, mapped

    def summed(parts):
        return mul_nt(jnp.concatenate(parts, axis=1), pick)

    def placed(value):
        return pltpu.roll(value, first_here, axis=1)

    total, mapped = products(x_ref, end, weight_e, maps[:, 0 : 2 * state])
    sums[:, write_sum] += total
    sums[:, future] += placed(summed(mapped))

    total, mapped = products(dy_ref, start, weight_s, maps[:, 2 * state : 4 * state])
    sums[:, read_sum] += total
    sums[:, past] += placed(summed(mapped))

    both = jnp.broadcast_to(jnp.sum(start * end, axis=0, keepdims=True), (8, lanes))
    top, low = halves(both)
    through[...] += placed(mul_nt(top, pick) + mul_nt(low, pick))

    @pl.when(turn == pl.num_programs(0) - 1)
    def _():
        rate = -jnp.exp(decay_ref[...])
        step = step_ref[...]
        gate = jax.nn.sigmoid(raw_ref[...].astype(F32) + bias_ref[...])
        finish = cum_ref[rows - 1 : rows, :]
        ahead = sums[:, future]
        decay_grad = (
            within_ref[...]
            + mul_exact(triangle(rows, lambda r, c: r <= c), sums[:, past])
            + mul_exact(triangle(rows, lambda r, c: r > c), ahead)
            + jnp.exp(finish) * scale * through[0:1, :]
        )
        ratio = jnp.where(step > 1e-30, gate / jnp.maximum(step, 1e-30), 1.0)
        raw_grad = (own_ref[...] + ahead) * ratio + rate * decay_grad * gate
        map_sum = sums[:, 2 * heads :]
        write_all = map_sum[:, 0:state] + map_sum[:, state : 2 * state]
        read_all = map_sum[:, 2 * state : 3 * state] + map_sum[:, 3 * state :]
        map_grad = jnp.concatenate([write_all, read_all], axis=1) + map_ref[...]
        table_ref[...] = jnp.concatenate([raw_grad.T, map_grad.T], axis=0).astype(BF16)


def grad_kernel(head_width, scale, first_head, waits, *refs):
    step_ref, cum_ref, write_ref, skip_ref, dy_ref, inner_ref, answer_ref = refs[:7]
    grad_ref, weight_e, maps, picks = refs[7 + waits :]
    turn = pl.program_id(0)
    rows, lanes = dy_ref.shape
    heads = step_ref.shape[1]
    state = write_ref.shape[0]
    group = lanes // head_width

    @pl.when(turn == 0)
    def _():
        cum = cum_ref[...]
        finish = cum[rows - 1 : rows, :]
        weight_e[...] = step_ref[...] * jnp.exp(finish - cum) * scale
        write = write_ref[...].astype(F32).T.astype(BF16)
        maps[...] = jnp.concatenate([write, write], axis=1)
        picks[...] = spread_picks(group, heads, lanes, head_width)

    first_here = first_head + turn * group
    end_parts = jnp.concatenate(halves(read_answer(answer_ref, state, 1)), axis=0)
    skip = jnp.broadcast_to(skip_ref[...], (16, heads))
    skip = spread_heads(skip, first_here, picks[...], group)[0:1]
    carried = mul(maps[...], end_parts) * spread_heads(weight_e[...], first_here, picks[...], group)
    inner = inner_ref[...].astype(F32)
    grad_ref[...] = (inner + skip * dy_ref[...].astype(F32) + carried).astype(BF16)


def deal_kernel(place_ref, layer_ref, after_ref, *out_refs):
    width = out_refs[0].shape[2]
    for turn, out_ref in enumerate(out_refs):
        start = pl.multiple_of((place_ref[0] ^ turn) * width, width)
        out_ref[0, :, :] = layer_ref[:, pl.ds(start, width)]


def product_kernel(planes, wide, place_ref, *refs):
    table_refs, layer_refs = refs[:wide], refs[wide : 2 * wide]
    out_refs = refs[-3 - planes : -3]
    table_all, layer_all, sems = refs[-3:]
    columns, rows = table_refs[0].shape
    loads = [
        pltpu.make_async_copy(ref, table_all.at[turn], sems.at[planes, turn])
        for turn, ref in enumerate(table_refs)
    ]
    for plane in range(planes):
        source = place_ref[1] ^ plane
        loads += [
            pltpu.make_async_copy(
                ref.at[source], layer_all.at[plane, pl.ds(turn * rows, rows)], sems.at[plane, turn]
            )
            for turn, ref in enumerate(layer_refs)
        ]
    for load in loads:
        load.start()
    for load in loads[:wide]:
        load.wait()
    table = jnp.concatenate([table_all[turn] for turn in range(wide)], axis=1)
    most = jnp.max(jnp.abs(table.astype(F32)), axis=0, keepdims=True)
    most = jnp.max(most, axis=1, keepdims=True)
    power = power_for(LAYER_BOUND * wide * rows * most)
    forth = jnp.exp2(power)
    for plane, out_ref in enumerate(out_refs):
        for load in loads[(plane + 1) * wide : (plane + 2) * wide]:
            load.wait()
        out_ref[0:columns, :] = encode(mul(table, layer_all[plane]) * forth)
        out_ref[columns:, :] = jnp.broadcast_to(power, out_ref[columns:, :].shape).astype(BF16)


def gather_kernel(factor, planes, *refs):
    part_refs, out_ref = refs[:planes], refs[-1]
    columns = out_ref.shape[1]
    total = jnp.zeros((columns, out_ref.shape[0]), F32)
    for part_ref in part_refs:
        power = part_ref[columns:, :].astype(F32)[0:1]
        total += decode(part_ref[0:columns, :]) * jnp.exp2(-power)
    out_ref[...] = (total * factor).T


def swap(array, axis, turn):
    if turn == 0:
        return array
    count = lax.axis_size(axis)
    return lax.ppermute(array, axis, [(one, one ^ turn) for one in range(count)])


def whole(shape):
    return pl.BlockSpec(shape, lambda i: (0,) * len(shape))


def call(kernel, steps, in_specs, out, scratch, aliases=None):
    return pl.pallas_call(
        kernel,
        grid=(steps,),
        in_specs=in_specs,
        out_specs=[spec for spec, _, _ in out],
        out_shape=[jax.ShapeDtypeStruct(dims, dtype) for _, dims, dtype in out],
        scratch_shapes=[pltpu.VMEM(dims, dtype) for dims, dtype in scratch],
        compiler_params=pltpu.CompilerParams(vmem_limit_bytes=VMEM_LIMIT),
        cost_estimate=SHORT,
        input_output_aliases=aliases or {},
    )


def body(
    layer_input,
    head_inputs,
    output_grad,
    step_raw,
    state_write,
    state_read,
    decay_log,
    step_bias,
    skip_gain,
):
    rows, channels = head_inputs.shape
    heads = step_raw.shape[1]
    head_width = channels // heads
    state = state_write.shape[1]
    model = layer_input.shape[1]
    columns = heads + 2 * state
    axes = ("wide", "seq")
    wide, planes = lax.axis_size("wide"), lax.axis_size("seq")
    blocks = wide * planes
    own_model = model // blocks
    scale = float(rows * blocks * state) ** -0.5
    owner_lanes = channels // blocks
    piece_lanes = max(owner_lanes, 128)
    pieces = channels // piece_lanes
    depth = 2 * state + META
    bias = step_bias[None, :]
    decay = decay_log[None, :]
    skip = skip_gain[None, :]
    write_t, read_t = state_write.T, state_read.T

    summary_lanes = SUMMARY_HEADS * head_width
    carry_lanes = CARRY_HEADS * head_width
    grad_lanes = GRAD_HEADS * head_width

    def tokens(width, first=0):
        return pl.BlockSpec((rows, width), lambda i: (0, first + i))

    def messages(width, first=0):
        return pl.BlockSpec((width // piece_lanes, depth, piece_lanes), lambda i: (first + i, 0, 0))

    head_spec = whole((rows, heads))
    line_spec = whole((1, heads))
    map_spec = whole((state, rows))
    head_out = (head_spec, (rows, heads), F32)

    def exchange(array):
        return lax.all_to_all(array, axes, split_axis=0, concat_axis=0, tiled=True)

    def to_owner(array):
        if owner_lanes < piece_lanes:
            split = array.reshape(pieces, depth, piece_lanes // owner_lanes, owner_lanes)
            array = jnp.moveaxis(split, 2, 1).reshape(blocks, depth, owner_lanes)
        return exchange(array)

    def from_owner(array):
        array = exchange(array)
        if owner_lanes < piece_lanes:
            split = array.reshape(pieces, piece_lanes // owner_lanes, depth, owner_lanes)
            array = jnp.moveaxis(split, 1, 2).reshape(pieces, depth, piece_lanes)
        return array

    with jax.named_scope("summaries"):
        message, step, cum = call(
            functools.partial(summary_kernel, head_width),
            channels // summary_lanes,
            [head_spec, line_spec, line_spec, map_spec, map_spec]
            + [tokens(summary_lanes), tokens(summary_lanes)],
            [
                (messages(summary_lanes), (pieces, depth, piece_lanes), BF16),
                head_out,
                head_out,
            ],
            [((heads, rows), F32), ((heads, rows), F32), ((META, heads), BF16)],
        )(step_raw, bias, decay, write_t, read_t, head_inputs, output_grad)
    place = jnp.stack([lax.axis_index("wide"), lax.axis_index("seq")]).astype(jnp.int32)
    with jax.named_scope("layer"):
        if own_model % 128:
            cut = jnp.transpose(layer_input.reshape(rows, planes, wide, own_model), (2, 1, 0, 3))
            dealt = [
                lax.dynamic_index_in_dim(cut, place[0] ^ turn, 0, False) for turn in range(wide)
            ]
        else:
            dealt = pl.pallas_call(
                deal_kernel,
                grid_spec=pltpu.PrefetchScalarGridSpec(
                    num_scalar_prefetch=1,
                    grid=(planes,),
                    in_specs=[
                        pl.BlockSpec((rows, wide * own_model), lambda i, p: (0, i)),
                        pl.BlockSpec(memory_space=pl.ANY),
                    ],
                    out_specs=[pl.BlockSpec((1, rows, own_model), lambda i, p: (i, 0, 0))] * wide,
                ),
                out_shape=[jax.ShapeDtypeStruct((planes, rows, own_model), BF16)] * wide,
                compiler_params=pltpu.CompilerParams(vmem_limit_bytes=VMEM_LIMIT),
                cost_estimate=SHORT,
            )(place, layer_input, cum)
        layer_parts = [swap(one, "wide", turn) for turn, one in enumerate(dealt)]

    anywhere = pl.BlockSpec(memory_space=pltpu.HBM)
    firsts = [turn for turn in (1, 2, 4, 3, 5) if turn < wide]
    lasts = [layer_parts[turn] for turn in range(1, wide) if turn not in firsts]
    lasts, latest = lasts[:-1], lasts[-1:]
    with jax.named_scope("own_block"):
        width = PAIR_HEADS * head_width
        inner, own, within, maps = call(
            functools.partial(block_kernel, head_width, scale, 0, 1),
            channels // width,
            [head_spec, head_spec, map_spec, map_spec, tokens(width), tokens(width), anywhere],
            [
                (tokens(width), (rows, channels), BF16),
                head_out,
                head_out,
                (whole((rows, 2 * state)), (rows, 2 * state), F32),
            ],
            [
                ((rows, rows), F32),
                ((rows, heads), F32),
                ((heads, rows), F32),
                ((rows, rows), F32),
                ((heads, rows), F32),
            ],
        )(step, cum, write_t, read_t, head_inputs, output_grad, dealt[0])
    with jax.named_scope("scan"):
        after = [own] + [layer_parts[turn] for turn in firsts]
        scan_lanes = min(owner_lanes, 128)
        scan_spec = pl.BlockSpec((blocks, depth, scan_lanes), lambda i: (0, 0, i))
        (answer,) = call(
            scan_kernel,
            owner_lanes // scan_lanes,
            [scan_spec] + [anywhere] * len(after),
            [(scan_spec, (blocks, depth, owner_lanes), BF16)],
            [((2, blocks, scan_lanes), F32)],
        )(to_owner(message), *after)
        returned = from_owner(answer)

    with jax.named_scope("carried"):
        (table,) = call(
            functools.partial(carry_kernel, head_width, scale, len(lasts)),
            channels // carry_lanes,
            [head_spec, line_spec, line_spec, head_spec, head_spec, map_spec, map_spec]
            + [head_spec, head_spec, whole((rows, 2 * state))]
            + [tokens(carry_lanes), tokens(carry_lanes), messages(carry_lanes)]
            + [anywhere] * len(lasts),
            [(whole((columns, rows)), (columns, rows), BF16)],
            [
                ((rows, 2 * heads + 4 * state), F32),
                ((8, heads), F32),
                ((rows, heads), F32),
                ((rows, heads), F32),
                ((rows, 4 * state), F32),
                ((2 * heads, carry_lanes), BF16),
            ],
        )(
            *(step_raw, bias, decay, step, cum, write_t, read_t, own, within, maps),
            *(head_inputs, output_grad, returned, *lasts),
        )

    def grad_part_of(first, last, grad, keep):
        in_specs = [head_spec, head_spec, map_spec, line_spec]
        in_specs += [tokens(grad_lanes, first), tokens(grad_lanes, first)]
        in_specs += [messages(grad_lanes, first)]
        in_specs += [anywhere] * len(grad)
        (grad,) = call(
            functools.partial(grad_kernel, head_width, scale, first * GRAD_HEADS, len(grad)),
            last - first,
            in_specs,
            [(tokens(grad_lanes, first), (rows, channels), BF16)],
            [((rows, heads), F32), ((rows, 2 * state), BF16), ((heads, grad_lanes), BF16)],
            {len(in_specs) - 1: 0} if keep else {},
        )(step, cum, write_t, skip, output_grad, inner, returned, *grad)
        return grad

    grad_steps = channels // grad_lanes
    with jax.named_scope("grad_x"):
        grad_first = grad_part_of(0, 1, [table] + latest, False)

    with jax.named_scope("projection"):
        tables = [table]
        for turn in range(1, wide):
            tables.append(swap(tables[turn - 1], "wide", 1) if turn % 2 else swap(table, "wide", turn))
        coded = (columns + META, own_model)
        products = pl.pallas_call(
            functools.partial(product_kernel, planes, wide),
            in_specs=[pl.BlockSpec(memory_space=pltpu.SMEM)] + [anywhere] * (2 * wide + 1),
            out_specs=[pl.BlockSpec(memory_space=pltpu.VMEM)] * planes,
            out_shape=[jax.ShapeDtypeStruct(coded, BF16)] * planes,
            scratch_shapes=[
                pltpu.VMEM((wide, columns, rows), BF16),
                pltpu.VMEM((planes, wide * rows, own_model), BF16),
                pltpu.SemaphoreType.DMA((planes + 1, wide)),
            ],
            compiler_params=pltpu.CompilerParams(vmem_limit_bytes=VMEM_LIMIT),
            cost_estimate=SHORT,
        )(place, *tables, *layer_parts, grad_first)
        grad_x = grad_part_of(1, grad_steps, [products[0], grad_first], True)
        sums = [swap(one, "seq", turn) for turn, one in enumerate(products)]
        (weight_grad,) = call(
            functools.partial(gather_kernel, 1.0 / math.sqrt(rows * blocks), planes),
            1,
            [whole(coded)] * planes + [anywhere],
            [(whole((own_model, columns)), (own_model, columns), F32)],
            [],
        )(*sums, grad_x)
    return grad_x, weight_grad


def solution(mesh):
    in_specs = (
        P(("wide", "seq"), None),
        P(("wide", "seq"), None),
        P(("wide", "seq"), None),
        P(("wide", "seq"), None),
        P(("wide", "seq"), None),
        P(("wide", "seq"), None),
        P(),
        P(),
        P(),
    )
    out_specs = (P(("wide", "seq"), None), P(("seq", "wide"), None))
    return jax.shard_map(body, mesh=mesh, in_specs=in_specs, out_specs=out_specs, check_vma=False)
```

```python
import functools
import math

import jax
import jax.numpy as jnp
from jax import lax
from jax.experimental import pallas as pl
from jax.experimental.pallas import tpu as pltpu
from jax.sharding import PartitionSpec as P

F32 = jnp.float32
BF16 = jnp.bfloat16
EXACT = lax.Precision.HIGHEST
VMEM_LIMIT = 64 * 1024 * 1024
TOP_POWER = 30.0
PRODUCT_BOUND = 30.0
LAYER_BOUND = 24.0
SUMMARY_HEADS = 32
CARRY_HEADS = 32
GRAD_HEADS = 32
PAIR_HEADS = 8
META = 8
SHORT = pl.CostEstimate(flops=1000, bytes_accessed=1000, transcendentals=0)


def mul(a, b):
    return lax.dot_general(a, b, (((1,), (0,)), ((), ())), preferred_element_type=F32)


def mul_nt(a, b):
    return lax.dot_general(a, b, (((1,), (1,)), ((), ())), preferred_element_type=F32)


def mul_exact(a, b, dims=((1,), (0,))):
    return lax.dot_general(a, b, (dims, ((), ())), preferred_element_type=F32, precision=EXACT)


def halves(value):
    top = value.astype(BF16)
    return top, (value - top.astype(F32)).astype(BF16)


def power_for(bound):
    power = jnp.floor(TOP_POWER - jnp.log2(jnp.maximum(bound, 1e-37)))
    return jnp.clip(power, -100.0, 100.0)


def thirds(value):
    top, rest = value.astype(BF16), value
    rest = rest - top.astype(F32)
    middle = rest.astype(BF16)
    return top, middle, (rest - middle.astype(F32)).astype(BF16)


def encode(value):
    square = value * value
    fourth = square * square
    return jnp.where(value < 0, -fourth, fourth).astype(BF16)


def decode(coded):
    coded = coded.astype(F32)
    size = jnp.maximum(jnp.abs(coded), 1e-37)
    inverse = lax.rsqrt(size)
    return coded * inverse * lax.rsqrt(size * inverse)


def head_selector(first_head, heads, lanes, head_width):
    row = lax.broadcasted_iota(jnp.int32, (heads, lanes), 0)
    lane = lax.broadcasted_iota(jnp.int32, (heads, lanes), 1)
    return jnp.where(row == first_head + lane // head_width, 1.0, 0.0).astype(BF16)


def triangle(length, keep):
    row = lax.broadcasted_iota(jnp.int32, (length, length), 0)
    col = lax.broadcasted_iota(jnp.int32, (length, length), 1)
    return jnp.where(keep(row, col), 1.0, 0.0).astype(F32)


def summary_kernel(
    head_width,
    raw_ref,
    bias_ref,
    decay_ref,
    write_ref,
    read_ref,
    x_ref,
    dy_ref,
    message_ref,
    step_ref,
    cum_ref,
    weight_f,
    weight_b,
    facts,
):
    turn = pl.program_id(0)
    heads = raw_ref.shape[1]
    rows, lanes = x_ref.shape
    state = write_ref.shape[0]

    @pl.when(turn == 0)
    def _():
        step = jax.nn.softplus(raw_ref[...].astype(F32) + bias_ref[...])
        rate = -jnp.exp(decay_ref[...])
        cum = mul_exact(triangle(rows, lambda r, c: r >= c), step * rate)
        finish = cum[rows - 1 : rows, :]
        forward = step * jnp.exp(finish - cum)
        backward = jnp.exp(cum)
        power_f = power_for(PRODUCT_BOUND * jnp.sum(forward, axis=0, keepdims=True))
        power_b = power_for(PRODUCT_BOUND * jnp.sum(backward, axis=0, keepdims=True))
        step_ref[...] = step
        cum_ref[...] = cum
        parts = thirds(jnp.maximum(finish, -1e30))
        facts[...] = jnp.concatenate(
            [part.astype(F32) for part in parts]
            + [power_f, power_b, jnp.zeros((META - 5, heads), F32)],
            axis=0,
        ).astype(BF16)
        weight_f[...] = (forward * jnp.exp2(power_f)).T
        weight_b[...] = (backward * jnp.exp2(power_b)).T

    group = lanes // head_width
    pair_lanes = 2 * head_width
    width = message_ref.shape[2]
    near = pl.ds(turn * group, group)
    pick = head_selector(turn * group, heads, lanes, head_width)
    fact = mul(facts[...], pick).astype(BF16)
    lane = lax.broadcasted_iota(jnp.int32, (state, pair_lanes), 1)
    ahead = (x_ref, write_ref[...].astype(F32), weight_f[near, :], 0)
    behind = (dy_ref, read_ref[...].astype(F32), weight_b[near, :], state)
    for pair in range(group // 2):
        span = slice(pair * pair_lanes, (pair + 1) * pair_lanes)
        owner, offset = pair * pair_lanes // width, pair * pair_lanes % width
        here = slice(offset, offset + pair_lanes)
        for tokens_ref, rows_t, weights, start in (ahead, behind):
            scaled = []
            for head in (2 * pair, 2 * pair + 1):
                scaled += halves(rows_t * weights[head : head + 1, :])
            product = mul(jnp.concatenate(scaled, axis=0), tokens_ref[:, span])
            early = product[0:state] + product[state : 2 * state]
            late = product[2 * state : 3 * state] + product[3 * state :]
            total = jnp.where(lane < head_width, early, late)
            message_ref[owner, start : start + state, here] = encode(total)
        message_ref[owner, 2 * state :, here] = fact[:, span]


def scan_kernel(message_ref, *rest):
    answer_ref, powers = rest[-2:]
    blocks, double, lanes = message_ref.shape
    state = (double - META) // 2
    top = 2.0**TOP_POWER

    def one(block, start, power_row, side, running, bound):
        facts = message_ref[block, 2 * state : double, :].astype(F32)
        decay = jnp.exp(facts[0:1] + facts[1:2] + facts[2:3])
        back = jnp.exp2(-facts[power_row : power_row + 1])
        power = power_for(bound)
        powers[side, pl.ds(block, 1), :] = power
        answer_ref[block, start : start + state, :] = encode(running * jnp.exp2(power))
        own = decode(message_ref[block, start : start + state, :]) * back
        return running * decay + own, bound * decay + top * back

    def both(block, carry):
        ahead, ahead_bound, behind, behind_bound = carry
        return one(block, 0, 3, 0, ahead, ahead_bound) + one(
            blocks - 1 - block, state, 4, 1, behind, behind_bound
        )

    zero, none = jnp.zeros((state, lanes), F32), jnp.zeros((1, lanes), F32)
    lax.fori_loop(0, blocks, both, (zero, none, zero, none), unroll=8)
    row = lax.broadcasted_iota(jnp.int32, (blocks, META, lanes), 1)
    ahead, behind = powers[0][:, None, :], powers[1][:, None, :]
    meta = jnp.where(row == 0, ahead, jnp.where(row == 1, behind, 0.0))
    answer_ref[:, 2 * state : double, :] = meta.astype(BF16)


def block_kernel(
    head_width,
    scale,
    first_head,
    waits,
    step_ref,
    cum_ref,
    write_ref,
    read_ref,
    x_ref,
    dy_ref,
    *rest,
):
    inner_ref, own_ref, within_ref, maps_ref = rest[waits : waits + 4]
    read_write, source, cum_rows, pair_sum, out_flow = rest[waits + 4 :]
    turn = pl.program_id(0)
    rows, lanes = x_ref.shape
    half = rows // 2
    heads = step_ref.shape[1]
    group = lanes // head_width

    @pl.when(turn == 0)
    def _():
        read_write[...] = scale * lax.dot_general(
            write_ref[...], read_ref[...], (((0,), (0,)), ((), ())), preferred_element_type=F32
        )
        source[...] = jnp.log(step_ref[...]) - cum_ref[...]
        cum_rows[...] = cum_ref[...].T
        pair_sum[...] = jnp.zeros_like(pair_sum)
        out_flow[...] = jnp.zeros_like(out_flow)
        own_ref[...] = jnp.zeros_like(own_ref)

    first = first_head + turn * group
    near = pltpu.roll(source[...], lax.rem(heads - first, heads), axis=1)
    near_cum = cum_rows[pl.ds(first, group), :]
    row = lax.broadcasted_iota(jnp.int32, (half, half), 0)
    col = lax.broadcasted_iota(jnp.int32, (half, half), 1)
    ahead = col >= row
    lane = lax.broadcasted_iota(jnp.int32, (half, 2 * head_width), 1)
    first_half = lane < head_width
    head_lane = lax.broadcasted_iota(jnp.int32, (half, heads), 1)
    flow_aa = read_write[0:half, 0:half]
    flow_ab = read_write[0:half, half:rows]
    flow_bb = read_write[half:rows, half:rows]
    sum_aa = jnp.zeros((half, half), F32)
    sum_ab = jnp.zeros((half, half), F32)
    sum_bb = jnp.zeros((half, half), F32)
    own_a = jnp.zeros((half, heads), F32)
    own_b = jnp.zeros((half, heads), F32)
    zero = jnp.zeros((half, 2 * head_width), BF16)
    flows = []
    for pair in range(group // 2):
        span = slice(pair * 2 * head_width, (pair + 1) * 2 * head_width)
        x_a, x_b = x_ref[0:half, span], x_ref[half:rows, span]
        dy_a, dy_b = dy_ref[0:half, span], dy_ref[half:rows, span]
        early_a, late_a = jnp.where(first_half, dy_a, zero), jnp.where(first_half, zero, dy_a)
        early_b, late_b = jnp.where(first_half, dy_b, zero), jnp.where(first_half, zero, dy_b)
        stack = jnp.concatenate([early_a, early_b, late_a, late_b], axis=0)
        stack_b = jnp.concatenate([early_b, late_b], axis=0)
        grad_a = mul_nt(x_a, stack)
        grad_b = mul_nt(x_b, stack_b)
        masks_a, masks_b = [], []
        for side in range(2):
            place = pair * 2 + side
            head = first + place
            from_a = near[0:half, place : place + 1]
            from_b = near[half:rows, place : place + 1]
            to_a = near_cum[place : place + 1, 0:half]
            to_b = near_cum[place : place + 1, half:rows]
            fade_aa = jnp.exp(jnp.where(ahead, to_a + from_a, -1e30))
            fade_ab = jnp.exp(to_b + from_a)
            fade_bb = jnp.exp(jnp.where(ahead, to_b + from_b, -1e30))
            weigh_aa = fade_aa * grad_a[:, side * rows : side * rows + half]
            weigh_ab = fade_ab * grad_a[:, side * rows + half : (side + 1) * rows]
            weigh_bb = fade_bb * grad_b[:, side * half : (side + 1) * half]
            sum_aa += weigh_aa
            sum_ab += weigh_ab
            sum_bb += weigh_bb
            masks_a += [(fade_aa * flow_aa).astype(BF16), (fade_ab * flow_ab).astype(BF16)]
            masks_b += [(fade_bb * flow_bb).astype(BF16)]
            pair_aa = weigh_aa * flow_aa
            pair_ab = weigh_ab * flow_ab
            pair_bb = weigh_bb * flow_bb
            flow_out = jnp.sum(pair_aa + pair_ab, axis=1, keepdims=True)
            own_a = jnp.where(head_lane == head, flow_out, own_a)
            flow_out = jnp.sum(pair_bb, axis=1, keepdims=True)
            own_b = jnp.where(head_lane == head, flow_out, own_b)
            flow_in = [
                jnp.sum(pair_aa, axis=0, keepdims=True),
                jnp.sum(pair_ab, axis=0, keepdims=True) + jnp.sum(pair_bb, axis=0, keepdims=True),
            ]
            flows.append(jnp.concatenate(flow_in, axis=1))
        inner_ref[0:half, span] = mul(jnp.concatenate(masks_a, axis=1), stack).astype(BF16)
        inner_ref[half:rows, span] = mul(jnp.concatenate(masks_b, axis=1), stack_b).astype(BF16)
    out_flow[pl.ds(first, group), :] = jnp.concatenate(flows, axis=0)
    pair_sum[0:half, 0:half] += sum_aa
    pair_sum[0:half, half:rows] += sum_ab
    pair_sum[half:rows, half:rows] += sum_bb
    own_ref[0:half, :] += own_a
    own_ref[half:rows, :] += own_b

    @pl.when(turn == pl.num_programs(0) - 1)
    def _():
        net = own_ref[...] - out_flow[...].T
        within_ref[...] = mul_exact(triangle(rows, lambda r, c: r > c), net)
        weighted = scale * pair_sum[...]
        maps_ref[...] = jnp.concatenate(
            [
                mul_exact(weighted, read_ref[...].astype(F32), ((1,), (1,))),
                mul_exact(weighted, write_ref[...].astype(F32), ((0,), (1,))),
            ],
            axis=1,
        )


def spread_heads(weight, first_head, picks, group):
    heads = weight.shape[1]
    near = pltpu.roll(weight, lax.rem(heads - first_head, heads), axis=1)
    top = near.astype(BF16).astype(F32)
    low = pltpu.roll(near - top, group, axis=1)
    lane = lax.broadcasted_iota(jnp.int32, near.shape, 1)
    return mul(jnp.where(lane < group, top, low).astype(BF16), picks)


def spread_picks(group, heads, lanes, head_width):
    row = lax.broadcasted_iota(jnp.int32, (heads, lanes), 0)
    lane = lax.broadcasted_iota(jnp.int32, (heads, lanes), 1)
    match = jnp.where(row < group, row, row - group) == lane // head_width
    return jnp.where(match, 1.0, 0.0).astype(BF16)


def read_answer(answer_ref, state, power_row):
    found = []
    start = power_row * state
    for piece in range(answer_ref.shape[0]):
        facts = answer_ref[piece, 2 * state :, :].astype(F32)
        back = jnp.exp2(-facts[power_row : power_row + 1])
        found.append(decode(answer_ref[piece, start : start + state, :]) * back)
    return jnp.concatenate(found, axis=1)


def carry_kernel(head_width, scale, waits, *refs):
    raw_ref, bias_ref, decay_ref, step_ref, cum_ref, write_ref, read_ref = refs[:7]
    own_ref, within_ref, map_ref, x_ref, dy_ref, answer_ref = refs[7:13]
    table_ref, sums, through, weight_e, weight_s, maps, picks = refs[13 + waits :]
    turn = pl.program_id(0)
    rows, lanes = x_ref.shape
    heads = step_ref.shape[1]
    state = write_ref.shape[0]
    group = lanes // head_width
    pair_lanes = 2 * head_width
    future, past = slice(0, heads), slice(heads, 2 * heads)
    write_sum = slice(2 * heads, 2 * heads + 2 * state)
    read_sum = slice(2 * heads + 2 * state, 2 * heads + 4 * state)

    @pl.when(turn == 0)
    def _():
        cum = cum_ref[...]
        finish = cum[rows - 1 : rows, :]
        weight_e[...] = step_ref[...] * jnp.exp(finish - cum) * scale
        weight_s[...] = jnp.exp(cum) * scale
        write, read = write_ref[...].astype(F32).T, read_ref[...].astype(F32).T
        maps[...] = jnp.concatenate([write, write, read, read], axis=1)
        picks[0:heads, :] = spread_picks(group, heads, lanes, head_width)
        picks[heads:, :] = head_selector(0, heads, lanes, head_width)
        sums[...] = jnp.zeros_like(sums)
        through[...] = jnp.zeros_like(through)

    first_here = turn * group
    pick = picks[heads:, :]
    early = lax.broadcasted_iota(jnp.int32, (state, pair_lanes), 1) < head_width
    none = jnp.zeros((state, pair_lanes), BF16)
    start = read_answer(answer_ref, state, 0)
    end = read_answer(answer_ref, state, 1)

    def products(tokens_ref, states, weight, map_columns):
        spread = spread_heads(weight[...], first_here, picks[0:heads, :], group)
        parts = halves(states)
        total, mapped = 0.0, []
        for pair in range(group // 2):
            span = slice(pair * pair_lanes, (pair + 1) * pair_lanes)
            blocks = [
                jnp.concatenate(
                    [jnp.where(early, part[:, span], none), jnp.where(early, none, part[:, span])],
                    axis=0,
                )
                for part in parts
            ]
            twice = jnp.concatenate([tokens_ref[:, span], tokens_ref[:, span]], axis=1)
            weighted = mul_nt(twice, jnp.concatenate(blocks, axis=1)) * spread[:, span]
            total += weighted
            mapped.append((weighted * map_columns).astype(BF16))
        return total, mapped

    def summed(parts):
        return mul_nt(jnp.concatenate(parts, axis=1), pick)

    def placed(value):
        return pltpu.roll(value, first_here, axis=1)

    total, mapped = products(x_ref, end, weight_e, maps[:, 0 : 2 * state])
    sums[:, write_sum] += total
    sums[:, future] += placed(summed(mapped))

    total, mapped = products(dy_ref, start, weight_s, maps[:, 2 * state : 4 * state])
    sums[:, read_sum] += total
    sums[:, past] += placed(summed(mapped))

    both = jnp.broadcast_to(jnp.sum(start * end, axis=0, keepdims=True), (8, lanes))
    top, low = halves(both)
    through[...] += placed(mul_nt(top, pick) + mul_nt(low, pick))

    @pl.when(turn == pl.num_programs(0) - 1)
    def _():
        rate = -jnp.exp(decay_ref[...])
        step = step_ref[...]
        gate = jax.nn.sigmoid(raw_ref[...].astype(F32) + bias_ref[...])
        finish = cum_ref[rows - 1 : rows, :]
        ahead = sums[:, future]
        decay_grad = (
            within_ref[...]
            + mul_exact(triangle(rows, lambda r, c: r <= c), sums[:, past])
            + mul_exact(triangle(rows, lambda r, c: r > c), ahead)
            + jnp.exp(finish) * scale * through[0:1, :]
        )
        ratio = jnp.where(step > 1e-30, gate / jnp.maximum(step, 1e-30), 1.0)
        raw_grad = (own_ref[...] + ahead) * ratio + rate * decay_grad * gate
        map_sum = sums[:, 2 * heads :]
        write_all = map_sum[:, 0:state] + map_sum[:, state : 2 * state]
        read_all = map_sum[:, 2 * state : 3 * state] + map_sum[:, 3 * state :]
        map_grad = jnp.concatenate([write_all, read_all], axis=1) + map_ref[...]
        table_ref[...] = jnp.concatenate([raw_grad.T, map_grad.T], axis=0).astype(BF16)


def grad_setup_kernel(scale, step_ref, cum_ref, write_ref, *rest):
    weight_ref, maps_ref = rest[-2:]
    cum = cum_ref[...]
    finish = cum[cum.shape[0] - 1 :, :]
    weight_ref[...] = step_ref[...] * jnp.exp(finish - cum) * scale
    write = write_ref[...].astype(F32).T.astype(BF16)
    maps_ref[...] = jnp.concatenate([write, write], axis=1)


def grad_kernel(head_width, *refs):
    weight_ref, maps_ref, skip_ref, dy_ref, inner_ref, answer_ref = refs[:6]
    grad_ref, picks = refs[-2:]
    turn = pl.program_id(0)
    lanes = dy_ref.shape[1]
    heads = skip_ref.shape[1]
    state = maps_ref.shape[1] // 2
    group = lanes // head_width

    @pl.when(turn == 0)
    def _():
        picks[...] = spread_picks(group, heads, lanes, head_width)

    first_here = turn * group
    end_parts = jnp.concatenate(halves(read_answer(answer_ref, state, 1)), axis=0)
    skip = jnp.broadcast_to(skip_ref[...], (16, heads))
    skip = spread_heads(skip, first_here, picks[...], group)[0:1]
    spread = spread_heads(weight_ref[...], first_here, picks[...], group)
    carried = mul(maps_ref[...], end_parts) * spread
    inner = inner_ref[...].astype(F32)
    grad_ref[...] = (inner + skip * dy_ref[...].astype(F32) + carried).astype(BF16)


def deal_kernel(place_ref, layer_ref, after_ref, *out_refs):
    width = out_refs[0].shape[2]
    for turn, out_ref in enumerate(out_refs):
        start = pl.multiple_of((place_ref[0] ^ turn) * width, width)
        out_ref[0, :, :] = layer_ref[:, pl.ds(start, width)]


def product_kernel(planes, wide, place_ref, *refs):
    table_refs, layer_refs = refs[:wide], refs[wide : 2 * wide]
    out_refs = refs[-3 - planes : -3]
    table_all, layer_all, sems = refs[-3:]
    columns, rows = table_refs[0].shape
    loads = [
        pltpu.make_async_copy(ref, table_all.at[turn], sems.at[planes, turn])
        for turn, ref in enumerate(table_refs)
    ]
    for plane in range(planes):
        source = place_ref[1] ^ plane
        loads += [
            pltpu.make_async_copy(
                ref.at[source], layer_all.at[plane, pl.ds(turn * rows, rows)], sems.at[plane, turn]
            )
            for turn, ref in enumerate(layer_refs)
        ]
    for load in loads:
        load.start()
    for load in loads[:wide]:
        load.wait()
    table = jnp.concatenate([table_all[turn] for turn in range(wide)], axis=1)
    most = jnp.max(jnp.abs(table.astype(F32)), axis=0, keepdims=True)
    most = jnp.max(most, axis=1, keepdims=True)
    power = power_for(LAYER_BOUND * wide * rows * most)
    forth = jnp.exp2(power)
    for plane, out_ref in enumerate(out_refs):
        for load in loads[(plane + 1) * wide : (plane + 2) * wide]:
            load.wait()
        out_ref[0:columns, :] = encode(mul(table, layer_all[plane]) * forth)
        out_ref[columns:, :] = jnp.broadcast_to(power, out_ref[columns:, :].shape).astype(BF16)


def gather_kernel(factor, planes, *refs):
    part_refs, out_ref = refs[:planes], refs[-1]
    columns = out_ref.shape[1]
    total = jnp.zeros((columns, out_ref.shape[0]), F32)
    for part_ref in part_refs:
        power = part_ref[columns:, :].astype(F32)[0:1]
        total += decode(part_ref[0:columns, :]) * jnp.exp2(-power)
    out_ref[...] = (total * factor).T


def swap(array, axis, turn):
    if turn == 0:
        return array
    count = lax.axis_size(axis)
    return lax.ppermute(array, axis, [(one, one ^ turn) for one in range(count)])


def whole(shape):
    return pl.BlockSpec(shape, lambda i: (0,) * len(shape))


def call(kernel, steps, in_specs, out, scratch, aliases=None):
    return pl.pallas_call(
        kernel,
        grid=(steps,),
        in_specs=in_specs,
        out_specs=[spec for spec, _, _ in out],
        out_shape=[jax.ShapeDtypeStruct(dims, dtype) for _, dims, dtype in out],
        scratch_shapes=[pltpu.VMEM(dims, dtype) for dims, dtype in scratch],
        compiler_params=pltpu.CompilerParams(vmem_limit_bytes=VMEM_LIMIT),
        cost_estimate=SHORT,
        input_output_aliases=aliases or {},
    )


def body(
    layer_input,
    head_inputs,
    output_grad,
    step_raw,
    state_write,
    state_read,
    decay_log,
    step_bias,
    skip_gain,
):
    rows, channels = head_inputs.shape
    heads = step_raw.shape[1]
    head_width = channels // heads
    state = state_write.shape[1]
    model = layer_input.shape[1]
    columns = heads + 2 * state
    axes = ("wide", "seq")
    wide, planes = lax.axis_size("wide"), lax.axis_size("seq")
    blocks = wide * planes
    own_model = model // blocks
    scale = float(rows * blocks * state) ** -0.5
    owner_lanes = channels // blocks
    piece_lanes = max(owner_lanes, 128)
    pieces = channels // piece_lanes
    depth = 2 * state + META
    bias = step_bias[None, :]
    decay = decay_log[None, :]
    skip = skip_gain[None, :]
    write_t, read_t = state_write.T, state_read.T

    summary_lanes = SUMMARY_HEADS * head_width
    carry_lanes = CARRY_HEADS * head_width
    grad_lanes = GRAD_HEADS * head_width

    def tokens(width, first=0):
        return pl.BlockSpec((rows, width), lambda i: (0, first + i))

    def messages(width, first=0):
        return pl.BlockSpec((width // piece_lanes, depth, piece_lanes), lambda i: (first + i, 0, 0))

    head_spec = whole((rows, heads))
    line_spec = whole((1, heads))
    map_spec = whole((state, rows))
    head_out = (head_spec, (rows, heads), F32)

    def exchange(array):
        return lax.all_to_all(array, axes, split_axis=0, concat_axis=0, tiled=True)

    def to_owner(array):
        if owner_lanes < piece_lanes:
            split = array.reshape(pieces, depth, piece_lanes // owner_lanes, owner_lanes)
            array = jnp.moveaxis(split, 2, 1).reshape(blocks, depth, owner_lanes)
        return exchange(array)

    def from_owner(array):
        array = exchange(array)
        if owner_lanes < piece_lanes:
            split = array.reshape(pieces, piece_lanes // owner_lanes, depth, owner_lanes)
            array = jnp.moveaxis(split, 1, 2).reshape(pieces, depth, piece_lanes)
        return array

    with jax.named_scope("summaries"):
        message, step, cum = call(
            functools.partial(summary_kernel, head_width),
            channels // summary_lanes,
            [head_spec, line_spec, line_spec, map_spec, map_spec]
            + [tokens(summary_lanes), tokens(summary_lanes)],
            [
                (messages(summary_lanes), (pieces, depth, piece_lanes), BF16),
                head_out,
                head_out,
            ],
            [((heads, rows), F32), ((heads, rows), F32), ((META, heads), BF16)],
        )(step_raw, bias, decay, write_t, read_t, head_inputs, output_grad)
    place = jnp.stack([lax.axis_index("wide"), lax.axis_index("seq")]).astype(jnp.int32)
    with jax.named_scope("layer"):
        if own_model % 128:
            cut = jnp.transpose(layer_input.reshape(rows, planes, wide, own_model), (2, 1, 0, 3))
            dealt = [
                lax.dynamic_index_in_dim(cut, place[0] ^ turn, 0, False) for turn in range(wide)
            ]
        else:
            dealt = pl.pallas_call(
                deal_kernel,
                grid_spec=pltpu.PrefetchScalarGridSpec(
                    num_scalar_prefetch=1,
                    grid=(planes,),
                    in_specs=[
                        pl.BlockSpec((rows, wide * own_model), lambda i, p: (0, i)),
                        pl.BlockSpec(memory_space=pl.ANY),
                    ],
                    out_specs=[pl.BlockSpec((1, rows, own_model), lambda i, p: (i, 0, 0))] * wide,
                ),
                out_shape=[jax.ShapeDtypeStruct((planes, rows, own_model), BF16)] * wide,
                compiler_params=pltpu.CompilerParams(vmem_limit_bytes=VMEM_LIMIT),
                cost_estimate=SHORT,
            )(place, layer_input, cum)
        layer_parts = [swap(one, "wide", turn) for turn, one in enumerate(dealt)]

    anywhere = pl.BlockSpec(memory_space=pltpu.HBM)
    firsts = [turn for turn in (1, 2, 4, 3, 5) if turn < wide]
    lasts = [layer_parts[turn] for turn in range(1, wide) if turn not in firsts]
    lasts, latest = lasts[:-1], lasts[-1:]
    with jax.named_scope("own_block"):
        width = PAIR_HEADS * head_width
        inner, own, within, maps = call(
            functools.partial(block_kernel, head_width, scale, 0, 1),
            channels // width,
            [head_spec, head_spec, map_spec, map_spec, tokens(width), tokens(width), anywhere],
            [
                (tokens(width), (rows, channels), BF16),
                head_out,
                head_out,
                (whole((rows, 2 * state)), (rows, 2 * state), F32),
            ],
            [
                ((rows, rows), F32),
                ((rows, heads), F32),
                ((heads, rows), F32),
                ((rows, rows), F32),
                ((heads, rows), F32),
            ],
        )(step, cum, write_t, read_t, head_inputs, output_grad, dealt[0])
    with jax.named_scope("scan"):
        after = [own] + [layer_parts[turn] for turn in firsts]
        scan_lanes = min(owner_lanes, 128)
        scan_spec = pl.BlockSpec((blocks, depth, scan_lanes), lambda i: (0, 0, i))
        (answer,) = call(
            scan_kernel,
            owner_lanes // scan_lanes,
            [scan_spec] + [anywhere] * len(after),
            [(scan_spec, (blocks, depth, owner_lanes), BF16)],
            [((2, blocks, scan_lanes), F32)],
        )(to_owner(message), *after)
        returned = from_owner(answer)

    with jax.named_scope("carried"):
        (table,) = call(
            functools.partial(carry_kernel, head_width, scale, len(lasts)),
            channels // carry_lanes,
            [head_spec, line_spec, line_spec, head_spec, head_spec, map_spec, map_spec]
            + [head_spec, head_spec, whole((rows, 2 * state))]
            + [tokens(carry_lanes), tokens(carry_lanes), messages(carry_lanes)]
            + [anywhere] * len(lasts),
            [(whole((columns, rows)), (columns, rows), BF16)],
            [
                ((rows, 2 * heads + 4 * state), F32),
                ((8, heads), F32),
                ((rows, heads), F32),
                ((rows, heads), F32),
                ((rows, 4 * state), F32),
                ((2 * heads, carry_lanes), BF16),
            ],
        )(
            *(step_raw, bias, decay, step, cum, write_t, read_t, own, within, maps),
            *(head_inputs, output_grad, returned, *lasts),
        )

    with jax.named_scope("grad_x"):
        grad_maps = whole((rows, 2 * state))
        grad_weight, grad_map = call(
            functools.partial(grad_setup_kernel, scale),
            1,
            [head_spec, head_spec, map_spec] + [anywhere] * (1 + len(latest)),
            [head_out, (grad_maps, (rows, 2 * state), BF16)],
            [],
        )(step, cum, write_t, table, *latest)

    with jax.named_scope("projection"):
        tables = [table]
        for turn in range(1, wide):
            tables.append(swap(tables[turn - 1], "wide", 1) if turn % 2 else swap(table, "wide", turn))
        coded = (columns + META, own_model)
        products = pl.pallas_call(
            functools.partial(product_kernel, planes, wide),
            in_specs=[pl.BlockSpec(memory_space=pltpu.SMEM)] + [anywhere] * (2 * wide + 1),
            out_specs=[pl.BlockSpec(memory_space=pltpu.VMEM)] * planes,
            out_shape=[jax.ShapeDtypeStruct(coded, BF16)] * planes,
            scratch_shapes=[
                pltpu.VMEM((wide, columns, rows), BF16),
                pltpu.VMEM((planes, wide * rows, own_model), BF16),
                pltpu.SemaphoreType.DMA((planes + 1, wide)),
            ],
            compiler_params=pltpu.CompilerParams(vmem_limit_bytes=VMEM_LIMIT),
            cost_estimate=SHORT,
        )(place, *tables, *layer_parts, grad_weight)
        (grad_x,) = call(
            functools.partial(grad_kernel, head_width),
            channels // grad_lanes,
            [head_spec, grad_maps, line_spec, tokens(grad_lanes), tokens(grad_lanes)]
            + [messages(grad_lanes), anywhere],
            [(tokens(grad_lanes), (rows, channels), BF16)],
            [((heads, grad_lanes), BF16)],
        )(grad_weight, grad_map, skip, output_grad, inner, returned, products[0])
        sums = [swap(one, "seq", turn) for turn, one in enumerate(products)]
        (weight_grad,) = call(
            functools.partial(gather_kernel, 1.0 / math.sqrt(rows * blocks), planes),
            1,
            [whole(coded)] * planes + [anywhere],
            [(whole((own_model, columns)), (own_model, columns), F32)],
            [],
        )(*sums, grad_x)
    return grad_x, weight_grad


def solution(mesh):
    in_specs = (
        P(("wide", "seq"), None),
        P(("wide", "seq"), None),
        P(("wide", "seq"), None),
        P(("wide", "seq"), None),
        P(("wide", "seq"), None),
        P(("wide", "seq"), None),
        P(),
        P(),
        P(),
    )
    out_specs = (P(("wide", "seq"), None), P(("seq", "wide"), None))
    return jax.shard_map(body, mesh=mesh, in_specs=in_specs, out_specs=out_specs, check_vma=False)
```

```python
import functools
import math

import jax
import jax.numpy as jnp
from jax import lax
from jax.experimental import pallas as pl
from jax.experimental.pallas import tpu as pltpu
from jax.sharding import PartitionSpec as P

F32 = jnp.float32
BF16 = jnp.bfloat16
EXACT = lax.Precision.HIGHEST
VMEM_LIMIT = 64 * 1024 * 1024
TOP_POWER = 30.0
PRODUCT_BOUND = 30.0
LAYER_BOUND = 24.0
SUMMARY_HEADS = 32
CARRY_HEADS = 32
GRAD_HEADS = 32
PAIR_HEADS = 8
META = 8
SHORT = pl.CostEstimate(flops=1000, bytes_accessed=1000, transcendentals=0)


def mul(a, b):
    return lax.dot_general(a, b, (((1,), (0,)), ((), ())), preferred_element_type=F32)


def mul_nt(a, b):
    return lax.dot_general(a, b, (((1,), (1,)), ((), ())), preferred_element_type=F32)


def mul_exact(a, b, dims=((1,), (0,))):
    return lax.dot_general(a, b, (dims, ((), ())), preferred_element_type=F32, precision=EXACT)


def halves(value):
    top = value.astype(BF16)
    return top, (value - top.astype(F32)).astype(BF16)


def power_for(bound):
    power = jnp.floor(TOP_POWER - jnp.log2(jnp.maximum(bound, 1e-37)))
    return jnp.clip(power, -100.0, 100.0)


def thirds(value):
    top, rest = value.astype(BF16), value
    rest = rest - top.astype(F32)
    middle = rest.astype(BF16)
    return top, middle, (rest - middle.astype(F32)).astype(BF16)


def encode(value):
    square = value * value
    fourth = square * square
    return jnp.where(value < 0, -fourth, fourth).astype(BF16)


def decode(coded):
    coded = coded.astype(F32)
    size = jnp.maximum(jnp.abs(coded), 1e-37)
    inverse = lax.rsqrt(size)
    return coded * inverse * lax.rsqrt(size * inverse)


def head_selector(first_head, heads, lanes, head_width):
    row = lax.broadcasted_iota(jnp.int32, (heads, lanes), 0)
    lane = lax.broadcasted_iota(jnp.int32, (heads, lanes), 1)
    return jnp.where(row == first_head + lane // head_width, 1.0, 0.0).astype(BF16)


def triangle(length, keep):
    row = lax.broadcasted_iota(jnp.int32, (length, length), 0)
    col = lax.broadcasted_iota(jnp.int32, (length, length), 1)
    return jnp.where(keep(row, col), 1.0, 0.0).astype(F32)


def summary_kernel(
    head_width,
    raw_ref,
    bias_ref,
    decay_ref,
    write_ref,
    read_ref,
    x_ref,
    dy_ref,
    message_ref,
    step_ref,
    cum_ref,
    weight_f,
    weight_b,
    facts,
):
    turn = pl.program_id(0)
    heads = raw_ref.shape[1]
    rows, lanes = x_ref.shape
    state = write_ref.shape[0]

    @pl.when(turn == 0)
    def _():
        step = jax.nn.softplus(raw_ref[...].astype(F32) + bias_ref[...])
        rate = -jnp.exp(decay_ref[...])
        cum = mul_exact(triangle(rows, lambda r, c: r >= c), step * rate)
        finish = cum[rows - 1 : rows, :]
        forward = step * jnp.exp(finish - cum)
        backward = jnp.exp(cum)
        power_f = power_for(PRODUCT_BOUND * jnp.sum(forward, axis=0, keepdims=True))
        power_b = power_for(PRODUCT_BOUND * jnp.sum(backward, axis=0, keepdims=True))
        step_ref[...] = step
        cum_ref[...] = cum
        parts = thirds(jnp.maximum(finish, -1e30))
        facts[...] = jnp.concatenate(
            [part.astype(F32) for part in parts]
            + [power_f, power_b, jnp.zeros((META - 5, heads), F32)],
            axis=0,
        ).astype(BF16)
        weight_f[...] = (forward * jnp.exp2(power_f)).T
        weight_b[...] = (backward * jnp.exp2(power_b)).T

    group = lanes // head_width
    pair_lanes = 2 * head_width
    width = message_ref.shape[2]
    near = pl.ds(turn * group, group)
    pick = head_selector(turn * group, heads, lanes, head_width)
    fact = mul(facts[...], pick).astype(BF16)
    lane = lax.broadcasted_iota(jnp.int32, (state, pair_lanes), 1)
    ahead = (x_ref, write_ref[...].astype(F32), weight_f[near, :], 0)
    behind = (dy_ref, read_ref[...].astype(F32), weight_b[near, :], state)
    for pair in range(group // 2):
        span = slice(pair * pair_lanes, (pair + 1) * pair_lanes)
        owner, offset = pair * pair_lanes // width, pair * pair_lanes % width
        here = slice(offset, offset + pair_lanes)
        for tokens_ref, rows_t, weights, start in (ahead, behind):
            scaled = []
            for head in (2 * pair, 2 * pair + 1):
                scaled += halves(rows_t * weights[head : head + 1, :])
            product = mul(jnp.concatenate(scaled, axis=0), tokens_ref[:, span])
            early = product[0:state] + product[state : 2 * state]
            late = product[2 * state : 3 * state] + product[3 * state :]
            total = jnp.where(lane < head_width, early, late)
            message_ref[owner, start : start + state, here] = encode(total)
        message_ref[owner, 2 * state :, here] = fact[:, span]


def scan_kernel(message_ref, *rest):
    answer_ref, powers = rest[-2:]
    blocks, double, lanes = message_ref.shape
    state = (double - META) // 2
    top = 2.0**TOP_POWER

    def one(block, start, power_row, side, running, bound):
        facts = message_ref[block, 2 * state : double, :].astype(F32)
        decay = jnp.exp(facts[0:1] + facts[1:2] + facts[2:3])
        back = jnp.exp2(-facts[power_row : power_row + 1])
        power = power_for(bound)
        powers[side, pl.ds(block, 1), :] = power
        answer_ref[block, start : start + state, :] = encode(running * jnp.exp2(power))
        own = decode(message_ref[block, start : start + state, :]) * back
        return running * decay + own, bound * decay + top * back

    def both(block, carry):
        ahead, ahead_bound, behind, behind_bound = carry
        return one(block, 0, 3, 0, ahead, ahead_bound) + one(
            blocks - 1 - block, state, 4, 1, behind, behind_bound
        )

    zero, none = jnp.zeros((state, lanes), F32), jnp.zeros((1, lanes), F32)
    lax.fori_loop(0, blocks, both, (zero, none, zero, none), unroll=8)
    row = lax.broadcasted_iota(jnp.int32, (blocks, META, lanes), 1)
    ahead, behind = powers[0][:, None, :], powers[1][:, None, :]
    meta = jnp.where(row == 0, ahead, jnp.where(row == 1, behind, 0.0))
    answer_ref[:, 2 * state : double, :] = meta.astype(BF16)


def block_kernel(
    head_width,
    scale,
    first_head,
    waits,
    step_ref,
    cum_ref,
    write_ref,
    read_ref,
    x_ref,
    dy_ref,
    *rest,
):
    inner_ref, own_ref, within_ref, maps_ref = rest[waits : waits + 4]
    read_write, source, cum_rows, pair_sum, out_flow = rest[waits + 4 :]
    turn = pl.program_id(0)
    rows, lanes = x_ref.shape
    half = rows // 2
    heads = step_ref.shape[1]
    group = lanes // head_width

    @pl.when(turn == 0)
    def _():
        read_write[...] = scale * lax.dot_general(
            write_ref[...], read_ref[...], (((0,), (0,)), ((), ())), preferred_element_type=F32
        )
        source[...] = jnp.log(step_ref[...]) - cum_ref[...]
        cum_rows[...] = cum_ref[...].T
        pair_sum[...] = jnp.zeros_like(pair_sum)
        out_flow[...] = jnp.zeros_like(out_flow)
        own_ref[...] = jnp.zeros_like(own_ref)

    first = first_head + turn * group
    near = pltpu.roll(source[...], lax.rem(heads - first, heads), axis=1)
    near_cum = cum_rows[pl.ds(first, group), :]
    row = lax.broadcasted_iota(jnp.int32, (half, half), 0)
    col = lax.broadcasted_iota(jnp.int32, (half, half), 1)
    ahead = col >= row
    lane = lax.broadcasted_iota(jnp.int32, (half, 2 * head_width), 1)
    first_half = lane < head_width
    head_lane = lax.broadcasted_iota(jnp.int32, (half, heads), 1)
    flow_aa = read_write[0:half, 0:half]
    flow_ab = read_write[0:half, half:rows]
    flow_bb = read_write[half:rows, half:rows]
    sum_aa = jnp.zeros((half, half), F32)
    sum_ab = jnp.zeros((half, half), F32)
    sum_bb = jnp.zeros((half, half), F32)
    own_a = jnp.zeros((half, heads), F32)
    own_b = jnp.zeros((half, heads), F32)
    zero = jnp.zeros((half, 2 * head_width), BF16)
    flows = []
    for pair in range(group // 2):
        span = slice(pair * 2 * head_width, (pair + 1) * 2 * head_width)
        x_a, x_b = x_ref[0:half, span], x_ref[half:rows, span]
        dy_a, dy_b = dy_ref[0:half, span], dy_ref[half:rows, span]
        early_a, late_a = jnp.where(first_half, dy_a, zero), jnp.where(first_half, zero, dy_a)
        early_b, late_b = jnp.where(first_half, dy_b, zero), jnp.where(first_half, zero, dy_b)
        stack = jnp.concatenate([early_a, early_b, late_a, late_b], axis=0)
        stack_b = jnp.concatenate([early_b, late_b], axis=0)
        grad_a = mul_nt(x_a, stack)
        grad_b = mul_nt(x_b, stack_b)
        masks_a, masks_b = [], []
        for side in range(2):
            place = pair * 2 + side
            head = first + place
            from_a = near[0:half, place : place + 1]
            from_b = near[half:rows, place : place + 1]
            to_a = near_cum[place : place + 1, 0:half]
            to_b = near_cum[place : place + 1, half:rows]
            fade_aa = jnp.exp(jnp.where(ahead, to_a + from_a, -1e30))
            fade_ab = jnp.exp(to_b + from_a)
            fade_bb = jnp.exp(jnp.where(ahead, to_b + from_b, -1e30))
            weigh_aa = fade_aa * grad_a[:, side * rows : side * rows + half]
            weigh_ab = fade_ab * grad_a[:, side * rows + half : (side + 1) * rows]
            weigh_bb = fade_bb * grad_b[:, side * half : (side + 1) * half]
            sum_aa += weigh_aa
            sum_ab += weigh_ab
            sum_bb += weigh_bb
            masks_a += [(fade_aa * flow_aa).astype(BF16), (fade_ab * flow_ab).astype(BF16)]
            masks_b += [(fade_bb * flow_bb).astype(BF16)]
            pair_aa = weigh_aa * flow_aa
            pair_ab = weigh_ab * flow_ab
            pair_bb = weigh_bb * flow_bb
            flow_out = jnp.sum(pair_aa + pair_ab, axis=1, keepdims=True)
            own_a = jnp.where(head_lane == head, flow_out, own_a)
            flow_out = jnp.sum(pair_bb, axis=1, keepdims=True)
            own_b = jnp.where(head_lane == head, flow_out, own_b)
            flow_in = [
                jnp.sum(pair_aa, axis=0, keepdims=True),
                jnp.sum(pair_ab, axis=0, keepdims=True) + jnp.sum(pair_bb, axis=0, keepdims=True),
            ]
            flows.append(jnp.concatenate(flow_in, axis=1))
        inner_ref[0:half, span] = mul(jnp.concatenate(masks_a, axis=1), stack).astype(BF16)
        inner_ref[half:rows, span] = mul(jnp.concatenate(masks_b, axis=1), stack_b).astype(BF16)
    out_flow[pl.ds(first, group), :] = jnp.concatenate(flows, axis=0)
    pair_sum[0:half, 0:half] += sum_aa
    pair_sum[0:half, half:rows] += sum_ab
    pair_sum[half:rows, half:rows] += sum_bb
    own_ref[0:half, :] += own_a
    own_ref[half:rows, :] += own_b

    @pl.when(turn == pl.num_programs(0) - 1)
    def _():
        net = own_ref[...] - out_flow[...].T
        within_ref[...] = mul_exact(triangle(rows, lambda r, c: r > c), net)
        weighted = scale * pair_sum[...]
        maps_ref[...] = jnp.concatenate(
            [
                mul_exact(weighted, read_ref[...].astype(F32), ((1,), (1,))),
                mul_exact(weighted, write_ref[...].astype(F32), ((0,), (1,))),
            ],
            axis=1,
        )


def spread_heads(weight, first_head, picks, group):
    heads = weight.shape[1]
    near = pltpu.roll(weight, lax.rem(heads - first_head, heads), axis=1)
    top = near.astype(BF16).astype(F32)
    low = pltpu.roll(near - top, group, axis=1)
    lane = lax.broadcasted_iota(jnp.int32, near.shape, 1)
    return mul(jnp.where(lane < group, top, low).astype(BF16), picks)


def spread_picks(group, heads, lanes, head_width):
    row = lax.broadcasted_iota(jnp.int32, (heads, lanes), 0)
    lane = lax.broadcasted_iota(jnp.int32, (heads, lanes), 1)
    match = jnp.where(row < group, row, row - group) == lane // head_width
    return jnp.where(match, 1.0, 0.0).astype(BF16)


def read_answer(answer_ref, state, power_row):
    found = []
    start = power_row * state
    for piece in range(answer_ref.shape[0]):
        facts = answer_ref[piece, 2 * state :, :].astype(F32)
        back = jnp.exp2(-facts[power_row : power_row + 1])
        found.append(decode(answer_ref[piece, start : start + state, :]) * back)
    return jnp.concatenate(found, axis=1)


def carry_setup_kernel(head_width, scale, *refs):
    raw_ref, bias_ref, decay_ref, step_ref, cum_ref, write_ref, read_ref, own_ref, within_ref = refs[:9]
    weight_ref, maps_ref, pick_ref, sum_ref, gate_ref = refs[-5:]
    rows, heads = step_ref.shape
    lanes = pick_ref.shape[1]
    group = lanes // head_width
    step, cum = step_ref[...], cum_ref[...]
    finish = cum[rows - 1 : rows, :]
    weight_ref[0] = step * jnp.exp(finish - cum) * scale
    weight_ref[1] = jnp.exp(cum) * scale
    write, read = write_ref[...].astype(F32).T, read_ref[...].astype(F32).T
    maps_ref[...] = jnp.concatenate([write, write, read, read], axis=1)
    pick_ref[0:heads, :] = spread_picks(group, heads, lanes, head_width)
    pick_ref[heads:, :] = head_selector(0, heads, lanes, head_width)
    sum_ref[0] = triangle(rows, lambda r, c: r <= c).astype(BF16)
    sum_ref[1] = triangle(rows, lambda r, c: r > c).astype(BF16)
    gate = jax.nn.sigmoid(raw_ref[...].astype(F32) + bias_ref[...])
    ratio = jnp.where(step > 1e-30, gate / jnp.maximum(step, 1e-30), 1.0)
    slope = -jnp.exp(decay_ref[...]) * gate
    gate_ref[0] = ratio
    gate_ref[1] = slope
    gate_ref[2] = own_ref[...] * ratio + slope * within_ref[...]
    gate_ref[3] = slope * (jnp.exp(finish) * scale)


def carry_kernel(head_width, waits, *refs):
    weight_ref, maps, picks, sum_ref, gate_ref, map_ref, x_ref, dy_ref, answer_ref = refs[:9]
    table_ref, sums, through = refs[9 + waits :]
    turn = pl.program_id(0)
    lanes = x_ref.shape[1]
    heads = gate_ref.shape[2]
    state = maps.shape[1] // 4
    group = lanes // head_width
    pair_lanes = 2 * head_width
    future, past = slice(0, heads), slice(heads, 2 * heads)
    write_sum = slice(2 * heads, 2 * heads + 2 * state)
    read_sum = slice(2 * heads + 2 * state, 2 * heads + 4 * state)

    @pl.when(turn == 0)
    def _():
        sums[...] = jnp.zeros_like(sums)
        through[...] = jnp.zeros_like(through)

    first_here = turn * group
    pick = picks[heads:, :]
    early = lax.broadcasted_iota(jnp.int32, (state, pair_lanes), 1) < head_width
    none = jnp.zeros((state, pair_lanes), BF16)
    start = read_answer(answer_ref, state, 0)
    end = read_answer(answer_ref, state, 1)

    def products(tokens_ref, states, weight, map_columns):
        spread = spread_heads(weight, first_here, picks[0:heads, :], group)
        parts = halves(states)
        total, mapped = 0.0, []
        for pair in range(group // 2):
            span = slice(pair * pair_lanes, (pair + 1) * pair_lanes)
            blocks = [
                jnp.concatenate(
                    [jnp.where(early, part[:, span], none), jnp.where(early, none, part[:, span])],
                    axis=0,
                )
                for part in parts
            ]
            twice = jnp.concatenate([tokens_ref[:, span], tokens_ref[:, span]], axis=1)
            weighted = mul_nt(twice, jnp.concatenate(blocks, axis=1)) * spread[:, span]
            total += weighted
            mapped.append((weighted * map_columns).astype(BF16))
        return total, mapped

    def summed(parts):
        return mul_nt(jnp.concatenate(parts, axis=1), pick)

    def placed(value):
        return pltpu.roll(value, first_here, axis=1)

    total, mapped = products(x_ref, end, weight_ref[0], maps[:, 0 : 2 * state])
    sums[:, write_sum] += total
    sums[:, future] += placed(summed(mapped))

    total, mapped = products(dy_ref, start, weight_ref[1], maps[:, 2 * state : 4 * state])
    sums[:, read_sum] += total
    sums[:, past] += placed(summed(mapped))

    both = jnp.broadcast_to(jnp.sum(start * end, axis=0, keepdims=True), (8, lanes))
    top, low = halves(both)
    through[...] += placed(mul_nt(top, pick) + mul_nt(low, pick))

    @pl.when(turn == pl.num_programs(0) - 1)
    def _():
        def running(which, value):
            parts = mul(sum_ref[which], jnp.concatenate(thirds(value), axis=1))
            return parts[:, 0:heads] + parts[:, heads : 2 * heads] + parts[:, 2 * heads :]

        ahead = sums[:, future]
        raw_grad = gate_ref[1] * (running(0, sums[:, past]) + running(1, ahead))
        raw_grad += ahead * gate_ref[0] + gate_ref[2] + gate_ref[3] * through[0:1, :]
        map_sum = sums[:, 2 * heads :]
        write_all = map_sum[:, 0:state] + map_sum[:, state : 2 * state]
        read_all = map_sum[:, 2 * state : 3 * state] + map_sum[:, 3 * state :]
        map_grad = jnp.concatenate([write_all, read_all], axis=1) + map_ref[...]
        table_ref[...] = jnp.concatenate([raw_grad.T, map_grad.T], axis=0).astype(BF16)


def grad_setup_kernel(scale, step_ref, cum_ref, write_ref, *rest):
    weight_ref, maps_ref = rest[-2:]
    cum = cum_ref[...]
    finish = cum[cum.shape[0] - 1 :, :]
    weight_ref[...] = step_ref[...] * jnp.exp(finish - cum) * scale
    write = write_ref[...].astype(F32).T.astype(BF16)
    maps_ref[...] = jnp.concatenate([write, write], axis=1)


def grad_kernel(head_width, *refs):
    weight_ref, maps_ref, skip_ref, dy_ref, inner_ref, answer_ref = refs[:6]
    grad_ref, picks = refs[-2:]
    turn = pl.program_id(0)
    lanes = dy_ref.shape[1]
    heads = skip_ref.shape[1]
    state = maps_ref.shape[1] // 2
    group = lanes // head_width

    @pl.when(turn == 0)
    def _():
        picks[...] = spread_picks(group, heads, lanes, head_width)

    first_here = turn * group
    end_parts = jnp.concatenate(halves(read_answer(answer_ref, state, 1)), axis=0)
    skip = jnp.broadcast_to(skip_ref[...], (16, heads))
    skip = spread_heads(skip, first_here, picks[...], group)[0:1]
    spread = spread_heads(weight_ref[...], first_here, picks[...], group)
    carried = mul(maps_ref[...], end_parts) * spread
    inner = inner_ref[...].astype(F32)
    grad_ref[...] = (inner + skip * dy_ref[...].astype(F32) + carried).astype(BF16)


def deal_kernel(place_ref, layer_ref, after_ref, *out_refs):
    width = out_refs[0].shape[2]
    for turn, out_ref in enumerate(out_refs):
        start = pl.multiple_of((place_ref[0] ^ turn) * width, width)
        out_ref[0, :, :] = layer_ref[:, pl.ds(start, width)]


def product_kernel(planes, wide, place_ref, *refs):
    table_refs, layer_refs = refs[:wide], refs[wide : 2 * wide]
    out_refs = refs[-3 - planes : -3]
    table_all, layer_all, sems = refs[-3:]
    columns, rows = table_refs[0].shape
    loads = [
        pltpu.make_async_copy(ref, table_all.at[turn], sems.at[planes, turn])
        for turn, ref in enumerate(table_refs)
    ]
    for plane in range(planes):
        source = place_ref[1] ^ plane
        loads += [
            pltpu.make_async_copy(
                ref.at[source], layer_all.at[plane, pl.ds(turn * rows, rows)], sems.at[plane, turn]
            )
            for turn, ref in enumerate(layer_refs)
        ]
    for load in loads:
        load.start()
    for load in loads[:wide]:
        load.wait()
    table = jnp.concatenate([table_all[turn] for turn in range(wide)], axis=1)
    most = jnp.max(jnp.abs(table.astype(F32)), axis=0, keepdims=True)
    most = jnp.max(most, axis=1, keepdims=True)
    power = power_for(LAYER_BOUND * wide * rows * most)
    forth = jnp.exp2(power)
    for plane, out_ref in enumerate(out_refs):
        for load in loads[(plane + 1) * wide : (plane + 2) * wide]:
            load.wait()
        out_ref[0:columns, :] = encode(mul(table, layer_all[plane]) * forth)
        out_ref[columns:, :] = jnp.broadcast_to(power, out_ref[columns:, :].shape).astype(BF16)


def gather_kernel(factor, planes, *refs):
    part_refs, out_ref = refs[:planes], refs[-1]
    columns = out_ref.shape[1]
    total = jnp.zeros((columns, out_ref.shape[0]), F32)
    for part_ref in part_refs:
        power = part_ref[columns:, :].astype(F32)[0:1]
        total += decode(part_ref[0:columns, :]) * jnp.exp2(-power)
    out_ref[...] = (total * factor).T


def swap(array, axis, turn):
    if turn == 0:
        return array
    count = lax.axis_size(axis)
    return lax.ppermute(array, axis, [(one, one ^ turn) for one in range(count)])


def whole(shape):
    return pl.BlockSpec(shape, lambda i: (0,) * len(shape))


def call(kernel, steps, in_specs, out, scratch, aliases=None):
    return pl.pallas_call(
        kernel,
        grid=(steps,),
        in_specs=in_specs,
        out_specs=[spec for spec, _, _ in out],
        out_shape=[jax.ShapeDtypeStruct(dims, dtype) for _, dims, dtype in out],
        scratch_shapes=[pltpu.VMEM(dims, dtype) for dims, dtype in scratch],
        compiler_params=pltpu.CompilerParams(vmem_limit_bytes=VMEM_LIMIT),
        cost_estimate=SHORT,
        input_output_aliases=aliases or {},
    )


def body(
    layer_input,
    head_inputs,
    output_grad,
    step_raw,
    state_write,
    state_read,
    decay_log,
    step_bias,
    skip_gain,
):
    rows, channels = head_inputs.shape
    heads = step_raw.shape[1]
    head_width = channels // heads
    state = state_write.shape[1]
    model = layer_input.shape[1]
    columns = heads + 2 * state
    axes = ("wide", "seq")
    wide, planes = lax.axis_size("wide"), lax.axis_size("seq")
    blocks = wide * planes
    own_model = model // blocks
    scale = float(rows * blocks * state) ** -0.5
    owner_lanes = channels // blocks
    piece_lanes = max(owner_lanes, 128)
    pieces = channels // piece_lanes
    depth = 2 * state + META
    bias = step_bias[None, :]
    decay = decay_log[None, :]
    skip = skip_gain[None, :]
    write_t, read_t = state_write.T, state_read.T

    summary_lanes = SUMMARY_HEADS * head_width
    carry_lanes = CARRY_HEADS * head_width
    grad_lanes = GRAD_HEADS * head_width

    def tokens(width, first=0):
        return pl.BlockSpec((rows, width), lambda i: (0, first + i))

    def messages(width, first=0):
        return pl.BlockSpec((width // piece_lanes, depth, piece_lanes), lambda i: (first + i, 0, 0))

    head_spec = whole((rows, heads))
    line_spec = whole((1, heads))
    map_spec = whole((state, rows))
    head_out = (head_spec, (rows, heads), F32)

    def exchange(array):
        return lax.all_to_all(array, axes, split_axis=0, concat_axis=0, tiled=True)

    def to_owner(array):
        if owner_lanes < piece_lanes:
            split = array.reshape(pieces, depth, piece_lanes // owner_lanes, owner_lanes)
            array = jnp.moveaxis(split, 2, 1).reshape(blocks, depth, owner_lanes)
        return exchange(array)

    def from_owner(array):
        array = exchange(array)
        if owner_lanes < piece_lanes:
            split = array.reshape(pieces, piece_lanes // owner_lanes, depth, owner_lanes)
            array = jnp.moveaxis(split, 1, 2).reshape(pieces, depth, piece_lanes)
        return array

    with jax.named_scope("summaries"):
        message, step, cum = call(
            functools.partial(summary_kernel, head_width),
            channels // summary_lanes,
            [head_spec, line_spec, line_spec, map_spec, map_spec]
            + [tokens(summary_lanes), tokens(summary_lanes)],
            [
                (messages(summary_lanes), (pieces, depth, piece_lanes), BF16),
                head_out,
                head_out,
            ],
            [((heads, rows), F32), ((heads, rows), F32), ((META, heads), BF16)],
        )(step_raw, bias, decay, write_t, read_t, head_inputs, output_grad)
    place = jnp.stack([lax.axis_index("wide"), lax.axis_index("seq")]).astype(jnp.int32)
    with jax.named_scope("layer"):
        if own_model % 128:
            cut = jnp.transpose(layer_input.reshape(rows, planes, wide, own_model), (2, 1, 0, 3))
            dealt = [
                lax.dynamic_index_in_dim(cut, place[0] ^ turn, 0, False) for turn in range(wide)
            ]
        else:
            dealt = pl.pallas_call(
                deal_kernel,
                grid_spec=pltpu.PrefetchScalarGridSpec(
                    num_scalar_prefetch=1,
                    grid=(planes,),
                    in_specs=[
                        pl.BlockSpec((rows, wide * own_model), lambda i, p: (0, i)),
                        pl.BlockSpec(memory_space=pl.ANY),
                    ],
                    out_specs=[pl.BlockSpec((1, rows, own_model), lambda i, p: (i, 0, 0))] * wide,
                ),
                out_shape=[jax.ShapeDtypeStruct((planes, rows, own_model), BF16)] * wide,
                compiler_params=pltpu.CompilerParams(vmem_limit_bytes=VMEM_LIMIT),
                cost_estimate=SHORT,
            )(place, layer_input, cum)
        layer_parts = [swap(one, "wide", turn) for turn, one in enumerate(dealt)]

    anywhere = pl.BlockSpec(memory_space=pltpu.HBM)
    firsts = [turn for turn in (1, 2, 4, 3, 5) if turn < wide]
    lasts = [layer_parts[turn] for turn in range(1, wide) if turn not in firsts]
    lasts, latest = lasts[:-1], lasts[-1:]
    with jax.named_scope("own_block"):
        width = PAIR_HEADS * head_width
        inner, own, within, maps = call(
            functools.partial(block_kernel, head_width, scale, 0, 1),
            channels // width,
            [head_spec, head_spec, map_spec, map_spec, tokens(width), tokens(width), anywhere],
            [
                (tokens(width), (rows, channels), BF16),
                head_out,
                head_out,
                (whole((rows, 2 * state)), (rows, 2 * state), F32),
            ],
            [
                ((rows, rows), F32),
                ((rows, heads), F32),
                ((heads, rows), F32),
                ((rows, rows), F32),
                ((heads, rows), F32),
            ],
        )(step, cum, write_t, read_t, head_inputs, output_grad, dealt[0])
    with jax.named_scope("scan"):
        after = [own] + [layer_parts[turn] for turn in firsts]
        scan_lanes = min(owner_lanes, 128)
        scan_spec = pl.BlockSpec((blocks, depth, scan_lanes), lambda i: (0, 0, i))
        (answer,) = call(
            scan_kernel,
            owner_lanes // scan_lanes,
            [scan_spec] + [anywhere] * len(after),
            [(scan_spec, (blocks, depth, owner_lanes), BF16)],
            [((2, blocks, scan_lanes), F32)],
        )(to_owner(message), *after)
        returned = from_owner(answer)

    with jax.named_scope("carried"):
        setup_dims = [
            ((2, rows, heads), F32),
            ((rows, 4 * state), F32),
            ((2 * heads, carry_lanes), BF16),
            ((2, rows, rows), BF16),
            ((4, rows, heads), F32),
        ]
        setup = call(
            functools.partial(carry_setup_kernel, head_width, scale),
            1,
            [head_spec, line_spec, line_spec, head_spec, head_spec, map_spec, map_spec]
            + [head_spec, head_spec, anywhere],
            [(whole(dims), dims, dtype) for dims, dtype in setup_dims],
            [],
        )(step_raw, bias, decay, step, cum, write_t, read_t, own, within, answer)
        (table,) = call(
            functools.partial(carry_kernel, head_width, len(lasts)),
            channels // carry_lanes,
            [whole(dims) for dims, _ in setup_dims]
            + [whole((rows, 2 * state)), tokens(carry_lanes), tokens(carry_lanes)]
            + [messages(carry_lanes)]
            + [anywhere] * len(lasts),
            [(whole((columns, rows)), (columns, rows), BF16)],
            [((rows, 2 * heads + 4 * state), F32), ((8, heads), F32)],
        )(*setup, maps, head_inputs, output_grad, returned, *lasts)

    with jax.named_scope("grad_x"):
        grad_maps = whole((rows, 2 * state))
        grad_weight, grad_map = call(
            functools.partial(grad_setup_kernel, scale),
            1,
            [head_spec, head_spec, map_spec] + [anywhere] * (1 + len(latest)),
            [head_out, (grad_maps, (rows, 2 * state), BF16)],
            [],
        )(step, cum, write_t, table, *latest)

    with jax.named_scope("projection"):
        tables = [table]
        for turn in range(1, wide):
            tables.append(swap(tables[turn - 1], "wide", 1) if turn % 2 else swap(table, "wide", turn))
        coded = (columns + META, own_model)
        products = pl.pallas_call(
            functools.partial(product_kernel, planes, wide),
            in_specs=[pl.BlockSpec(memory_space=pltpu.SMEM)] + [anywhere] * (2 * wide + 1),
            out_specs=[pl.BlockSpec(memory_space=pltpu.VMEM)] * planes,
            out_shape=[jax.ShapeDtypeStruct(coded, BF16)] * planes,
            scratch_shapes=[
                pltpu.VMEM((wide, columns, rows), BF16),
                pltpu.VMEM((planes, wide * rows, own_model), BF16),
                pltpu.SemaphoreType.DMA((planes + 1, wide)),
            ],
            compiler_params=pltpu.CompilerParams(vmem_limit_bytes=VMEM_LIMIT),
            cost_estimate=SHORT,
        )(place, *tables, *layer_parts, grad_weight)
        (grad_x,) = call(
            functools.partial(grad_kernel, head_width),
            channels // grad_lanes,
            [head_spec, grad_maps, line_spec, tokens(grad_lanes), tokens(grad_lanes)]
            + [messages(grad_lanes), anywhere],
            [(tokens(grad_lanes), (rows, channels), BF16)],
            [((heads, grad_lanes), BF16)],
        )(grad_weight, grad_map, skip, output_grad, inner, returned, products[0])
        sums = [swap(one, "seq", turn) for turn, one in enumerate(products)]
        (weight_grad,) = call(
            functools.partial(gather_kernel, 1.0 / math.sqrt(rows * blocks), planes),
            1,
            [whole(coded)] * planes + [anywhere],
            [(whole((own_model, columns)), (own_model, columns), F32)],
            [],
        )(*sums, grad_x)
    return grad_x, weight_grad


def solution(mesh):
    in_specs = (
        P(("wide", "seq"), None),
        P(("wide", "seq"), None),
        P(("wide", "seq"), None),
        P(("wide", "seq"), None),
        P(("wide", "seq"), None),
        P(("wide", "seq"), None),
        P(),
        P(),
        P(),
    )
    out_specs = (P(("wide", "seq"), None), P(("seq", "wide"), None))
    return jax.shard_map(body, mesh=mesh, in_specs=in_specs, out_specs=out_specs, check_vma=False)
```

```python
import functools
import math

import jax
import jax.numpy as jnp
from jax import lax
from jax.experimental import pallas as pl
from jax.experimental.pallas import tpu as pltpu
from jax.sharding import PartitionSpec as P

F32 = jnp.float32
BF16 = jnp.bfloat16
EXACT = lax.Precision.HIGHEST
VMEM_LIMIT = 64 * 1024 * 1024
TOP_POWER = 30.0
PRODUCT_BOUND = 30.0
LAYER_BOUND = 24.0
SUMMARY_HEADS = 64
CARRY_HEADS = 64
GRAD_HEADS = 32
PAIR_HEADS = 8
META = 8
SHORT = pl.CostEstimate(flops=1000, bytes_accessed=1000, transcendentals=0)


def mul(a, b):
    return lax.dot_general(a, b, (((1,), (0,)), ((), ())), preferred_element_type=F32)


def mul_nt(a, b):
    return lax.dot_general(a, b, (((1,), (1,)), ((), ())), preferred_element_type=F32)


def mul_exact(a, b, dims=((1,), (0,))):
    return lax.dot_general(a, b, (dims, ((), ())), preferred_element_type=F32, precision=EXACT)


def halves(value):
    top = value.astype(BF16)
    return top, (value - top.astype(F32)).astype(BF16)


def power_for(bound):
    power = jnp.floor(TOP_POWER - jnp.log2(jnp.maximum(bound, 1e-37)))
    return jnp.clip(power, -100.0, 100.0)


def thirds(value):
    top, rest = value.astype(BF16), value
    rest = rest - top.astype(F32)
    middle = rest.astype(BF16)
    return top, middle, (rest - middle.astype(F32)).astype(BF16)


def encode(value):
    square = value * value
    fourth = square * square
    return jnp.where(value < 0, -fourth, fourth).astype(BF16)


def decode(coded):
    coded = coded.astype(F32)
    size = jnp.maximum(jnp.abs(coded), 1e-37)
    inverse = lax.rsqrt(size)
    return coded * inverse * lax.rsqrt(size * inverse)


def head_selector(first_head, heads, lanes, head_width):
    row = lax.broadcasted_iota(jnp.int32, (heads, lanes), 0)
    lane = lax.broadcasted_iota(jnp.int32, (heads, lanes), 1)
    return jnp.where(row == first_head + lane // head_width, 1.0, 0.0).astype(BF16)


def triangle(length, keep):
    row = lax.broadcasted_iota(jnp.int32, (length, length), 0)
    col = lax.broadcasted_iota(jnp.int32, (length, length), 1)
    return jnp.where(keep(row, col), 1.0, 0.0).astype(F32)


def summary_kernel(
    head_width,
    raw_ref,
    bias_ref,
    decay_ref,
    write_ref,
    read_ref,
    x_ref,
    dy_ref,
    message_ref,
    step_ref,
    cum_ref,
    weight_f,
    weight_b,
    facts,
):
    turn = pl.program_id(0)
    heads = raw_ref.shape[1]
    rows, lanes = x_ref.shape
    state = write_ref.shape[0]

    @pl.when(turn == 0)
    def _():
        step = jax.nn.softplus(raw_ref[...].astype(F32) + bias_ref[...])
        rate = -jnp.exp(decay_ref[...])
        cum = mul_exact(triangle(rows, lambda r, c: r >= c), step * rate)
        finish = cum[rows - 1 : rows, :]
        forward = step * jnp.exp(finish - cum)
        backward = jnp.exp(cum)
        power_f = power_for(PRODUCT_BOUND * jnp.sum(forward, axis=0, keepdims=True))
        power_b = power_for(PRODUCT_BOUND * jnp.sum(backward, axis=0, keepdims=True))
        step_ref[...] = step
        cum_ref[...] = cum
        parts = thirds(jnp.maximum(finish, -1e30))
        facts[...] = jnp.concatenate(
            [part.astype(F32) for part in parts]
            + [power_f, power_b, jnp.zeros((META - 5, heads), F32)],
            axis=0,
        ).astype(BF16)
        weight_f[...] = (forward * jnp.exp2(power_f)).T
        weight_b[...] = (backward * jnp.exp2(power_b)).T

    group = lanes // head_width
    pair_lanes = 2 * head_width
    width = message_ref.shape[2]
    near = pl.ds(turn * group, group)
    pick = head_selector(turn * group, heads, lanes, head_width)
    fact = mul(facts[...], pick).astype(BF16)
    lane = lax.broadcasted_iota(jnp.int32, (state, pair_lanes), 1)
    ahead = (x_ref, write_ref[...].astype(F32), weight_f[near, :], 0)
    behind = (dy_ref, read_ref[...].astype(F32), weight_b[near, :], state)
    for pair in range(group // 2):
        span = slice(pair * pair_lanes, (pair + 1) * pair_lanes)
        owner, offset = pair * pair_lanes // width, pair * pair_lanes % width
        here = slice(offset, offset + pair_lanes)
        for tokens_ref, rows_t, weights, start in (ahead, behind):
            scaled = []
            for head in (2 * pair, 2 * pair + 1):
                scaled += halves(rows_t * weights[head : head + 1, :])
            product = mul(jnp.concatenate(scaled, axis=0), tokens_ref[:, span])
            early = product[0:state] + product[state : 2 * state]
            late = product[2 * state : 3 * state] + product[3 * state :]
            total = jnp.where(lane < head_width, early, late)
            message_ref[owner, start : start + state, here] = encode(total)
        message_ref[owner, 2 * state :, here] = fact[:, span]


def scan_kernel(message_ref, *rest):
    answer_ref, powers = rest[-2:]
    blocks, double, lanes = message_ref.shape
    state = (double - META) // 2
    top = 2.0**TOP_POWER

    def one(block, start, power_row, side, running, bound):
        facts = message_ref[block, 2 * state : double, :].astype(F32)
        decay = jnp.exp(facts[0:1] + facts[1:2] + facts[2:3])
        back = jnp.exp2(-facts[power_row : power_row + 1])
        power = power_for(bound)
        powers[side, pl.ds(block, 1), :] = power
        answer_ref[block, start : start + state, :] = encode(running * jnp.exp2(power))
        own = decode(message_ref[block, start : start + state, :]) * back
        return running * decay + own, bound * decay + top * back

    def both(block, carry):
        ahead, ahead_bound, behind, behind_bound = carry
        return one(block, 0, 3, 0, ahead, ahead_bound) + one(
            blocks - 1 - block, state, 4, 1, behind, behind_bound
        )

    zero, none = jnp.zeros((state, lanes), F32), jnp.zeros((1, lanes), F32)
    lax.fori_loop(0, blocks, both, (zero, none, zero, none), unroll=8)
    row = lax.broadcasted_iota(jnp.int32, (blocks, META, lanes), 1)
    ahead, behind = powers[0][:, None, :], powers[1][:, None, :]
    meta = jnp.where(row == 0, ahead, jnp.where(row == 1, behind, 0.0))
    answer_ref[:, 2 * state : double, :] = meta.astype(BF16)


def block_kernel(
    head_width,
    scale,
    first_head,
    waits,
    step_ref,
    cum_ref,
    write_ref,
    read_ref,
    x_ref,
    dy_ref,
    *rest,
):
    inner_ref, own_ref, within_ref, maps_ref = rest[waits : waits + 4]
    read_write, source, cum_rows, pair_sum, out_flow = rest[waits + 4 :]
    turn = pl.program_id(0)
    rows, lanes = x_ref.shape
    half = rows // 2
    heads = step_ref.shape[1]
    group = lanes // head_width

    @pl.when(turn == 0)
    def _():
        read_write[...] = scale * lax.dot_general(
            write_ref[...], read_ref[...], (((0,), (0,)), ((), ())), preferred_element_type=F32
        )
        source[...] = jnp.log(step_ref[...]) - cum_ref[...]
        cum_rows[...] = cum_ref[...].T
        pair_sum[...] = jnp.zeros_like(pair_sum)
        out_flow[...] = jnp.zeros_like(out_flow)
        own_ref[...] = jnp.zeros_like(own_ref)

    first = first_head + turn * group
    near = pltpu.roll(source[...], lax.rem(heads - first, heads), axis=1)
    near_cum = cum_rows[pl.ds(first, group), :]
    row = lax.broadcasted_iota(jnp.int32, (half, half), 0)
    col = lax.broadcasted_iota(jnp.int32, (half, half), 1)
    ahead = col >= row
    lane = lax.broadcasted_iota(jnp.int32, (half, 2 * head_width), 1)
    first_half = lane < head_width
    head_lane = lax.broadcasted_iota(jnp.int32, (half, heads), 1)
    flow_aa = read_write[0:half, 0:half]
    flow_ab = read_write[0:half, half:rows]
    flow_bb = read_write[half:rows, half:rows]
    sum_aa = jnp.zeros((half, half), F32)
    sum_ab = jnp.zeros((half, half), F32)
    sum_bb = jnp.zeros((half, half), F32)
    own_a = jnp.zeros((half, heads), F32)
    own_b = jnp.zeros((half, heads), F32)
    zero = jnp.zeros((half, 2 * head_width), BF16)
    flows = []
    for pair in range(group // 2):
        span = slice(pair * 2 * head_width, (pair + 1) * 2 * head_width)
        x_a, x_b = x_ref[0:half, span], x_ref[half:rows, span]
        dy_a, dy_b = dy_ref[0:half, span], dy_ref[half:rows, span]
        early_a, late_a = jnp.where(first_half, dy_a, zero), jnp.where(first_half, zero, dy_a)
        early_b, late_b = jnp.where(first_half, dy_b, zero), jnp.where(first_half, zero, dy_b)
        stack = jnp.concatenate([early_a, early_b, late_a, late_b], axis=0)
        stack_b = jnp.concatenate([early_b, late_b], axis=0)
        grad_a = mul_nt(x_a, stack)
        grad_b = mul_nt(x_b, stack_b)
        masks_a, masks_b = [], []
        for side in range(2):
            place = pair * 2 + side
            head = first + place
            from_a = near[0:half, place : place + 1]
            from_b = near[half:rows, place : place + 1]
            to_a = near_cum[place : place + 1, 0:half]
            to_b = near_cum[place : place + 1, half:rows]
            fade_aa = jnp.exp(jnp.where(ahead, to_a + from_a, -1e30))
            fade_ab = jnp.exp(to_b + from_a)
            fade_bb = jnp.exp(jnp.where(ahead, to_b + from_b, -1e30))
            weigh_aa = fade_aa * grad_a[:, side * rows : side * rows + half]
            weigh_ab = fade_ab * grad_a[:, side * rows + half : (side + 1) * rows]
            weigh_bb = fade_bb * grad_b[:, side * half : (side + 1) * half]
            sum_aa += weigh_aa
            sum_ab += weigh_ab
            sum_bb += weigh_bb
            masks_a += [(fade_aa * flow_aa).astype(BF16), (fade_ab * flow_ab).astype(BF16)]
            masks_b += [(fade_bb * flow_bb).astype(BF16)]
            pair_aa = weigh_aa * flow_aa
            pair_ab = weigh_ab * flow_ab
            pair_bb = weigh_bb * flow_bb
            flow_out = jnp.sum(pair_aa + pair_ab, axis=1, keepdims=True)
            own_a = jnp.where(head_lane == head, flow_out, own_a)
            flow_out = jnp.sum(pair_bb, axis=1, keepdims=True)
            own_b = jnp.where(head_lane == head, flow_out, own_b)
            flow_in = [
                jnp.sum(pair_aa, axis=0, keepdims=True),
                jnp.sum(pair_ab, axis=0, keepdims=True) + jnp.sum(pair_bb, axis=0, keepdims=True),
            ]
            flows.append(jnp.concatenate(flow_in, axis=1))
        inner_ref[0:half, span] = mul(jnp.concatenate(masks_a, axis=1), stack).astype(BF16)
        inner_ref[half:rows, span] = mul(jnp.concatenate(masks_b, axis=1), stack_b).astype(BF16)
    out_flow[pl.ds(first, group), :] = jnp.concatenate(flows, axis=0)
    pair_sum[0:half, 0:half] += sum_aa
    pair_sum[0:half, half:rows] += sum_ab
    pair_sum[half:rows, half:rows] += sum_bb
    own_ref[0:half, :] += own_a
    own_ref[half:rows, :] += own_b

    @pl.when(turn == pl.num_programs(0) - 1)
    def _():
        net = own_ref[...] - out_flow[...].T
        within_ref[...] = mul_exact(triangle(rows, lambda r, c: r > c), net)
        weighted = scale * pair_sum[...]
        maps_ref[...] = jnp.concatenate(
            [
                mul_exact(weighted, read_ref[...].astype(F32), ((1,), (1,))),
                mul_exact(weighted, write_ref[...].astype(F32), ((0,), (1,))),
            ],
            axis=1,
        )


def spread_heads(weight, first_head, picks, group):
    heads = weight.shape[1]
    near = pltpu.roll(weight, lax.rem(heads - first_head, heads), axis=1)
    top = near.astype(BF16).astype(F32)
    low = pltpu.roll(near - top, group, axis=1)
    lane = lax.broadcasted_iota(jnp.int32, near.shape, 1)
    return mul(jnp.where(lane < group, top, low).astype(BF16), picks)


def spread_picks(group, heads, lanes, head_width):
    row = lax.broadcasted_iota(jnp.int32, (heads, lanes), 0)
    lane = lax.broadcasted_iota(jnp.int32, (heads, lanes), 1)
    match = jnp.where(row < group, row, row - group) == lane // head_width
    return jnp.where(match, 1.0, 0.0).astype(BF16)


def read_answer(answer_ref, state, power_row):
    found = []
    start = power_row * state
    for piece in range(answer_ref.shape[0]):
        facts = answer_ref[piece, 2 * state :, :].astype(F32)
        back = jnp.exp2(-facts[power_row : power_row + 1])
        found.append(decode(answer_ref[piece, start : start + state, :]) * back)
    return jnp.concatenate(found, axis=1)


def carry_kernel(head_width, scale, waits, *refs):
    raw_ref, bias_ref, decay_ref, step_ref, cum_ref, write_ref, read_ref = refs[:7]
    own_ref, within_ref, map_ref, x_ref, dy_ref, answer_ref = refs[7:13]
    table_ref, sums, through, weight_e, weight_s, maps, picks = refs[13 + waits :]
    turn = pl.program_id(0)
    rows, lanes = x_ref.shape
    heads = step_ref.shape[1]
    state = write_ref.shape[0]
    group = lanes // head_width
    pair_lanes = 2 * head_width
    future, past = slice(0, heads), slice(heads, 2 * heads)
    write_sum = slice(2 * heads, 2 * heads + 2 * state)
    read_sum = slice(2 * heads + 2 * state, 2 * heads + 4 * state)

    @pl.when(turn == 0)
    def _():
        cum = cum_ref[...]
        finish = cum[rows - 1 : rows, :]
        weight_e[...] = step_ref[...] * jnp.exp(finish - cum) * scale
        weight_s[...] = jnp.exp(cum) * scale
        write, read = write_ref[...].astype(F32).T, read_ref[...].astype(F32).T
        maps[...] = jnp.concatenate([write, write, read, read], axis=1)
        picks[0:heads, :] = spread_picks(group, heads, lanes, head_width)
        picks[heads:, :] = head_selector(0, heads, lanes, head_width)
        sums[...] = jnp.zeros_like(sums)
        through[...] = jnp.zeros_like(through)

    first_here = turn * group
    pick = picks[heads:, :]
    early = lax.broadcasted_iota(jnp.int32, (state, pair_lanes), 1) < head_width
    none = jnp.zeros((state, pair_lanes), BF16)
    start = read_answer(answer_ref, state, 0)
    end = read_answer(answer_ref, state, 1)

    def products(tokens_ref, states, weight, map_columns):
        spread = spread_heads(weight[...], first_here, picks[0:heads, :], group)
        parts = halves(states)
        total, mapped = 0.0, []
        for pair in range(group // 2):
            span = slice(pair * pair_lanes, (pair + 1) * pair_lanes)
            blocks = [
                jnp.concatenate(
                    [jnp.where(early, part[:, span], none), jnp.where(early, none, part[:, span])],
                    axis=0,
                )
                for part in parts
            ]
            twice = jnp.concatenate([tokens_ref[:, span], tokens_ref[:, span]], axis=1)
            weighted = mul_nt(twice, jnp.concatenate(blocks, axis=1)) * spread[:, span]
            total += weighted
            mapped.append((weighted * map_columns).astype(BF16))
        return total, mapped

    def summed(parts):
        return mul_nt(jnp.concatenate(parts, axis=1), pick)

    def placed(value):
        return pltpu.roll(value, first_here, axis=1)

    total, mapped = products(x_ref, end, weight_e, maps[:, 0 : 2 * state])
    sums[:, write_sum] += total
    sums[:, future] += placed(summed(mapped))

    total, mapped = products(dy_ref, start, weight_s, maps[:, 2 * state : 4 * state])
    sums[:, read_sum] += total
    sums[:, past] += placed(summed(mapped))

    both = jnp.broadcast_to(jnp.sum(start * end, axis=0, keepdims=True), (8, lanes))
    top, low = halves(both)
    through[...] += placed(mul_nt(top, pick) + mul_nt(low, pick))

    @pl.when(turn == pl.num_programs(0) - 1)
    def _():
        rate = -jnp.exp(decay_ref[...])
        step = step_ref[...]
        gate = jax.nn.sigmoid(raw_ref[...].astype(F32) + bias_ref[...])
        finish = cum_ref[rows - 1 : rows, :]
        ahead = sums[:, future]
        decay_grad = (
            within_ref[...]
            + mul_exact(triangle(rows, lambda r, c: r <= c), sums[:, past])
            + mul_exact(triangle(rows, lambda r, c: r > c), ahead)
            + jnp.exp(finish) * scale * through[0:1, :]
        )
        ratio = jnp.where(step > 1e-30, gate / jnp.maximum(step, 1e-30), 1.0)
        raw_grad = (own_ref[...] + ahead) * ratio + rate * decay_grad * gate
        map_sum = sums[:, 2 * heads :]
        write_all = map_sum[:, 0:state] + map_sum[:, state : 2 * state]
        read_all = map_sum[:, 2 * state : 3 * state] + map_sum[:, 3 * state :]
        map_grad = jnp.concatenate([write_all, read_all], axis=1) + map_ref[...]
        table_ref[...] = jnp.concatenate([raw_grad.T, map_grad.T], axis=0).astype(BF16)


def grad_setup_kernel(scale, step_ref, cum_ref, write_ref, *rest):
    weight_ref, maps_ref = rest[-2:]
    cum = cum_ref[...]
    finish = cum[cum.shape[0] - 1 :, :]
    weight_ref[...] = step_ref[...] * jnp.exp(finish - cum) * scale
    write = write_ref[...].astype(F32).T.astype(BF16)
    maps_ref[...] = jnp.concatenate([write, write], axis=1)


def grad_kernel(head_width, *refs):
    weight_ref, maps_ref, skip_ref, dy_ref, inner_ref, answer_ref = refs[:6]
    grad_ref, picks = refs[-2:]
    turn = pl.program_id(0)
    lanes = dy_ref.shape[1]
    heads = skip_ref.shape[1]
    state = maps_ref.shape[1] // 2
    group = lanes // head_width

    @pl.when(turn == 0)
    def _():
        picks[...] = spread_picks(group, heads, lanes, head_width)

    first_here = turn * group
    end_parts = jnp.concatenate(halves(read_answer(answer_ref, state, 1)), axis=0)
    skip = jnp.broadcast_to(skip_ref[...], (16, heads))
    skip = spread_heads(skip, first_here, picks[...], group)[0:1]
    spread = spread_heads(weight_ref[...], first_here, picks[...], group)
    carried = mul(maps_ref[...], end_parts) * spread
    inner = inner_ref[...].astype(F32)
    grad_ref[...] = (inner + skip * dy_ref[...].astype(F32) + carried).astype(BF16)


def deal_kernel(place_ref, layer_ref, after_ref, *out_refs):
    width = out_refs[0].shape[2]
    for turn, out_ref in enumerate(out_refs):
        start = pl.multiple_of((place_ref[0] ^ turn) * width, width)
        out_ref[0, :, :] = layer_ref[:, pl.ds(start, width)]


def product_kernel(planes, wide, place_ref, *refs):
    table_refs, layer_refs = refs[:wide], refs[wide : 2 * wide]
    out_refs = refs[-3 - planes : -3]
    table_all, layer_all, sems = refs[-3:]
    columns, rows = table_refs[0].shape
    loads = [
        pltpu.make_async_copy(ref, table_all.at[turn], sems.at[planes, turn])
        for turn, ref in enumerate(table_refs)
    ]
    for plane in range(planes):
        source = place_ref[1] ^ plane
        loads += [
            pltpu.make_async_copy(
                ref.at[source], layer_all.at[plane, pl.ds(turn * rows, rows)], sems.at[plane, turn]
            )
            for turn, ref in enumerate(layer_refs)
        ]
    for load in loads:
        load.start()
    for load in loads[:wide]:
        load.wait()
    table = jnp.concatenate([table_all[turn] for turn in range(wide)], axis=1)
    most = jnp.max(jnp.abs(table.astype(F32)), axis=0, keepdims=True)
    most = jnp.max(most, axis=1, keepdims=True)
    power = power_for(LAYER_BOUND * wide * rows * most)
    forth = jnp.exp2(power)
    for plane, out_ref in enumerate(out_refs):
        for load in loads[(plane + 1) * wide : (plane + 2) * wide]:
            load.wait()
        out_ref[0:columns, :] = encode(mul(table, layer_all[plane]) * forth)
        out_ref[columns:, :] = jnp.broadcast_to(power, out_ref[columns:, :].shape).astype(BF16)


def gather_kernel(factor, planes, *refs):
    part_refs, out_ref = refs[:planes], refs[-1]
    columns = out_ref.shape[1]
    total = jnp.zeros((columns, out_ref.shape[0]), F32)
    for part_ref in part_refs:
        power = part_ref[columns:, :].astype(F32)[0:1]
        total += decode(part_ref[0:columns, :]) * jnp.exp2(-power)
    out_ref[...] = (total * factor).T


def swap(array, axis, turn):
    if turn == 0:
        return array
    count = lax.axis_size(axis)
    return lax.ppermute(array, axis, [(one, one ^ turn) for one in range(count)])


def whole(shape):
    return pl.BlockSpec(shape, lambda i: (0,) * len(shape))


def call(kernel, steps, in_specs, out, scratch, aliases=None):
    return pl.pallas_call(
        kernel,
        grid=(steps,),
        in_specs=in_specs,
        out_specs=[spec for spec, _, _ in out],
        out_shape=[jax.ShapeDtypeStruct(dims, dtype) for _, dims, dtype in out],
        scratch_shapes=[pltpu.VMEM(dims, dtype) for dims, dtype in scratch],
        compiler_params=pltpu.CompilerParams(vmem_limit_bytes=VMEM_LIMIT),
        cost_estimate=SHORT,
        input_output_aliases=aliases or {},
    )


def body(
    layer_input,
    head_inputs,
    output_grad,
    step_raw,
    state_write,
    state_read,
    decay_log,
    step_bias,
    skip_gain,
):
    rows, channels = head_inputs.shape
    heads = step_raw.shape[1]
    head_width = channels // heads
    state = state_write.shape[1]
    model = layer_input.shape[1]
    columns = heads + 2 * state
    axes = ("wide", "seq")
    wide, planes = lax.axis_size("wide"), lax.axis_size("seq")
    blocks = wide * planes
    own_model = model // blocks
    scale = float(rows * blocks * state) ** -0.5
    owner_lanes = channels // blocks
    piece_lanes = max(owner_lanes, 128)
    pieces = channels // piece_lanes
    depth = 2 * state + META
    bias = step_bias[None, :]
    decay = decay_log[None, :]
    skip = skip_gain[None, :]
    write_t, read_t = state_write.T, state_read.T

    summary_lanes = SUMMARY_HEADS * head_width
    carry_lanes = CARRY_HEADS * head_width
    grad_lanes = GRAD_HEADS * head_width

    def tokens(width, first=0):
        return pl.BlockSpec((rows, width), lambda i: (0, first + i))

    def messages(width, first=0):
        return pl.BlockSpec((width // piece_lanes, depth, piece_lanes), lambda i: (first + i, 0, 0))

    head_spec = whole((rows, heads))
    line_spec = whole((1, heads))
    map_spec = whole((state, rows))
    head_out = (head_spec, (rows, heads), F32)

    def exchange(array):
        return lax.all_to_all(array, axes, split_axis=0, concat_axis=0, tiled=True)

    def to_owner(array):
        if owner_lanes < piece_lanes:
            split = array.reshape(pieces, depth, piece_lanes // owner_lanes, owner_lanes)
            array = jnp.moveaxis(split, 2, 1).reshape(blocks, depth, owner_lanes)
        return exchange(array)

    def from_owner(array):
        array = exchange(array)
        if owner_lanes < piece_lanes:
            split = array.reshape(pieces, piece_lanes // owner_lanes, depth, owner_lanes)
            array = jnp.moveaxis(split, 1, 2).reshape(pieces, depth, piece_lanes)
        return array

    with jax.named_scope("summaries"):
        message, step, cum = call(
            functools.partial(summary_kernel, head_width),
            channels // summary_lanes,
            [head_spec, line_spec, line_spec, map_spec, map_spec]
            + [tokens(summary_lanes), tokens(summary_lanes)],
            [
                (messages(summary_lanes), (pieces, depth, piece_lanes), BF16),
                head_out,
                head_out,
            ],
            [((heads, rows), F32), ((heads, rows), F32), ((META, heads), BF16)],
        )(step_raw, bias, decay, write_t, read_t, head_inputs, output_grad)
    place = jnp.stack([lax.axis_index("wide"), lax.axis_index("seq")]).astype(jnp.int32)
    with jax.named_scope("layer"):
        if own_model % 128:
            cut = jnp.transpose(layer_input.reshape(rows, planes, wide, own_model), (2, 1, 0, 3))
            dealt = [
                lax.dynamic_index_in_dim(cut, place[0] ^ turn, 0, False) for turn in range(wide)
            ]
        else:
            dealt = pl.pallas_call(
                deal_kernel,
                grid_spec=pltpu.PrefetchScalarGridSpec(
                    num_scalar_prefetch=1,
                    grid=(planes,),
                    in_specs=[
                        pl.BlockSpec((rows, wide * own_model), lambda i, p: (0, i)),
                        pl.BlockSpec(memory_space=pl.ANY),
                    ],
                    out_specs=[pl.BlockSpec((1, rows, own_model), lambda i, p: (i, 0, 0))] * wide,
                ),
                out_shape=[jax.ShapeDtypeStruct((planes, rows, own_model), BF16)] * wide,
                compiler_params=pltpu.CompilerParams(vmem_limit_bytes=VMEM_LIMIT),
                cost_estimate=SHORT,
            )(place, layer_input, cum)
        layer_parts = [swap(one, "wide", turn) for turn, one in enumerate(dealt)]

    anywhere = pl.BlockSpec(memory_space=pltpu.HBM)
    firsts = [turn for turn in (1, 2, 4, 3, 5) if turn < wide]
    lasts = [layer_parts[turn] for turn in range(1, wide) if turn not in firsts]
    lasts, latest = lasts[:-1], lasts[-1:]
    with jax.named_scope("own_block"):
        width = PAIR_HEADS * head_width
        inner, own, within, maps = call(
            functools.partial(block_kernel, head_width, scale, 0, 1),
            channels // width,
            [head_spec, head_spec, map_spec, map_spec, tokens(width), tokens(width), anywhere],
            [
                (tokens(width), (rows, channels), BF16),
                head_out,
                head_out,
                (whole((rows, 2 * state)), (rows, 2 * state), F32),
            ],
            [
                ((rows, rows), F32),
                ((rows, heads), F32),
                ((heads, rows), F32),
                ((rows, rows), F32),
                ((heads, rows), F32),
            ],
        )(step, cum, write_t, read_t, head_inputs, output_grad, dealt[0])
    with jax.named_scope("scan"):
        after = [own] + [layer_parts[turn] for turn in firsts]
        scan_lanes = min(owner_lanes, 128)
        scan_spec = pl.BlockSpec((blocks, depth, scan_lanes), lambda i: (0, 0, i))
        (answer,) = call(
            scan_kernel,
            owner_lanes // scan_lanes,
            [scan_spec] + [anywhere] * len(after),
            [(scan_spec, (blocks, depth, owner_lanes), BF16)],
            [((2, blocks, scan_lanes), F32)],
        )(to_owner(message), *after)
        returned = from_owner(answer)

    with jax.named_scope("carried"):
        (table,) = call(
            functools.partial(carry_kernel, head_width, scale, len(lasts)),
            channels // carry_lanes,
            [head_spec, line_spec, line_spec, head_spec, head_spec, map_spec, map_spec]
            + [head_spec, head_spec, whole((rows, 2 * state))]
            + [tokens(carry_lanes), tokens(carry_lanes), messages(carry_lanes)]
            + [anywhere] * len(lasts),
            [(whole((columns, rows)), (columns, rows), BF16)],
            [
                ((rows, 2 * heads + 4 * state), F32),
                ((8, heads), F32),
                ((rows, heads), F32),
                ((rows, heads), F32),
                ((rows, 4 * state), F32),
                ((2 * heads, carry_lanes), BF16),
            ],
        )(
            *(step_raw, bias, decay, step, cum, write_t, read_t, own, within, maps),
            *(head_inputs, output_grad, returned, *lasts),
        )

    with jax.named_scope("grad_x"):
        grad_maps = whole((rows, 2 * state))
        grad_weight, grad_map = call(
            functools.partial(grad_setup_kernel, scale),
            1,
            [head_spec, head_spec, map_spec] + [anywhere] * (1 + len(latest)),
            [head_out, (grad_maps, (rows, 2 * state), BF16)],
            [],
        )(step, cum, write_t, table, *latest)

    with jax.named_scope("projection"):
        tables = [table]
        for turn in range(1, wide):
            tables.append(swap(tables[turn - 1], "wide", 1) if turn % 2 else swap(table, "wide", turn))
        coded = (columns + META, own_model)
        products = pl.pallas_call(
            functools.partial(product_kernel, planes, wide),
            in_specs=[pl.BlockSpec(memory_space=pltpu.SMEM)] + [anywhere] * (2 * wide + 1),
            out_specs=[pl.BlockSpec(memory_space=pltpu.VMEM)] * planes,
            out_shape=[jax.ShapeDtypeStruct(coded, BF16)] * planes,
            scratch_shapes=[
                pltpu.VMEM((wide, columns, rows), BF16),
                pltpu.VMEM((planes, wide * rows, own_model), BF16),
                pltpu.SemaphoreType.DMA((planes + 1, wide)),
            ],
            compiler_params=pltpu.CompilerParams(vmem_limit_bytes=VMEM_LIMIT),
            cost_estimate=SHORT,
        )(place, *tables, *layer_parts, grad_weight)
        (grad_x,) = call(
            functools.partial(grad_kernel, head_width),
            channels // grad_lanes,
            [head_spec, grad_maps, line_spec, tokens(grad_lanes), tokens(grad_lanes)]
            + [messages(grad_lanes), anywhere],
            [(tokens(grad_lanes), (rows, channels), BF16)],
            [((heads, grad_lanes), BF16)],
        )(grad_weight, grad_map, skip, output_grad, inner, returned, products[0])
        sums = [swap(one, "seq", turn) for turn, one in enumerate(products)]
        (weight_grad,) = call(
            functools.partial(gather_kernel, 1.0 / math.sqrt(rows * blocks), planes),
            1,
            [whole(coded)] * planes + [anywhere],
            [(whole((own_model, columns)), (own_model, columns), F32)],
            [],
        )(*sums, grad_x)
    return grad_x, weight_grad


def solution(mesh):
    in_specs = (
        P(("wide", "seq"), None),
        P(("wide", "seq"), None),
        P(("wide", "seq"), None),
        P(("wide", "seq"), None),
        P(("wide", "seq"), None),
        P(("wide", "seq"), None),
        P(),
        P(),
        P(),
    )
    out_specs = (P(("wide", "seq"), None), P(("seq", "wide"), None))
    return jax.shard_map(body, mesh=mesh, in_specs=in_specs, out_specs=out_specs, check_vma=False)
```
